32 devices in a mesh: groups: 2 (over y), scan: 16 (over z, x, core).
Axes of the slice: x: 2, y: 2, z: 4, core: 2. Of those that a mesh axis runs over, the one named last changes fastest.
Arguments:
- object_tiles: float32 [32, 4, 128, 1024], P(('groups', 'scan')), parts along dimension 0, may hold values from -4.2 to 4.2
- probe: float32 [4, 256, 256], P('groups'), parts along dimension 0, may hold values from -4.2 to 4.2
- measured: bfloat16 [192, 256, 256], P(('groups', 'scan')), parts along dimension 0, may hold values from 0 to 2
- positions: int32 [32, 6, 2], P('groups'), parts along dimension 0, may hold values from 0 to 240, as said below
- counts: int32 [32], P('groups'), parts along dimension 0, may hold values from 1 to 6, 32 in all
- owner_map: int32 [16], replicated, may hold values from 0 to 15, each once
Outputs:
- object_grad: float32 [32, 4, 128, 1024], P(('groups', 'scan')), parts along dimension 0
- probe_grad: float32 [4, 256, 256], P('groups'), parts along dimension 0
The draws below stay inside these ranges and needn't reach their ends.
There are 2 independent parts, one for each index of `groups`. The reference program is written for one: setup_inputs(seed, part) draws one part's arguments, and reference() takes and returns one part's arrays. A program takes and returns all parts, laid end to end along the dimension named above; an argument that names none is the same for every part. Nothing has to cross between parts.
Inputs may be any that keep to these rules, and one draw needn't show every extreme that they name: positions[j, k] = (row, column) of the top-left tile of scan owner j's slot k; the window of 16 x 16 tiles lies inside the 32 x 256 grid: rows at most 16, columns at most 240. Scan owner j's live patterns are its first counts[j] slots; the counts sum to exactly 32. `owner_map`: a permutation.
All inputs are finite; a program needn't handle non-finite values.
Results may differ from the reference program's by a relative error of at most 0.0003.
Values may be sent and summed in bfloat16 or wider, within the bound.
No kernel may reach another device: no remote copies, remote signals or barrier semaphores. Data moves between devices by JAX's collectives and lax.ppermute only.
A program may use at most 256 MiB of HBM per device.

```python
import math
import jax
import jax.numpy as jnp
import numpy as np
from jax import lax

WIN = 256
TILE = 16
SLICES = 2
MEAN = 2
TLR = 4
TLC = 128
CAP = 6
WT = 16
PLANE = 1024
GR = 32
GC = 256
PATTERNS = 96
N_SCAN = 16


def draw_positions(key, part):
    key = jax.random.fold_in(key, 11)
    row_key, col_key, pick_key = jax.random.split(key, 3)
    row_starts = jax.random.randint(row_key, (N_SCAN, CAP), 0, GR - WT + 1)
    col_starts = jax.random.randint(col_key, (N_SCAN, CAP), 0, GC - WT + 1)
    chosen = jax.random.randint(pick_key, (), 0, N_SCAN)
    row_starts = row_starts.at[chosen, 0].set(GR - WT).at[chosen, 1].set(0)
    col_starts = col_starts.at[chosen, 0].set(GC - WT).at[chosen, 1].set(0)
    return jnp.stack([row_starts, col_starts], axis=2).astype(jnp.int32)


def level_of(key, shape, cuts, low, top_value):
    def one(position, shards_of):
        draws = jax.random.uniform(jax.random.fold_in(jax.random.fold_in(key, 6), position), (shards_of,), jnp.float32, low / len(cuts), top_value / len(cuts))
        return jnp.repeat(jnp.exp(draws), shape[position] // shards_of).reshape((-1,) + (1,) * (len(shape) - position - 1))

    loudness = one(*cuts[0])
    for cut in cuts[1:]:
        loudness = loudness * one(*cut)
    return loudness


def split_up(count, total, reach, slope):
    portions = [(1 << 20) // math.isqrt(standing ** slope) + 1 for standing in range(2, count + 1)]
    rest, given = total - reach - (count - 1), [1] * (count - 1)
    while rest > 0:
        free = [i for i in range(count - 1) if given[i] < reach]
        whole, remaining = sum([portions[i] for i in free]), rest
        for i in free:
            more = min(reach - given[i], max(1, remaining * portions[i] // whole), rest)
            given[i] = given[i] + more
            rest = rest - more
    return np.array([reach] + given)


def ragged(rng, number_of, total, bound, slope):
    if number_of == 2:
        one = jax.random.randint(rng, (), max(1, total - bound), min(bound, total - 1) + 1)
        return jnp.stack([one, total - one])
    lengths = jnp.asarray(split_up(number_of, total, bound, slope), jnp.int32)
    couples = (number_of - 1) // 2
    donor, sink = lengths[1:1 + 2 * couples:2], lengths[2:2 + 2 * couples:2]
    slack = jnp.minimum(donor - 1, bound - sink)
    shifted = jax.random.randint(jax.random.fold_in(rng, 1), (couples,), 0, 1 << 20) % (slack + 1)
    lengths = lengths.at[1:1 + 2 * couples:2].set(donor - shifted).at[2:2 + 2 * couples:2].set(sink + shifted)
    return lengths[jax.random.permutation(jax.random.fold_in(rng, 2), number_of)]


def bell_draw(rng, dims, scale, limit, cuts=(), held_as=jnp.bfloat16):
    values = jax.random.normal(rng, dims, jnp.float32) * scale
    if len(cuts) > 0:
        values = level_of(rng, dims, cuts, -0.22, 0.18) * values
    return jnp.clip(values, min=-limit, max=limit).astype(held_as)


def setup_inputs(seed: int = 0, part: int = 0) -> dict:
    seeds = jax.random.split(jax.random.key(seed), 7)
    part_keys = jax.random.split(jax.random.fold_in(seeds[6], part), 7)
    object_tiles = bell_draw(part_keys[0], (N_SCAN, TLR, TLC, PLANE), 0.7, 4.2, ((0, 16),), jnp.float32)
    probe = bell_draw(part_keys[1], (2, WIN, WIN), 0.7, 4.2, (), jnp.float32)
    measured = jnp.clip(2.0 * jax.random.uniform(part_keys[2], (PATTERNS, WIN, WIN), jnp.float32) ** level_of(part_keys[2], (PATTERNS, WIN, WIN), ((0, 16),), -0.2, 0.2), 0.0, 2.0).astype(jnp.bfloat16)
    positions = draw_positions(jax.random.fold_in(jax.random.fold_in(seeds[6], part), 71), part)
    counts = ragged(part_keys[4], N_SCAN, N_SCAN * MEAN, CAP, 2).astype(jnp.int32)
    owner_map = jax.random.permutation(seeds[5], N_SCAN).astype(jnp.int32)
    return {"object_tiles": object_tiles, "probe": probe, "measured": measured, "positions": positions, "counts": counts, "owner_map": owner_map}


chirp_scale = 1.5


def propagator():
    iota_range = lax.iota(jnp.int32, WIN)
    frequency = ((iota_range + WIN // 2) % WIN - WIN // 2).astype(jnp.float32) / (WIN // 2)
    phases = chirp_scale * (frequency[:, None] ** 2 + frequency[None, :] ** 2)
    return jnp.cos(phases), -jnp.sin(phases)


def to_window(tile_block):
    slot_count = tile_block.shape[0]
    across = WIN // TILE
    shaped = tile_block.reshape(slot_count, across, across, SLICES, 2, TILE, TILE)
    shaped = shaped.transpose(0, 3, 4, 1, 5, 2, 6)
    return shaped.reshape(slot_count, SLICES, 2, WIN, WIN)


def to_tiles(window):
    slot_count = window.shape[0]
    across = WIN // TILE
    shaped = window.reshape(slot_count, SLICES, 2, across, TILE, across, TILE)
    shaped = shaped.transpose(0, 3, 5, 1, 2, 4, 6)
    return shaped.reshape(slot_count, across, across, SLICES * 2 * TILE * TILE)


def reference(object_tiles, probe, measured, positions, counts, owner_map):
    columns = N_SCAN // 8
    across = WIN // TILE
    by_class = jnp.take(object_tiles, owner_map, axis=0)
    tile_grid = by_class.reshape(8, columns, TLR, TLC, PLANE).transpose(2, 0, 3, 1, 4).reshape(GR, GC, PLANE)
    prop_re, prop_im = propagator()
    propagate = lax.complex(prop_re, prop_im)
    probe_wave = lax.complex(probe[0], probe[1])
    live_flags = (lax.iota(jnp.int32, CAP)[None, :] < counts[:, None]).astype(jnp.float32).reshape(-1)
    corners = positions.reshape(-1, 2)

    def visit_slot(state_pair, slot_item):
        grid_grad, probe_grad = state_pair
        corner, intensity, weight = slot_item
        corner_start = (corner[0], corner[1], jnp.int32(0))
        tile_block = lax.dynamic_slice(tile_grid, corner_start, (across, across, PLANE))
        window = to_window(tile_block[None])[0]
        front_slab = lax.complex(window[0, 0], window[0, 1])
        back_slab = lax.complex(window[1, 0], window[1, 1])
        entrance = probe_wave * front_slab
        middle = jnp.fft.ifft2(propagate * jnp.fft.fft2(entrance, norm="ortho"), norm="ortho")
        exit_wave = middle * back_slab
        far_field = jnp.fft.fft2(exit_wave, norm="ortho")
        misfit = (jnp.real(far_field) ** 2 + jnp.imag(far_field) ** 2 - intensity.astype(jnp.float32)) * weight
        near_field = jnp.fft.ifft2(misfit * far_field, norm="ortho")
        grad_back = jnp.conj(middle) * near_field
        grad_middle = jnp.conj(back_slab) * near_field
        grad_enter = jnp.fft.ifft2(jnp.conj(propagate) * jnp.fft.fft2(grad_middle, norm="ortho"), norm="ortho")
        grad_front = jnp.conj(probe_wave) * grad_enter
        grad_probe = jnp.conj(front_slab) * grad_enter
        stacked = jnp.stack([jnp.stack([jnp.real(grad_front), jnp.imag(grad_front)]),
                             jnp.stack([jnp.real(grad_back), jnp.imag(grad_back)])])
        tiles_grad = to_tiles(stacked[None])[0]
        current = lax.dynamic_slice(grid_grad, corner_start, (across, across, PLANE))
        grid_grad = lax.dynamic_update_slice(grid_grad, current + tiles_grad, corner_start)
        probe_grad = probe_grad + jnp.stack([jnp.real(grad_probe), jnp.imag(grad_probe)])
        return (grid_grad, probe_grad), None

    start_pair = (jnp.zeros((GR, GC, PLANE), jnp.float32), jnp.zeros((2, WIN, WIN), jnp.float32))
    (grid_grad, probe_grad), unused = lax.scan(visit_slot, start_pair, (corners, measured, live_flags))
    grad_class = grid_grad.reshape(TLR, 8, TLC, columns, PLANE).transpose(1, 3, 0, 2, 4).reshape(N_SCAN, TLR, TLC, PLANE)
    object_grad = jnp.zeros_like(object_tiles).at[owner_map].set(grad_class)
    return object_grad, probe_grad
```

```python
import functools
import math

import jax
import jax.numpy as jnp
import numpy as np
from jax import lax
from jax.experimental import pallas as pl
from jax.experimental.pallas import tpu as pltpu
from jax.sharding import PartitionSpec as P

WIN = 256
TILE = 16
ACROSS = WIN // TILE
SLICES = 2
MEAN = 2
CAP = 6
CHIRP = 1.5
HALF = SLICES * TILE * TILE
LANES = 128
BLOCKS = HALF // LANES
SCALE_ROWS = 8
STEPS = 32.0
LEVELS = 32700.0
LN2 = math.log(2.0)

f32 = jnp.float32
i32 = jnp.int32
bf16 = jnp.bfloat16
SMEM = pl.BlockSpec(memory_space=pltpu.SMEM)
VMEM = pl.BlockSpec(memory_space=pltpu.VMEM)


class Geometry:
    def __init__(self, owners, grid_rows, grid_cols):
        self.owners = owners
        self.columns = owners // 8
        self.rows_a = ACROSS // 8
        self.cols_b = ACROSS // self.columns
        self.tiles = self.rows_a * self.cols_b
        self.grid_rows = grid_rows
        self.grid_cols = grid_cols
        self.piece = WIN // owners
        self.group = min(8, self.piece)
        self.block = -(-(BLOCKS * self.tiles + SCALE_ROWS) // 8) * 8
        self.probe_at = BLOCKS * self.tiles
        self.block_probe = -(-(self.probe_at + 2 * self.piece + SCALE_ROWS) // 8) * 8


def params(megabytes):
    return pltpu.CompilerParams(vmem_limit_bytes=megabytes << 20)


def tables():
    k = np.arange(16)
    root = np.exp(-2j * np.pi * np.outer(k, k) / 16) / 4
    kron = np.kron(root, root)

    def halves(x):
        hi = x.astype(np.float32).astype(jnp.bfloat16)
        lo = (x - hi.astype(np.float64)).astype(np.float32).astype(jnp.bfloat16)
        return hi, lo

    re_hi, re_lo = halves(kron.real)
    im_hi, im_lo = halves(kron.imag)
    hi = np.block([[re_hi, im_hi], [-im_hi, re_hi]])
    lo = np.block([[re_lo, im_lo], [-im_lo, re_lo]])
    right = np.concatenate([hi, hi, lo], axis=0)
    left = np.ascontiguousarray(right.T)
    low_u, low_v = np.divmod(np.arange(256), 16)
    twiddle = np.exp(
        -2j * np.pi * (np.outer(low_u, low_u) + np.outer(low_v, low_v)) / WIN
    )
    u = low_u[:, None] + 16 * low_u[None, :]
    v = low_v[:, None] + 16 * low_v[None, :]
    freq = lambda w: ((w + WIN // 2) % WIN - WIN // 2) / (WIN // 2)
    chirp = np.exp(-1j * CHIRP * (freq(u) ** 2 + freq(v) ** 2))
    pack = lambda z: np.stack([z.real, z.imag]).astype(np.float32)
    return left, right, pack(twiddle), pack(chirp)


def row_scale(x):
    peak = jnp.maximum(jnp.max(jnp.abs(x), axis=1, keepdims=True), 1e-30)
    return jnp.floor(jnp.log(peak) * (STEPS / LN2)) + 2.0


def encode(low, high):
    k_low, k_high = row_scale(low), row_scale(high)
    q_low = jnp.round(low * (jnp.exp(k_low * (-LN2 / STEPS)) * LEVELS)).astype(i32)
    q_high = jnp.round(high * (jnp.exp(k_high * (-LN2 / STEPS)) * LEVELS)).astype(i32)
    return (q_high << 16) | (q_low & 0xFFFF), k_low, k_high


def unscale(k):
    return jnp.exp(k.astype(f32) * (LN2 / STEPS)) * (1.0 / LEVELS)


def decode(words, k_low, k_high):
    low = ((words << 16) >> 16).astype(f32) * k_low
    high = (words >> 16).astype(f32) * k_high
    return low, high


def put_scales(scales, rows):
    lane = lax.broadcasted_iota(i32, (rows, LANES), 1)
    out = jnp.zeros((rows, LANES), f32)
    for i, k in enumerate(scales):
        out = jnp.where(lane == i, k, out)
    return out.astype(i32)


def plan_kernel(geo, counts_ref, positions_ref, plan_ref):
    n = geo.owners

    def spare(g):
        return jnp.maximum(counts_ref[g] - MEAN, 0)

    def body(o, carry):
        own = counts_ref[o] >= MEAN

        def behind(state):
            g, used = state
            return jnp.logical_and(
                jnp.logical_not(own),
                jnp.logical_and(used >= spare(g), g < n - 1),
            )

        g, used = lax.while_loop(behind, lambda state: (state[0] + 1, jnp.int32(0)), carry)
        dev = jnp.where(own, o, g)
        slot = jnp.where(own, 1, jnp.minimum(MEAN + used, CAP - 1))
        plan_ref[o] = positions_ref[o * CAP * 2]
        plan_ref[n + o] = positions_ref[o * CAP * 2 + 1]
        plan_ref[2 * n + o] = positions_ref[(dev * CAP + slot) * 2]
        plan_ref[3 * n + o] = positions_ref[(dev * CAP + slot) * 2 + 1]
        plan_ref[4 * n + o] = dev
        plan_ref[5 * n + o] = slot
        return g, jnp.where(own, used, used + 1)

    lax.fori_loop(0, n, body, (jnp.int32(0), jnp.int32(0)))


def make_plan(geo, counts, positions):
    return pl.pallas_call(
        functools.partial(plan_kernel, geo),
        out_shape=jax.ShapeDtypeStruct((6 * geo.owners,), i32),
        in_specs=[SMEM, SMEM],
        out_specs=SMEM,
        name="plan",
    )(counts, positions)


def first_row(geo, slot, o, plan_ref, mine_ref):
    n, columns = geo.owners, geo.columns
    row, col = plan_ref[2 * slot * n + o], plan_ref[(2 * slot + 1) * n + o]
    own_class = mine_ref[1]
    row = row + ((own_class // columns - row) & 7)
    col = col + ((own_class % columns - col) & (columns - 1))
    return (row // 8) * geo.grid_cols + col // columns


def gather_kernel(geo, slot, plan_ref, mine_ref, tiles_hbm, out_ref, tiles_ref, sems):
    b = geo.cols_b
    copies = [
        pltpu.make_async_copy(tiles_hbm.at[:, pl.ds(j * LANES, LANES)], tiles_ref.at[j], sems.at[j])
        for j in range(2 * BLOCKS)
    ]
    for copy in copies:
        copy.start()
    for copy in copies:
        copy.wait()

    def body(o, _):
        start = first_row(geo, slot, o, plan_ref, mine_ref)
        scales = []
        for a in range(geo.rows_a):
            x = [tiles_ref[j, pl.ds(start + a * geo.grid_cols, b), :] for j in range(2 * BLOCKS)]
            words, k_low, k_high = encode(
                jnp.concatenate(x[:BLOCKS], axis=1), jnp.concatenate(x[BLOCKS:], axis=1)
            )
            scales += [k_low, k_high]
            for j in range(BLOCKS):
                out_ref[o, pl.ds(j * geo.tiles + a * b, b), :] = words[:, j * LANES : (j + 1) * LANES]
        out_ref[o, pl.ds(BLOCKS * geo.tiles, b), :] = put_scales(scales, b)
        return 0

    lax.fori_loop(0, geo.owners, body, 0)


def gather_tiles(geo, slot, plan, mine, tiles):
    return pl.pallas_call(
        functools.partial(gather_kernel, geo, slot),
        out_shape=jax.ShapeDtypeStruct((geo.owners, geo.block, LANES), i32),
        in_specs=[SMEM, SMEM, pl.BlockSpec(memory_space=pl.ANY)],
        out_specs=VMEM,
        scratch_shapes=[
            pltpu.VMEM((2 * BLOCKS, geo.grid_rows * geo.grid_cols, LANES), f32),
            pltpu.SemaphoreType.DMA((2 * BLOCKS,)),
        ],
        compiler_params=params(32),
        cost_estimate=pl.CostEstimate(flops=1 << 23, bytes_accessed=4 << 20, transcendentals=0),
        name=f"gather{slot}",
    )(plan, mine, tiles)


def forward_kernel(geo, plan_ref, held_ref, out_ref):
    n = geo.owners

    def body(o, _):
        dev, slot = plan_ref[4 * n + o], plan_ref[5 * n + o]
        out_ref[o] = held_ref[dev, jnp.maximum(slot - MEAN, 0)]
        return 0

    lax.fori_loop(0, n, body, 0)


def choose_pieces(geo, plan, held):
    return pl.pallas_call(
        functools.partial(forward_kernel, geo),
        out_shape=jax.ShapeDtypeStruct((geo.owners,) + held.shape[2:], held.dtype),
        in_specs=[SMEM, VMEM],
        out_specs=VMEM,
        compiler_params=params(32),
        name="pieces",
    )(plan, held)


def swap_tile_digits(x):
    parts = x.reshape(16, 2, 8, WIN)
    grid = [[parts[:, r, :, c * LANES : (c + 1) * LANES].reshape(LANES, LANES) for c in range(2)] for r in range(2)]
    row = lax.broadcasted_iota(i32, (LANES, LANES), 0)
    lane = lax.broadcasted_iota(i32, (LANES, LANES), 1)

    def inner(q):
        for s in (4, 2, 1):
            shift = s * 16
            row_bit = (row & s) != 0
            lane_bit = (lane & shift) != 0
            rows = jnp.where(row_bit, pltpu.roll(q, s, 0), pltpu.roll(q, LANES - s, 0))
            both = jnp.where(lane_bit, pltpu.roll(rows, shift, 1), pltpu.roll(rows, LANES - shift, 1))
            q = jnp.where(row_bit == lane_bit, q, both)
        return q.reshape(16, 1, 8, LANES)

    upper = jnp.concatenate([inner(grid[0][0]), inner(grid[1][0])], axis=3)
    lower = jnp.concatenate([inner(grid[0][1]), inner(grid[1][1])], axis=3)
    return jnp.concatenate([upper, lower], axis=1).reshape(WIN, WIN)


def frequency_digits(x):
    turned = x.T
    lane = lax.broadcasted_iota(i32, (16, LANES), 1)
    halves = []
    for c in range(2):
        rows = [turned[16 * i : 16 * (i + 1), c * LANES : (c + 1) * LANES] for i in range(16)]
        for s in (1, 2, 4, 8):
            lane_bit = (lane & s) != 0
            new = list(rows)
            for i in range(16):
                if i & s == 0:
                    low, high = rows[i], rows[i | s]
                    new[i] = jnp.where(lane_bit, pltpu.roll(high, s, 1), low)
                    new[i | s] = jnp.where(lane_bit, high, pltpu.roll(low, LANES - s, 1))
            rows = new
        halves.append(jnp.concatenate(rows, axis=0))
    return jnp.concatenate(halves, axis=1)


def prepare_kernel(probe_ref, measured_ref, probe_out, measured_out):
    for c in range(2):
        probe_out[c] = swap_tile_digits(probe_ref[c])
    measured_out[0] = frequency_digits(measured_ref[0].astype(f32))


def prepare(probe, measured):
    return pl.pallas_call(
        prepare_kernel,
        out_shape=(
            jax.ShapeDtypeStruct((2, WIN, WIN), f32),
            jax.ShapeDtypeStruct((1, WIN, WIN), f32),
        ),
        grid=(1,),
        in_specs=[
            pl.BlockSpec((2, WIN, WIN), lambda i: (0, 0, 0)),
            pl.BlockSpec((1, WIN, WIN), lambda i: (0, 0, 0)),
        ],
        out_specs=(
            pl.BlockSpec((2, WIN, WIN), lambda i: (0, 0, 0)),
            pl.BlockSpec((1, WIN, WIN), lambda i: (0, 0, 0)),
        ),
        compiler_params=params(32),
        cost_estimate=pl.CostEstimate(flops=1 << 22, bytes_accessed=2 << 20, transcendentals=0),
        name="prepare",
    )(probe, measured)


def second_kernel(plan_ref, mine_ref, measured_ref, arrived_ref, out_ref, *, owners):
    own = plan_ref[4 * owners + mine_ref[0]] == mine_ref[0]
    x = jnp.where(own, measured_ref[0].astype(f32), arrived_ref[...].astype(f32))
    out_ref[0] = frequency_digits(x)


def second_pattern(geo, plan, mine, measured, arrived):
    return pl.pallas_call(
        functools.partial(second_kernel, owners=geo.owners),
        out_shape=jax.ShapeDtypeStruct((1, WIN, WIN), f32),
        grid=(1,),
        in_specs=[
            SMEM,
            SMEM,
            pl.BlockSpec((1, WIN, WIN), lambda i: (1, 0, 0)),
            pl.BlockSpec((WIN, WIN), lambda i: (0, 0)),
        ],
        out_specs=pl.BlockSpec((1, WIN, WIN), lambda i: (0, 0, 0)),
        compiler_params=params(32),
        cost_estimate=pl.CostEstimate(flops=1 << 22, bytes_accessed=1 << 20, transcendentals=0),
        name="second",
    )(plan, mine, measured, arrived)


def split(x):
    hi = x.astype(bf16)
    return hi, (x - hi.astype(f32)).astype(bf16)


def times_right(z, right_ref):
    re_hi, re_lo = split(z[0])
    im_hi, im_lo = split(z[1])
    data = jnp.concatenate([re_hi, im_hi, re_lo, im_lo, re_hi, im_hi], axis=1)
    out = jnp.dot(data, right_ref[...], preferred_element_type=f32)
    return out[:, :WIN], out[:, WIN:]


def times_left(z, left_ref):
    re_hi, re_lo = split(z[0])
    im_hi, im_lo = split(z[1])
    data = jnp.concatenate([re_hi, im_hi, re_lo, im_lo, re_hi, im_hi], axis=0)
    out = jnp.dot(left_ref[...], data, preferred_element_type=f32)
    return out[:WIN], out[WIN:]


def product(x, y):
    return x[0] * y[0] - x[1] * y[1], x[0] * y[1] + x[1] * y[0]


def product_conj(x, y):
    return x[0] * y[0] + x[1] * y[1], x[0] * y[1] - x[1] * y[0]


def conj(x):
    return x[0], -x[1]


def pattern_kernel(
    geo, slot, plan_ref, mine_ref, map_ref, in_ref, probe_ref, intensity_ref,
    left_ref, right_ref, twiddle_ref, chirp_ref, *rest
):
    if slot == 0:
        out_ref, total_ref, tile_ref = rest
    else:
        before_ref, out_ref, tile_ref = rest
    n, columns, b = geo.owners, geo.columns, geo.cols_b
    row = plan_ref[2 * slot * n + mine_ref[0]]
    col = plan_ref[(2 * slot + 1) * n + mine_ref[0]]

    def source(k):
        alpha, beta = k // columns, k % columns
        return map_ref[((row + alpha) & 7) * columns + ((col + beta) & (columns - 1))]

    def tile_rows(k, a):
        alpha, beta = k // columns, k % columns
        return pl.ds((8 * a + alpha) * ACROSS + beta, b, columns)

    def unpack(k, _):
        src = source(k)
        scales = unscale(in_ref[src, pl.ds(BLOCKS * geo.tiles, b), :])
        for a in range(geo.rows_a):
            k_low, k_high = scales[:, 2 * a : 2 * a + 1], scales[:, 2 * a + 1 : 2 * a + 2]
            for j in range(BLOCKS):
                words = in_ref[src, pl.ds(j * geo.tiles + a * b, b), :]
                low, high = decode(words, k_low, k_high)
                tile_ref[j, tile_rows(k, a), :] = low
                tile_ref[BLOCKS + j, tile_rows(k, a), :] = high
        return 0

    lax.fori_loop(0, n, unpack, 0)

    def plane(i):
        return jnp.concatenate([tile_ref[2 * i], tile_ref[2 * i + 1]], axis=1)

    def put_plane(i, x):
        tile_ref[2 * i] = x[:, :LANES]
        tile_ref[2 * i + 1] = x[:, LANES:]

    twiddle = lambda: (twiddle_ref[0], twiddle_ref[1])
    chirp = lambda: (chirp_ref[0], chirp_ref[1])
    probe = lambda: (probe_ref[0], probe_ref[1])
    front = lambda: (plane(0), plane(1))
    back = lambda: (plane(2), plane(3))

    def spectrum(z):
        return times_right(product(twiddle(), times_left(z, left_ref)), right_ref)

    def conj_inverse(z_conj):
        return times_left(product(twiddle(), times_right(z_conj, right_ref)), left_ref)

    entrance = product(probe(), front())
    middle_conj = conj_inverse(conj(product(chirp(), spectrum(entrance))))
    far = spectrum(product_conj(middle_conj, back()))
    misfit = far[0] * far[0] + far[1] * far[1] - intensity_ref[0]
    near_conj = conj_inverse((misfit * far[0], -(misfit * far[1])))
    grad_middle = conj(product(back(), near_conj))
    grad_back = product(middle_conj, conj(near_conj))
    enter_conj = conj_inverse(product_conj(spectrum(grad_middle), chirp()))
    enter = conj(enter_conj)
    grad_probe = product_conj(front(), enter)
    grad_front = product_conj(probe(), enter)
    put_plane(0, grad_front[0])
    put_plane(1, grad_front[1])
    put_plane(2, grad_back[0])
    put_plane(3, grad_back[1])

    def pack(k, _):
        dst = source(k)
        scales = []
        for a in range(geo.rows_a):
            x = [tile_ref[j, tile_rows(k, a), :] for j in range(2 * BLOCKS)]
            words, k_low, k_high = encode(
                jnp.concatenate(x[:BLOCKS], axis=1), jnp.concatenate(x[BLOCKS:], axis=1)
            )
            scales += [k_low, k_high]
            for j in range(BLOCKS):
                out_ref[dst, pl.ds(j * geo.tiles + a * b, b), :] = words[:, j * LANES : (j + 1) * LANES]
        at = geo.block_probe if slot else geo.block
        out_ref[dst, pl.ds(at - SCALE_ROWS, b), :] = put_scales(scales, b)
        return 0

    lax.fori_loop(0, n, pack, 0)
    if slot == 0:
        total_ref[0], total_ref[1] = grad_probe
        return
    tile_ref[0] = (before_ref[0] + grad_probe[0])[:, :LANES]
    tile_ref[1] = (before_ref[0] + grad_probe[0])[:, LANES:]
    tile_ref[2] = (before_ref[1] + grad_probe[1])[:, :LANES]
    tile_ref[3] = (before_ref[1] + grad_probe[1])[:, LANES:]
    g = geo.group
    lane = lax.broadcasted_iota(i32, (g, LANES), 1)

    def pieces(o, _):
        first = 2 * geo.rows_a
        scales = out_ref[o, pl.ds(geo.block_probe - SCALE_ROWS, g), :]
        for i in range(geo.piece // g):
            rows = pl.ds(o * geo.piece + i * g, g)
            x = [tile_ref[j, rows, :] for j in range(4)]
            words, k_low, k_high = encode(
                jnp.concatenate(x[:2], axis=1), jnp.concatenate(x[2:], axis=1)
            )
            scales = jnp.where(lane == first + 2 * i, k_low.astype(i32), scales)
            scales = jnp.where(lane == first + 2 * i + 1, k_high.astype(i32), scales)
            for j in range(2):
                at = geo.probe_at + j * geo.piece + i * g
                out_ref[o, pl.ds(at, g), :] = words[:, j * LANES : (j + 1) * LANES]
        out_ref[o, pl.ds(geo.block_probe - SCALE_ROWS, g), :] = scales
        return 0

    lax.fori_loop(0, n, pieces, 0)


def pattern(geo, slot, plan, mine, owner_map, incoming, probe, intensity, consts, before=None):
    rows = geo.block_probe if slot else geo.block
    out = jax.ShapeDtypeStruct((geo.owners, rows, LANES), i32)
    total = jax.ShapeDtypeStruct((2, WIN, WIN), f32)
    extra = () if slot == 0 else (before,)
    return pl.pallas_call(
        functools.partial(pattern_kernel, geo, slot),
        out_shape=(out, total) if slot == 0 else out,
        in_specs=[SMEM, SMEM, SMEM] + [VMEM] * (7 + len(extra)),
        out_specs=(VMEM, VMEM) if slot == 0 else VMEM,
        scratch_shapes=[pltpu.VMEM((2 * BLOCKS, WIN, LANES), f32)],
        compiler_params=params(48),
        cost_estimate=pl.CostEstimate(flops=13 << 30, bytes_accessed=8 << 20, transcendentals=0),
        name=f"pattern{slot}",
    )(plan, mine, owner_map, incoming, probe, intensity, *consts, *extra)


def add_kernel(geo, slot, plan_ref, mine_ref, in_ref, *rest):
    b = geo.cols_b
    if slot == 0:
        (grad_ref,) = rest
        grad_ref[...] = jnp.zeros_like(grad_ref)
        at = geo.block - SCALE_ROWS
    else:
        before_ref, grad_hbm, probe_ref, grad_ref, sems = rest
        grad_ref[...] = before_ref[...]
        at = geo.block_probe - SCALE_ROWS

    def body(o, _):
        start = first_row(geo, slot, o, plan_ref, mine_ref)
        scales = unscale(in_ref[o, pl.ds(at, b), :])
        for a in range(geo.rows_a):
            k_low, k_high = scales[:, 2 * a : 2 * a + 1], scales[:, 2 * a + 1 : 2 * a + 2]
            rows = pl.ds(start + a * geo.grid_cols, b)
            for j in range(BLOCKS):
                words = in_ref[o, pl.ds(j * geo.tiles + a * b, b), :]
                low, high = decode(words, k_low, k_high)
                grad_ref[j, rows, :] += low
                grad_ref[BLOCKS + j, rows, :] += high
        return 0

    lax.fori_loop(0, geo.owners, body, 0)
    if slot == 0:
        return
    copies = [
        pltpu.make_async_copy(grad_ref.at[j], grad_hbm.at[:, pl.ds(j * LANES, LANES)], sems.at[j])
        for j in range(2 * BLOCKS)
    ]
    for copy in copies:
        copy.start()
    g, first = geo.group, 2 * geo.rows_a

    def add_piece(o, sums):
        scales = unscale(in_ref[o, pl.ds(at, g), :])
        new = []
        for i in range(geo.piece // g):
            k_low = scales[:, first + 2 * i : first + 2 * i + 1]
            k_high = scales[:, first + 2 * i + 1 : first + 2 * i + 2]
            for j in range(2):
                words = in_ref[o, pl.ds(geo.probe_at + j * geo.piece + i * g, g), :]
                low, high = decode(words, k_low, k_high)
                new += [sums[len(new)] + low, sums[len(new) + 1] + high]
        return tuple(new)

    count = geo.piece // g * 4
    sums = lax.fori_loop(0, geo.owners, add_piece, (jnp.zeros((g, LANES), f32),) * count)
    for i in range(geo.piece // g):
        for j in range(2):
            for c in range(2):
                probe_ref[c, pl.ds(i * g, g), pl.ds(j * LANES, LANES)] = sums[i * 4 + j * 2 + c]
    for copy in copies:
        copy.wait()


def add_up(geo, slot, plan, mine, returned, before=None):
    split_shape = (2 * BLOCKS, geo.grid_rows * geo.grid_cols, LANES)
    if slot == 0:
        out_shape, out_specs, scratch = jax.ShapeDtypeStruct(split_shape, f32), VMEM, []
    else:
        out_shape = (
            jax.ShapeDtypeStruct((geo.grid_rows * geo.grid_cols, 2 * HALF), f32),
            jax.ShapeDtypeStruct((2, geo.piece, WIN), f32),
        )
        out_specs = (pl.BlockSpec(memory_space=pl.ANY), VMEM)
        scratch = [pltpu.VMEM(split_shape, f32), pltpu.SemaphoreType.DMA((2 * BLOCKS,))]
    extra = () if slot == 0 else (before,)
    return pl.pallas_call(
        functools.partial(add_kernel, geo, slot),
        out_shape=out_shape,
        in_specs=[SMEM, SMEM] + [VMEM] * (1 + len(extra)),
        out_specs=out_specs,
        scratch_shapes=scratch,
        compiler_params=params(32),
        cost_estimate=pl.CostEstimate(flops=1 << 23, bytes_accessed=4 << 20, transcendentals=0),
        name=f"add{slot}",
    )(plan, mine, returned, *extra)


def finish_kernel(in_ref, out_ref):
    for c in range(2):
        x = in_ref[:, c].reshape(WIN, WIN)
        out_ref[c] = swap_tile_digits(x)


def finish_probe(parts):
    return pl.pallas_call(
        finish_kernel,
        out_shape=jax.ShapeDtypeStruct((2, WIN, WIN), f32),
        in_specs=[VMEM],
        out_specs=VMEM,
        compiler_params=params(32),
        name="finish",
    )(parts)


def exchange(x):
    return lax.all_to_all(x, "scan", split_axis=0, concat_axis=0, tiled=True)


def local(object_tiles, probe, measured, positions, counts, owner_map):
    n = lax.axis_size("scan")
    geo = Geometry(n, object_tiles.shape[1], object_tiles.shape[2])
    me = lax.axis_index("scan")
    consts = [jnp.asarray(t) for t in tables()]
    tiles = object_tiles.reshape(geo.grid_rows * geo.grid_cols, 2 * HALF)

    own_class = jnp.sum(jnp.where(owner_map == me, lax.iota(i32, n), 0))
    mine = jnp.stack([me.astype(i32), own_class.astype(i32)])
    plan = make_plan(geo, counts, positions.reshape(-1))

    spare = measured[MEAN:].reshape(CAP - MEAN, n, geo.piece, WIN).transpose(1, 0, 2, 3)
    held = exchange(spare)
    sent0 = gather_tiles(geo, 0, plan, mine, tiles)
    come0 = exchange(sent0)
    sent1 = gather_tiles(geo, 1, plan, mine, tiles)
    come1 = exchange(sent1)
    arrived = exchange(choose_pieces(geo, plan, held)).reshape(WIN, WIN)
    probe_t, intensity0 = prepare(probe, measured)
    intensity1 = second_pattern(geo, plan, mine, measured, arrived)

    back0, total0 = pattern(geo, 0, plan, mine, owner_map, come0, probe_t, intensity0, consts)
    ret0 = exchange(back0)
    back1 = pattern(geo, 1, plan, mine, owner_map, come1, probe_t, intensity1, consts, total0)
    ret1 = exchange(back1)
    grad0 = add_up(geo, 0, plan, mine, ret0)
    grad, piece = add_up(geo, 1, plan, mine, ret1, grad0)
    parts = lax.all_gather(piece, "scan", axis=0, tiled=False)
    probe_grad = finish_probe(parts.reshape(n, 2, geo.piece, WIN))
    return grad.reshape(object_tiles.shape), probe_grad


def solution(mesh):
    return jax.shard_map(
        local,
        mesh=mesh,
        in_specs=(
            P(("groups", "scan"), None, None, None),
            P("groups", None, None),
            P(("groups", "scan"), None, None),
            P("groups", None, None),
            P("groups"),
            P(),
        ),
        out_specs=(P(("groups", "scan"), None, None, None), P("groups", None, None)),
        check_vma=False,
    )
```

```python
import functools
import math

import jax
import jax.numpy as jnp
import numpy as np
from jax import lax
from jax.experimental import pallas as pl
from jax.experimental.pallas import tpu as pltpu
from jax.sharding import PartitionSpec as P

WIN = 256
TILE = 16
ACROSS = WIN // TILE
SLICES = 2
MEAN = 2
CAP = 6
CHIRP = 1.5
HALF = SLICES * TILE * TILE
LANES = 128
BLOCKS = HALF // LANES
SCALE_ROWS = 8
STEPS = 32.0
LEVELS = 32700.0
LN2 = math.log(2.0)

f32 = jnp.float32
i32 = jnp.int32
bf16 = jnp.bfloat16
SMEM = pl.BlockSpec(memory_space=pltpu.SMEM)
VMEM = pl.BlockSpec(memory_space=pltpu.VMEM)


class Geometry:
    def __init__(self, owners, grid_rows, grid_cols):
        self.owners = owners
        self.columns = owners // 8
        self.rows_a = ACROSS // 8
        self.cols_b = ACROSS // self.columns
        self.tiles = self.rows_a * self.cols_b
        self.grid_rows = grid_rows
        self.grid_cols = grid_cols
        self.piece = WIN // owners
        self.group = min(8, self.piece)
        up = lambda rows: -(-(rows + SCALE_ROWS) // 8) * 8
        self.data = BLOCKS * self.tiles
        self.block = up(self.data)
        self.block_moved = up(self.data + self.piece)
        self.block_probe = up(2 * self.piece)


def params(megabytes):
    return pltpu.CompilerParams(vmem_limit_bytes=megabytes << 20)


def tables():
    k = np.arange(16)
    root = np.exp(-2j * np.pi * np.outer(k, k) / 16) / 4
    kron = np.kron(root, root)

    def halves(x):
        hi = x.astype(np.float32).astype(jnp.bfloat16)
        lo = (x - hi.astype(np.float64)).astype(np.float32).astype(jnp.bfloat16)
        return hi, lo

    re_hi, re_lo = halves(kron.real)
    im_hi, im_lo = halves(kron.imag)
    hi = np.block([[re_hi, im_hi], [-im_hi, re_hi]])
    lo = np.block([[re_lo, im_lo], [-im_lo, re_lo]])
    right = np.concatenate([hi, hi, lo], axis=0)
    left = np.ascontiguousarray(right.T)
    low_u, low_v = np.divmod(np.arange(256), 16)
    twiddle = np.exp(
        -2j * np.pi * (np.outer(low_u, low_u) + np.outer(low_v, low_v)) / WIN
    )
    u = low_u[:, None] + 16 * low_u[None, :]
    v = low_v[:, None] + 16 * low_v[None, :]
    freq = lambda w: ((w + WIN // 2) % WIN - WIN // 2) / (WIN // 2)
    chirp = np.exp(-1j * CHIRP * (freq(u) ** 2 + freq(v) ** 2))
    pack = lambda z: np.stack([z.real, z.imag]).astype(np.float32)
    return left, right, pack(twiddle), pack(chirp)


def row_scale(x):
    peak = jnp.maximum(jnp.max(jnp.abs(x), axis=1, keepdims=True), 1e-30)
    return jnp.floor(jnp.log(peak) * (STEPS / LN2)) + 2.0


def encode(low, high):
    k_low, k_high = row_scale(low), row_scale(high)
    q_low = jnp.round(low * (jnp.exp(k_low * (-LN2 / STEPS)) * LEVELS)).astype(i32)
    q_high = jnp.round(high * (jnp.exp(k_high * (-LN2 / STEPS)) * LEVELS)).astype(i32)
    return (q_high << 16) | (q_low & 0xFFFF), k_low, k_high


def unscale(k):
    return jnp.exp(k.astype(f32) * (LN2 / STEPS)) * (1.0 / LEVELS)


def decode(words, k_low, k_high):
    low = ((words << 16) >> 16).astype(f32) * k_low
    high = (words >> 16).astype(f32) * k_high
    return low, high


def put_scales(scales, rows):
    lane = lax.broadcasted_iota(i32, (rows, LANES), 1)
    out = jnp.zeros((rows, LANES), f32)
    for i, k in enumerate(scales):
        out = jnp.where(lane == i, k, out)
    return out.astype(i32)


def plan_kernel(geo, counts_ref, positions_ref, map_ref, plan_ref, mine_ref):
    n = geo.owners
    me = lax.axis_index("scan").astype(i32)
    mine_ref[0] = me

    def spare(g):
        return jnp.maximum(counts_ref[g] - MEAN, 0)

    def body(o, carry):
        own = counts_ref[o] >= MEAN

        def behind(state):
            g, used = state
            return jnp.logical_and(
                jnp.logical_not(own),
                jnp.logical_and(used >= spare(g), g < n - 1),
            )

        g, used = lax.while_loop(behind, lambda state: (state[0] + 1, jnp.int32(0)), carry)
        dev = jnp.where(own, o, g)
        slot = jnp.where(own, 1, jnp.minimum(MEAN + used, CAP - 1))
        plan_ref[o] = positions_ref[o * CAP * 2]
        plan_ref[n + o] = positions_ref[o * CAP * 2 + 1]
        plan_ref[2 * n + o] = positions_ref[(dev * CAP + slot) * 2]
        plan_ref[3 * n + o] = positions_ref[(dev * CAP + slot) * 2 + 1]
        plan_ref[4 * n + o] = dev
        plan_ref[5 * n + o] = slot

        @pl.when(map_ref[o] == me)
        def _():
            mine_ref[1] = o

        return g, jnp.where(own, used, used + 1)

    lax.fori_loop(0, n, body, (jnp.int32(0), jnp.int32(0)))


def make_plan(geo, counts, positions, owner_map):
    return pl.pallas_call(
        functools.partial(plan_kernel, geo),
        out_shape=(jax.ShapeDtypeStruct((6 * geo.owners,), i32), jax.ShapeDtypeStruct((2,), i32)),
        in_specs=[SMEM, SMEM, SMEM],
        out_specs=(SMEM, SMEM),
        name="plan",
    )(counts, positions, owner_map)


def first_row(geo, slot, o, plan_ref, mine_ref):
    n, columns = geo.owners, geo.columns
    row, col = plan_ref[2 * slot * n + o], plan_ref[(2 * slot + 1) * n + o]
    own_class = mine_ref[1]
    row = row + ((own_class // columns - row) & 7)
    col = col + ((own_class % columns - col) & (columns - 1))
    return (row // 8) * geo.grid_cols + col // columns


def gather_kernel(geo, slot, plan_ref, mine_ref, tiles_hbm, *rest):
    if slot == 0:
        out_ref, tiles_ref, sems = rest
    else:
        held_ref, out_ref, tiles_ref, sems = rest
    n, b, g = geo.owners, geo.cols_b, geo.group
    at = out_ref.shape[1] - SCALE_ROWS
    lane = lax.broadcasted_iota(i32, (g, LANES), 1)
    copies = [
        pltpu.make_async_copy(tiles_hbm.at[:, pl.ds(j * LANES, LANES)], tiles_ref.at[j], sems.at[j])
        for j in range(2 * BLOCKS)
    ]
    for copy in copies:
        copy.start()
    for copy in copies:
        copy.wait()

    def body(o, _):
        start = first_row(geo, slot, o, plan_ref, mine_ref)
        scales = []
        for a in range(geo.rows_a):
            x = [tiles_ref[j, pl.ds(start + a * geo.grid_cols, b), :] for j in range(2 * BLOCKS)]
            words, k_low, k_high = encode(
                jnp.concatenate(x[:BLOCKS], axis=1), jnp.concatenate(x[BLOCKS:], axis=1)
            )
            scales += [k_low, k_high]
            for j in range(BLOCKS):
                out_ref[o, pl.ds(j * geo.tiles + a * b, b), :] = words[:, j * LANES : (j + 1) * LANES]
        out_ref[o, pl.ds(at, b), :] = put_scales(scales, b)
        if slot == 1:
            dev, spare = plan_ref[4 * n + o], plan_ref[5 * n + o] - MEAN
            piece = held_ref[dev, jnp.maximum(spare, 0)].astype(f32)
            marks = out_ref[o, pl.ds(at, g), :]
            for i in range(geo.piece // g):
                x = piece[i * g : (i + 1) * g]
                words, k_low, k_high = encode(x[:, :LANES], x[:, LANES:])
                marks = jnp.where(lane == len(scales) + 2 * i, k_low.astype(i32), marks)
                marks = jnp.where(lane == len(scales) + 2 * i + 1, k_high.astype(i32), marks)
                out_ref[o, pl.ds(geo.data + i * g, g), :] = words
            out_ref[o, pl.ds(at, g), :] = marks
        return 0

    lax.fori_loop(0, geo.owners, body, 0, unroll=4)


def gather_tiles(geo, slot, plan, mine, tiles, held=None):
    rows = geo.block_moved if slot else geo.block
    extra = () if slot == 0 else (held,)
    return pl.pallas_call(
        functools.partial(gather_kernel, geo, slot),
        out_shape=jax.ShapeDtypeStruct((geo.owners, rows, LANES), i32),
        in_specs=[SMEM, SMEM, pl.BlockSpec(memory_space=pl.ANY)] + [VMEM] * len(extra),
        out_specs=VMEM,
        scratch_shapes=[
            pltpu.VMEM((2 * BLOCKS, geo.grid_rows * geo.grid_cols, LANES), f32),
            pltpu.SemaphoreType.DMA((2 * BLOCKS,)),
        ],
        compiler_params=params(32),
        cost_estimate=pl.CostEstimate(flops=1 << 23, bytes_accessed=4 << 20, transcendentals=0),
        name=f"gather{slot}",
    )(plan, mine, tiles, *extra)


def swap_tile_digits(x):
    parts = x.reshape(16, 2, 8, WIN)
    grid = [[parts[:, r, :, c * LANES : (c + 1) * LANES].reshape(LANES, LANES) for c in range(2)] for r in range(2)]
    row = lax.broadcasted_iota(i32, (LANES, LANES), 0)
    lane = lax.broadcasted_iota(i32, (LANES, LANES), 1)

    def inner(q):
        for s in (4, 2, 1):
            shift = s * 16
            row_bit = (row & s) != 0
            lane_bit = (lane & shift) != 0
            rows = jnp.where(row_bit, pltpu.roll(q, s, 0), pltpu.roll(q, LANES - s, 0))
            both = jnp.where(lane_bit, pltpu.roll(rows, shift, 1), pltpu.roll(rows, LANES - shift, 1))
            q = jnp.where(row_bit == lane_bit, q, both)
        return q.reshape(16, 1, 8, LANES)

    upper = jnp.concatenate([inner(grid[0][0]), inner(grid[1][0])], axis=3)
    lower = jnp.concatenate([inner(grid[0][1]), inner(grid[1][1])], axis=3)
    return jnp.concatenate([upper, lower], axis=1).reshape(WIN, WIN)


def frequency_digits(x):
    turned = x.T
    lane = lax.broadcasted_iota(i32, (16, LANES), 1)
    halves = []
    for c in range(2):
        rows = [turned[16 * i : 16 * (i + 1), c * LANES : (c + 1) * LANES] for i in range(16)]
        for s in (1, 2, 4, 8):
            lane_bit = (lane & s) != 0
            new = list(rows)
            for i in range(16):
                if i & s == 0:
                    low, high = rows[i], rows[i | s]
                    new[i] = jnp.where(lane_bit, pltpu.roll(high, s, 1), low)
                    new[i | s] = jnp.where(lane_bit, high, pltpu.roll(low, LANES - s, 1))
            rows = new
        halves.append(jnp.concatenate(rows, axis=0))
    return jnp.concatenate(halves, axis=1)


def prepare_kernel(probe_ref, measured_ref, probe_out, measured_out):
    for c in range(2):
        probe_out[c] = swap_tile_digits(probe_ref[c])
    for k in range(MEAN):
        measured_out[k] = frequency_digits(measured_ref[k].astype(f32))


def prepare(probe, measured):
    return pl.pallas_call(
        prepare_kernel,
        out_shape=(
            jax.ShapeDtypeStruct((2, WIN, WIN), f32),
            jax.ShapeDtypeStruct((MEAN, WIN, WIN), f32),
        ),
        grid=(1,),
        in_specs=[
            pl.BlockSpec((2, WIN, WIN), lambda i: (0, 0, 0)),
            pl.BlockSpec((MEAN, WIN, WIN), lambda i: (0, 0, 0)),
        ],
        out_specs=(
            pl.BlockSpec((2, WIN, WIN), lambda i: (0, 0, 0)),
            pl.BlockSpec((MEAN, WIN, WIN), lambda i: (0, 0, 0)),
        ),
        compiler_params=params(32),
        cost_estimate=pl.CostEstimate(flops=1 << 22, bytes_accessed=2 << 20, transcendentals=0),
        name="prepare",
    )(probe, measured)


def split(x):
    hi = x.astype(bf16)
    return hi, (x - hi.astype(f32)).astype(bf16)


def times_right(z, right_ref):
    re_hi, re_lo = split(z[0])
    im_hi, im_lo = split(z[1])
    data = jnp.concatenate([re_hi, im_hi, re_lo, im_lo, re_hi, im_hi], axis=1)
    out = jnp.dot(data, right_ref[...], preferred_element_type=f32)
    return out[:, :WIN], out[:, WIN:]


def times_left(z, left_ref):
    re_hi, re_lo = split(z[0])
    im_hi, im_lo = split(z[1])
    data = jnp.concatenate([re_hi, im_hi, re_lo, im_lo, re_hi, im_hi], axis=0)
    out = jnp.dot(left_ref[...], data, preferred_element_type=f32)
    return out[:WIN], out[WIN:]


def product(x, y):
    return x[0] * y[0] - x[1] * y[1], x[0] * y[1] + x[1] * y[0]


def product_conj(x, y):
    return x[0] * y[0] + x[1] * y[1], x[0] * y[1] - x[1] * y[0]


def conj(x):
    return x[0], -x[1]


def pattern_kernel(
    geo, slot, plan_ref, mine_ref, map_ref, in_ref, probe_ref, intensity_ref,
    left_hbm, right_hbm, twiddle_hbm, chirp_hbm, *rest
):
    if slot == 0:
        out_ref, total_ref, tile_ref, left_ref, right_ref, twiddle_ref, chirp_ref, sems = rest
    else:
        before_ref, out_ref, pieces_ref, moved_ref, tile_ref, left_ref, right_ref, twiddle_ref, chirp_ref, sems = rest
    tables_in = [
        pltpu.make_async_copy(src, dst, sems.at[i])
        for i, (src, dst) in enumerate(
            [(left_hbm, left_ref), (twiddle_hbm, twiddle_ref), (right_hbm, right_ref), (chirp_hbm, chirp_ref)]
        )
    ]
    for copy in tables_in:
        copy.start()
    n, columns, b, g = geo.owners, geo.columns, geo.cols_b, geo.group
    me = mine_ref[0]
    row = plan_ref[2 * slot * n + me]
    col = plan_ref[(2 * slot + 1) * n + me]
    in_at = in_ref.shape[1] - SCALE_ROWS
    first = 2 * geo.rows_a

    def source(k):
        alpha, beta = k // columns, k % columns
        return map_ref[((row + alpha) & 7) * columns + ((col + beta) & (columns - 1))]

    def tile_rows(k, a):
        alpha, beta = k // columns, k % columns
        return pl.ds((8 * a + alpha) * ACROSS + beta, b, columns)

    def unpack(k, _):
        src = source(k)
        scales = unscale(in_ref[src, pl.ds(in_at, b), :])
        for a in range(geo.rows_a):
            k_low, k_high = scales[:, 2 * a : 2 * a + 1], scales[:, 2 * a + 1 : 2 * a + 2]
            for j in range(BLOCKS):
                words = in_ref[src, pl.ds(j * geo.tiles + a * b, b), :]
                low, high = decode(words, k_low, k_high)
                tile_ref[j, tile_rows(k, a), :] = low
                tile_ref[BLOCKS + j, tile_rows(k, a), :] = high
        return 0

    lax.fori_loop(0, n, unpack, 0, unroll=4)

    def plane(i):
        return jnp.concatenate([tile_ref[2 * i], tile_ref[2 * i + 1]], axis=1)

    def put_plane(i, x):
        tile_ref[2 * i] = x[:, :LANES]
        tile_ref[2 * i + 1] = x[:, LANES:]

    twiddle = lambda: (twiddle_ref[0], twiddle_ref[1])
    chirp = lambda: (chirp_ref[0], chirp_ref[1])
    probe = lambda: (probe_ref[0], probe_ref[1])
    front = lambda: (plane(0), plane(1))
    back = lambda: (plane(2), plane(3))

    def spectrum(z):
        return times_right(product(twiddle(), times_left(z, left_ref)), right_ref)

    def conj_inverse(z_conj):
        return times_left(product(twiddle(), times_right(z_conj, right_ref)), left_ref)

    if slot == 0:
        intensity = intensity_ref[0]
    else:

        def piece(j):
            scales = unscale(in_ref[j, pl.ds(in_at, g), :])
            parts = []
            for i in range(geo.piece // g):
                k = first + 2 * i
                words = in_ref[j, pl.ds(geo.data + i * g, g), :]
                parts.append(jnp.concatenate(decode(words, scales[:, k : k + 1], scales[:, k + 1 : k + 2]), axis=1))
            return jnp.concatenate(parts, axis=0)

        def place(j, _):
            tile_rows = pl.ds(j * geo.piece, geo.piece)
            x = piece(j)
            moved_ref[0, tile_rows, :] = x[:, :LANES]
            moved_ref[1, tile_rows, :] = x[:, LANES:]
            return 0

        lax.fori_loop(0, n, place, 0, unroll=4)
        arrived = frequency_digits(jnp.concatenate([moved_ref[0], moved_ref[1]], axis=1))
        moved_ref[0] = arrived[:, :LANES]
        moved_ref[1] = arrived[:, LANES:]
        own = plan_ref[4 * n + me] == me
        for c in range(2):
            lanes = pl.ds(c * LANES, LANES)
            moved_ref[c] = jnp.where(own, intensity_ref[1, :, lanes], moved_ref[c])

    for copy in tables_in:
        copy.wait()
    entrance = product(probe(), front())
    middle_conj = conj_inverse(conj(product(chirp(), spectrum(entrance))))
    far = spectrum(product_conj(middle_conj, back()))
    if slot == 1:
        intensity = jnp.concatenate([moved_ref[0], moved_ref[1]], axis=1)
    misfit = far[0] * far[0] + far[1] * far[1] - intensity
    near_conj = conj_inverse((misfit * far[0], -(misfit * far[1])))
    grad_middle = conj(product(back(), near_conj))
    grad_back = product(middle_conj, conj(near_conj))
    enter_conj = conj_inverse(product_conj(spectrum(grad_middle), chirp()))
    enter = conj(enter_conj)
    grad_probe = product_conj(front(), enter)
    grad_front = product_conj(probe(), enter)
    put_plane(0, grad_front[0])
    put_plane(1, grad_front[1])
    put_plane(2, grad_back[0])
    put_plane(3, grad_back[1])

    def pack(k, _):
        dst = source(k)
        scales = []
        for a in range(geo.rows_a):
            x = [tile_ref[j, tile_rows(k, a), :] for j in range(2 * BLOCKS)]
            words, k_low, k_high = encode(
                jnp.concatenate(x[:BLOCKS], axis=1), jnp.concatenate(x[BLOCKS:], axis=1)
            )
            scales += [k_low, k_high]
            for j in range(BLOCKS):
                out_ref[dst, pl.ds(j * geo.tiles + a * b, b), :] = words[:, j * LANES : (j + 1) * LANES]
        out_ref[dst, pl.ds(geo.block - SCALE_ROWS, b), :] = put_scales(scales, b)
        return 0

    lax.fori_loop(0, n, pack, 0, unroll=4)
    if slot == 0:
        total_ref[0], total_ref[1] = grad_probe
        return
    tile_ref[0] = (before_ref[0] + grad_probe[0])[:, :LANES]
    tile_ref[1] = (before_ref[0] + grad_probe[0])[:, LANES:]
    tile_ref[2] = (before_ref[1] + grad_probe[1])[:, :LANES]
    tile_ref[3] = (before_ref[1] + grad_probe[1])[:, LANES:]

    def pieces(o, _):
        scales = []
        for i in range(geo.piece // g):
            rows = pl.ds(o * geo.piece + i * g, g)
            x = [tile_ref[j, rows, :] for j in range(4)]
            words, k_low, k_high = encode(
                jnp.concatenate(x[:2], axis=1), jnp.concatenate(x[2:], axis=1)
            )
            scales += [k_low, k_high]
            for j in range(2):
                pieces_ref[o, pl.ds(j * geo.piece + i * g, g), :] = words[:, j * LANES : (j + 1) * LANES]
        pieces_ref[o, pl.ds(geo.block_probe - SCALE_ROWS, g), :] = put_scales(scales, g)
        return 0

    lax.fori_loop(0, n, pieces, 0, unroll=4)


def pattern(geo, slot, plan, mine, owner_map, incoming, probe, intensity, consts, before=None):
    out = jax.ShapeDtypeStruct((geo.owners, geo.block, LANES), i32)
    total = jax.ShapeDtypeStruct((2, WIN, WIN), f32)
    pieces = jax.ShapeDtypeStruct((geo.owners, geo.block_probe, LANES), i32)
    extra = () if slot == 0 else (before,)
    moved = [] if slot == 0 else [pltpu.VMEM((2, WIN, LANES), f32)]
    return pl.pallas_call(
        functools.partial(pattern_kernel, geo, slot),
        out_shape=(out, pieces if slot else total),
        in_specs=[SMEM] * 3 + [VMEM] * 3 + [pl.BlockSpec(memory_space=pl.ANY)] * 4 + [VMEM] * len(extra),
        out_specs=(VMEM, VMEM),
        scratch_shapes=moved
        + [pltpu.VMEM((2 * BLOCKS, WIN, LANES), f32)]
        + [pltpu.VMEM(c.shape, c.dtype) for c in consts]
        + [pltpu.SemaphoreType.DMA((len(consts),))],
        compiler_params=params(48),
        cost_estimate=pl.CostEstimate(flops=13 << 30, bytes_accessed=8 << 20, transcendentals=0),
        name=f"pattern{slot}",
    )(plan, mine, owner_map, incoming, probe, intensity, *consts, *extra)


def add_kernel(geo, slot, plan_ref, mine_ref, in_ref, *rest):
    b = geo.cols_b
    if slot == 0:
        (grad_ref,) = rest
        grad_ref[...] = jnp.zeros_like(grad_ref)
    else:
        before_ref, grad_hbm, grad_ref, sems = rest
        grad_ref[...] = before_ref[...]

    def body(o, _):
        start = first_row(geo, slot, o, plan_ref, mine_ref)
        scales = unscale(in_ref[o, pl.ds(geo.block - SCALE_ROWS, b), :])
        for a in range(geo.rows_a):
            k_low, k_high = scales[:, 2 * a : 2 * a + 1], scales[:, 2 * a + 1 : 2 * a + 2]
            rows = pl.ds(start + a * geo.grid_cols, b)
            for j in range(BLOCKS):
                words = in_ref[o, pl.ds(j * geo.tiles + a * b, b), :]
                low, high = decode(words, k_low, k_high)
                grad_ref[j, rows, :] += low
                grad_ref[BLOCKS + j, rows, :] += high
        return 0

    lax.fori_loop(0, geo.owners, body, 0, unroll=2)
    if slot == 0:
        return
    copies = [
        pltpu.make_async_copy(grad_ref.at[j], grad_hbm.at[:, pl.ds(j * LANES, LANES)], sems.at[j])
        for j in range(2 * BLOCKS)
    ]
    for copy in copies:
        copy.start()
    for copy in copies:
        copy.wait()


def add_up(geo, slot, plan, mine, returned, before=None):
    split_shape = (2 * BLOCKS, geo.grid_rows * geo.grid_cols, LANES)
    if slot == 0:
        out_shape, out_specs, scratch = jax.ShapeDtypeStruct(split_shape, f32), VMEM, []
    else:
        out_shape = jax.ShapeDtypeStruct((geo.grid_rows * geo.grid_cols, 2 * HALF), f32)
        out_specs = pl.BlockSpec(memory_space=pl.ANY)
        scratch = [pltpu.VMEM(split_shape, f32), pltpu.SemaphoreType.DMA((2 * BLOCKS,))]
    extra = () if slot == 0 else (before,)
    return pl.pallas_call(
        functools.partial(add_kernel, geo, slot),
        out_shape=out_shape,
        in_specs=[SMEM, SMEM] + [VMEM] * (1 + len(extra)),
        out_specs=out_specs,
        scratch_shapes=scratch,
        compiler_params=params(32),
        cost_estimate=pl.CostEstimate(flops=1 << 23, bytes_accessed=4 << 20, transcendentals=0),
        name=f"add{slot}",
    )(plan, mine, returned, *extra)


def sum_kernel(geo, in_ref, probe_ref):
    g = geo.group

    def add_piece(o, sums):
        scales = unscale(in_ref[o, pl.ds(geo.block_probe - SCALE_ROWS, g), :])
        new = []
        for i in range(geo.piece // g):
            k_low, k_high = scales[:, 2 * i : 2 * i + 1], scales[:, 2 * i + 1 : 2 * i + 2]
            for j in range(2):
                words = in_ref[o, pl.ds(j * geo.piece + i * g, g), :]
                low, high = decode(words, k_low, k_high)
                new += [sums[len(new)] + low, sums[len(new) + 1] + high]
        return tuple(new)

    count = geo.piece // g * 4
    sums = lax.fori_loop(0, geo.owners, add_piece, (jnp.zeros((g, LANES), f32),) * count, unroll=4)
    for i in range(geo.piece // g):
        for j in range(2):
            for c in range(2):
                probe_ref[c, pl.ds(i * g, g), pl.ds(j * LANES, LANES)] = sums[i * 4 + j * 2 + c]


def sum_pieces(geo, returned):
    return pl.pallas_call(
        functools.partial(sum_kernel, geo),
        out_shape=jax.ShapeDtypeStruct((2, geo.piece, WIN), f32),
        in_specs=[VMEM],
        out_specs=VMEM,
        compiler_params=params(32),
        name="sum",
    )(returned)


def finish_kernel(in_ref, out_ref):
    for c in range(2):
        x = in_ref[:, c].reshape(WIN, WIN)
        out_ref[c] = swap_tile_digits(x)


def finish_probe(parts):
    return pl.pallas_call(
        finish_kernel,
        out_shape=jax.ShapeDtypeStruct((2, WIN, WIN), f32),
        in_specs=[VMEM],
        out_specs=VMEM,
        compiler_params=params(32),
        name="finish",
    )(parts)


def exchange(x):
    return lax.all_to_all(x, "scan", split_axis=0, concat_axis=0, tiled=True)


def local(object_tiles, probe, measured, positions, counts, owner_map):
    n = lax.axis_size("scan")
    geo = Geometry(n, object_tiles.shape[1], object_tiles.shape[2])
    consts = [jnp.asarray(t) for t in tables()]
    tiles = object_tiles.reshape(geo.grid_rows * geo.grid_cols, 2 * HALF)

    plan, mine = make_plan(geo, counts, positions.reshape(-1), owner_map)

    spare = measured[MEAN:].reshape(CAP - MEAN, n, geo.piece, WIN).transpose(1, 0, 2, 3)
    held = exchange(spare)
    sent0 = gather_tiles(geo, 0, plan, mine, tiles)
    sent0, held = lax.optimization_barrier((sent0, held))
    come0 = exchange(sent0)
    sent1 = gather_tiles(geo, 1, plan, mine, tiles, held)
    sent1, come0 = lax.optimization_barrier((sent1, come0))
    come1 = exchange(sent1)
    probe_t, intensity = prepare(probe, measured)

    back0, total0 = pattern(geo, 0, plan, mine, owner_map, come0, probe_t, intensity, consts)
    back0, come1 = lax.optimization_barrier((back0, come1))
    ret0 = exchange(back0)
    back1, pieces = pattern(geo, 1, plan, mine, owner_map, come1, probe_t, intensity, consts, total0)
    pieces, ret0 = lax.optimization_barrier((pieces, ret0))
    pieces = exchange(pieces)
    back1, pieces = lax.optimization_barrier((back1, pieces))
    ret1 = exchange(back1)
    parts = lax.all_gather(sum_pieces(geo, pieces), "scan", axis=0, tiled=False)
    grad0 = add_up(geo, 0, plan, mine, ret0)
    grad = add_up(geo, 1, plan, mine, ret1, grad0)
    probe_grad = finish_probe(parts.reshape(n, 2, geo.piece, WIN))
    return grad.reshape(object_tiles.shape), probe_grad


def solution(mesh):
    return jax.shard_map(
        local,
        mesh=mesh,
        in_specs=(
            P(("groups", "scan"), None, None, None),
            P("groups", None, None),
            P(("groups", "scan"), None, None),
            P("groups", None, None),
            P("groups"),
            P(),
        ),
        out_specs=(P(("groups", "scan"), None, None, None), P("groups", None, None)),
        check_vma=False,
    )
```

```python
import functools
import math

import jax
import jax.numpy as jnp
import numpy as np
from jax import lax
from jax.experimental import pallas as pl
from jax.experimental.pallas import tpu as pltpu
from jax.sharding import PartitionSpec as P

WIN = 256
TILE = 16
ACROSS = WIN // TILE
SLICES = 2
MEAN = 2
CAP = 6
CHIRP = 1.5
HALF = SLICES * TILE * TILE
LANES = 128
BLOCKS = HALF // LANES
SCALE_ROWS = 8
STEPS = 32.0
LEVELS = 32700.0
LN2 = math.log(2.0)

f32 = jnp.float32
i32 = jnp.int32
bf16 = jnp.bfloat16
SMEM = pl.BlockSpec(memory_space=pltpu.SMEM)
VMEM = pl.BlockSpec(memory_space=pltpu.VMEM)
ANY = pl.BlockSpec(memory_space=pl.ANY)


class Geometry:
    def __init__(self, owners, grid_rows, grid_cols):
        self.owners = owners
        self.columns = owners // 8
        self.rows_a = ACROSS // 8
        self.cols_b = ACROSS // self.columns
        self.tiles = self.rows_a * self.cols_b
        self.grid_rows = grid_rows
        self.grid_cols = grid_cols
        self.piece = WIN // owners
        self.group = min(8, self.piece)
        self.listed = owners <= 16
        self.arrays = owners if self.listed else 1
        up = lambda rows: -(-(rows + SCALE_ROWS) // 8) * 8
        self.data = BLOCKS * self.tiles
        self.block = up(self.data)
        self.block_moved = up(self.data + self.piece)
        self.block_probe = up(2 * self.piece)


    def at(self, o, me):
        return o ^ me if self.listed else o

    def blocks(self, shape, dtype):
        whole = shape if self.listed else (self.owners,) + shape
        return [jax.ShapeDtypeStruct(whole, dtype)] * self.arrays

    def stage(self, shape, dtype):
        return [pltpu.VMEM((self.owners,) + shape, dtype), pltpu.SemaphoreType.DMA((self.arrays,))]

    def copies(self, refs, stage, sems, out=False):
        made = []
        for k, ref in enumerate(refs):
            held = stage.at[k] if self.listed else stage
            made.append(pltpu.make_async_copy(*((held, ref) if out else (ref, held)), sems.at[k]))
        return made


def start(copies):
    for copy in copies:
        copy.start()


def wait(copies):
    for copy in copies:
        copy.wait()


def params(megabytes=58):
    return pltpu.CompilerParams(vmem_limit_bytes=megabytes << 20)


def tables():
    k = np.arange(16)
    root = np.exp(-2j * np.pi * np.outer(k, k) / 16) / 4
    kron = np.kron(root, root)

    def halves(x):
        hi = x.astype(np.float32).astype(jnp.bfloat16)
        lo = (x - hi.astype(np.float64)).astype(np.float32).astype(jnp.bfloat16)
        return hi, lo

    re_hi, re_lo = halves(kron.real)
    im_hi, im_lo = halves(kron.imag)
    hi = np.block([[re_hi, im_hi], [-im_hi, re_hi]])
    lo = np.block([[re_lo, im_lo], [-im_lo, re_lo]])
    right = np.concatenate([hi, hi, lo], axis=0)
    left = np.ascontiguousarray(right.T)
    low_u, low_v = np.divmod(np.arange(256), 16)
    twiddle = np.exp(
        -2j * np.pi * (np.outer(low_u, low_u) + np.outer(low_v, low_v)) / WIN
    )
    u = low_u[:, None] + 16 * low_u[None, :]
    v = low_v[:, None] + 16 * low_v[None, :]
    freq = lambda w: ((w + WIN // 2) % WIN - WIN // 2) / (WIN // 2)
    chirp = np.exp(-1j * CHIRP * (freq(u) ** 2 + freq(v) ** 2))
    pack = lambda z: np.stack([z.real, z.imag]).astype(np.float32)
    return left, right, pack(twiddle), pack(chirp)


def row_scale(x):
    peak = jnp.maximum(jnp.max(jnp.abs(x), axis=1, keepdims=True), 1e-30)
    return jnp.floor(jnp.log(peak) * (STEPS / LN2)) + 2.0


def encode(low, high):
    k_low, k_high = row_scale(low), row_scale(high)
    q_low = jnp.round(low * (jnp.exp(k_low * (-LN2 / STEPS)) * LEVELS)).astype(i32)
    q_high = jnp.round(high * (jnp.exp(k_high * (-LN2 / STEPS)) * LEVELS)).astype(i32)
    return (q_high << 16) | (q_low & 0xFFFF), k_low, k_high


def unscale(k):
    return jnp.exp(k.astype(f32) * (LN2 / STEPS)) * (1.0 / LEVELS)


def decode(words, k_low, k_high):
    low = ((words << 16) >> 16).astype(f32) * k_low
    high = (words >> 16).astype(f32) * k_high
    return low, high


def put_scales(scales, rows):
    lane = lax.broadcasted_iota(i32, (rows, LANES), 1)
    out = jnp.zeros((rows, LANES), f32)
    for i, k in enumerate(scales):
        out = jnp.where(lane == i, k, out)
    return out.astype(i32)


def plan_kernel(geo, counts_ref, positions_ref, map_ref, plan_ref, mine_ref):
    n = geo.owners
    me = lax.axis_index("scan").astype(i32)
    mine_ref[0] = me

    def spare(g):
        return jnp.maximum(counts_ref[g] - MEAN, 0)

    def body(o, carry):
        own = counts_ref[o] >= MEAN

        def behind(state):
            g, used = state
            return jnp.logical_and(
                jnp.logical_not(own),
                jnp.logical_and(used >= spare(g), g < n - 1),
            )

        g, used = lax.while_loop(behind, lambda state: (state[0] + 1, jnp.int32(0)), carry)
        dev = jnp.where(own, o, g)
        slot = jnp.where(own, 1, jnp.minimum(MEAN + used, CAP - 1))
        plan_ref[o] = positions_ref[o * CAP * 2]
        plan_ref[n + o] = positions_ref[o * CAP * 2 + 1]
        plan_ref[2 * n + o] = positions_ref[(dev * CAP + slot) * 2]
        plan_ref[3 * n + o] = positions_ref[(dev * CAP + slot) * 2 + 1]
        plan_ref[4 * n + o] = dev
        plan_ref[5 * n + o] = slot

        @pl.when(map_ref[o] == me)
        def _():
            mine_ref[1] = o

        return g, jnp.where(own, used, used + 1)

    lax.fori_loop(0, n, body, (jnp.int32(0), jnp.int32(0)))


def make_plan(geo, counts, positions, owner_map):
    return pl.pallas_call(
        functools.partial(plan_kernel, geo),
        out_shape=(jax.ShapeDtypeStruct((6 * geo.owners,), i32), jax.ShapeDtypeStruct((2,), i32)),
        in_specs=[SMEM, SMEM, SMEM],
        out_specs=(SMEM, SMEM),
        name="plan",
    )(counts, positions, owner_map)


def first_row(geo, slot, o, plan_ref, mine_ref):
    n, columns = geo.owners, geo.columns
    row, col = plan_ref[2 * slot * n + o], plan_ref[(2 * slot + 1) * n + o]
    own_class = mine_ref[1]
    row = row + ((own_class // columns - row) & 7)
    col = col + ((own_class % columns - col) & (columns - 1))
    return (row // 8) * geo.grid_cols + col // columns


def gather_kernel(geo, slot, plan_ref, mine_ref, tiles_hbm, *rest):
    n, b, g = geo.owners, geo.cols_b, geo.group
    held_hbm, rest = (rest[: geo.arrays], rest[geo.arrays :]) if slot else ((), rest)
    out_hbm, rest = rest[: geo.arrays], rest[geo.arrays :]
    tiles_ref, sems, out_ref, out_sems = rest[:4]
    at = out_ref.shape[1] - SCALE_ROWS
    lane = lax.broadcasted_iota(i32, (g, LANES), 1)
    me = mine_ref[0]
    copies = [
        pltpu.make_async_copy(tiles_hbm.at[:, pl.ds(j * LANES, LANES)], tiles_ref.at[j], sems.at[j])
        for j in range(2 * BLOCKS)
    ]
    if slot:
        held_ref, held_sems = rest[4:]
        copies += geo.copies(held_hbm, held_ref, held_sems)
    start(copies)
    wait(copies)

    def body(o, _):
        row = first_row(geo, slot, o, plan_ref, mine_ref)
        to = geo.at(o, me)
        scales = []
        for a in range(geo.rows_a):
            x = [tiles_ref[j, pl.ds(row + a * geo.grid_cols, b), :] for j in range(2 * BLOCKS)]
            words, k_low, k_high = encode(
                jnp.concatenate(x[:BLOCKS], axis=1), jnp.concatenate(x[BLOCKS:], axis=1)
            )
            scales += [k_low, k_high]
            for j in range(BLOCKS):
                out_ref[to, pl.ds(j * geo.tiles + a * b, b), :] = words[:, j * LANES : (j + 1) * LANES]
        out_ref[to, pl.ds(at, b), :] = put_scales(scales, b)
        if slot == 1:
            dev, spare = plan_ref[4 * n + o], plan_ref[5 * n + o] - MEAN
            piece = held_ref[geo.at(dev, me), jnp.maximum(spare, 0)].astype(f32)
            marks = out_ref[to, pl.ds(at, g), :]
            for i in range(geo.piece // g):
                x = piece[i * g : (i + 1) * g]
                words, k_low, k_high = encode(x[:, :LANES], x[:, LANES:])
                marks = jnp.where(lane == len(scales) + 2 * i, k_low.astype(i32), marks)
                marks = jnp.where(lane == len(scales) + 2 * i + 1, k_high.astype(i32), marks)
                out_ref[to, pl.ds(geo.data + i * g, g), :] = words
            out_ref[to, pl.ds(at, g), :] = marks
        return 0

    lax.fori_loop(0, geo.owners, body, 0, unroll=4)
    out = geo.copies(out_hbm, out_ref, out_sems, out=True)
    start(out)
    wait(out)


def gather_tiles(geo, slot, plan, mine, tiles, held=()):
    rows = geo.block_moved if slot else geo.block
    return pl.pallas_call(
        functools.partial(gather_kernel, geo, slot),
        out_shape=geo.blocks((rows, LANES), i32),
        in_specs=[SMEM, SMEM, ANY] + [ANY] * len(held),
        out_specs=[ANY] * geo.arrays,
        scratch_shapes=[
            pltpu.VMEM((2 * BLOCKS, geo.grid_rows * geo.grid_cols, LANES), f32),
            pltpu.SemaphoreType.DMA((2 * BLOCKS,)),
        ]
        + geo.stage((rows, LANES), i32)
        + (geo.stage((CAP - MEAN, geo.piece, WIN), bf16) if slot else []),
        compiler_params=params(),
        cost_estimate=pl.CostEstimate(flops=1 << 23, bytes_accessed=4 << 20, transcendentals=0),
        name=f"gather{slot}",
    )(plan, mine, tiles, *held)


def spare_kernel(geo, measured_hbm, *rest):
    out, sems = rest[:-1], rest[-1]
    me = lax.axis_index("scan").astype(i32)
    copies = []
    for k in range(geo.owners):
        rows = pl.ds(pl.multiple_of((me ^ k) * geo.piece, geo.piece), geo.piece)
        copies.append(pltpu.make_async_copy(measured_hbm.at[pl.ds(MEAN, CAP - MEAN), rows], out[k], sems.at[k]))
    start(copies)
    wait(copies)


def spare_pieces(geo, measured):
    if not geo.listed:
        spare = measured[MEAN:].reshape(CAP - MEAN, geo.owners, geo.piece, WIN)
        return [spare.transpose(1, 0, 2, 3)]
    return pl.pallas_call(
        functools.partial(spare_kernel, geo),
        out_shape=geo.blocks((CAP - MEAN, geo.piece, WIN), bf16),
        in_specs=[ANY],
        out_specs=[ANY] * geo.owners,
        scratch_shapes=[pltpu.SemaphoreType.DMA((geo.owners,))],
        compiler_params=params(),
        name="spare",
    )(measured)


def swap_tile_digits(x):
    parts = x.reshape(16, 2, 8, WIN)
    grid = [[parts[:, r, :, c * LANES : (c + 1) * LANES].reshape(LANES, LANES) for c in range(2)] for r in range(2)]
    row = lax.broadcasted_iota(i32, (LANES, LANES), 0)
    lane = lax.broadcasted_iota(i32, (LANES, LANES), 1)

    def inner(q):
        for s in (4, 2, 1):
            shift = s * 16
            row_bit = (row & s) != 0
            lane_bit = (lane & shift) != 0
            rows = jnp.where(row_bit, pltpu.roll(q, s, 0), pltpu.roll(q, LANES - s, 0))
            both = jnp.where(lane_bit, pltpu.roll(rows, shift, 1), pltpu.roll(rows, LANES - shift, 1))
            q = jnp.where(row_bit == lane_bit, q, both)
        return q.reshape(16, 1, 8, LANES)

    upper = jnp.concatenate([inner(grid[0][0]), inner(grid[1][0])], axis=3)
    lower = jnp.concatenate([inner(grid[0][1]), inner(grid[1][1])], axis=3)
    return jnp.concatenate([upper, lower], axis=1).reshape(WIN, WIN)


def frequency_digits(x):
    turned = x.T
    lane = lax.broadcasted_iota(i32, (16, LANES), 1)
    halves = []
    for c in range(2):
        rows = [turned[16 * i : 16 * (i + 1), c * LANES : (c + 1) * LANES] for i in range(16)]
        for s in (1, 2, 4, 8):
            lane_bit = (lane & s) != 0
            new = list(rows)
            for i in range(16):
                if i & s == 0:
                    low, high = rows[i], rows[i | s]
                    new[i] = jnp.where(lane_bit, pltpu.roll(high, s, 1), low)
                    new[i | s] = jnp.where(lane_bit, high, pltpu.roll(low, LANES - s, 1))
            rows = new
        halves.append(jnp.concatenate(rows, axis=0))
    return jnp.concatenate(halves, axis=1)


def prepare_kernel(probe_ref, measured_ref, probe_out, measured_out):
    for c in range(2):
        probe_out[c] = swap_tile_digits(probe_ref[c])
    for k in range(MEAN):
        measured_out[k] = frequency_digits(measured_ref[k].astype(f32))


def prepare(probe, measured):
    return pl.pallas_call(
        prepare_kernel,
        out_shape=(
            jax.ShapeDtypeStruct((2, WIN, WIN), f32),
            jax.ShapeDtypeStruct((MEAN, WIN, WIN), f32),
        ),
        grid=(1,),
        in_specs=[
            pl.BlockSpec((2, WIN, WIN), lambda i: (0, 0, 0)),
            pl.BlockSpec((MEAN, WIN, WIN), lambda i: (0, 0, 0)),
        ],
        out_specs=(
            pl.BlockSpec((2, WIN, WIN), lambda i: (0, 0, 0)),
            pl.BlockSpec((MEAN, WIN, WIN), lambda i: (0, 0, 0)),
        ),
        compiler_params=params(),
        cost_estimate=pl.CostEstimate(flops=1 << 22, bytes_accessed=2 << 20, transcendentals=0),
        name="prepare",
    )(probe, measured)


def split(x):
    hi = x.astype(bf16)
    return hi, (x - hi.astype(f32)).astype(bf16)


def times_right(z, right_ref):
    re_hi, re_lo = split(z[0])
    im_hi, im_lo = split(z[1])
    data = jnp.concatenate([re_hi, im_hi, re_lo, im_lo, re_hi, im_hi], axis=1)
    out = jnp.dot(data, right_ref[...], preferred_element_type=f32)
    return out[:, :WIN], out[:, WIN:]


def times_left(z, left_ref):
    re_hi, re_lo = split(z[0])
    im_hi, im_lo = split(z[1])
    data = jnp.concatenate([re_hi, im_hi, re_lo, im_lo, re_hi, im_hi], axis=0)
    out = jnp.dot(left_ref[...], data, preferred_element_type=f32)
    return out[:WIN], out[WIN:]


def product(x, y):
    return x[0] * y[0] - x[1] * y[1], x[0] * y[1] + x[1] * y[0]


def product_conj(x, y):
    return x[0] * y[0] + x[1] * y[1], x[0] * y[1] - x[1] * y[0]


def conj(x):
    return x[0], -x[1]


def pattern_kernel(geo, slot, plan_ref, mine_ref, map_ref, *rest):
    in_hbm, rest = rest[: geo.arrays], rest[geo.arrays :]
    probe_ref, intensity_ref, left_hbm, right_hbm, twiddle_hbm, chirp_hbm, *rest = rest
    if slot == 0:
        out_hbm, rest = rest[: geo.arrays], rest[geo.arrays :]
        total_ref, *rest = rest
    else:
        before_ref, *rest = rest
        out_hbm, rest = rest[: geo.arrays], rest[geo.arrays :]
        pieces_hbm, rest = rest[: geo.arrays], rest[geo.arrays :]
        moved_ref, pieces_ref, pieces_sems, *rest = rest
    in_ref, in_sems, out_ref, out_sems, tile_ref, left_ref, right_ref, twiddle_ref, chirp_ref, sems = rest
    tables_in = [
        pltpu.make_async_copy(src, dst, sems.at[i])
        for i, (src, dst) in enumerate(
            [(left_hbm, left_ref), (twiddle_hbm, twiddle_ref), (right_hbm, right_ref), (chirp_hbm, chirp_ref)]
        )
    ]
    coming = geo.copies(in_hbm, in_ref, in_sems)
    start(coming)
    start(tables_in)
    n, columns, b, g = geo.owners, geo.columns, geo.cols_b, geo.group
    me = mine_ref[0]
    row = plan_ref[2 * slot * n + me]
    col = plan_ref[(2 * slot + 1) * n + me]
    in_at = in_ref.shape[1] - SCALE_ROWS
    first = 2 * geo.rows_a

    def source(k):
        alpha, beta = k // columns, k % columns
        return map_ref[((row + alpha) & 7) * columns + ((col + beta) & (columns - 1))]

    def tile_rows(k, a):
        alpha, beta = k // columns, k % columns
        return pl.ds((8 * a + alpha) * ACROSS + beta, b, columns)

    wait(coming)

    def unpack(k, _):
        src = geo.at(source(k), me)
        scales = unscale(in_ref[src, pl.ds(in_at, b), :])
        for a in range(geo.rows_a):
            k_low, k_high = scales[:, 2 * a : 2 * a + 1], scales[:, 2 * a + 1 : 2 * a + 2]
            for j in range(BLOCKS):
                words = in_ref[src, pl.ds(j * geo.tiles + a * b, b), :]
                low, high = decode(words, k_low, k_high)
                tile_ref[j, tile_rows(k, a), :] = low
                tile_ref[BLOCKS + j, tile_rows(k, a), :] = high
        return 0

    lax.fori_loop(0, n, unpack, 0, unroll=4)

    def plane(i):
        return jnp.concatenate([tile_ref[2 * i], tile_ref[2 * i + 1]], axis=1)

    def put_plane(i, x):
        tile_ref[2 * i] = x[:, :LANES]
        tile_ref[2 * i + 1] = x[:, LANES:]

    twiddle = lambda: (twiddle_ref[0], twiddle_ref[1])
    chirp = lambda: (chirp_ref[0], chirp_ref[1])
    probe = lambda: (probe_ref[0], probe_ref[1])
    front = lambda: (plane(0), plane(1))
    back = lambda: (plane(2), plane(3))

    def spectrum(z):
        return times_right(product(twiddle(), times_left(z, left_ref)), right_ref)

    def conj_inverse(z_conj):
        return times_left(product(twiddle(), times_right(z_conj, right_ref)), left_ref)

    if slot == 0:
        intensity = intensity_ref[0]
    else:

        def piece(o):
            j = geo.at(o, me)
            scales = unscale(in_ref[j, pl.ds(in_at, g), :])
            parts = []
            for i in range(geo.piece // g):
                k = first + 2 * i
                words = in_ref[j, pl.ds(geo.data + i * g, g), :]
                parts.append(jnp.concatenate(decode(words, scales[:, k : k + 1], scales[:, k + 1 : k + 2]), axis=1))
            return jnp.concatenate(parts, axis=0)

        def place(j, _):
            tile_rows = pl.ds(j * geo.piece, geo.piece)
            x = piece(j)
            moved_ref[0, tile_rows, :] = x[:, :LANES]
            moved_ref[1, tile_rows, :] = x[:, LANES:]
            return 0

        lax.fori_loop(0, n, place, 0, unroll=4)
        arrived = frequency_digits(jnp.concatenate([moved_ref[0], moved_ref[1]], axis=1))
        moved_ref[0] = arrived[:, :LANES]
        moved_ref[1] = arrived[:, LANES:]
        own = plan_ref[4 * n + me] == me
        for c in range(2):
            lanes = pl.ds(c * LANES, LANES)
            moved_ref[c] = jnp.where(own, intensity_ref[1, :, lanes], moved_ref[c])

    wait(tables_in)
    entrance = product(probe(), front())
    middle_conj = conj_inverse(conj(product(chirp(), spectrum(entrance))))
    far = spectrum(product_conj(middle_conj, back()))
    if slot == 1:
        intensity = jnp.concatenate([moved_ref[0], moved_ref[1]], axis=1)
    misfit = far[0] * far[0] + far[1] * far[1] - intensity
    near_conj = conj_inverse((misfit * far[0], -(misfit * far[1])))
    grad_middle = conj(product(back(), near_conj))
    grad_back = product(middle_conj, conj(near_conj))
    enter_conj = conj_inverse(product_conj(spectrum(grad_middle), chirp()))
    enter = conj(enter_conj)
    grad_probe = product_conj(front(), enter)
    grad_front = product_conj(probe(), enter)
    put_plane(0, grad_front[0])
    put_plane(1, grad_front[1])
    put_plane(2, grad_back[0])
    put_plane(3, grad_back[1])

    def pack(k, _):
        dst = geo.at(source(k), me)
        scales = []
        for a in range(geo.rows_a):
            x = [tile_ref[j, tile_rows(k, a), :] for j in range(2 * BLOCKS)]
            words, k_low, k_high = encode(
                jnp.concatenate(x[:BLOCKS], axis=1), jnp.concatenate(x[BLOCKS:], axis=1)
            )
            scales += [k_low, k_high]
            for j in range(BLOCKS):
                out_ref[dst, pl.ds(j * geo.tiles + a * b, b), :] = words[:, j * LANES : (j + 1) * LANES]
        out_ref[dst, pl.ds(geo.block - SCALE_ROWS, b), :] = put_scales(scales, b)
        return 0

    lax.fori_loop(0, n, pack, 0, unroll=4)
    going = geo.copies(out_hbm, out_ref, out_sems, out=True)
    start(going)
    if slot == 0:
        total_ref[0], total_ref[1] = grad_probe
        wait(going)
        return
    tile_ref[0] = (before_ref[0] + grad_probe[0])[:, :LANES]
    tile_ref[1] = (before_ref[0] + grad_probe[0])[:, LANES:]
    tile_ref[2] = (before_ref[1] + grad_probe[1])[:, :LANES]
    tile_ref[3] = (before_ref[1] + grad_probe[1])[:, LANES:]

    def pieces(o, _):
        scales = []
        to = geo.at(o, me)
        for i in range(geo.piece // g):
            rows = pl.ds(o * geo.piece + i * g, g)
            x = [tile_ref[j, rows, :] for j in range(4)]
            words, k_low, k_high = encode(
                jnp.concatenate(x[:2], axis=1), jnp.concatenate(x[2:], axis=1)
            )
            scales += [k_low, k_high]
            for j in range(2):
                pieces_ref[to, pl.ds(j * geo.piece + i * g, g), :] = words[:, j * LANES : (j + 1) * LANES]
        pieces_ref[to, pl.ds(geo.block_probe - SCALE_ROWS, g), :] = put_scales(scales, g)
        return 0

    lax.fori_loop(0, n, pieces, 0, unroll=4)
    going_pieces = geo.copies(pieces_hbm, pieces_ref, pieces_sems, out=True)
    start(going_pieces)
    wait(going)
    wait(going_pieces)


def pattern(geo, slot, plan, mine, owner_map, incoming, probe, intensity, consts, before=None):
    out = geo.blocks((geo.block, LANES), i32)
    total = [jax.ShapeDtypeStruct((2, WIN, WIN), f32)]
    pieces = geo.blocks((geo.block_probe, LANES), i32)
    extra = () if slot == 0 else (before,)
    scratch = []
    if slot:
        scratch = [pltpu.VMEM((2, WIN, LANES), f32)] + geo.stage((geo.block_probe, LANES), i32)
    got = pl.pallas_call(
        functools.partial(pattern_kernel, geo, slot),
        out_shape=out + (pieces if slot else total),
        in_specs=[SMEM] * 3 + [ANY] * geo.arrays + [VMEM] * 2 + [ANY] * 4 + [VMEM] * len(extra),
        out_specs=[ANY] * geo.arrays + ([ANY] * geo.arrays if slot else [VMEM]),
        scratch_shapes=scratch
        + geo.stage(incoming[0].shape[-2:], i32)
        + geo.stage((geo.block, LANES), i32)
        + [pltpu.VMEM((2 * BLOCKS, WIN, LANES), f32)]
        + [pltpu.VMEM(c.shape, c.dtype) for c in consts]
        + [pltpu.SemaphoreType.DMA((len(consts),))],
        compiler_params=params(),
        cost_estimate=pl.CostEstimate(flops=13 << 30, bytes_accessed=8 << 20, transcendentals=0),
        name=f"pattern{slot}",
    )(plan, mine, owner_map, *incoming, probe, intensity, *consts, *extra)
    return got[: geo.arrays], got[geo.arrays :]


def add_kernel(geo, slot, plan_ref, mine_ref, *rest):
    b, me = geo.cols_b, mine_ref[0]
    in_hbm, rest = rest[: geo.arrays], rest[geo.arrays :]
    in_ref, in_sems = rest[-2:]
    coming = geo.copies(in_hbm, in_ref, in_sems)
    start(coming)
    if slot == 0:
        grad_ref = rest[0]
        grad_ref[...] = jnp.zeros_like(grad_ref)
    else:
        before_hbm, grad_hbm, grad_ref, sems, before_sem = rest[:5]
        before = pltpu.make_async_copy(before_hbm, grad_ref, before_sem)
        before.start()
        before.wait()
    wait(coming)

    def body(o, _):
        row = first_row(geo, slot, o, plan_ref, mine_ref)
        j_in = geo.at(o, me)
        scales = unscale(in_ref[j_in, pl.ds(geo.block - SCALE_ROWS, b), :])
        for a in range(geo.rows_a):
            k_low, k_high = scales[:, 2 * a : 2 * a + 1], scales[:, 2 * a + 1 : 2 * a + 2]
            rows = pl.ds(row + a * geo.grid_cols, b)
            for j in range(BLOCKS):
                words = in_ref[j_in, pl.ds(j * geo.tiles + a * b, b), :]
                low, high = decode(words, k_low, k_high)
                grad_ref[j, rows, :] += low
                grad_ref[BLOCKS + j, rows, :] += high
        return 0

    lax.fori_loop(0, geo.owners, body, 0, unroll=2)
    if slot == 0:
        return
    copies = [
        pltpu.make_async_copy(grad_ref.at[j], grad_hbm.at[:, pl.ds(j * LANES, LANES)], sems.at[j])
        for j in range(2 * BLOCKS)
    ]
    start(copies)
    wait(copies)


def add_up(geo, slot, plan, mine, returned, before=None):
    split_shape = (2 * BLOCKS, geo.grid_rows * geo.grid_cols, LANES)
    if slot == 0:
        out_shape, out_specs, scratch = jax.ShapeDtypeStruct(split_shape, f32), VMEM, []
    else:
        out_shape = jax.ShapeDtypeStruct((geo.grid_rows * geo.grid_cols, 2 * HALF), f32)
        out_specs = ANY
        scratch = [
            pltpu.VMEM(split_shape, f32),
            pltpu.SemaphoreType.DMA((2 * BLOCKS,)),
            pltpu.SemaphoreType.DMA,
        ]
    extra = () if slot == 0 else (before,)
    return pl.pallas_call(
        functools.partial(add_kernel, geo, slot),
        out_shape=out_shape,
        in_specs=[SMEM, SMEM] + [ANY] * (geo.arrays + len(extra)),
        out_specs=out_specs,
        scratch_shapes=scratch + geo.stage((geo.block, LANES), i32),
        compiler_params=params(),
        cost_estimate=pl.CostEstimate(flops=1 << 23, bytes_accessed=4 << 20, transcendentals=0),
        name=f"add{slot}",
    )(plan, mine, *returned, *extra)


def sum_kernel(geo, *refs):
    in_hbm, probe_ref, in_ref, in_sems = refs[: geo.arrays], *refs[geo.arrays :]
    g = geo.group
    coming = geo.copies(in_hbm, in_ref, in_sems)
    start(coming)
    wait(coming)

    def add_piece(o, sums):
        scales = unscale(in_ref[o, pl.ds(geo.block_probe - SCALE_ROWS, g), :])
        new = []
        for i in range(geo.piece // g):
            k_low, k_high = scales[:, 2 * i : 2 * i + 1], scales[:, 2 * i + 1 : 2 * i + 2]
            for j in range(2):
                words = in_ref[o, pl.ds(j * geo.piece + i * g, g), :]
                low, high = decode(words, k_low, k_high)
                new += [sums[len(new)] + low, sums[len(new) + 1] + high]
        return tuple(new)

    count = geo.piece // g * 4
    sums = lax.fori_loop(0, geo.owners, add_piece, (jnp.zeros((g, LANES), f32),) * count, unroll=4)
    for i in range(geo.piece // g):
        for j in range(2):
            for c in range(2):
                probe_ref[c, pl.ds(i * g, g), pl.ds(j * LANES, LANES)] = sums[i * 4 + j * 2 + c]


def sum_pieces(geo, returned):
    return pl.pallas_call(
        functools.partial(sum_kernel, geo),
        out_shape=jax.ShapeDtypeStruct((2, geo.piece, WIN), f32),
        in_specs=[ANY] * geo.arrays,
        out_specs=VMEM,
        scratch_shapes=geo.stage((geo.block_probe, LANES), i32),
        compiler_params=params(),
        name="sum",
    )(*returned)


def finish_kernel(geo, mine_ref, *refs):
    parts, out_ref, whole_ref, sems = refs[: geo.arrays], *refs[geo.arrays :]
    if geo.listed:
        copies = []
        for k, part in enumerate(parts):
            rows = pl.ds(pl.multiple_of((mine_ref[0] ^ k) * geo.piece, geo.piece), geo.piece)
            copies.append(pltpu.make_async_copy(part, whole_ref.at[:, rows], sems.at[k]))
    else:
        copies = [pltpu.make_async_copy(parts[0], whole_ref, sems.at[0])]
    start(copies)
    wait(copies)
    for c in range(2):
        out_ref[c] = swap_tile_digits(whole_ref[c])


def finish_probe(geo, mine, parts):
    return pl.pallas_call(
        functools.partial(finish_kernel, geo),
        out_shape=jax.ShapeDtypeStruct((2, WIN, WIN), f32),
        in_specs=[SMEM] + [ANY] * geo.arrays,
        out_specs=VMEM,
        scratch_shapes=[pltpu.VMEM((2, WIN, WIN), f32), pltpu.SemaphoreType.DMA((geo.arrays,))],
        compiler_params=params(),
        name="finish",
    )(mine, *parts)


def to_partners(geo, send):
    n = geo.owners
    return [send(0)] + [
        lax.ppermute(send(k), "scan", [(i, i ^ k) for i in range(n)]) for k in range(1, n)
    ]


def exchange(geo, blocks):
    if geo.listed:
        return to_partners(geo, lambda k: blocks[k])
    return [lax.all_to_all(blocks[0], "scan", split_axis=0, concat_axis=0, tiled=True)]


def gather_parts(geo, piece):
    if geo.listed:
        return to_partners(geo, lambda k: piece)
    parts = lax.all_gather(piece, "scan", axis=0, tiled=False)
    return [parts.transpose(1, 0, 2, 3).reshape(2, WIN, WIN)]


def local(object_tiles, probe, measured, positions, counts, owner_map):
    n = lax.axis_size("scan")
    geo = Geometry(n, object_tiles.shape[1], object_tiles.shape[2])
    consts = [jnp.asarray(t) for t in tables()]
    tiles = object_tiles.reshape(geo.grid_rows * geo.grid_cols, 2 * HALF)

    plan, mine = make_plan(geo, counts, positions.reshape(-1), owner_map)

    held = exchange(geo, spare_pieces(geo, measured))
    come0 = exchange(geo, gather_tiles(geo, 0, plan, mine, tiles))
    come1 = exchange(geo, gather_tiles(geo, 1, plan, mine, tiles, held))
    probe_t, intensity = prepare(probe, measured)

    back0, (total0,) = pattern(geo, 0, plan, mine, owner_map, come0, probe_t, intensity, consts)
    ret0 = exchange(geo, back0)
    back1, pieces = pattern(geo, 1, plan, mine, owner_map, come1, probe_t, intensity, consts, total0)
    parts = gather_parts(geo, sum_pieces(geo, exchange(geo, pieces)))
    ret1 = exchange(geo, back1)
    grad0 = add_up(geo, 0, plan, mine, ret0)
    grad = add_up(geo, 1, plan, mine, ret1, grad0)
    probe_grad = finish_probe(geo, mine, parts)
    return grad.reshape(object_tiles.shape), probe_grad


def solution(mesh):
    return jax.shard_map(
        local,
        mesh=mesh,
        in_specs=(
            P(("groups", "scan"), None, None, None),
            P("groups", None, None),
            P(("groups", "scan"), None, None),
            P("groups", None, None),
            P("groups"),
            P(),
        ),
        out_specs=(P(("groups", "scan"), None, None, None), P("groups", None, None)),
        check_vma=False,
    )
```

```python
import functools
import math

import jax
import jax.numpy as jnp
import numpy as np
from jax import lax
from jax.experimental import pallas as pl
from jax.experimental.pallas import tpu as pltpu
from jax.sharding import PartitionSpec as P

WIN = 256
TILE = 16
ACROSS = WIN // TILE
SLICES = 2
MEAN = 2
CAP = 6
CHIRP = 1.5
HALF = SLICES * TILE * TILE
LANES = 128
BLOCKS = HALF // LANES
SCALE_ROWS = 8
STEPS = 32.0
LEVELS = 32700.0
LN2 = math.log(2.0)

f32 = jnp.float32
i32 = jnp.int32
bf16 = jnp.bfloat16
SMEM = pl.BlockSpec(memory_space=pltpu.SMEM)
VMEM = pl.BlockSpec(memory_space=pltpu.VMEM)
ANY = pl.BlockSpec(memory_space=pl.ANY)


class Geometry:
    def __init__(self, owners, grid_rows, grid_cols):
        self.owners = owners
        self.columns = owners // 8
        self.rows_a = ACROSS // 8
        self.cols_b = ACROSS // self.columns
        self.tiles = self.rows_a * self.cols_b
        self.grid_rows = grid_rows
        self.grid_cols = grid_cols
        self.piece = WIN // owners
        self.group = min(8, self.piece)
        up = lambda rows: -(-(rows + SCALE_ROWS) // 8) * 8
        self.data = BLOCKS * self.tiles
        self.block = up(self.data)
        self.block_sent = up(MEAN * self.data + self.piece)
        self.block_probe = up(self.data + 2 * self.piece)


def params(megabytes=58):
    return pltpu.CompilerParams(vmem_limit_bytes=megabytes << 20)


def tables():
    k = np.arange(16)
    root = np.exp(-2j * np.pi * np.outer(k, k) / 16) / 4
    kron = np.kron(root, root)

    def halves(x):
        hi = x.astype(np.float32).astype(jnp.bfloat16)
        lo = (x - hi.astype(np.float64)).astype(np.float32).astype(jnp.bfloat16)
        return hi, lo

    re_hi, re_lo = halves(kron.real)
    im_hi, im_lo = halves(kron.imag)
    hi = np.block([[re_hi, im_hi], [-im_hi, re_hi]])
    lo = np.block([[re_lo, im_lo], [-im_lo, re_lo]])
    right = np.concatenate([hi, hi, lo], axis=0)
    left = np.ascontiguousarray(right.T)
    low_u, low_v = np.divmod(np.arange(256), 16)
    twiddle = np.exp(
        -2j * np.pi * (np.outer(low_u, low_u) + np.outer(low_v, low_v)) / WIN
    )
    u = low_u[:, None] + 16 * low_u[None, :]
    v = low_v[:, None] + 16 * low_v[None, :]
    freq = lambda w: ((w + WIN // 2) % WIN - WIN // 2) / (WIN // 2)
    chirp = np.exp(-1j * CHIRP * (freq(u) ** 2 + freq(v) ** 2))
    pack = lambda z: np.stack([z.real, z.imag]).astype(np.float32)
    return left, right, pack(twiddle), pack(chirp)


def row_scale(x):
    peak = jnp.maximum(jnp.max(jnp.abs(x), axis=1, keepdims=True), 1e-30)
    return jnp.floor(jnp.log(peak) * (STEPS / LN2)) + 2.0


def encode(low, high):
    k_low, k_high = row_scale(low), row_scale(high)
    q_low = jnp.round(low * (jnp.exp(k_low * (-LN2 / STEPS)) * LEVELS)).astype(i32)
    q_high = jnp.round(high * (jnp.exp(k_high * (-LN2 / STEPS)) * LEVELS)).astype(i32)
    return (q_high << 16) | (q_low & 0xFFFF), k_low, k_high


def unscale(k):
    return jnp.exp(k.astype(f32) * (LN2 / STEPS)) * (1.0 / LEVELS)


def decode(words, k_low, k_high):
    low = ((words << 16) >> 16).astype(f32) * k_low
    high = (words >> 16).astype(f32) * k_high
    return low, high


def put_scales(scales, rows):
    lane = lax.broadcasted_iota(i32, (rows, LANES), 1)
    out = jnp.zeros((rows, LANES), f32)
    for i, k in enumerate(scales):
        out = jnp.where(lane == i, k, out)
    return out.astype(i32)


def plan_kernel(geo, counts_ref, positions_ref, map_ref, plan_ref, mine_ref):
    n = geo.owners
    me = lax.axis_index("scan").astype(i32)
    mine_ref[0] = me

    def spare(g):
        return jnp.maximum(counts_ref[g] - MEAN, 0)

    def body(o, carry):
        own = counts_ref[o] >= MEAN

        def behind(state):
            g, used = state
            return jnp.logical_and(
                jnp.logical_not(own),
                jnp.logical_and(used >= spare(g), g < n - 1),
            )

        g, used = lax.while_loop(behind, lambda state: (state[0] + 1, jnp.int32(0)), carry)
        dev = jnp.where(own, o, g)
        slot = jnp.where(own, 1, jnp.minimum(MEAN + used, CAP - 1))
        plan_ref[o] = positions_ref[o * CAP * 2]
        plan_ref[n + o] = positions_ref[o * CAP * 2 + 1]
        plan_ref[2 * n + o] = positions_ref[(dev * CAP + slot) * 2]
        plan_ref[3 * n + o] = positions_ref[(dev * CAP + slot) * 2 + 1]
        plan_ref[4 * n + o] = dev
        plan_ref[5 * n + o] = slot

        @pl.when(map_ref[o] == me)
        def _():
            mine_ref[1] = o

        return g, jnp.where(own, used, used + 1)

    lax.fori_loop(0, n, body, (jnp.int32(0), jnp.int32(0)))


def make_plan(geo, counts, positions, owner_map):
    return pl.pallas_call(
        functools.partial(plan_kernel, geo),
        out_shape=(jax.ShapeDtypeStruct((6 * geo.owners,), i32), jax.ShapeDtypeStruct((2,), i32)),
        in_specs=[SMEM, SMEM, SMEM],
        out_specs=(SMEM, SMEM),
        name="plan",
    )(counts, positions, owner_map)


def first_row(geo, slot, o, plan_ref, mine_ref):
    n, columns = geo.owners, geo.columns
    row, col = plan_ref[2 * slot * n + o], plan_ref[(2 * slot + 1) * n + o]
    own_class = mine_ref[1]
    row = row + ((own_class // columns - row) & 7)
    col = col + ((own_class % columns - col) & (columns - 1))
    return (row // 8) * geo.grid_cols + col // columns


def gather_kernel(geo, plan_ref, mine_ref, tiles_hbm, out_ref, tiles_ref, sems):
    n, b = geo.owners, geo.cols_b
    at = geo.block_sent - SCALE_ROWS
    copies = [
        pltpu.make_async_copy(tiles_hbm.at[:, pl.ds(j * LANES, LANES)], tiles_ref.at[j], sems.at[j])
        for j in range(2 * BLOCKS)
    ]
    for copy in copies:
        copy.start()
    for copy in copies:
        copy.wait()

    def body(o, _):
        scales = []
        for slot in range(MEAN):
            start = first_row(geo, slot, o, plan_ref, mine_ref)
            for a in range(geo.rows_a):
                x = [tiles_ref[j, pl.ds(start + a * geo.grid_cols, b), :] for j in range(2 * BLOCKS)]
                words, k_low, k_high = encode(
                    jnp.concatenate(x[:BLOCKS], axis=1), jnp.concatenate(x[BLOCKS:], axis=1)
                )
                scales += [k_low, k_high]
                for j in range(BLOCKS):
                    rows = pl.ds(slot * geo.data + j * geo.tiles + a * b, b)
                    out_ref[o, rows, :] = words[:, j * LANES : (j + 1) * LANES]
        out_ref[o, pl.ds(at, b), :] = put_scales(scales, b)
        return 0

    lax.fori_loop(0, n, body, 0, unroll=4)


def gather_tiles(geo, plan, mine, tiles):
    return pl.pallas_call(
        functools.partial(gather_kernel, geo),
        out_shape=jax.ShapeDtypeStruct((geo.owners, geo.block_sent, LANES), i32),
        in_specs=[SMEM, SMEM, ANY],
        out_specs=VMEM,
        scratch_shapes=[
            pltpu.VMEM((2 * BLOCKS, geo.grid_rows * geo.grid_cols, LANES), f32),
            pltpu.SemaphoreType.DMA((2 * BLOCKS,)),
        ],
        compiler_params=params(),
        cost_estimate=pl.CostEstimate(flops=1 << 23, bytes_accessed=4 << 20, transcendentals=0),
        name="gather",
    )(plan, mine, tiles)


def moved_kernel(geo, plan_ref, held_ref, sent_in, sent_hbm, tail_ref, sems):
    n, g = geo.owners, geo.group
    tail = geo.block_sent - MEAN * geo.data
    at = tail - SCALE_ROWS
    lane = lax.broadcasted_iota(i32, (g, LANES), 1)
    fetch = pltpu.make_async_copy(
        sent_hbm.at[:, pl.ds(MEAN * geo.data + at, SCALE_ROWS)], tail_ref.at[:, pl.ds(at, SCALE_ROWS)], sems.at[0]
    )
    fetch.start()
    fetch.wait()

    def pieces(o, _):
        first = 2 * geo.rows_a * MEAN
        dev, spare = plan_ref[4 * n + o], plan_ref[5 * n + o] - MEAN
        piece = held_ref[dev, jnp.maximum(spare, 0)].astype(f32)
        marks = tail_ref[o, pl.ds(at, g), :]
        for i in range(geo.piece // g):
            x = piece[i * g : (i + 1) * g]
            words, k_low, k_high = encode(x[:, :LANES], x[:, LANES:])
            marks = jnp.where(lane == first + 2 * i, k_low.astype(i32), marks)
            marks = jnp.where(lane == first + 2 * i + 1, k_high.astype(i32), marks)
            tail_ref[o, pl.ds(i * g, g), :] = words
        tail_ref[o, pl.ds(at, g), :] = marks
        return 0

    lax.fori_loop(0, n, pieces, 0, unroll=4)
    store = pltpu.make_async_copy(tail_ref, sent_hbm.at[:, pl.ds(MEAN * geo.data, tail)], sems.at[1])
    store.start()
    store.wait()


def add_moved(geo, plan, held, sent):
    return pl.pallas_call(
        functools.partial(moved_kernel, geo),
        out_shape=jax.ShapeDtypeStruct(sent.shape, sent.dtype),
        in_specs=[SMEM, VMEM, ANY],
        out_specs=ANY,
        input_output_aliases={2: 0},
        scratch_shapes=[
            pltpu.VMEM((geo.owners, geo.block_sent - MEAN * geo.data, LANES), i32),
            pltpu.SemaphoreType.DMA((2,)),
        ],
        compiler_params=params(),
        name="moved",
    )(plan, held, sent)


def spare_kernel(geo, measured_ref, out_ref):
    for o in range(geo.owners):
        for k in range(CAP - MEAN):
            out_ref[o, k] = measured_ref[MEAN + k, o * geo.piece : (o + 1) * geo.piece, :]


def spare_pieces(geo, measured):
    if geo.piece % 16:
        spare = measured[MEAN:].reshape(CAP - MEAN, geo.owners, geo.piece, WIN)
        return spare.transpose(1, 0, 2, 3)
    return pl.pallas_call(
        functools.partial(spare_kernel, geo),
        out_shape=jax.ShapeDtypeStruct((geo.owners, CAP - MEAN, geo.piece, WIN), bf16),
        in_specs=[VMEM],
        out_specs=VMEM,
        compiler_params=params(),
        name="spare",
    )(measured)


def swap_tile_digits(x):
    parts = x.reshape(16, 2, 8, WIN)
    grid = [[parts[:, r, :, c * LANES : (c + 1) * LANES].reshape(LANES, LANES) for c in range(2)] for r in range(2)]
    row = lax.broadcasted_iota(i32, (LANES, LANES), 0)
    lane = lax.broadcasted_iota(i32, (LANES, LANES), 1)

    def inner(q):
        for s in (4, 2, 1):
            shift = s * 16
            row_bit = (row & s) != 0
            lane_bit = (lane & shift) != 0
            rows = jnp.where(row_bit, pltpu.roll(q, s, 0), pltpu.roll(q, LANES - s, 0))
            both = jnp.where(lane_bit, pltpu.roll(rows, shift, 1), pltpu.roll(rows, LANES - shift, 1))
            q = jnp.where(row_bit == lane_bit, q, both)
        return q.reshape(16, 1, 8, LANES)

    upper = jnp.concatenate([inner(grid[0][0]), inner(grid[1][0])], axis=3)
    lower = jnp.concatenate([inner(grid[0][1]), inner(grid[1][1])], axis=3)
    return jnp.concatenate([upper, lower], axis=1).reshape(WIN, WIN)


def frequency_digits(x):
    turned = x.T
    lane = lax.broadcasted_iota(i32, (16, LANES), 1)
    halves = []
    for c in range(2):
        rows = [turned[16 * i : 16 * (i + 1), c * LANES : (c + 1) * LANES] for i in range(16)]
        for s in (1, 2, 4, 8):
            lane_bit = (lane & s) != 0
            new = list(rows)
            for i in range(16):
                if i & s == 0:
                    low, high = rows[i], rows[i | s]
                    new[i] = jnp.where(lane_bit, pltpu.roll(high, s, 1), low)
                    new[i | s] = jnp.where(lane_bit, high, pltpu.roll(low, LANES - s, 1))
            rows = new
        halves.append(jnp.concatenate(rows, axis=0))
    return jnp.concatenate(halves, axis=1)


def prepare_kernel(probe_ref, measured_ref, probe_out, measured_out):
    for c in range(2):
        probe_out[c] = swap_tile_digits(probe_ref[c])
    for k in range(MEAN):
        measured_out[k] = frequency_digits(measured_ref[k].astype(f32))


def prepare(probe, measured):
    return pl.pallas_call(
        prepare_kernel,
        out_shape=(
            jax.ShapeDtypeStruct((2, WIN, WIN), f32),
            jax.ShapeDtypeStruct((MEAN, WIN, WIN), f32),
        ),
        grid=(1,),
        in_specs=[
            pl.BlockSpec((2, WIN, WIN), lambda i: (0, 0, 0)),
            pl.BlockSpec((MEAN, WIN, WIN), lambda i: (0, 0, 0)),
        ],
        out_specs=(
            pl.BlockSpec((2, WIN, WIN), lambda i: (0, 0, 0)),
            pl.BlockSpec((MEAN, WIN, WIN), lambda i: (0, 0, 0)),
        ),
        compiler_params=params(),
        cost_estimate=pl.CostEstimate(flops=1 << 22, bytes_accessed=2 << 20, transcendentals=0),
        name="prepare",
    )(probe, measured)


def split(x):
    hi = x.astype(bf16)
    return hi, (x - hi.astype(f32)).astype(bf16)


def times_right(zs, right_ref):
    rows = []
    for z in zs:
        re_hi, re_lo = split(z[0])
        im_hi, im_lo = split(z[1])
        rows.append(jnp.concatenate([re_hi, im_hi, re_lo, im_lo, re_hi, im_hi], axis=1))
    out = jnp.dot(jnp.concatenate(rows, axis=0), right_ref[...], preferred_element_type=f32)
    return [(out[i * WIN : (i + 1) * WIN, :WIN], out[i * WIN : (i + 1) * WIN, WIN:]) for i in range(len(zs))]


def times_left(zs, left_ref):
    columns = []
    for z in zs:
        re_hi, re_lo = split(z[0])
        im_hi, im_lo = split(z[1])
        columns.append(jnp.concatenate([re_hi, im_hi, re_lo, im_lo, re_hi, im_hi], axis=0))
    out = jnp.dot(left_ref[...], jnp.concatenate(columns, axis=1), preferred_element_type=f32)
    return [(out[:WIN, i * WIN : (i + 1) * WIN], out[WIN:, i * WIN : (i + 1) * WIN]) for i in range(len(zs))]


def product(x, y):
    return x[0] * y[0] - x[1] * y[1], x[0] * y[1] + x[1] * y[0]


def product_conj(x, y):
    return x[0] * y[0] + x[1] * y[1], x[0] * y[1] - x[1] * y[0]


def conj(x):
    return x[0], -x[1]


def pattern_kernel(
    geo, plan_ref, mine_ref, map_ref, in_ref, probe_ref, intensity_ref,
    left_hbm, right_hbm, twiddle_hbm, chirp_hbm,
    first_ref, second_ref, tile_ref, moved_ref, left_ref, right_ref, twiddle_ref, chirp_ref, sems,
):
    tables_in = [
        pltpu.make_async_copy(src, dst, sems.at[i])
        for i, (src, dst) in enumerate(
            [(left_hbm, left_ref), (twiddle_hbm, twiddle_ref), (right_hbm, right_ref), (chirp_hbm, chirp_ref)]
        )
    ]
    for copy in tables_in:
        copy.start()
    n, columns, b, g = geo.owners, geo.columns, geo.cols_b, geo.group
    me = mine_ref[0]
    in_at = geo.block_sent - SCALE_ROWS
    slots = range(MEAN)

    def source(slot, k):
        row, col = plan_ref[2 * slot * n + me], plan_ref[(2 * slot + 1) * n + me]
        return map_ref[((row + k // columns) & 7) * columns + ((col + k % columns) & (columns - 1))]

    def tile_rows(k, a):
        return pl.ds((8 * a + k // columns) * ACROSS + k % columns, b, columns)

    def unpack(k, _):
        for slot in slots:
            src = source(slot, k)
            scales = unscale(in_ref[src, pl.ds(in_at, b), :])
            for a in range(geo.rows_a):
                at = 2 * (geo.rows_a * slot + a)
                k_low, k_high = scales[:, at : at + 1], scales[:, at + 1 : at + 2]
                for j in range(BLOCKS):
                    words = in_ref[src, pl.ds(slot * geo.data + j * geo.tiles + a * b, b), :]
                    low, high = decode(words, k_low, k_high)
                    tile_ref[slot, j, tile_rows(k, a), :] = low
                    tile_ref[slot, BLOCKS + j, tile_rows(k, a), :] = high
        return 0

    lax.fori_loop(0, n, unpack, 0, unroll=4)

    def place(o, _):
        scales = unscale(in_ref[o, pl.ds(in_at, g), :])
        for i in range(geo.piece // g):
            at = 2 * (geo.rows_a * MEAN + i)
            words = in_ref[o, pl.ds(MEAN * geo.data + i * g, g), :]
            low, high = decode(words, scales[:, at : at + 1], scales[:, at + 1 : at + 2])
            rows = pl.ds(o * geo.piece + i * g, g)
            moved_ref[0, rows, :] = low
            moved_ref[1, rows, :] = high
        return 0

    lax.fori_loop(0, n, place, 0, unroll=4)
    arrived = frequency_digits(jnp.concatenate([moved_ref[0], moved_ref[1]], axis=1))
    own = plan_ref[4 * n + me] == me
    for c in range(2):
        lanes = slice(c * LANES, (c + 1) * LANES)
        moved_ref[c] = jnp.where(own, intensity_ref[1, :, lanes], arrived[:, lanes])

    def intensity(slot):
        return jnp.concatenate([moved_ref[0], moved_ref[1]], axis=1) if slot else intensity_ref[0]

    def plane(slot, i):
        return jnp.concatenate([tile_ref[slot, 2 * i], tile_ref[slot, 2 * i + 1]], axis=1)

    def put_plane(slot, i, x):
        tile_ref[slot, 2 * i] = x[:, :LANES]
        tile_ref[slot, 2 * i + 1] = x[:, LANES:]

    twiddle = lambda: (twiddle_ref[0], twiddle_ref[1])
    chirp = lambda: (chirp_ref[0], chirp_ref[1])
    probe = lambda: (probe_ref[0], probe_ref[1])
    front = lambda slot: (plane(slot, 0), plane(slot, 1))
    back = lambda slot: (plane(slot, 2), plane(slot, 3))

    def spectrum(zs):
        return times_right([product(twiddle(), z) for z in times_left(zs, left_ref)], right_ref)

    def conj_inverse(zs):
        return times_left([product(twiddle(), z) for z in times_right(zs, right_ref)], left_ref)

    for copy in tables_in:
        copy.wait()
    middle = conj_inverse(
        [conj(product(chirp(), f)) for f in spectrum([product(probe(), front(s)) for s in slots])]
    )
    far = spectrum([product_conj(middle[s], back(s)) for s in slots])
    scaled = []
    for s in slots:
        misfit = far[s][0] * far[s][0] + far[s][1] * far[s][1] - intensity(s)
        scaled.append((misfit * far[s][0], -(misfit * far[s][1])))
    near = conj_inverse(scaled)
    grad_middle = [conj(product(back(s), near[s])) for s in slots]
    for s in slots:
        grad_back = product(middle[s], conj(near[s]))
        put_plane(s, 2, grad_back[0])
        put_plane(s, 3, grad_back[1])
    enter = [conj(e) for e in conj_inverse([product_conj(f, chirp()) for f in spectrum(grad_middle)])]
    parts = [product_conj(front(s), enter[s]) for s in slots]
    for s in slots:
        grad_front = product_conj(probe(), enter[s])
        put_plane(s, 0, grad_front[0])
        put_plane(s, 1, grad_front[1])

    def pack(slot, k, out_ref):
        dst = source(slot, k)
        scales = []
        for a in range(geo.rows_a):
            x = [tile_ref[slot, j, tile_rows(k, a), :] for j in range(2 * BLOCKS)]
            words, k_low, k_high = encode(
                jnp.concatenate(x[:BLOCKS], axis=1), jnp.concatenate(x[BLOCKS:], axis=1)
            )
            scales += [k_low, k_high]
            for j in range(BLOCKS):
                out_ref[dst, pl.ds(j * geo.tiles + a * b, b), :] = words[:, j * LANES : (j + 1) * LANES]
        out_ref[dst, pl.ds(out_ref.shape[1] - SCALE_ROWS, b), :] = put_scales(scales, b)

    def pack_both(k, _):
        pack(0, k, first_ref)
        pack(1, k, second_ref)
        return 0

    lax.fori_loop(0, n, pack_both, 0, unroll=2)
    for c in range(2):
        total = parts[0][c] + parts[1][c]
        tile_ref[0, 2 * c] = total[:, :LANES]
        tile_ref[0, 2 * c + 1] = total[:, LANES:]
    lane = lax.broadcasted_iota(i32, (g, LANES), 1)
    first = 2 * geo.rows_a
    out_at = geo.block_probe - SCALE_ROWS

    def pieces(o, _):
        marks = first_ref[o, pl.ds(out_at, g), :]
        for i in range(geo.piece // g):
            rows = pl.ds(o * geo.piece + i * g, g)
            x = [tile_ref[0, j, rows, :] for j in range(4)]
            words, k_low, k_high = encode(
                jnp.concatenate(x[:2], axis=1), jnp.concatenate(x[2:], axis=1)
            )
            marks = jnp.where(lane == first + 2 * i, k_low.astype(i32), marks)
            marks = jnp.where(lane == first + 2 * i + 1, k_high.astype(i32), marks)
            for j in range(2):
                rows = pl.ds(geo.data + j * geo.piece + i * g, g)
                first_ref[o, rows, :] = words[:, j * LANES : (j + 1) * LANES]
        first_ref[o, pl.ds(out_at, g), :] = marks
        return 0

    lax.fori_loop(0, n, pieces, 0, unroll=4)


def patterns(geo, plan, mine, owner_map, incoming, probe, intensity, consts):
    return pl.pallas_call(
        functools.partial(pattern_kernel, geo),
        out_shape=(
            jax.ShapeDtypeStruct((geo.owners, geo.block_probe, LANES), i32),
            jax.ShapeDtypeStruct((geo.owners, geo.block, LANES), i32),
        ),
        in_specs=[SMEM] * 3 + [VMEM] * 3 + [ANY] * 4,
        out_specs=(VMEM, VMEM),
        scratch_shapes=[
            pltpu.VMEM((MEAN, 2 * BLOCKS, WIN, LANES), f32),
            pltpu.VMEM((2, WIN, LANES), f32),
        ]
        + [pltpu.VMEM(c.shape, c.dtype) for c in consts]
        + [pltpu.SemaphoreType.DMA((len(consts),))],
        compiler_params=params(),
        cost_estimate=pl.CostEstimate(flops=26 << 30, bytes_accessed=8 << 20, transcendentals=0),
        name="patterns",
    )(plan, mine, owner_map, incoming, probe, intensity, *consts)


def add_kernel(geo, slot, plan_ref, mine_ref, in_ref, *rest):
    b = geo.cols_b
    if slot == 0:
        (grad_ref,) = rest
        grad_ref[...] = jnp.zeros_like(grad_ref)
    else:
        before_ref, grad_hbm, grad_ref, sems = rest
        grad_ref[...] = before_ref[...]

    def body(o, _):
        start = first_row(geo, slot, o, plan_ref, mine_ref)
        scales = unscale(in_ref[o, pl.ds(in_ref.shape[1] - SCALE_ROWS, b), :])
        for a in range(geo.rows_a):
            k_low, k_high = scales[:, 2 * a : 2 * a + 1], scales[:, 2 * a + 1 : 2 * a + 2]
            rows = pl.ds(start + a * geo.grid_cols, b)
            for j in range(BLOCKS):
                words = in_ref[o, pl.ds(j * geo.tiles + a * b, b), :]
                low, high = decode(words, k_low, k_high)
                grad_ref[j, rows, :] += low
                grad_ref[BLOCKS + j, rows, :] += high
        return 0

    lax.fori_loop(0, geo.owners, body, 0, unroll=2)
    if slot == 0:
        return
    copies = [
        pltpu.make_async_copy(grad_ref.at[j], grad_hbm.at[:, pl.ds(j * LANES, LANES)], sems.at[j])
        for j in range(2 * BLOCKS)
    ]
    for copy in copies:
        copy.start()
    for copy in copies:
        copy.wait()


def add_up(geo, slot, plan, mine, returned, before=None):
    split_shape = (2 * BLOCKS, geo.grid_rows * geo.grid_cols, LANES)
    if slot == 0:
        out_shape, out_specs, scratch = jax.ShapeDtypeStruct(split_shape, f32), VMEM, []
    else:
        out_shape = jax.ShapeDtypeStruct((geo.grid_rows * geo.grid_cols, 2 * HALF), f32)
        out_specs = pl.BlockSpec(memory_space=pl.ANY)
        scratch = [pltpu.VMEM(split_shape, f32), pltpu.SemaphoreType.DMA((2 * BLOCKS,))]
    extra = () if slot == 0 else (before,)
    return pl.pallas_call(
        functools.partial(add_kernel, geo, slot),
        out_shape=out_shape,
        in_specs=[SMEM, SMEM] + [VMEM] * (1 + len(extra)),
        out_specs=out_specs,
        scratch_shapes=scratch,
        compiler_params=params(),
        cost_estimate=pl.CostEstimate(flops=1 << 23, bytes_accessed=4 << 20, transcendentals=0),
        name=f"add{slot}",
    )(plan, mine, returned, *extra)


def sum_kernel(geo, in_ref, probe_ref):
    g = geo.group

    def add_piece(o, sums):
        scales = unscale(in_ref[o, pl.ds(geo.block_probe - SCALE_ROWS, g), :])
        new = []
        for i in range(geo.piece // g):
            at = 2 * (geo.rows_a + i)
            k_low, k_high = scales[:, at : at + 1], scales[:, at + 1 : at + 2]
            for j in range(2):
                words = in_ref[o, pl.ds(geo.data + j * geo.piece + i * g, g), :]
                low, high = decode(words, k_low, k_high)
                new += [sums[len(new)] + low, sums[len(new) + 1] + high]
        return tuple(new)

    count = geo.piece // g * 4
    sums = lax.fori_loop(0, geo.owners, add_piece, (jnp.zeros((g, LANES), f32),) * count, unroll=4)
    for i in range(geo.piece // g):
        for j in range(2):
            for c in range(2):
                probe_ref[c, pl.ds(i * g, g), pl.ds(j * LANES, LANES)] = sums[i * 4 + j * 2 + c]


def sum_pieces(geo, returned):
    return pl.pallas_call(
        functools.partial(sum_kernel, geo),
        out_shape=jax.ShapeDtypeStruct((2, geo.piece, WIN), f32),
        in_specs=[VMEM],
        out_specs=VMEM,
        compiler_params=params(),
        name="sum",
    )(returned)


def swap_kernel(in_ref, out_ref):
    for c in range(2):
        out_ref[c] = swap_tile_digits(in_ref[c])


def finish_kernel(geo, masks, mine_ref, *refs):
    *parts, out_ref, whole_ref, sems = refs
    copies, owner = [], [mine_ref[0]]
    for mask in masks:
        owner = owner + [o ^ mask for o in owner]
    if not masks:
        owner = range(geo.owners)
    held = [part.at[i] for part in parts for i in range(part.shape[0])]
    for o, piece in zip(owner, held):
        rows = pl.ds(pl.multiple_of(o * geo.piece, geo.piece), geo.piece)
        copies.append(pltpu.make_async_copy(piece, whole_ref.at[:, rows], sems.at[len(copies)]))
    for copy in copies:
        copy.start()
    for copy in copies:
        copy.wait()
    for c in range(2):
        out_ref[c] = swap_tile_digits(whole_ref[c])


def finish_probe(geo, mine, piece):
    n = geo.owners
    if geo.piece % 8:
        parts = lax.all_gather(piece, "scan", axis=0, tiled=False)
        return pl.pallas_call(
            swap_kernel,
            out_shape=jax.ShapeDtypeStruct((2, WIN, WIN), f32),
            in_specs=[VMEM],
            out_specs=VMEM,
            compiler_params=params(),
            name="finish",
        )(parts.transpose(1, 0, 2, 3).reshape(2, WIN, WIN))
    masks = []
    parts = [piece[None]]
    mask = n // 2
    while mask:
        held = jnp.concatenate(parts, axis=0) if len(parts) > 1 else parts[0]
        parts = [held, lax.ppermute(held, "scan", [(i, i ^ mask) for i in range(n)])]
        masks.append(mask)
        mask //= 2
    return pl.pallas_call(
        functools.partial(finish_kernel, geo, masks),
        out_shape=jax.ShapeDtypeStruct((2, WIN, WIN), f32),
        in_specs=[SMEM, ANY, ANY],
        out_specs=VMEM,
        scratch_shapes=[pltpu.VMEM((2, WIN, WIN), f32), pltpu.SemaphoreType.DMA((n,))],
        compiler_params=params(),
        name="finish",
    )(mine, *parts)


def exchange(x):
    return lax.all_to_all(x, "scan", split_axis=0, concat_axis=0, tiled=True)


def local(object_tiles, probe, measured, positions, counts, owner_map):
    n = lax.axis_size("scan")
    geo = Geometry(n, object_tiles.shape[1], object_tiles.shape[2])
    consts = [jnp.asarray(t) for t in tables()]
    tiles = object_tiles.reshape(geo.grid_rows * geo.grid_cols, 2 * HALF)

    plan, mine = make_plan(geo, counts, positions.reshape(-1), owner_map)

    held = exchange(spare_pieces(geo, measured))
    come = exchange(add_moved(geo, plan, held, gather_tiles(geo, plan, mine, tiles)))
    probe_t, intensity = prepare(probe, measured)
    back0, back1 = patterns(geo, plan, mine, owner_map, come, probe_t, intensity, consts)
    ret0 = exchange(back0)
    back1, ret0 = lax.optimization_barrier((back1, ret0))
    ret1 = exchange(back1)
    probe_grad = finish_probe(geo, mine, sum_pieces(geo, ret0))
    grad0 = add_up(geo, 0, plan, mine, ret0)
    grad = add_up(geo, 1, plan, mine, ret1, grad0)
    return grad.reshape(object_tiles.shape), probe_grad


def solution(mesh):
    return jax.shard_map(
        local,
        mesh=mesh,
        in_specs=(
            P(("groups", "scan"), None, None, None),
            P("groups", None, None),
            P(("groups", "scan"), None, None),
            P("groups", None, None),
            P("groups"),
            P(),
        ),
        out_specs=(P(("groups", "scan"), None, None, None), P("groups", None, None)),
        check_vma=False,
    )
```

```python
import functools
import math

import jax
import jax.numpy as jnp
import numpy as np
from jax import lax
from jax.experimental import pallas as pl
from jax.experimental.pallas import tpu as pltpu
from jax.sharding import PartitionSpec as P

WIN = 256
TILE = 16
ACROSS = WIN // TILE
SLICES = 2
MEAN = 2
CAP = 6
CHIRP = 1.5
HALF = SLICES * TILE * TILE
LANES = 128
BLOCKS = HALF // LANES
SCALE_ROWS = 8
SPREAD = 4
QUARTER = WIN // SPREAD
STEPS = 32.0
LEVELS = 32700.0
LN2 = math.log(2.0)

f32 = jnp.float32
i32 = jnp.int32
bf16 = jnp.bfloat16
SMEM = pl.BlockSpec(memory_space=pltpu.SMEM)
VMEM = pl.BlockSpec(memory_space=pltpu.VMEM)
ANY = pl.BlockSpec(memory_space=pl.ANY)


class Geometry:
    def __init__(self, owners, grid_rows, grid_cols):
        self.owners = owners
        self.columns = owners // 8
        self.rows_a = ACROSS // 8
        self.cols_b = ACROSS // self.columns
        self.tiles = self.rows_a * self.cols_b
        self.grid_rows = grid_rows
        self.grid_cols = grid_cols
        self.piece = WIN // owners
        self.group = min(8, self.piece)
        up = lambda rows: -(-(rows + SCALE_ROWS) // 8) * 8
        self.data = BLOCKS * self.tiles
        self.block_sent = up(MEAN * self.data + QUARTER)
        self.block_back = up(MEAN * self.data + 2 * self.piece)
        self.block_probe = up(2 * self.piece)


def params(megabytes=58):
    return pltpu.CompilerParams(vmem_limit_bytes=megabytes << 20)


def tables():
    k = np.arange(16)
    root = np.exp(-2j * np.pi * np.outer(k, k) / 16) / 4
    kron = np.kron(root, root)

    def halves(x):
        hi = x.astype(np.float32).astype(jnp.bfloat16)
        lo = (x - hi.astype(np.float64)).astype(np.float32).astype(jnp.bfloat16)
        return hi, lo

    re_hi, re_lo = halves(kron.real)
    im_hi, im_lo = halves(kron.imag)
    hi = np.block([[re_hi, im_hi], [-im_hi, re_hi]])
    lo = np.block([[re_lo, im_lo], [-im_lo, re_lo]])
    right = np.concatenate([hi, hi, lo], axis=0)
    left = np.ascontiguousarray(right.T)
    low_u, low_v = np.divmod(np.arange(256), 16)
    twiddle = np.exp(
        -2j * np.pi * (np.outer(low_u, low_u) + np.outer(low_v, low_v)) / WIN
    )
    u = low_u[:, None] + 16 * low_u[None, :]
    v = low_v[:, None] + 16 * low_v[None, :]
    freq = lambda w: ((w + WIN // 2) % WIN - WIN // 2) / (WIN // 2)
    chirp = np.exp(-1j * CHIRP * (freq(u) ** 2 + freq(v) ** 2))
    pack = lambda z: np.stack([z.real, z.imag]).astype(np.float32)
    return left, right, pack(twiddle), pack(chirp)


def row_scale(x):
    peak = jnp.maximum(jnp.max(jnp.abs(x), axis=1, keepdims=True), 1e-30)
    return jnp.floor(jnp.log(peak) * (STEPS / LN2)) + 2.0


def encode(low, high):
    k_low, k_high = row_scale(low), row_scale(high)
    q_low = jnp.round(low * (jnp.exp(k_low * (-LN2 / STEPS)) * LEVELS)).astype(i32)
    q_high = jnp.round(high * (jnp.exp(k_high * (-LN2 / STEPS)) * LEVELS)).astype(i32)
    return (q_high << 16) | (q_low & 0xFFFF), k_low, k_high


def unscale(k):
    return jnp.exp(k.astype(f32) * (LN2 / STEPS)) * (1.0 / LEVELS)


def decode(words, k_low, k_high):
    low = ((words << 16) >> 16).astype(f32) * k_low
    high = (words >> 16).astype(f32) * k_high
    return low, high


def put_scales(scales, rows):
    lane = lax.broadcasted_iota(i32, (rows, LANES), 1)
    out = jnp.zeros((rows, LANES), f32)
    for i, k in enumerate(scales):
        out = jnp.where(lane == i, k, out)
    return out.astype(i32)


def plan_kernel(geo, counts_ref, positions_ref, map_ref, plan_ref, mine_ref):
    n = geo.owners
    me = lax.axis_index("scan").astype(i32)
    mine_ref[0] = me

    def spare(g):
        return jnp.maximum(counts_ref[g] - MEAN, 0)

    def body(o, carry):
        own = counts_ref[o] >= MEAN

        def behind(state):
            g, used = state
            return jnp.logical_and(
                jnp.logical_not(own),
                jnp.logical_and(used >= spare(g), g < n - 1),
            )

        g, used = lax.while_loop(behind, lambda state: (state[0] + 1, jnp.int32(0)), carry)
        dev = jnp.where(own, o, g)
        slot = jnp.where(own, 1, jnp.minimum(MEAN + used, CAP - 1))
        plan_ref[o] = positions_ref[o * CAP * 2]
        plan_ref[n + o] = positions_ref[o * CAP * 2 + 1]
        plan_ref[2 * n + o] = positions_ref[(dev * CAP + slot) * 2]
        plan_ref[3 * n + o] = positions_ref[(dev * CAP + slot) * 2 + 1]
        plan_ref[4 * n + o] = dev
        plan_ref[5 * n + o] = slot

        @pl.when(map_ref[o] == me)
        def _():
            mine_ref[1] = o

        return g, jnp.where(own, used, used + 1)

    lax.fori_loop(0, n, body, (jnp.int32(0), jnp.int32(0)))


def make_plan(geo, counts, positions, owner_map):
    return pl.pallas_call(
        functools.partial(plan_kernel, geo),
        out_shape=(jax.ShapeDtypeStruct((6 * geo.owners,), i32), jax.ShapeDtypeStruct((2,), i32)),
        in_specs=[SMEM, SMEM, SMEM],
        out_specs=(SMEM, SMEM),
        name="plan",
    )(counts, positions, owner_map)


def first_row(geo, slot, o, plan_ref, mine_ref):
    n, columns = geo.owners, geo.columns
    row, col = plan_ref[2 * slot * n + o], plan_ref[(2 * slot + 1) * n + o]
    own_class = mine_ref[1]
    row = row + ((own_class // columns - row) & 7)
    col = col + ((own_class % columns - col) & (columns - 1))
    return (row // 8) * geo.grid_cols + col // columns


def gather_kernel(geo, plan_ref, mine_ref, tiles_hbm, out_ref, tiles_ref, sems):
    n, b = geo.owners, geo.cols_b
    at = geo.block_sent - SCALE_ROWS
    copies = [
        pltpu.make_async_copy(tiles_hbm.at[:, pl.ds(j * LANES, LANES)], tiles_ref.at[j], sems.at[j])
        for j in range(2 * BLOCKS)
    ]
    for copy in copies:
        copy.start()
    for copy in copies:
        copy.wait()

    def body(o, _):
        scales = []
        for slot in range(MEAN):
            start = first_row(geo, slot, o, plan_ref, mine_ref)
            for a in range(geo.rows_a):
                x = [tiles_ref[j, pl.ds(start + a * geo.grid_cols, b), :] for j in range(2 * BLOCKS)]
                words, k_low, k_high = encode(
                    jnp.concatenate(x[:BLOCKS], axis=1), jnp.concatenate(x[BLOCKS:], axis=1)
                )
                scales += [k_low, k_high]
                for j in range(BLOCKS):
                    rows = pl.ds(slot * geo.data + j * geo.tiles + a * b, b)
                    out_ref[o, rows, :] = words[:, j * LANES : (j + 1) * LANES]
        out_ref[o, pl.ds(at, b), :] = put_scales(scales, b)
        return 0

    lax.fori_loop(0, n, body, 0, unroll=4)


def gather_tiles(geo, plan, mine, tiles):
    return pl.pallas_call(
        functools.partial(gather_kernel, geo),
        out_shape=jax.ShapeDtypeStruct((geo.owners, geo.block_sent, LANES), i32),
        in_specs=[SMEM, SMEM, ANY],
        out_specs=VMEM,
        scratch_shapes=[
            pltpu.VMEM((2 * BLOCKS, geo.grid_rows * geo.grid_cols, LANES), f32),
            pltpu.SemaphoreType.DMA((2 * BLOCKS,)),
        ],
        compiler_params=params(),
        cost_estimate=pl.CostEstimate(flops=1 << 23, bytes_accessed=4 << 20, transcendentals=0),
        name="gather",
    )(plan, mine, tiles)


def moved_kernel(geo, plan_ref, mine_ref, own_ref, near1, near2, near3, sent_in, sent_hbm, held_ref, tail_ref, sems):
    n, me = geo.owners, mine_ref[0]
    tail = geo.block_sent - MEAN * geo.data
    at = tail - SCALE_ROWS
    lane = lax.broadcasted_iota(i32, (SCALE_ROWS, LANES), 1)
    first = 2 * geo.rows_a * MEAN
    fetch = [
        pltpu.make_async_copy(
            sent_hbm.at[:, pl.ds(MEAN * geo.data + at, SCALE_ROWS)], tail_ref.at[:, pl.ds(at, SCALE_ROWS)], sems.at[0]
        )
    ]
    for k, near in enumerate((own_ref, near1, near2, near3)):
        fetch.append(pltpu.make_async_copy(near, held_ref.at[k], sems.at[1 + k]))
    for copy in fetch:
        copy.start()
    for copy in fetch:
        copy.wait()

    def quarter(o, _):
        dev, spare = plan_ref[4 * n + o], plan_ref[5 * n + o] - MEAN
        near = dev ^ me

        @pl.when(near < SPREAD)
        def _():
            x = held_ref[near & (SPREAD - 1), jnp.maximum(spare, 0)].astype(f32)
            marks = tail_ref[o, pl.ds(at, SCALE_ROWS), :]
            for i in range(QUARTER // 8):
                part = x[8 * i : 8 * (i + 1)]
                k = row_scale(part)
                scaled = jnp.round(part * (jnp.exp(k * (-LN2 / STEPS)) * LEVELS)).astype(i32)
                marks = jnp.where(lane == first + i, k.astype(i32), marks)
                tail_ref[o, pl.ds(8 * i, 8), :] = (scaled[:, LANES:] << 16) | (scaled[:, :LANES] & 0xFFFF)
            tail_ref[o, pl.ds(at, SCALE_ROWS), :] = marks

        return 0

    lax.fori_loop(0, n, quarter, 0)
    store = pltpu.make_async_copy(tail_ref, sent_hbm.at[:, pl.ds(MEAN * geo.data, tail)], sems.at[0])
    store.start()
    store.wait()


def add_moved(geo, plan, mine, held, sent):
    return pl.pallas_call(
        functools.partial(moved_kernel, geo),
        out_shape=jax.ShapeDtypeStruct(sent.shape, sent.dtype),
        in_specs=[SMEM, SMEM] + [ANY] * (SPREAD + 1),
        out_specs=ANY,
        input_output_aliases={2 + SPREAD: 0},
        scratch_shapes=[
            pltpu.VMEM((SPREAD, CAP - MEAN, QUARTER, WIN), bf16),
            pltpu.VMEM((geo.owners, geo.block_sent - MEAN * geo.data, LANES), i32),
            pltpu.SemaphoreType.DMA((SPREAD + 1,)),
        ],
        compiler_params=params(),
        name="moved",
    )(plan, mine, *held, sent)


def spare_kernel(measured_hbm, *rest):
    outs, measured_ref, sem = rest[:SPREAD], rest[SPREAD], rest[SPREAD + 1]
    copy = pltpu.make_async_copy(measured_hbm.at[pl.ds(MEAN, CAP - MEAN)], measured_ref, sem)
    copy.start()
    copy.wait()
    me = lax.axis_index("scan").astype(i32)
    for k, out_ref in enumerate(outs):
        rows = pl.ds(pl.multiple_of(((me ^ k) & (SPREAD - 1)) * QUARTER, QUARTER), QUARTER)
        for slot in range(CAP - MEAN):
            out_ref[slot] = measured_ref[slot, rows, :]


def near_quarters(geo, measured):
    shape = jax.ShapeDtypeStruct((CAP - MEAN, QUARTER, WIN), bf16)
    quarters = pl.pallas_call(
        spare_kernel,
        out_shape=[shape] * SPREAD,
        in_specs=[ANY],
        out_specs=[VMEM] * SPREAD,
        scratch_shapes=[pltpu.VMEM((CAP - MEAN, WIN, WIN), bf16), pltpu.SemaphoreType.DMA],
        compiler_params=params(),
        name="spare",
    )(measured)
    n = geo.owners
    return [quarters[0]] + [
        lax.ppermute(quarters[k], "scan", [(i, i ^ k) for i in range(n)]) for k in range(1, SPREAD)
    ]


def swap_tile_digits(x):
    parts = x.reshape(16, 2, 8, WIN)
    grid = [[parts[:, r, :, c * LANES : (c + 1) * LANES].reshape(LANES, LANES) for c in range(2)] for r in range(2)]
    row = lax.broadcasted_iota(i32, (LANES, LANES), 0)
    lane = lax.broadcasted_iota(i32, (LANES, LANES), 1)

    def inner(q):
        for s in (4, 2, 1):
            shift = s * 16
            row_bit = (row & s) != 0
            lane_bit = (lane & shift) != 0
            rows = jnp.where(row_bit, pltpu.roll(q, s, 0), pltpu.roll(q, LANES - s, 0))
            both = jnp.where(lane_bit, pltpu.roll(rows, shift, 1), pltpu.roll(rows, LANES - shift, 1))
            q = jnp.where(row_bit == lane_bit, q, both)
        return q.reshape(16, 1, 8, LANES)

    upper = jnp.concatenate([inner(grid[0][0]), inner(grid[1][0])], axis=3)
    lower = jnp.concatenate([inner(grid[0][1]), inner(grid[1][1])], axis=3)
    return jnp.concatenate([upper, lower], axis=1).reshape(WIN, WIN)


def frequency_digits(x):
    turned = x.T
    lane = lax.broadcasted_iota(i32, (16, LANES), 1)
    halves = []
    for c in range(2):
        rows = [turned[16 * i : 16 * (i + 1), c * LANES : (c + 1) * LANES] for i in range(16)]
        for s in (1, 2, 4, 8):
            lane_bit = (lane & s) != 0
            new = list(rows)
            for i in range(16):
                if i & s == 0:
                    low, high = rows[i], rows[i | s]
                    new[i] = jnp.where(lane_bit, pltpu.roll(high, s, 1), low)
                    new[i | s] = jnp.where(lane_bit, high, pltpu.roll(low, LANES - s, 1))
            rows = new
        halves.append(jnp.concatenate(rows, axis=0))
    return jnp.concatenate(halves, axis=1)


def prepare_kernel(probe_ref, measured_ref, probe_out, measured_out):
    for c in range(2):
        probe_out[c] = swap_tile_digits(probe_ref[c])
    for k in range(MEAN):
        measured_out[k] = frequency_digits(measured_ref[k].astype(f32))


def prepare(probe, measured):
    return pl.pallas_call(
        prepare_kernel,
        out_shape=(
            jax.ShapeDtypeStruct((2, WIN, WIN), f32),
            jax.ShapeDtypeStruct((MEAN, WIN, WIN), f32),
        ),
        grid=(1,),
        in_specs=[
            pl.BlockSpec((2, WIN, WIN), lambda i: (0, 0, 0)),
            pl.BlockSpec((MEAN, WIN, WIN), lambda i: (0, 0, 0)),
        ],
        out_specs=(
            pl.BlockSpec((2, WIN, WIN), lambda i: (0, 0, 0)),
            pl.BlockSpec((MEAN, WIN, WIN), lambda i: (0, 0, 0)),
        ),
        compiler_params=params(),
        cost_estimate=pl.CostEstimate(flops=1 << 22, bytes_accessed=2 << 20, transcendentals=0),
        name="prepare",
    )(probe, measured)


def split(x):
    hi = x.astype(bf16)
    return hi, (x - hi.astype(f32)).astype(bf16)


def times_right(zs, right_ref):
    rows = []
    for z in zs:
        re_hi, re_lo = split(z[0])
        im_hi, im_lo = split(z[1])
        rows.append(jnp.concatenate([re_hi, im_hi, re_lo, im_lo, re_hi, im_hi], axis=1))
    out = jnp.dot(jnp.concatenate(rows, axis=0), right_ref[...], preferred_element_type=f32)
    return [(out[i * WIN : (i + 1) * WIN, :WIN], out[i * WIN : (i + 1) * WIN, WIN:]) for i in range(len(zs))]


def times_left(zs, left_ref):
    columns = []
    for z in zs:
        re_hi, re_lo = split(z[0])
        im_hi, im_lo = split(z[1])
        columns.append(jnp.concatenate([re_hi, im_hi, re_lo, im_lo, re_hi, im_hi], axis=0))
    out = jnp.dot(left_ref[...], jnp.concatenate(columns, axis=1), preferred_element_type=f32)
    return [(out[:WIN, i * WIN : (i + 1) * WIN], out[WIN:, i * WIN : (i + 1) * WIN]) for i in range(len(zs))]


def product(x, y):
    return x[0] * y[0] - x[1] * y[1], x[0] * y[1] + x[1] * y[0]


def product_conj(x, y):
    return x[0] * y[0] + x[1] * y[1], x[0] * y[1] - x[1] * y[0]


def conj(x):
    return x[0], -x[1]


def pattern_kernel(
    geo, plan_ref, mine_ref, map_ref, in_ref, probe_ref, intensity_ref,
    left_hbm, right_hbm, twiddle_hbm, chirp_hbm,
    out_ref, tile_ref, moved_ref, left_ref, right_ref, twiddle_ref, chirp_ref, sems,
):
    tables_in = [
        pltpu.make_async_copy(src, dst, sems.at[i])
        for i, (src, dst) in enumerate(
            [(left_hbm, left_ref), (twiddle_hbm, twiddle_ref), (right_hbm, right_ref), (chirp_hbm, chirp_ref)]
        )
    ]
    for copy in tables_in:
        copy.start()
    n, columns, b, g = geo.owners, geo.columns, geo.cols_b, geo.group
    me = mine_ref[0]
    in_at = geo.block_sent - SCALE_ROWS
    slots = range(MEAN)

    def source(slot, k):
        row, col = plan_ref[2 * slot * n + me], plan_ref[(2 * slot + 1) * n + me]
        return map_ref[((row + k // columns) & 7) * columns + ((col + k % columns) & (columns - 1))]

    def tile_rows(k, a):
        return pl.ds((8 * a + k // columns) * ACROSS + k % columns, b, columns)

    def unpack(k, _):
        for slot in slots:
            src = source(slot, k)
            scales = unscale(in_ref[src, pl.ds(in_at, b), :])
            for a in range(geo.rows_a):
                at = 2 * (geo.rows_a * slot + a)
                k_low, k_high = scales[:, at : at + 1], scales[:, at + 1 : at + 2]
                for j in range(BLOCKS):
                    words = in_ref[src, pl.ds(slot * geo.data + j * geo.tiles + a * b, b), :]
                    low, high = decode(words, k_low, k_high)
                    tile_ref[slot, j, tile_rows(k, a), :] = low
                    tile_ref[slot, BLOCKS + j, tile_rows(k, a), :] = high
        return 0

    lax.fori_loop(0, n, unpack, 0, unroll=4)

    dev = plan_ref[4 * n + me]
    for q in range(SPREAD):
        holder = (dev & -SPREAD) + q
        scales = unscale(in_ref[holder, pl.ds(in_at, SCALE_ROWS), :])
        for i in range(QUARTER // 8):
            at = 2 * geo.rows_a * MEAN + i
            words = in_ref[holder, pl.ds(MEAN * geo.data + 8 * i, 8), :]
            low, high = decode(words, scales[:, at : at + 1], scales[:, at : at + 1])
            rows = pl.ds(q * QUARTER + 8 * i, 8)
            moved_ref[0, rows, :] = low
            moved_ref[1, rows, :] = high
    arrived = frequency_digits(jnp.concatenate([moved_ref[0], moved_ref[1]], axis=1))
    own = dev == me
    for c in range(2):
        lanes = slice(c * LANES, (c + 1) * LANES)
        moved_ref[c] = jnp.where(own, intensity_ref[1, :, lanes], arrived[:, lanes])

    def intensity(slot):
        return jnp.concatenate([moved_ref[0], moved_ref[1]], axis=1) if slot else intensity_ref[0]

    def plane(slot, i):
        return jnp.concatenate([tile_ref[slot, 2 * i], tile_ref[slot, 2 * i + 1]], axis=1)

    def put_plane(slot, i, x):
        tile_ref[slot, 2 * i] = x[:, :LANES]
        tile_ref[slot, 2 * i + 1] = x[:, LANES:]

    twiddle = lambda: (twiddle_ref[0], twiddle_ref[1])
    chirp = lambda: (chirp_ref[0], chirp_ref[1])
    probe = lambda: (probe_ref[0], probe_ref[1])
    front = lambda slot: (plane(slot, 0), plane(slot, 1))
    back = lambda slot: (plane(slot, 2), plane(slot, 3))

    def spectrum(zs):
        return times_right([product(twiddle(), z) for z in times_left(zs, left_ref)], right_ref)

    def conj_inverse(zs):
        return times_left([product(twiddle(), z) for z in times_right(zs, right_ref)], left_ref)

    for copy in tables_in:
        copy.wait()
    middle = conj_inverse(
        [conj(product(chirp(), f)) for f in spectrum([product(probe(), front(s)) for s in slots])]
    )
    far = spectrum([product_conj(middle[s], back(s)) for s in slots])
    scaled = []
    for s in slots:
        misfit = far[s][0] * far[s][0] + far[s][1] * far[s][1] - intensity(s)
        scaled.append((misfit * far[s][0], -(misfit * far[s][1])))
    near = conj_inverse(scaled)
    grad_middle = [conj(product(back(s), near[s])) for s in slots]
    for s in slots:
        grad_back = product(middle[s], conj(near[s]))
        put_plane(s, 2, grad_back[0])
        put_plane(s, 3, grad_back[1])
    enter = [conj(e) for e in conj_inverse([product_conj(f, chirp()) for f in spectrum(grad_middle)])]
    parts = [product_conj(front(s), enter[s]) for s in slots]
    for s in slots:
        grad_front = product_conj(probe(), enter[s])
        put_plane(s, 0, grad_front[0])
        put_plane(s, 1, grad_front[1])

    out_at = geo.block_back - SCALE_ROWS

    def put_marks(o, first, scales):
        rows = scales[0].shape[0]
        lane = lax.broadcasted_iota(i32, (rows, LANES), 1)
        marks = out_ref[o, pl.ds(out_at, rows), :]
        for i, k in enumerate(scales):
            marks = jnp.where(lane == first + i, k.astype(i32), marks)
        out_ref[o, pl.ds(out_at, rows), :] = marks

    def pack(k, _):
        for slot in slots:
            dst = source(slot, k)
            scales = []
            for a in range(geo.rows_a):
                x = [tile_ref[slot, j, tile_rows(k, a), :] for j in range(2 * BLOCKS)]
                words, k_low, k_high = encode(
                    jnp.concatenate(x[:BLOCKS], axis=1), jnp.concatenate(x[BLOCKS:], axis=1)
                )
                scales += [k_low, k_high]
                for j in range(BLOCKS):
                    rows = pl.ds(slot * geo.data + j * geo.tiles + a * b, b)
                    out_ref[dst, rows, :] = words[:, j * LANES : (j + 1) * LANES]
            put_marks(dst, 2 * geo.rows_a * slot, scales)
        return 0

    lax.fori_loop(0, n, pack, 0, unroll=2)
    for c in range(2):
        total = parts[0][c] + parts[1][c]
        tile_ref[0, 2 * c] = total[:, :LANES]
        tile_ref[0, 2 * c + 1] = total[:, LANES:]

    def pieces(o, _):
        scales = []
        for i in range(geo.piece // g):
            rows = pl.ds(o * geo.piece + i * g, g)
            x = [tile_ref[0, j, rows, :] for j in range(4)]
            words, k_low, k_high = encode(
                jnp.concatenate(x[:2], axis=1), jnp.concatenate(x[2:], axis=1)
            )
            scales += [k_low, k_high]
            for j in range(2):
                rows = pl.ds(MEAN * geo.data + j * geo.piece + i * g, g)
                out_ref[o, rows, :] = words[:, j * LANES : (j + 1) * LANES]
        put_marks(o, 2 * geo.rows_a * MEAN, scales)
        return 0

    lax.fori_loop(0, n, pieces, 0, unroll=4)


def patterns(geo, plan, mine, owner_map, incoming, probe, intensity, consts):
    return pl.pallas_call(
        functools.partial(pattern_kernel, geo),
        out_shape=jax.ShapeDtypeStruct((geo.owners, geo.block_back, LANES), i32),
        in_specs=[SMEM] * 3 + [VMEM] * 3 + [ANY] * 4,
        out_specs=VMEM,
        scratch_shapes=[
            pltpu.VMEM((MEAN, 2 * BLOCKS, WIN, LANES), f32),
            pltpu.VMEM((2, WIN, LANES), f32),
        ]
        + [pltpu.VMEM(c.shape, c.dtype) for c in consts]
        + [pltpu.SemaphoreType.DMA((len(consts),))],
        compiler_params=params(),
        cost_estimate=pl.CostEstimate(flops=26 << 30, bytes_accessed=8 << 20, transcendentals=0),
        name="patterns",
    )(plan, mine, owner_map, incoming, probe, intensity, *consts)


def add_kernel(geo, plan_ref, mine_ref, in_ref, grad_hbm, grad_ref, sems):
    b = geo.cols_b
    grad_ref[...] = jnp.zeros_like(grad_ref)

    def body(o, _):
        scales = unscale(in_ref[o, pl.ds(geo.block_back - SCALE_ROWS, b), :])
        for slot in range(MEAN):
            start = first_row(geo, slot, o, plan_ref, mine_ref)
            for a in range(geo.rows_a):
                at = 2 * (geo.rows_a * slot + a)
                k_low, k_high = scales[:, at : at + 1], scales[:, at + 1 : at + 2]
                rows = pl.ds(start + a * geo.grid_cols, b)
                for j in range(BLOCKS):
                    words = in_ref[o, pl.ds(slot * geo.data + j * geo.tiles + a * b, b), :]
                    low, high = decode(words, k_low, k_high)
                    grad_ref[j, rows, :] += low
                    grad_ref[BLOCKS + j, rows, :] += high
        return 0

    lax.fori_loop(0, geo.owners, body, 0, unroll=2)
    copies = [
        pltpu.make_async_copy(grad_ref.at[j], grad_hbm.at[:, pl.ds(j * LANES, LANES)], sems.at[j])
        for j in range(2 * BLOCKS)
    ]
    for copy in copies:
        copy.start()
    for copy in copies:
        copy.wait()


def add_up(geo, plan, mine, returned):
    return pl.pallas_call(
        functools.partial(add_kernel, geo),
        out_shape=jax.ShapeDtypeStruct((geo.grid_rows * geo.grid_cols, 2 * HALF), f32),
        in_specs=[SMEM, SMEM, VMEM],
        out_specs=ANY,
        scratch_shapes=[
            pltpu.VMEM((2 * BLOCKS, geo.grid_rows * geo.grid_cols, LANES), f32),
            pltpu.SemaphoreType.DMA((2 * BLOCKS,)),
        ],
        compiler_params=params(),
        cost_estimate=pl.CostEstimate(flops=1 << 23, bytes_accessed=4 << 20, transcendentals=0),
        name="add",
    )(plan, mine, returned)


def sum_kernel(geo, in_hbm, out_ref, in_ref, sem):
    g = geo.group
    rows = geo.block_back - MEAN * geo.data
    copy = pltpu.make_async_copy(in_hbm.at[:, pl.ds(MEAN * geo.data, rows)], in_ref, sem)
    copy.start()
    copy.wait()
    count = geo.piece // g

    def add_piece(o, sums):
        scales = unscale(in_ref[o, pl.ds(rows - SCALE_ROWS, g), :])
        new = []
        for i in range(count):
            at = 2 * (geo.rows_a * MEAN + i)
            k_low, k_high = scales[:, at : at + 1], scales[:, at + 1 : at + 2]
            for j in range(2):
                words = in_ref[o, pl.ds(j * geo.piece + i * g, g), :]
                low, high = decode(words, k_low, k_high)
                new += [sums[len(new)] + low, sums[len(new) + 1] + high]
        return tuple(new)

    sums = lax.fori_loop(0, geo.owners, add_piece, (jnp.zeros((g, LANES), f32),) * (4 * count), unroll=4)
    parts, scales = [], []
    for i in range(count):
        low = jnp.concatenate([sums[4 * i], sums[4 * i + 2]], axis=1)
        high = jnp.concatenate([sums[4 * i + 1], sums[4 * i + 3]], axis=1)
        words, k_low, k_high = encode(low, high)
        parts.append(words)
        scales += [k_low, k_high]
    marks = put_scales(scales, g)

    def spread(o, _):
        for i in range(count):
            for j in range(2):
                out_ref[o, pl.ds(j * geo.piece + i * g, g), :] = parts[i][:, j * LANES : (j + 1) * LANES]
        out_ref[o, pl.ds(geo.block_probe - SCALE_ROWS, g), :] = marks
        return 0

    lax.fori_loop(0, geo.owners, spread, 0)


def sum_pieces(geo, returned):
    return pl.pallas_call(
        functools.partial(sum_kernel, geo),
        out_shape=jax.ShapeDtypeStruct((geo.owners, geo.block_probe, LANES), i32),
        in_specs=[ANY],
        out_specs=VMEM,
        scratch_shapes=[
            pltpu.VMEM((geo.owners, geo.block_back - MEAN * geo.data, LANES), i32),
            pltpu.SemaphoreType.DMA,
        ],
        compiler_params=params(),
        name="sum",
    )(returned)


def finish_kernel(geo, in_ref, out_ref, whole_ref):
    g = geo.group

    def place(o, _):
        scales = unscale(in_ref[o, pl.ds(geo.block_probe - SCALE_ROWS, g), :])
        for i in range(geo.piece // g):
            k_low, k_high = scales[:, 2 * i : 2 * i + 1], scales[:, 2 * i + 1 : 2 * i + 2]
            for j in range(2):
                words = in_ref[o, pl.ds(j * geo.piece + i * g, g), :]
                low, high = decode(words, k_low, k_high)
                rows = pl.ds(o * geo.piece + i * g, g)
                whole_ref[0, j, rows, :] = low
                whole_ref[1, j, rows, :] = high
        return 0

    lax.fori_loop(0, geo.owners, place, 0, unroll=4)
    for c in range(2):
        out_ref[c] = swap_tile_digits(jnp.concatenate([whole_ref[c, 0], whole_ref[c, 1]], axis=1))


def finish_probe(geo, parts):
    return pl.pallas_call(
        functools.partial(finish_kernel, geo),
        out_shape=jax.ShapeDtypeStruct((2, WIN, WIN), f32),
        in_specs=[VMEM],
        out_specs=VMEM,
        scratch_shapes=[pltpu.VMEM((2, 2, WIN, LANES), f32)],
        compiler_params=params(),
        name="finish",
    )(parts)


def exchange(x):
    return lax.all_to_all(x, "scan", split_axis=0, concat_axis=0, tiled=True)


def local(object_tiles, probe, measured, positions, counts, owner_map):
    n = lax.axis_size("scan")
    geo = Geometry(n, object_tiles.shape[1], object_tiles.shape[2])
    consts = [jnp.asarray(t) for t in tables()]
    tiles = object_tiles.reshape(geo.grid_rows * geo.grid_cols, 2 * HALF)

    plan, mine = make_plan(geo, counts, positions.reshape(-1), owner_map)

    held = near_quarters(geo, measured)
    come = exchange(add_moved(geo, plan, mine, held, gather_tiles(geo, plan, mine, tiles)))
    probe_t, intensity = prepare(probe, measured)
    returned = exchange(patterns(geo, plan, mine, owner_map, come, probe_t, intensity, consts))
    probe_grad = finish_probe(geo, exchange(sum_pieces(geo, returned)))
    grad = add_up(geo, plan, mine, returned)
    return grad.reshape(object_tiles.shape), probe_grad


def solution(mesh):
    return jax.shard_map(
        local,
        mesh=mesh,
        in_specs=(
            P(("groups", "scan"), None, None, None),
            P("groups", None, None),
            P(("groups", "scan"), None, None),
            P("groups", None, None),
            P("groups"),
            P(),
        ),
        out_specs=(P(("groups", "scan"), None, None, None), P("groups", None, None)),
        check_vma=False,
    )
```

```python
import functools
import math

import jax
import jax.numpy as jnp
import numpy as np
from jax import lax
from jax.experimental import pallas as pl
from jax.experimental.pallas import tpu as pltpu
from jax.sharding import PartitionSpec as P

WIN = 256
TILE = 16
ACROSS = WIN // TILE
SLICES = 2
MEAN = 2
CAP = 6
CHIRP = 1.5
HALF = SLICES * TILE * TILE
LANES = 128
BLOCKS = HALF // LANES
SCALE_ROWS = 8
SPREAD = 4
QUARTER = WIN // SPREAD
STEPS = 32.0
LEVELS = 32700.0
LN2 = math.log(2.0)

f32 = jnp.float32
i32 = jnp.int32
bf16 = jnp.bfloat16
SMEM = pl.BlockSpec(memory_space=pltpu.SMEM)
VMEM = pl.BlockSpec(memory_space=pltpu.VMEM)
ANY = pl.BlockSpec(memory_space=pl.ANY)


class Geometry:
    def __init__(self, owners, grid_rows, grid_cols):
        self.owners = owners
        self.columns = owners // 8
        self.rows_a = ACROSS // 8
        self.cols_b = ACROSS // self.columns
        self.tiles = self.rows_a * self.cols_b
        self.grid_rows = grid_rows
        self.grid_cols = grid_cols
        self.piece = WIN // owners
        self.group = min(8, self.piece)
        self.whole_blocks = self.piece % 16 == 0
        up = lambda rows: -(-(rows + SCALE_ROWS) // 8) * 8
        self.data = BLOCKS * self.tiles
        self.block_sent = up(MEAN * self.data)
        self.block_moved = up(QUARTER)
        self.block_back = up(MEAN * self.data + 2 * self.piece)
        self.block_probe = up(2 * self.piece)


def params(megabytes=58):
    return pltpu.CompilerParams(vmem_limit_bytes=megabytes << 20)


def tables():
    k = np.arange(16)
    root = np.exp(-2j * np.pi * np.outer(k, k) / 16) / 4
    kron = np.kron(root, root)

    def halves(x):
        hi = x.astype(np.float32).astype(jnp.bfloat16)
        lo = (x - hi.astype(np.float64)).astype(np.float32).astype(jnp.bfloat16)
        return hi, lo

    re_hi, re_lo = halves(kron.real)
    im_hi, im_lo = halves(kron.imag)
    hi = np.block([[re_hi, im_hi], [-im_hi, re_hi]])
    lo = np.block([[re_lo, im_lo], [-im_lo, re_lo]])
    right = np.concatenate([hi, hi, lo], axis=0)
    left = np.ascontiguousarray(right.T)
    low_u, low_v = np.divmod(np.arange(256), 16)
    twiddle = np.exp(
        -2j * np.pi * (np.outer(low_u, low_u) + np.outer(low_v, low_v)) / WIN
    )
    u = low_u[:, None] + 16 * low_u[None, :]
    v = low_v[:, None] + 16 * low_v[None, :]
    freq = lambda w: ((w + WIN // 2) % WIN - WIN // 2) / (WIN // 2)
    chirp = np.exp(-1j * CHIRP * (freq(u) ** 2 + freq(v) ** 2))
    pack = lambda z: np.stack([z.real, z.imag]).astype(np.float32)
    return left, right, pack(twiddle), pack(chirp)


def row_scale(x):
    peak = jnp.maximum(jnp.max(jnp.abs(x), axis=1, keepdims=True), 1e-30)
    return jnp.floor(jnp.log(peak) * (STEPS / LN2)) + 2.0


def encode(low, high):
    k_low, k_high = row_scale(low), row_scale(high)
    q_low = jnp.round(low * (jnp.exp(k_low * (-LN2 / STEPS)) * LEVELS)).astype(i32)
    q_high = jnp.round(high * (jnp.exp(k_high * (-LN2 / STEPS)) * LEVELS)).astype(i32)
    return (q_high << 16) | (q_low & 0xFFFF), k_low, k_high


def unscale(k):
    return jnp.exp(k.astype(f32) * (LN2 / STEPS)) * (1.0 / LEVELS)


def decode(words, k_low, k_high):
    low = ((words << 16) >> 16).astype(f32) * k_low
    high = (words >> 16).astype(f32) * k_high
    return low, high


def put_scales(scales, rows):
    lane = lax.broadcasted_iota(i32, (rows, LANES), 1)
    out = jnp.zeros((rows, LANES), f32)
    for i, k in enumerate(scales):
        out = jnp.where(lane == i, k, out)
    return out.astype(i32)


def make_plan(geo, counts_ref, positions_ref, map_ref, plan_ref, mine_ref):
    n = geo.owners
    me = lax.axis_index("scan").astype(i32)
    mine_ref[0] = me

    def spare(g):
        return jnp.maximum(counts_ref[g] - MEAN, 0)

    def body(o, carry):
        own = counts_ref[o] >= MEAN

        def behind(state):
            g, used = state
            return jnp.logical_and(
                jnp.logical_not(own),
                jnp.logical_and(used >= spare(g), g < n - 1),
            )

        g, used = lax.while_loop(behind, lambda state: (state[0] + 1, jnp.int32(0)), carry)
        dev = jnp.where(own, o, g)
        slot = jnp.where(own, 1, jnp.minimum(MEAN + used, CAP - 1))
        plan_ref[o] = positions_ref[0, 0, o]
        plan_ref[n + o] = positions_ref[0, 1, o]
        plan_ref[2 * n + o] = positions_ref[slot, 0, dev]
        plan_ref[3 * n + o] = positions_ref[slot, 1, dev]
        plan_ref[4 * n + o] = dev
        plan_ref[5 * n + o] = slot

        @pl.when(map_ref[o] == me)
        def _():
            mine_ref[1] = o

        return g, jnp.where(own, used, used + 1)

    lax.fori_loop(0, n, body, (jnp.int32(0), jnp.int32(0)))


def first_row(geo, slot, o, plan_ref, mine_ref):
    n, columns = geo.owners, geo.columns
    row, col = plan_ref[2 * slot * n + o], plan_ref[(2 * slot + 1) * n + o]
    own_class = mine_ref[1]
    row = row + ((own_class // columns - row) & 7)
    col = col + ((own_class % columns - col) & (columns - 1))
    return (row // 8) * geo.grid_cols + col // columns


def gather_kernel(
    geo, counts_ref, positions_ref, map_ref, tiles_hbm, plan_ref, mine_ref, out_ref, tiles_ref, sems
):
    n, b = geo.owners, geo.cols_b
    at = geo.block_sent - SCALE_ROWS
    copies = [
        pltpu.make_async_copy(tiles_hbm.at[:, pl.ds(j * LANES, LANES)], tiles_ref.at[j], sems.at[j])
        for j in range(2 * BLOCKS)
    ]
    for copy in copies:
        copy.start()
    make_plan(geo, counts_ref, positions_ref, map_ref, plan_ref, mine_ref)
    for copy in copies:
        copy.wait()

    def body(o, _):
        scales = []
        for slot in range(MEAN):
            start = first_row(geo, slot, o, plan_ref, mine_ref)
            for a in range(geo.rows_a):
                x = [tiles_ref[j, pl.ds(start + a * geo.grid_cols, b), :] for j in range(2 * BLOCKS)]
                words, k_low, k_high = encode(
                    jnp.concatenate(x[:BLOCKS], axis=1), jnp.concatenate(x[BLOCKS:], axis=1)
                )
                scales += [k_low, k_high]
                for j in range(BLOCKS):
                    rows = pl.ds(slot * geo.data + j * geo.tiles + a * b, b)
                    out_ref[o, rows, :] = words[:, j * LANES : (j + 1) * LANES]
        out_ref[o, pl.ds(at, b), :] = put_scales(scales, b)
        return 0

    lax.fori_loop(0, n, body, 0, unroll=4)


def gather_tiles(geo, counts, positions, owner_map, tiles):
    return pl.pallas_call(
        functools.partial(gather_kernel, geo),
        out_shape=(
            jax.ShapeDtypeStruct((6 * geo.owners,), i32),
            jax.ShapeDtypeStruct((2,), i32),
            jax.ShapeDtypeStruct((geo.owners, geo.block_sent, LANES), i32),
        ),
        in_specs=[SMEM, SMEM, SMEM, ANY],
        out_specs=(SMEM, SMEM, VMEM),
        scratch_shapes=[
            pltpu.VMEM((2 * BLOCKS, geo.grid_rows * geo.grid_cols, LANES), f32),
            pltpu.SemaphoreType.DMA((2 * BLOCKS,)),
        ],
        compiler_params=params(),
        cost_estimate=pl.CostEstimate(flops=1 << 23, bytes_accessed=4 << 20, transcendentals=0),
        name="gather",
    )(counts, positions, owner_map, tiles)


def moved_kernel(geo, plan_ref, mine_ref, own_ref, near1, near2, near3, out_ref, held_ref, sems):
    n, me = geo.owners, mine_ref[0]
    at = geo.block_moved - SCALE_ROWS
    fetch = [
        pltpu.make_async_copy(near, held_ref.at[k], sems.at[k])
        for k, near in enumerate((own_ref, near1, near2, near3))
    ]
    for copy in fetch:
        copy.start()
    for copy in fetch:
        copy.wait()

    def quarter(o, _):
        dev, spare = plan_ref[4 * n + o], plan_ref[5 * n + o] - MEAN
        near = dev ^ me

        @pl.when(near < SPREAD)
        def _():
            x = held_ref[near & (SPREAD - 1), jnp.maximum(spare, 0)].astype(f32)
            scales = []
            for i in range(QUARTER // 8):
                part = x[8 * i : 8 * (i + 1)]
                k = row_scale(part)
                scaled = jnp.round(part * (jnp.exp(k * (-LN2 / STEPS)) * LEVELS)).astype(i32)
                scales.append(k)
                out_ref[o, pl.ds(8 * i, 8), :] = (scaled[:, LANES:] << 16) | (scaled[:, :LANES] & 0xFFFF)
            out_ref[o, pl.ds(at, SCALE_ROWS), :] = put_scales(scales, SCALE_ROWS)

        return 0

    lax.fori_loop(0, n, quarter, 0)


def moved_quarters(geo, plan, mine, held):
    return pl.pallas_call(
        functools.partial(moved_kernel, geo),
        out_shape=jax.ShapeDtypeStruct((geo.owners, geo.block_moved, LANES), i32),
        in_specs=[SMEM, SMEM] + [ANY] * SPREAD,
        out_specs=VMEM,
        scratch_shapes=[
            pltpu.VMEM((SPREAD, CAP - MEAN, QUARTER, WIN), bf16),
            pltpu.SemaphoreType.DMA((SPREAD,)),
        ],
        compiler_params=params(),
        name="moved",
    )(plan, mine, *held)


def spare_kernel(measured_hbm, *rest):
    outs, measured_ref, sem = rest[:SPREAD], rest[SPREAD], rest[SPREAD + 1]
    copy = pltpu.make_async_copy(measured_hbm.at[pl.ds(MEAN, CAP - MEAN)], measured_ref, sem)
    copy.start()
    copy.wait()
    me = lax.axis_index("scan").astype(i32)
    for k, out_ref in enumerate(outs):
        rows = pl.ds(pl.multiple_of(((me ^ k) & (SPREAD - 1)) * QUARTER, QUARTER), QUARTER)
        for slot in range(CAP - MEAN):
            out_ref[slot] = measured_ref[slot, rows, :]


def near_quarters(geo, measured):
    shape = jax.ShapeDtypeStruct((CAP - MEAN, QUARTER, WIN), bf16)
    quarters = pl.pallas_call(
        spare_kernel,
        out_shape=[shape] * SPREAD,
        in_specs=[ANY],
        out_specs=[VMEM] * SPREAD,
        scratch_shapes=[pltpu.VMEM((CAP - MEAN, WIN, WIN), bf16), pltpu.SemaphoreType.DMA],
        compiler_params=params(),
        name="spare",
    )(measured)
    n = geo.owners
    return [quarters[0]] + [
        lax.ppermute(quarters[k], "scan", [(i, i ^ k) for i in range(n)]) for k in range(1, SPREAD)
    ]


def swap_tile_digits(x):
    blocks = x.shape[0] // 16
    rows = 8 * blocks
    parts = x.reshape(blocks, 2, 8, WIN)
    grid = [[parts[:, r, :, c * LANES : (c + 1) * LANES].reshape(rows, LANES) for c in range(2)] for r in range(2)]
    row = lax.broadcasted_iota(i32, (rows, LANES), 0)
    lane = lax.broadcasted_iota(i32, (rows, LANES), 1)

    def inner(q):
        for s in (4, 2, 1):
            shift = s * 16
            row_bit = (row & s) != 0
            lane_bit = (lane & shift) != 0
            moved = jnp.where(row_bit, pltpu.roll(q, s, 0), pltpu.roll(q, rows - s, 0))
            both = jnp.where(lane_bit, pltpu.roll(moved, shift, 1), pltpu.roll(moved, LANES - shift, 1))
            q = jnp.where(row_bit == lane_bit, q, both)
        return q.reshape(blocks, 1, 8, LANES)

    upper = jnp.concatenate([inner(grid[0][0]), inner(grid[1][0])], axis=3)
    lower = jnp.concatenate([inner(grid[0][1]), inner(grid[1][1])], axis=3)
    return jnp.concatenate([upper, lower], axis=1).reshape(16 * blocks, WIN)


def frequency_digits(x):
    turned = x.T
    lane = lax.broadcasted_iota(i32, (16, LANES), 1)
    halves = []
    for c in range(2):
        rows = [turned[16 * i : 16 * (i + 1), c * LANES : (c + 1) * LANES] for i in range(16)]
        for s in (1, 2, 4, 8):
            lane_bit = (lane & s) != 0
            new = list(rows)
            for i in range(16):
                if i & s == 0:
                    low, high = rows[i], rows[i | s]
                    new[i] = jnp.where(lane_bit, pltpu.roll(high, s, 1), low)
                    new[i | s] = jnp.where(lane_bit, high, pltpu.roll(low, LANES - s, 1))
            rows = new
        halves.append(jnp.concatenate(rows, axis=0))
    return jnp.concatenate(halves, axis=1)


def prepare_kernel(probe_ref, measured_ref, probe_out, measured_out):
    for c in range(2):
        probe_out[c] = swap_tile_digits(probe_ref[c])
    for k in range(MEAN):
        measured_out[k] = frequency_digits(measured_ref[k].astype(f32))


def prepare(probe, measured):
    return pl.pallas_call(
        prepare_kernel,
        out_shape=(
            jax.ShapeDtypeStruct((2, WIN, WIN), f32),
            jax.ShapeDtypeStruct((MEAN, WIN, WIN), f32),
        ),
        grid=(1,),
        in_specs=[
            pl.BlockSpec((2, WIN, WIN), lambda i: (0, 0, 0)),
            pl.BlockSpec((MEAN, WIN, WIN), lambda i: (0, 0, 0)),
        ],
        out_specs=(
            pl.BlockSpec((2, WIN, WIN), lambda i: (0, 0, 0)),
            pl.BlockSpec((MEAN, WIN, WIN), lambda i: (0, 0, 0)),
        ),
        compiler_params=params(),
        cost_estimate=pl.CostEstimate(flops=1 << 22, bytes_accessed=2 << 20, transcendentals=0),
        name="prepare",
    )(probe, measured)


def split(x):
    hi = x.astype(bf16)
    return hi, (x - hi.astype(f32)).astype(bf16)


def times_right(zs, right_ref):
    rows = []
    for z in zs:
        re_hi, re_lo = split(z[0])
        im_hi, im_lo = split(z[1])
        rows.append(jnp.concatenate([re_hi, im_hi, re_lo, im_lo, re_hi, im_hi], axis=1))
    out = jnp.dot(jnp.concatenate(rows, axis=0), right_ref[...], preferred_element_type=f32)
    return [(out[i * WIN : (i + 1) * WIN, :WIN], out[i * WIN : (i + 1) * WIN, WIN:]) for i in range(len(zs))]


def times_left(zs, left_ref):
    columns = []
    for z in zs:
        re_hi, re_lo = split(z[0])
        im_hi, im_lo = split(z[1])
        columns.append(jnp.concatenate([re_hi, im_hi, re_lo, im_lo, re_hi, im_hi], axis=0))
    out = jnp.dot(left_ref[...], jnp.concatenate(columns, axis=1), preferred_element_type=f32)
    return [(out[:WIN, i * WIN : (i + 1) * WIN], out[WIN:, i * WIN : (i + 1) * WIN]) for i in range(len(zs))]


def product(x, y):
    return x[0] * y[0] - x[1] * y[1], x[0] * y[1] + x[1] * y[0]


def product_conj(x, y):
    return x[0] * y[0] + x[1] * y[1], x[0] * y[1] - x[1] * y[0]


def conj(x):
    return x[0], -x[1]


class Tables:
    def __init__(self, hbm, vmem, sems):
        self.copies = [pltpu.make_async_copy(src, dst, sems.at[i]) for i, (src, dst) in enumerate(zip(hbm, vmem))]
        self.left, self.right, self.twiddle_ref, self.chirp_ref = vmem
        for i in (0, 2, 1, 3):
            self.copies[i].start()

    def wait(self):
        for copy in self.copies:
            copy.wait()

    def twiddle(self):
        return self.twiddle_ref[0], self.twiddle_ref[1]

    def chirp(self):
        return self.chirp_ref[0], self.chirp_ref[1]

    def spectrum(self, zs):
        return times_right([product(self.twiddle(), z) for z in times_left(zs, self.left)], self.right)

    def conj_inverse(self, zs):
        return times_left([product(self.twiddle(), z) for z in times_right(zs, self.right)], self.left)


def source(geo, slot, k, plan_ref, mine_ref, map_ref):
    n, columns, me = geo.owners, geo.columns, mine_ref[0]
    row, col = plan_ref[2 * slot * n + me], plan_ref[(2 * slot + 1) * n + me]
    return map_ref[((row + k // columns) & 7) * columns + ((col + k % columns) & (columns - 1))]


def tile_rows(geo, k, a):
    return pl.ds((8 * a + k // geo.columns) * ACROSS + k % geo.columns, geo.cols_b, geo.columns)


def plane(ref, i):
    return jnp.concatenate([ref[2 * i], ref[2 * i + 1]], axis=1)


def put_plane(ref, i, x):
    ref[2 * i] = x[:, :LANES]
    ref[2 * i + 1] = x[:, LANES:]


def put_marks(out_ref, o, at, first, scales):
    rows = scales[0].shape[0]
    lane = lax.broadcasted_iota(i32, (rows, LANES), 1)
    marks = out_ref[o, pl.ds(at, rows), :]
    for i, k in enumerate(scales):
        marks = jnp.where(lane == first + i, k.astype(i32), marks)
    out_ref[o, pl.ds(at, rows), :] = marks


def pack_tiles(geo, slot, refs, tile_ref, out_ref, at, marks_at):
    b = geo.cols_b

    def pack(k, _):
        dst = source(geo, slot, k, *refs)
        scales = []
        for a in range(geo.rows_a):
            x = [tile_ref[j, tile_rows(geo, k, a), :] for j in range(2 * BLOCKS)]
            words, k_low, k_high = encode(
                jnp.concatenate(x[:BLOCKS], axis=1), jnp.concatenate(x[BLOCKS:], axis=1)
            )
            scales += [k_low, k_high]
            for j in range(BLOCKS):
                rows = pl.ds(at + j * geo.tiles + a * b, b)
                out_ref[dst, rows, :] = words[:, j * LANES : (j + 1) * LANES]
        put_marks(out_ref, dst, marks_at, 2 * geo.rows_a * slot, scales)
        return 0

    lax.fori_loop(0, geo.owners, pack, 0, unroll=4)


def backward(tables, probe, tile_ref, middle, far, intensity):
    front = plane(tile_ref, 0), plane(tile_ref, 1)
    back = plane(tile_ref, 2), plane(tile_ref, 3)
    misfit = far[0] * far[0] + far[1] * far[1] - intensity
    (near,) = tables.conj_inverse([(misfit * far[0], -(misfit * far[1]))])
    grad_middle = conj(product(back, near))
    grad_back = product(middle, conj(near))
    put_plane(tile_ref, 2, grad_back[0])
    put_plane(tile_ref, 3, grad_back[1])
    (f,) = tables.spectrum([grad_middle])
    (e,) = tables.conj_inverse([product_conj(f, tables.chirp())])
    enter = conj(e)
    grad_front = product_conj(probe, enter)
    grad_probe = product_conj(front, enter)
    put_plane(tile_ref, 0, grad_front[0])
    put_plane(tile_ref, 1, grad_front[1])
    return grad_probe


def forward_kernel(
    geo, plan_ref, mine_ref, map_ref, in_ref, probe_ref, intensity_ref, *rest
):
    hbm, rest = rest[:4], rest[4:]
    out_ref, tile1_ref, waves_ref, tile0_ref, *rest = rest
    tables = Tables(hbm, rest[:4], rest[4])
    n, b = geo.owners, geo.cols_b
    refs = plan_ref, mine_ref, map_ref
    at = geo.block_sent - SCALE_ROWS
    tiles = tile0_ref, tile1_ref

    def unpack(k, _):
        for slot in range(MEAN):
            src = source(geo, slot, k, *refs)
            scales = unscale(in_ref[src, pl.ds(at, b), :])
            for a in range(geo.rows_a):
                c = 2 * (geo.rows_a * slot + a)
                for j in range(BLOCKS):
                    words = in_ref[src, pl.ds(slot * geo.data + j * geo.tiles + a * b, b), :]
                    low, high = decode(words, scales[:, c : c + 1], scales[:, c + 1 : c + 2])
                    tiles[slot][j, tile_rows(geo, k, a), :] = low
                    tiles[slot][BLOCKS + j, tile_rows(geo, k, a), :] = high
        return 0

    lax.fori_loop(0, n, unpack, 0, unroll=4)
    probe = lambda: (probe_ref[0], probe_ref[1])
    tables.wait()
    entrance = [product(probe(), (plane(t, 0), plane(t, 1))) for t in tiles]
    middle = tables.conj_inverse([conj(product(tables.chirp(), f)) for f in tables.spectrum(entrance)])
    far = tables.spectrum([product_conj(middle[s], (plane(t, 2), plane(t, 3))) for s, t in enumerate(tiles)])
    for c in range(2):
        waves_ref[c] = middle[1][c]
        waves_ref[2 + c] = far[1][c]
    grad_probe = backward(tables, probe(), tile0_ref, middle[0], far[0], intensity_ref[0])
    for c in range(2):
        waves_ref[4 + c] = grad_probe[c]
    pack_tiles(geo, 0, refs, tile0_ref, out_ref, 0, geo.block_back - SCALE_ROWS)


def backward_kernel(
    geo, plan_ref, mine_ref, map_ref, moved_in, probe_ref, intensity_ref, tile_in, waves_ref, back_in, *rest
):
    hbm, rest = rest[:4], rest[4:]
    back_hbm, tile_ref, moved_ref, out_ref, *rest = rest
    tables = Tables(hbm, rest[:4], rest[4])
    sems = rest[5]
    n, g, me = geo.owners, geo.group, mine_ref[0]
    refs = plan_ref, mine_ref, map_ref
    rows = geo.block_back - geo.data
    marks_at = rows - SCALE_ROWS
    fetch = [
        pltpu.make_async_copy(
            back_hbm.at[:, pl.ds(geo.data + marks_at, SCALE_ROWS)], out_ref.at[:, pl.ds(marks_at, SCALE_ROWS)], sems.at[0]
        ),
        pltpu.make_async_copy(tile_in, tile_ref, sems.at[1]),
    ]
    for copy in fetch:
        copy.start()

    dev = plan_ref[4 * n + me]
    for q in range(SPREAD):
        holder = (dev & -SPREAD) + q
        scales = unscale(moved_in[holder, pl.ds(geo.block_moved - SCALE_ROWS, SCALE_ROWS), :])
        for i in range(QUARTER // 8):
            words = moved_in[holder, pl.ds(8 * i, 8), :]
            low, high = decode(words, scales[:, i : i + 1], scales[:, i : i + 1])
            moved_ref[0, pl.ds(q * QUARTER + 8 * i, 8), :] = low
            moved_ref[1, pl.ds(q * QUARTER + 8 * i, 8), :] = high
    arrived = frequency_digits(jnp.concatenate([moved_ref[0], moved_ref[1]], axis=1))
    intensity = jnp.where(dev == me, intensity_ref[1], arrived)
    for copy in fetch:
        copy.wait()
    tables.wait()
    grad_probe = backward(
        tables, (probe_ref[0], probe_ref[1]), tile_ref,
        (waves_ref[0], waves_ref[1]), (waves_ref[2], waves_ref[3]), intensity,
    )
    pack_tiles(geo, 1, refs, tile_ref, out_ref, 0, marks_at)
    for c in range(2):
        put_plane(tile_ref, c, waves_ref[4 + c] + grad_probe[c])

    def pieces(o, _):
        scales = []
        for i in range(geo.piece // g):
            x = [tile_ref[j, pl.ds(o * geo.piece + i * g, g), :] for j in range(4)]
            words, k_low, k_high = encode(
                jnp.concatenate(x[:2], axis=1), jnp.concatenate(x[2:], axis=1)
            )
            scales += [k_low, k_high]
            for j in range(2):
                at = pl.ds(geo.data + j * geo.piece + i * g, g)
                out_ref[o, at, :] = words[:, j * LANES : (j + 1) * LANES]
        put_marks(out_ref, o, marks_at, 2 * geo.rows_a * MEAN, scales)
        return 0

    lax.fori_loop(0, n, pieces, 0, unroll=4)
    store = pltpu.make_async_copy(out_ref, back_hbm.at[:, pl.ds(geo.data, rows)], sems.at[0])
    store.start()
    store.wait()


def table_scratch(consts):
    return [pltpu.VMEM(c.shape, c.dtype) for c in consts] + [pltpu.SemaphoreType.DMA((len(consts),))]


def forward(geo, plan, mine, owner_map, come, probe, intensity, consts):
    tile = (2 * BLOCKS, WIN, LANES)
    return pl.pallas_call(
        functools.partial(forward_kernel, geo),
        out_shape=(
            jax.ShapeDtypeStruct((geo.owners, geo.block_back, LANES), i32),
            jax.ShapeDtypeStruct(tile, f32),
            jax.ShapeDtypeStruct((6, WIN, WIN), f32),
        ),
        in_specs=[SMEM] * 3 + [VMEM] * 3 + [ANY] * 4,
        out_specs=(VMEM, VMEM, VMEM),
        scratch_shapes=[pltpu.VMEM(tile, f32)] + table_scratch(consts),
        compiler_params=params(),
        cost_estimate=pl.CostEstimate(flops=20 << 30, bytes_accessed=8 << 20, transcendentals=0),
        name="forward",
    )(plan, mine, owner_map, come, probe, intensity, *consts)


def finish_second(geo, plan, mine, owner_map, moved, probe, intensity, tile, waves, back, consts):
    return pl.pallas_call(
        functools.partial(backward_kernel, geo),
        out_shape=jax.ShapeDtypeStruct(back.shape, i32),
        in_specs=[SMEM] * 3 + [VMEM] * 3 + [ANY, VMEM, ANY] + [ANY] * 4,
        out_specs=ANY,
        input_output_aliases={8: 0},
        scratch_shapes=[
            pltpu.VMEM(tile.shape, f32),
            pltpu.VMEM((2, WIN, LANES), f32),
            pltpu.VMEM((geo.owners, geo.block_back - geo.data, LANES), i32),
        ]
        + table_scratch(consts)
        + [pltpu.SemaphoreType.DMA((2,))],
        compiler_params=params(),
        cost_estimate=pl.CostEstimate(flops=6 << 30, bytes_accessed=8 << 20, transcendentals=0),
        name="backward",
    )(plan, mine, owner_map, moved, probe, intensity, tile, waves, back, *consts)


def add_kernel(geo, plan_ref, mine_ref, in_ref, grad_hbm, grad_ref, sems):
    b = geo.cols_b
    grad_ref[...] = jnp.zeros_like(grad_ref)

    def body(o, _):
        scales = unscale(in_ref[o, pl.ds(geo.block_back - SCALE_ROWS, b), :])
        for slot in range(MEAN):
            start = first_row(geo, slot, o, plan_ref, mine_ref)
            for a in range(geo.rows_a):
                at = 2 * (geo.rows_a * slot + a)
                k_low, k_high = scales[:, at : at + 1], scales[:, at + 1 : at + 2]
                rows = pl.ds(start + a * geo.grid_cols, b)
                for j in range(BLOCKS):
                    words = in_ref[o, pl.ds(slot * geo.data + j * geo.tiles + a * b, b), :]
                    low, high = decode(words, k_low, k_high)
                    grad_ref[j, rows, :] += low
                    grad_ref[BLOCKS + j, rows, :] += high
        return 0

    lax.fori_loop(0, geo.owners, body, 0, unroll=2)
    copies = [
        pltpu.make_async_copy(grad_ref.at[j], grad_hbm.at[:, pl.ds(j * LANES, LANES)], sems.at[j])
        for j in range(2 * BLOCKS)
    ]
    for copy in copies:
        copy.start()
    for copy in copies:
        copy.wait()


def add_up(geo, plan, mine, returned):
    return pl.pallas_call(
        functools.partial(add_kernel, geo),
        out_shape=jax.ShapeDtypeStruct((geo.grid_rows * geo.grid_cols, 2 * HALF), f32),
        in_specs=[SMEM, SMEM, VMEM],
        out_specs=ANY,
        scratch_shapes=[
            pltpu.VMEM((2 * BLOCKS, geo.grid_rows * geo.grid_cols, LANES), f32),
            pltpu.SemaphoreType.DMA((2 * BLOCKS,)),
        ],
        compiler_params=params(),
        cost_estimate=pl.CostEstimate(flops=1 << 23, bytes_accessed=4 << 20, transcendentals=0),
        name="add",
    )(plan, mine, returned)


def sum_kernel(geo, in_hbm, out_ref, in_ref, sem):
    g = geo.group
    rows = geo.block_back - MEAN * geo.data
    copy = pltpu.make_async_copy(in_hbm.at[:, pl.ds(MEAN * geo.data, rows)], in_ref, sem)
    copy.start()
    copy.wait()
    count = geo.piece // g

    def add_piece(o, sums):
        scales = unscale(in_ref[o, pl.ds(rows - SCALE_ROWS, g), :])
        new = []
        for i in range(count):
            at = 2 * (geo.rows_a * MEAN + i)
            k_low, k_high = scales[:, at : at + 1], scales[:, at + 1 : at + 2]
            for j in range(2):
                words = in_ref[o, pl.ds(j * geo.piece + i * g, g), :]
                low, high = decode(words, k_low, k_high)
                new += [sums[len(new)] + low, sums[len(new) + 1] + high]
        return tuple(new)

    sums = lax.fori_loop(0, geo.owners, add_piece, (jnp.zeros((g, LANES), f32),) * (4 * count), unroll=4)
    parts, scales = [], []
    low = jnp.concatenate([jnp.concatenate([sums[4 * i], sums[4 * i + 2]], axis=1) for i in range(count)], axis=0)
    high = jnp.concatenate([jnp.concatenate([sums[4 * i + 1], sums[4 * i + 3]], axis=1) for i in range(count)], axis=0)
    if geo.whole_blocks:
        low, high = swap_tile_digits(low), swap_tile_digits(high)
    for i in range(count):
        rows = slice(i * g, (i + 1) * g)
        words, k_low, k_high = encode(low[rows], high[rows])
        parts.append(words)
        scales += [k_low, k_high]
    marks = put_scales(scales, g)

    def spread(o, _):
        for i in range(count):
            for j in range(2):
                out_ref[o, pl.ds(j * geo.piece + i * g, g), :] = parts[i][:, j * LANES : (j + 1) * LANES]
        out_ref[o, pl.ds(geo.block_probe - SCALE_ROWS, g), :] = marks
        return 0

    lax.fori_loop(0, geo.owners, spread, 0, unroll=4)


def sum_pieces(geo, returned):
    return pl.pallas_call(
        functools.partial(sum_kernel, geo),
        out_shape=jax.ShapeDtypeStruct((geo.owners, geo.block_probe, LANES), i32),
        in_specs=[ANY],
        out_specs=VMEM,
        scratch_shapes=[
            pltpu.VMEM((geo.owners, geo.block_back - MEAN * geo.data, LANES), i32),
            pltpu.SemaphoreType.DMA,
        ],
        compiler_params=params(),
        name="sum",
    )(returned)


def finish_kernel(geo, in_ref, out_ref, whole_ref):
    g = geo.group

    def place(o, _):
        scales = unscale(in_ref[o, pl.ds(geo.block_probe - SCALE_ROWS, g), :])
        for i in range(geo.piece // g):
            k_low, k_high = scales[:, 2 * i : 2 * i + 1], scales[:, 2 * i + 1 : 2 * i + 2]
            for j in range(2):
                words = in_ref[o, pl.ds(j * geo.piece + i * g, g), :]
                low, high = decode(words, k_low, k_high)
                rows = pl.ds(o * geo.piece + i * g, g)
                whole_ref[0, j, rows, :] = low
                whole_ref[1, j, rows, :] = high
        return 0

    lax.fori_loop(0, geo.owners, place, 0, unroll=4)
    for c in range(2):
        x = jnp.concatenate([whole_ref[c, 0], whole_ref[c, 1]], axis=1)
        out_ref[c] = x if geo.whole_blocks else swap_tile_digits(x)


def finish_probe(geo, parts):
    return pl.pallas_call(
        functools.partial(finish_kernel, geo),
        out_shape=jax.ShapeDtypeStruct((2, WIN, WIN), f32),
        in_specs=[VMEM],
        out_specs=VMEM,
        scratch_shapes=[pltpu.VMEM((2, 2, WIN, LANES), f32)],
        compiler_params=params(),
        name="finish",
    )(parts)


def exchange(x):
    return lax.all_to_all(x, "scan", split_axis=0, concat_axis=0, tiled=True)


def local(object_tiles, probe, measured, positions, counts, owner_map):
    n = lax.axis_size("scan")
    geo = Geometry(n, object_tiles.shape[1], object_tiles.shape[2])
    consts = [jnp.asarray(t) for t in tables()]
    tiles = object_tiles.reshape(geo.grid_rows * geo.grid_cols, 2 * HALF)

    plan, mine, sent = gather_tiles(geo, counts, positions.transpose(1, 2, 0), owner_map, tiles)
    sent, measured, probe = lax.optimization_barrier((sent, measured, probe))
    come = exchange(sent)
    held = near_quarters(geo, measured)
    moved = moved_quarters(geo, plan, mine, held)
    moved, come = lax.optimization_barrier((moved, come))
    moved = exchange(moved)
    probe_t, intensity = prepare(probe, measured)
    back, tile, waves = forward(geo, plan, mine, owner_map, come, probe_t, intensity, consts)
    back = finish_second(geo, plan, mine, owner_map, moved, probe_t, intensity, tile, waves, back, consts)
    returned = exchange(back)
    probe_grad = finish_probe(geo, exchange(sum_pieces(geo, returned)))
    grad = add_up(geo, plan, mine, returned)
    return grad.reshape(object_tiles.shape), probe_grad


def solution(mesh):
    return jax.shard_map(
        local,
        mesh=mesh,
        in_specs=(
            P(("groups", "scan"), None, None, None),
            P("groups", None, None),
            P(("groups", "scan"), None, None),
            P("groups", None, None),
            P("groups"),
            P(),
        ),
        out_specs=(P(("groups", "scan"), None, None, None), P("groups", None, None)),
        check_vma=False,
    )
```

```python
import functools
import math

import jax
import jax.numpy as jnp
import numpy as np
from jax import lax
from jax.experimental import pallas as pl
from jax.experimental.pallas import tpu as pltpu
from jax.sharding import PartitionSpec as P

WIN = 256
TILE = 16
ACROSS = WIN // TILE
SLICES = 2
MEAN = 2
CAP = 6
CHIRP = 1.5
HALF = SLICES * TILE * TILE
LANES = 128
BLOCKS = HALF // LANES
SCALE_ROWS = 8
SPREAD = 4
QUARTER = WIN // SPREAD
STEPS = 32.0
LEVELS = 32700.0
LN2 = math.log(2.0)

f32 = jnp.float32
i32 = jnp.int32
bf16 = jnp.bfloat16
SMEM = pl.BlockSpec(memory_space=pltpu.SMEM)
VMEM = pl.BlockSpec(memory_space=pltpu.VMEM)
ANY = pl.BlockSpec(memory_space=pl.ANY)


class Geometry:
    def __init__(self, owners, grid_rows, grid_cols):
        self.owners = owners
        self.columns = owners // 8
        self.rows_a = ACROSS // 8
        self.cols_b = ACROSS // self.columns
        self.tiles = self.rows_a * self.cols_b
        self.grid_rows = grid_rows
        self.grid_cols = grid_cols
        self.piece = WIN // owners
        self.group = min(8, self.piece)
        self.whole_blocks = self.piece % 16 == 0
        up = lambda rows: -(-(rows + SCALE_ROWS) // 8) * 8
        self.data = BLOCKS * self.tiles
        self.block_sent = up(MEAN * self.data)
        self.block_moved = up(QUARTER)
        self.block_back = up(MEAN * self.data + 2 * self.piece)
        self.block_probe = up(2 * self.piece)


def params(megabytes=58):
    return pltpu.CompilerParams(vmem_limit_bytes=megabytes << 20)


def tables():
    k = np.arange(16)
    root = np.exp(-2j * np.pi * np.outer(k, k) / 16) / 4
    kron = np.kron(root, root)

    def halves(x):
        hi = x.astype(np.float32).astype(jnp.bfloat16)
        lo = (x - hi.astype(np.float64)).astype(np.float32).astype(jnp.bfloat16)
        return hi, lo

    re_hi, re_lo = halves(kron.real)
    im_hi, im_lo = halves(kron.imag)
    hi = np.block([[re_hi, -im_hi], [im_hi, re_hi]])
    lo = np.block([[re_lo, -im_lo], [im_lo, re_lo]])
    left = np.concatenate([hi, hi, lo], axis=1)
    right = np.concatenate([re_hi, im_hi, re_hi, im_hi, re_lo, im_lo], axis=0)
    low_u, low_v = np.divmod(np.arange(256), 16)
    twiddle = np.exp(
        -2j * np.pi * (np.outer(low_u, low_u) + np.outer(low_v, low_v)) / WIN
    )
    u = low_u[:, None] + 16 * low_u[None, :]
    v = low_v[:, None] + 16 * low_v[None, :]
    freq = lambda w: ((w + WIN // 2) % WIN - WIN // 2) / (WIN // 2)
    chirp = np.exp(-1j * CHIRP * (freq(u) ** 2 + freq(v) ** 2))
    pack = lambda z: np.stack([z.real, z.imag]).astype(np.float32)
    return left, right, pack(twiddle), pack(chirp)


def row_scale(x):
    peak = jnp.maximum(jnp.max(jnp.abs(x), axis=1, keepdims=True), 1e-30)
    return jnp.floor(jnp.log(peak) * (STEPS / LN2)) + 2.0


def encode(low, high):
    k_low, k_high = row_scale(low), row_scale(high)
    q_low = jnp.round(low * (jnp.exp(k_low * (-LN2 / STEPS)) * LEVELS)).astype(i32)
    q_high = jnp.round(high * (jnp.exp(k_high * (-LN2 / STEPS)) * LEVELS)).astype(i32)
    return (q_high << 16) | (q_low & 0xFFFF), k_low, k_high


def unscale(k):
    return jnp.exp(k.astype(f32) * (LN2 / STEPS)) * (1.0 / LEVELS)


def decode(words, k_low, k_high):
    low = ((words << 16) >> 16).astype(f32) * k_low
    high = (words >> 16).astype(f32) * k_high
    return low, high


def put_scales(scales, rows):
    lane = lax.broadcasted_iota(i32, (rows, LANES), 1)
    out = jnp.zeros((rows, LANES), f32)
    for i, k in enumerate(scales):
        out = jnp.where(lane == i, k, out)
    return out.astype(i32)


def make_plan(geo, counts_ref, positions_ref, map_ref, plan_ref, mine_ref):
    n = geo.owners
    me = lax.axis_index("scan").astype(i32)
    mine_ref[0] = me

    def spare(g):
        return jnp.maximum(counts_ref[g] - MEAN, 0)

    def body(o, carry):
        own = counts_ref[o] >= MEAN

        def behind(state):
            g, used = state
            return jnp.logical_and(
                jnp.logical_not(own),
                jnp.logical_and(used >= spare(g), g < n - 1),
            )

        g, used = lax.while_loop(behind, lambda state: (state[0] + 1, jnp.int32(0)), carry)
        dev = jnp.where(own, o, g)
        slot = jnp.where(own, 1, jnp.minimum(MEAN + used, CAP - 1))
        plan_ref[o] = positions_ref[0, 0, o]
        plan_ref[n + o] = positions_ref[0, 1, o]
        plan_ref[2 * n + o] = positions_ref[slot, 0, dev]
        plan_ref[3 * n + o] = positions_ref[slot, 1, dev]
        plan_ref[4 * n + o] = dev
        plan_ref[5 * n + o] = slot

        @pl.when(map_ref[o] == me)
        def _():
            mine_ref[1] = o

        return g, jnp.where(own, used, used + 1)

    lax.fori_loop(0, n, body, (jnp.int32(0), jnp.int32(0)))


def first_row(geo, slot, o, plan_ref, mine_ref):
    n, columns = geo.owners, geo.columns
    row, col = plan_ref[2 * slot * n + o], plan_ref[(2 * slot + 1) * n + o]
    own_class = mine_ref[1]
    row = row + ((own_class // columns - row) & 7)
    col = col + ((own_class % columns - col) & (columns - 1))
    return (row // 8) * geo.grid_cols + col // columns


def gather_kernel(
    geo, counts_ref, positions_ref, map_ref, tiles_hbm, plan_ref, mine_ref, out_ref, tiles_ref, sems
):
    n, b = geo.owners, geo.cols_b
    at = geo.block_sent - SCALE_ROWS
    copies = [
        pltpu.make_async_copy(tiles_hbm.at[:, pl.ds(j * LANES, LANES)], tiles_ref.at[j], sems.at[j])
        for j in range(2 * BLOCKS)
    ]
    for copy in copies:
        copy.start()
    make_plan(geo, counts_ref, positions_ref, map_ref, plan_ref, mine_ref)
    for copy in copies:
        copy.wait()

    def body(o, _):
        scales = []
        for slot in range(MEAN):
            start = first_row(geo, slot, o, plan_ref, mine_ref)
            for a in range(geo.rows_a):
                x = [tiles_ref[j, pl.ds(start + a * geo.grid_cols, b), :] for j in range(2 * BLOCKS)]
                words, k_low, k_high = encode(
                    jnp.concatenate(x[:BLOCKS], axis=1), jnp.concatenate(x[BLOCKS:], axis=1)
                )
                scales += [k_low, k_high]
                for j in range(BLOCKS):
                    rows = pl.ds(slot * geo.data + j * geo.tiles + a * b, b)
                    out_ref[o, rows, :] = words[:, j * LANES : (j + 1) * LANES]
        out_ref[o, pl.ds(at, b), :] = put_scales(scales, b)
        return 0

    lax.fori_loop(0, n, body, 0, unroll=4)


def gather_tiles(geo, counts, positions, owner_map, tiles):
    return pl.pallas_call(
        functools.partial(gather_kernel, geo),
        out_shape=(
            jax.ShapeDtypeStruct((6 * geo.owners,), i32),
            jax.ShapeDtypeStruct((2,), i32),
            jax.ShapeDtypeStruct((geo.owners, geo.block_sent, LANES), i32),
        ),
        in_specs=[SMEM, SMEM, SMEM, ANY],
        out_specs=(SMEM, SMEM, VMEM),
        scratch_shapes=[
            pltpu.VMEM((2 * BLOCKS, geo.grid_rows * geo.grid_cols, LANES), f32),
            pltpu.SemaphoreType.DMA((2 * BLOCKS,)),
        ],
        compiler_params=params(),
        cost_estimate=pl.CostEstimate(flops=1 << 23, bytes_accessed=4 << 20, transcendentals=0),
        name="gather",
    )(counts, positions, owner_map, tiles)


def moved_kernel(geo, plan_ref, mine_ref, own_ref, near1, near2, near3, out_ref, held_ref, sems):
    n, me = geo.owners, mine_ref[0]
    at = geo.block_moved - SCALE_ROWS
    fetch = [
        pltpu.make_async_copy(near, held_ref.at[k], sems.at[k])
        for k, near in enumerate((own_ref, near1, near2, near3))
    ]
    for copy in fetch:
        copy.start()
    for copy in fetch:
        copy.wait()

    def quarter(o, _):
        dev, spare = plan_ref[4 * n + o], plan_ref[5 * n + o] - MEAN
        near = dev ^ me

        @pl.when(near < SPREAD)
        def _():
            x = held_ref[near & (SPREAD - 1), jnp.maximum(spare, 0)].astype(f32)
            scales = []
            for i in range(QUARTER // 8):
                part = x[8 * i : 8 * (i + 1)]
                k = row_scale(part)
                scaled = jnp.round(part * (jnp.exp(k * (-LN2 / STEPS)) * LEVELS)).astype(i32)
                scales.append(k)
                out_ref[o, pl.ds(8 * i, 8), :] = (scaled[:, LANES:] << 16) | (scaled[:, :LANES] & 0xFFFF)
            out_ref[o, pl.ds(at, SCALE_ROWS), :] = put_scales(scales, SCALE_ROWS)

        return 0

    lax.fori_loop(0, n, quarter, 0)


def moved_quarters(geo, plan, mine, held):
    return pl.pallas_call(
        functools.partial(moved_kernel, geo),
        out_shape=jax.ShapeDtypeStruct((geo.owners, geo.block_moved, LANES), i32),
        in_specs=[SMEM, SMEM] + [ANY] * SPREAD,
        out_specs=VMEM,
        scratch_shapes=[
            pltpu.VMEM((SPREAD, CAP - MEAN, QUARTER, WIN), bf16),
            pltpu.SemaphoreType.DMA((SPREAD,)),
        ],
        compiler_params=params(),
        name="moved",
    )(plan, mine, *held)


def spare_kernel(measured_hbm, *rest):
    outs, measured_ref, sem = rest[:SPREAD], rest[SPREAD], rest[SPREAD + 1]
    copy = pltpu.make_async_copy(measured_hbm.at[pl.ds(MEAN, CAP - MEAN)], measured_ref, sem)
    copy.start()
    copy.wait()
    me = lax.axis_index("scan").astype(i32)
    for k, out_ref in enumerate(outs):
        rows = pl.ds(pl.multiple_of(((me ^ k) & (SPREAD - 1)) * QUARTER, QUARTER), QUARTER)
        for slot in range(CAP - MEAN):
            out_ref[slot] = measured_ref[slot, rows, :]


def near_quarters(geo, measured):
    shape = jax.ShapeDtypeStruct((CAP - MEAN, QUARTER, WIN), bf16)
    quarters = pl.pallas_call(
        spare_kernel,
        out_shape=[shape] * SPREAD,
        in_specs=[ANY],
        out_specs=[VMEM] * SPREAD,
        scratch_shapes=[pltpu.VMEM((CAP - MEAN, WIN, WIN), bf16), pltpu.SemaphoreType.DMA],
        compiler_params=params(),
        name="spare",
    )(measured)
    n = geo.owners
    return [quarters[0]] + [
        lax.ppermute(quarters[k], "scan", [(i, i ^ k) for i in range(n)]) for k in range(1, SPREAD)
    ]


def swap_tile_digits(x):
    blocks = x.shape[0] // 16
    rows = 8 * blocks
    parts = x.reshape(blocks, 2, 8, WIN)
    grid = [[parts[:, r, :, c * LANES : (c + 1) * LANES].reshape(rows, LANES) for c in range(2)] for r in range(2)]
    row = lax.broadcasted_iota(i32, (rows, LANES), 0)
    lane = lax.broadcasted_iota(i32, (rows, LANES), 1)

    def inner(q):
        for s in (4, 2, 1):
            shift = s * 16
            row_bit = (row & s) != 0
            lane_bit = (lane & shift) != 0
            moved = jnp.where(row_bit, pltpu.roll(q, s, 0), pltpu.roll(q, rows - s, 0))
            both = jnp.where(lane_bit, pltpu.roll(moved, shift, 1), pltpu.roll(moved, LANES - shift, 1))
            q = jnp.where(row_bit == lane_bit, q, both)
        return q.reshape(blocks, 1, 8, LANES)

    upper = jnp.concatenate([inner(grid[0][0]), inner(grid[1][0])], axis=3)
    lower = jnp.concatenate([inner(grid[0][1]), inner(grid[1][1])], axis=3)
    return jnp.concatenate([upper, lower], axis=1).reshape(16 * blocks, WIN)


def frequency_digits(x):
    turned = x.T
    lane = lax.broadcasted_iota(i32, (16, LANES), 1)
    halves = []
    for c in range(2):
        rows = [turned[16 * i : 16 * (i + 1), c * LANES : (c + 1) * LANES] for i in range(16)]
        for s in (1, 2, 4, 8):
            lane_bit = (lane & s) != 0
            new = list(rows)
            for i in range(16):
                if i & s == 0:
                    low, high = rows[i], rows[i | s]
                    new[i] = jnp.where(lane_bit, pltpu.roll(high, s, 1), low)
                    new[i | s] = jnp.where(lane_bit, high, pltpu.roll(low, LANES - s, 1))
            rows = new
        halves.append(jnp.concatenate(rows, axis=0))
    return jnp.concatenate(halves, axis=1)


def prepare_kernel(probe_ref, measured_ref, probe_out, measured_out):
    for c in range(2):
        probe_out[c] = swap_tile_digits(probe_ref[c])
    for k in range(MEAN):
        measured_out[k] = frequency_digits(measured_ref[k].astype(f32))


def prepare(probe, measured):
    return pl.pallas_call(
        prepare_kernel,
        out_shape=(
            jax.ShapeDtypeStruct((2, WIN, WIN), f32),
            jax.ShapeDtypeStruct((MEAN, WIN, WIN), f32),
        ),
        grid=(1,),
        in_specs=[
            pl.BlockSpec((2, WIN, WIN), lambda i: (0, 0, 0)),
            pl.BlockSpec((MEAN, WIN, WIN), lambda i: (0, 0, 0)),
        ],
        out_specs=(
            pl.BlockSpec((2, WIN, WIN), lambda i: (0, 0, 0)),
            pl.BlockSpec((MEAN, WIN, WIN), lambda i: (0, 0, 0)),
        ),
        compiler_params=params(),
        cost_estimate=pl.CostEstimate(flops=1 << 22, bytes_accessed=2 << 20, transcendentals=0),
        name="prepare",
    )(probe, measured)


def split(x):
    hi = x.astype(bf16)
    return hi, (x - hi.astype(f32)).astype(bf16)


def times_right(zs, right_ref):
    rows = []
    for z in zs:
        re_hi, re_lo = split(z[0])
        im_hi, im_lo = split(z[1])
        rows.append(jnp.concatenate([re_hi, -im_hi, re_lo, -im_lo, re_hi, -im_hi], axis=1))
        rows.append(jnp.concatenate([im_hi, re_hi, im_lo, re_lo, im_hi, re_hi], axis=1))
    out = jnp.dot(jnp.concatenate(rows, axis=0), right_ref[...], preferred_element_type=f32)
    parts = [out[i * WIN : (i + 1) * WIN] for i in range(2 * len(zs))]
    return list(zip(parts[::2], parts[1::2]))


def times_left(zs, left_ref):
    columns = []
    for z in zs:
        re_hi, re_lo = split(z[0])
        im_hi, im_lo = split(z[1])
        columns.append(jnp.concatenate([re_hi, im_hi, re_lo, im_lo, re_hi, im_hi], axis=0))
    out = jnp.dot(left_ref[...], jnp.concatenate(columns, axis=1), preferred_element_type=f32)
    return [(out[:WIN, i * WIN : (i + 1) * WIN], out[WIN:, i * WIN : (i + 1) * WIN]) for i in range(len(zs))]


def product(x, y):
    return x[0] * y[0] - x[1] * y[1], x[0] * y[1] + x[1] * y[0]


def product_conj(x, y):
    return x[0] * y[0] + x[1] * y[1], x[0] * y[1] - x[1] * y[0]


def conj(x):
    return x[0], -x[1]


class Fetched:
    def __init__(self, copies):
        self.copies = {}
        for name, (src, dst, sem) in copies.items():
            self.copies[name] = pltpu.make_async_copy(src, dst, sem)
            self.copies[name].start()
        self.refs = {name: dst for name, (_, dst, _) in copies.items()}

    def __getitem__(self, name):
        if name in self.copies:
            self.copies.pop(name).wait()
        return self.refs[name]

    def pair(self, name):
        ref = self[name]
        return ref[0], ref[1]

    def spectrum(self, zs):
        zs = times_left(zs, self["left"])
        return times_right([product(self.pair("twiddle"), z) for z in zs], self["right"])

    def conj_inverse(self, zs):
        zs = times_right(zs, self["right"])
        return times_left([product(self.pair("twiddle"), z) for z in zs], self["left"])


def source(geo, slot, k, plan_ref, mine_ref, map_ref):
    n, columns, me = geo.owners, geo.columns, mine_ref[0]
    row, col = plan_ref[2 * slot * n + me], plan_ref[(2 * slot + 1) * n + me]
    return map_ref[((row + k // columns) & 7) * columns + ((col + k % columns) & (columns - 1))]


def tile_rows(geo, k, a):
    return pl.ds((8 * a + k // geo.columns) * ACROSS + k % geo.columns, geo.cols_b, geo.columns)


def plane(ref, i):
    return jnp.concatenate([ref[2 * i], ref[2 * i + 1]], axis=1)


def put_plane(ref, i, x):
    ref[2 * i] = x[:, :LANES]
    ref[2 * i + 1] = x[:, LANES:]


def put_marks(out_ref, o, at, first, scales):
    rows = scales[0].shape[0]
    lane = lax.broadcasted_iota(i32, (rows, LANES), 1)
    marks = out_ref[o, pl.ds(at, rows), :]
    for i, k in enumerate(scales):
        marks = jnp.where(lane == first + i, k.astype(i32), marks)
    out_ref[o, pl.ds(at, rows), :] = marks


def pack_tiles(geo, slot, refs, tile_ref, out_ref, at, marks_at):
    b = geo.cols_b

    def pack(k, _):
        dst = source(geo, slot, k, *refs)
        scales = []
        for a in range(geo.rows_a):
            x = [tile_ref[j, tile_rows(geo, k, a), :] for j in range(2 * BLOCKS)]
            words, k_low, k_high = encode(
                jnp.concatenate(x[:BLOCKS], axis=1), jnp.concatenate(x[BLOCKS:], axis=1)
            )
            scales += [k_low, k_high]
            for j in range(BLOCKS):
                rows = pl.ds(at + j * geo.tiles + a * b, b)
                out_ref[dst, rows, :] = words[:, j * LANES : (j + 1) * LANES]
        put_marks(out_ref, dst, marks_at, 2 * geo.rows_a * slot, scales)
        return 0

    lax.fori_loop(0, geo.owners, pack, 0, unroll=4)


def backward(fetched, tile_ref, middle, far, intensity):
    misfit = far[0] * far[0] + far[1] * far[1] - intensity
    (near,) = fetched.conj_inverse([(misfit * far[0], -(misfit * far[1]))])
    grad_middle = conj(product((plane(tile_ref, 2), plane(tile_ref, 3)), near))
    grad_back = product(middle(), conj(near))
    put_plane(tile_ref, 2, grad_back[0])
    put_plane(tile_ref, 3, grad_back[1])
    (f,) = fetched.spectrum([grad_middle])
    (e,) = fetched.conj_inverse([product_conj(f, fetched.pair("chirp"))])
    enter = conj(e)
    grad_probe = product_conj((plane(tile_ref, 0), plane(tile_ref, 1)), enter)
    grad_front = product_conj(fetched.pair("probe"), enter)
    put_plane(tile_ref, 0, grad_front[0])
    put_plane(tile_ref, 1, grad_front[1])
    return grad_probe


def forward_kernel(
    geo, plan_ref, mine_ref, map_ref, in_ref, probe_in, intensity_in, left_in, right_in, twiddle_in, chirp_in,
    back_hbm, tile1_hbm, waves_hbm,
    out_ref, tile0_ref, tile1_ref, waves_ref, probe_ref, intensity_ref, left_ref, right_ref, twiddle_ref, chirp_ref,
    sems,
):
    fetched = Fetched(
        {
            "probe": (probe_in, probe_ref, sems.at[0]),
            "left": (left_in, left_ref, sems.at[1]),
            "twiddle": (twiddle_in, twiddle_ref, sems.at[2]),
            "right": (right_in, right_ref, sems.at[3]),
            "chirp": (chirp_in, chirp_ref, sems.at[4]),
            "intensity": (intensity_in.at[0], intensity_ref, sems.at[5]),
        }
    )
    n, b = geo.owners, geo.cols_b
    refs = plan_ref, mine_ref, map_ref
    at = geo.block_sent - SCALE_ROWS
    tiles = tile0_ref, tile1_ref

    def unpack(k, _):
        for slot in range(MEAN):
            src = source(geo, slot, k, *refs)
            scales = unscale(in_ref[src, pl.ds(at, b), :])
            for a in range(geo.rows_a):
                c = 2 * (geo.rows_a * slot + a)
                for j in range(BLOCKS):
                    words = in_ref[src, pl.ds(slot * geo.data + j * geo.tiles + a * b, b), :]
                    low, high = decode(words, scales[:, c : c + 1], scales[:, c + 1 : c + 2])
                    tiles[slot][j, tile_rows(geo, k, a), :] = low
                    tiles[slot][BLOCKS + j, tile_rows(geo, k, a), :] = high
        return 0

    lax.fori_loop(0, n, unpack, 0, unroll=4)
    going = [pltpu.make_async_copy(tile1_ref, tile1_hbm, sems.at[6])]
    going[0].start()
    entrance = [product(fetched.pair("probe"), (plane(t, 0), plane(t, 1))) for t in tiles]
    waves = fetched.spectrum(entrance)
    middle = fetched.conj_inverse([conj(product(fetched.pair("chirp"), f)) for f in waves])
    far = fetched.spectrum([product_conj(middle[s], (plane(t, 2), plane(t, 3))) for s, t in enumerate(tiles)])
    for c in range(2):
        waves_ref[c] = far[1][c]
        waves_ref[2 + c] = middle[1][c]
    going.append(pltpu.make_async_copy(waves_ref.at[pl.ds(0, 4)], waves_hbm.at[pl.ds(0, 4)], sems.at[7]))
    going[1].start()
    intensity = fetched["intensity"]
    grad_probe = backward(fetched, tile0_ref, lambda: middle[0], far[0], intensity[...])
    for c in range(2):
        waves_ref[4 + c] = grad_probe[c]
    going.append(pltpu.make_async_copy(waves_ref.at[pl.ds(4, 2)], waves_hbm.at[pl.ds(4, 2)], sems.at[8]))
    going[2].start()
    pack_tiles(geo, 0, refs, tile0_ref, out_ref, 0, geo.data)
    for i, (src, dst, rows) in enumerate(
        [(0, 0, geo.data), (geo.data, geo.block_back - SCALE_ROWS, SCALE_ROWS)]
    ):
        going.append(
            pltpu.make_async_copy(out_ref.at[:, pl.ds(src, rows)], back_hbm.at[:, pl.ds(dst, rows)], sems.at[9 + i])
        )
        going[-1].start()
    for copy in going:
        copy.wait()


def backward_kernel(
    geo, plan_ref, mine_ref, map_ref, moved_in, probe_in, intensity_in, tile_in, waves_in, back_in,
    left_in, right_in, twiddle_in, chirp_in,
    back_hbm,
    out_ref, tile_ref, moved_ref, waves_ref, probe_ref, intensity_ref, left_ref, right_ref, twiddle_ref, chirp_ref,
    sems,
):
    n, g, me = geo.owners, geo.group, mine_ref[0]
    rows = geo.block_back - geo.data
    marks_at = rows - SCALE_ROWS
    pair = lambda ref, i: ref.at[pl.ds(2 * i, 2)]
    fetched = Fetched(
        {
            "far": (pair(waves_in, 0), pair(waves_ref, 0), sems.at[0]),
            "intensity": (intensity_in.at[1], intensity_ref, sems.at[1]),
            "right": (right_in, right_ref, sems.at[2]),
            "twiddle": (twiddle_in, twiddle_ref, sems.at[3]),
            "left": (left_in, left_ref, sems.at[4]),
            "tile": (tile_in, tile_ref, sems.at[5]),
            "middle": (pair(waves_in, 1), pair(waves_ref, 1), sems.at[6]),
            "chirp": (chirp_in, chirp_ref, sems.at[7]),
            "probe": (probe_in, probe_ref, sems.at[8]),
            "before": (pair(waves_in, 2), pair(waves_ref, 2), sems.at[9]),
            "marks": (
                back_hbm.at[:, pl.ds(geo.data + marks_at, SCALE_ROWS)],
                out_ref.at[:, pl.ds(marks_at, SCALE_ROWS)],
                sems.at[10],
            ),
        }
    )
    refs = plan_ref, mine_ref, map_ref
    dev = plan_ref[4 * n + me]
    for q in range(SPREAD):
        holder = (dev & -SPREAD) + q
        scales = unscale(moved_in[holder, pl.ds(geo.block_moved - SCALE_ROWS, SCALE_ROWS), :])
        for i in range(QUARTER // 8):
            words = moved_in[holder, pl.ds(8 * i, 8), :]
            low, high = decode(words, scales[:, i : i + 1], scales[:, i : i + 1])
            moved_ref[0, pl.ds(q * QUARTER + 8 * i, 8), :] = low
            moved_ref[1, pl.ds(q * QUARTER + 8 * i, 8), :] = high
    arrived = frequency_digits(jnp.concatenate([moved_ref[0], moved_ref[1]], axis=1))
    intensity = jnp.where(dev == me, fetched["intensity"][...], arrived)
    far = fetched.pair("far")
    fetched["tile"]
    grad_probe = backward(fetched, tile_ref, lambda: fetched.pair("middle"), far, intensity)
    fetched["marks"]
    pack_tiles(geo, 1, refs, tile_ref, out_ref, 0, marks_at)
    before = fetched.pair("before")
    for c in range(2):
        put_plane(tile_ref, c, before[c] + grad_probe[c])

    def pieces(o, _):
        scales = []
        for i in range(geo.piece // g):
            x = [tile_ref[j, pl.ds(o * geo.piece + i * g, g), :] for j in range(4)]
            words, k_low, k_high = encode(
                jnp.concatenate(x[:2], axis=1), jnp.concatenate(x[2:], axis=1)
            )
            scales += [k_low, k_high]
            for j in range(2):
                at = pl.ds(geo.data + j * geo.piece + i * g, g)
                out_ref[o, at, :] = words[:, j * LANES : (j + 1) * LANES]
        put_marks(out_ref, o, marks_at, 2 * geo.rows_a * MEAN, scales)
        return 0

    lax.fori_loop(0, n, pieces, 0, unroll=4)
    store = pltpu.make_async_copy(out_ref, back_hbm.at[:, pl.ds(geo.data, rows)], sems.at[0])
    store.start()
    store.wait()


def wave_scratch(consts, copies):
    return (
        [pltpu.VMEM((6, WIN, WIN), f32), pltpu.VMEM((2, WIN, WIN), f32), pltpu.VMEM((WIN, WIN), f32)]
        + [pltpu.VMEM(c.shape, c.dtype) for c in consts]
        + [pltpu.SemaphoreType.DMA((copies,))]
    )


def forward(geo, plan, mine, owner_map, come, probe, intensity, consts):
    tile = (2 * BLOCKS, WIN, LANES)
    return pl.pallas_call(
        functools.partial(forward_kernel, geo),
        out_shape=(
            jax.ShapeDtypeStruct((geo.owners, geo.block_back, LANES), i32),
            jax.ShapeDtypeStruct(tile, f32),
            jax.ShapeDtypeStruct((6, WIN, WIN), f32),
        ),
        in_specs=[SMEM] * 3 + [VMEM] + [ANY] * 6,
        out_specs=(ANY, ANY, ANY),
        scratch_shapes=[
            pltpu.VMEM((geo.owners, geo.data + SCALE_ROWS, LANES), i32),
            pltpu.VMEM(tile, f32),
            pltpu.VMEM(tile, f32),
        ]
        + wave_scratch(consts, 11),
        compiler_params=params(),
        cost_estimate=pl.CostEstimate(flops=20 << 30, bytes_accessed=8 << 20, transcendentals=0),
        name="forward",
    )(plan, mine, owner_map, come, probe, intensity, *consts)


def finish_second(geo, plan, mine, owner_map, moved, probe, intensity, tile, waves, back, consts):
    return pl.pallas_call(
        functools.partial(backward_kernel, geo),
        out_shape=jax.ShapeDtypeStruct(back.shape, i32),
        in_specs=[SMEM] * 3 + [VMEM] + [ANY] * 9,
        out_specs=ANY,
        input_output_aliases={8: 0},
        scratch_shapes=[
            pltpu.VMEM((geo.owners, geo.block_back - geo.data, LANES), i32),
            pltpu.VMEM(tile.shape, f32),
            pltpu.VMEM((2, WIN, LANES), f32),
        ]
        + wave_scratch(consts, 11),
        compiler_params=params(),
        cost_estimate=pl.CostEstimate(flops=6 << 30, bytes_accessed=8 << 20, transcendentals=0),
        name="backward",
    )(plan, mine, owner_map, moved, probe, intensity, tile, waves, back, *consts)


def add_kernel(geo, plan_ref, mine_ref, in_ref, grad_hbm, grad_ref, sems):
    b = geo.cols_b
    grad_ref[...] = jnp.zeros_like(grad_ref)

    def body(o, _):
        scales = unscale(in_ref[o, pl.ds(geo.block_back - SCALE_ROWS, b), :])
        for slot in range(MEAN):
            start = first_row(geo, slot, o, plan_ref, mine_ref)
            for a in range(geo.rows_a):
                at = 2 * (geo.rows_a * slot + a)
                k_low, k_high = scales[:, at : at + 1], scales[:, at + 1 : at + 2]
                rows = pl.ds(start + a * geo.grid_cols, b)
                for j in range(BLOCKS):
                    words = in_ref[o, pl.ds(slot * geo.data + j * geo.tiles + a * b, b), :]
                    low, high = decode(words, k_low, k_high)
                    grad_ref[j, rows, :] += low
                    grad_ref[BLOCKS + j, rows, :] += high
        return 0

    lax.fori_loop(0, geo.owners, body, 0, unroll=2)
    copies = [
        pltpu.make_async_copy(grad_ref.at[j], grad_hbm.at[:, pl.ds(j * LANES, LANES)], sems.at[j])
        for j in range(2 * BLOCKS)
    ]
    for copy in copies:
        copy.start()
    for copy in copies:
        copy.wait()


def add_up(geo, plan, mine, returned):
    return pl.pallas_call(
        functools.partial(add_kernel, geo),
        out_shape=jax.ShapeDtypeStruct((geo.grid_rows * geo.grid_cols, 2 * HALF), f32),
        in_specs=[SMEM, SMEM, VMEM],
        out_specs=ANY,
        scratch_shapes=[
            pltpu.VMEM((2 * BLOCKS, geo.grid_rows * geo.grid_cols, LANES), f32),
            pltpu.SemaphoreType.DMA((2 * BLOCKS,)),
        ],
        compiler_params=params(24),
        cost_estimate=pl.CostEstimate(flops=1 << 23, bytes_accessed=4 << 20, transcendentals=0),
        name="add",
    )(plan, mine, returned)


def sum_kernel(geo, in_hbm, out_ref, in_ref, sem):
    g = geo.group
    rows = geo.block_back - MEAN * geo.data
    copy = pltpu.make_async_copy(in_hbm.at[:, pl.ds(MEAN * geo.data, rows)], in_ref, sem)
    copy.start()
    copy.wait()
    count = geo.piece // g

    def add_piece(o, sums):
        scales = unscale(in_ref[o, pl.ds(rows - SCALE_ROWS, g), :])
        new = []
        for i in range(count):
            at = 2 * (geo.rows_a * MEAN + i)
            k_low, k_high = scales[:, at : at + 1], scales[:, at + 1 : at + 2]
            for j in range(2):
                words = in_ref[o, pl.ds(j * geo.piece + i * g, g), :]
                low, high = decode(words, k_low, k_high)
                new += [sums[len(new)] + low, sums[len(new) + 1] + high]
        return tuple(new)

    sums = lax.fori_loop(0, geo.owners, add_piece, (jnp.zeros((g, LANES), f32),) * (4 * count), unroll=4)
    parts, scales = [], []
    low = jnp.concatenate([jnp.concatenate([sums[4 * i], sums[4 * i + 2]], axis=1) for i in range(count)], axis=0)
    high = jnp.concatenate([jnp.concatenate([sums[4 * i + 1], sums[4 * i + 3]], axis=1) for i in range(count)], axis=0)
    if geo.whole_blocks:
        low, high = swap_tile_digits(low), swap_tile_digits(high)
    for i in range(count):
        rows = slice(i * g, (i + 1) * g)
        words, k_low, k_high = encode(low[rows], high[rows])
        parts.append(words)
        scales += [k_low, k_high]
    marks = put_scales(scales, g)

    def spread(o, _):
        for i in range(count):
            for j in range(2):
                out_ref[o, pl.ds(j * geo.piece + i * g, g), :] = parts[i][:, j * LANES : (j + 1) * LANES]
        out_ref[o, pl.ds(geo.block_probe - SCALE_ROWS, g), :] = marks
        return 0

    lax.fori_loop(0, geo.owners, spread, 0, unroll=4)


def sum_pieces(geo, returned):
    return pl.pallas_call(
        functools.partial(sum_kernel, geo),
        out_shape=jax.ShapeDtypeStruct((geo.owners, geo.block_probe, LANES), i32),
        in_specs=[ANY],
        out_specs=VMEM,
        scratch_shapes=[
            pltpu.VMEM((geo.owners, geo.block_back - MEAN * geo.data, LANES), i32),
            pltpu.SemaphoreType.DMA,
        ],
        compiler_params=params(24),
        name="sum",
    )(returned)


def finish_kernel(geo, in_ref, out_ref, whole_ref):
    g = geo.group

    def place(o, _):
        scales = unscale(in_ref[o, pl.ds(geo.block_probe - SCALE_ROWS, g), :])
        for i in range(geo.piece // g):
            k_low, k_high = scales[:, 2 * i : 2 * i + 1], scales[:, 2 * i + 1 : 2 * i + 2]
            for j in range(2):
                words = in_ref[o, pl.ds(j * geo.piece + i * g, g), :]
                for c, x in enumerate(decode(words, k_low, k_high)):
                    if geo.whole_blocks:
                        rows = pl.ds(pl.multiple_of(o * geo.piece + i * g, g), g)
                        out_ref[c, rows, pl.ds(j * LANES, LANES)] = x
                    else:
                        whole_ref[c, j, pl.ds(o * geo.piece + i * g, g), :] = x
        return 0

    lax.fori_loop(0, geo.owners, place, 0, unroll=4)
    if not geo.whole_blocks:
        for c in range(2):
            out_ref[c] = swap_tile_digits(jnp.concatenate([whole_ref[c, 0], whole_ref[c, 1]], axis=1))


def finish_probe(geo, parts):
    return pl.pallas_call(
        functools.partial(finish_kernel, geo),
        out_shape=jax.ShapeDtypeStruct((2, WIN, WIN), f32),
        in_specs=[VMEM],
        out_specs=VMEM,
        scratch_shapes=[pltpu.VMEM((2, 2, WIN, LANES), f32)],
        compiler_params=params(24),
        name="finish",
    )(parts)


def exchange(x):
    return lax.all_to_all(x, "scan", split_axis=0, concat_axis=0, tiled=True)


def local(object_tiles, probe, measured, positions, counts, owner_map):
    n = lax.axis_size("scan")
    geo = Geometry(n, object_tiles.shape[1], object_tiles.shape[2])
    consts = [jnp.asarray(t) for t in tables()]
    tiles = object_tiles.reshape(geo.grid_rows * geo.grid_cols, 2 * HALF)

    plan, mine, sent = gather_tiles(geo, counts, positions.transpose(1, 2, 0), owner_map, tiles)
    sent, measured, probe = lax.optimization_barrier((sent, measured, probe))
    come = exchange(sent)
    held = near_quarters(geo, measured)
    moved = moved_quarters(geo, plan, mine, held)
    moved, come = lax.optimization_barrier((moved, come))
    moved = exchange(moved)
    probe_t, intensity = prepare(probe, measured)
    back, tile, waves = forward(geo, plan, mine, owner_map, come, probe_t, intensity, consts)
    back = finish_second(geo, plan, mine, owner_map, moved, probe_t, intensity, tile, waves, back, consts)
    returned = exchange(back)
    probe_grad = finish_probe(geo, exchange(sum_pieces(geo, returned)))
    grad = add_up(geo, plan, mine, returned)
    return grad.reshape(object_tiles.shape), probe_grad


def solution(mesh):
    return jax.shard_map(
        local,
        mesh=mesh,
        in_specs=(
            P(("groups", "scan"), None, None, None),
            P("groups", None, None),
            P(("groups", "scan"), None, None),
            P("groups", None, None),
            P("groups"),
            P(),
        ),
        out_specs=(P(("groups", "scan"), None, None, None), P("groups", None, None)),
        check_vma=False,
    )
```

```python
import functools
import math

import jax
import jax.numpy as jnp
import numpy as np
from jax import lax
from jax.experimental import pallas as pl
from jax.experimental.pallas import tpu as pltpu
from jax.sharding import PartitionSpec as P

WIN = 256
TILE = 16
ACROSS = WIN // TILE
SLICES = 2
MEAN = 2
CAP = 6
CHIRP = 1.5
HALF = SLICES * TILE * TILE
LANES = 128
BLOCKS = HALF // LANES
SCALE_ROWS = 8
SPREAD = 4
QUARTER = WIN // SPREAD
STEPS = 32.0
LEVELS = 32700.0
LN2 = math.log(2.0)

f32 = jnp.float32
i32 = jnp.int32
bf16 = jnp.bfloat16
SMEM = pl.BlockSpec(memory_space=pltpu.SMEM)
VMEM = pl.BlockSpec(memory_space=pltpu.VMEM)
ANY = pl.BlockSpec(memory_space=pl.ANY)


class Geometry:
    def __init__(self, owners, grid_rows, grid_cols):
        self.owners = owners
        self.columns = owners // 8
        self.rows_a = ACROSS // 8
        self.cols_b = ACROSS // self.columns
        self.tiles = self.rows_a * self.cols_b
        self.grid_rows = grid_rows
        self.grid_cols = grid_cols
        self.piece = WIN // owners
        self.group = min(8, self.piece)
        self.whole_blocks = self.piece % 16 == 0
        up = lambda rows: -(-(rows + SCALE_ROWS) // 8) * 8
        self.data = BLOCKS * self.tiles
        self.block_sent = up(MEAN * self.data)
        self.block_moved = up(QUARTER)
        self.block_back = up(MEAN * self.data + 2 * self.piece)
        self.block_probe = up(2 * self.piece)


def params(megabytes=58):
    return pltpu.CompilerParams(vmem_limit_bytes=megabytes << 20)


def tables():
    k = np.arange(16)
    root = np.exp(-2j * np.pi * np.outer(k, k) / 16) / 4
    kron = np.kron(root, root)

    def halves(x):
        hi = x.astype(np.float32).astype(jnp.bfloat16)
        lo = (x - hi.astype(np.float64)).astype(np.float32).astype(jnp.bfloat16)
        return hi, lo

    re_hi, re_lo = halves(kron.real)
    im_hi, im_lo = halves(kron.imag)
    hi = np.block([[re_hi, -im_hi], [im_hi, re_hi]])
    lo = np.block([[re_lo, -im_lo], [im_lo, re_lo]])
    left = np.concatenate([hi, hi, lo], axis=1)
    right = np.ascontiguousarray(left.T)
    low_u, low_v = np.divmod(np.arange(256), 16)
    twiddle = np.exp(
        -2j * np.pi * (np.outer(low_u, low_u) + np.outer(low_v, low_v)) / WIN
    )
    u = low_u[:, None] + 16 * low_u[None, :]
    v = low_v[:, None] + 16 * low_v[None, :]
    freq = lambda w: ((w + WIN // 2) % WIN - WIN // 2) / (WIN // 2)
    chirp = np.exp(-1j * CHIRP * (freq(u) ** 2 + freq(v) ** 2))
    pack = lambda z: np.stack([z.real, z.imag]).astype(np.float32)
    return left, right, pack(twiddle), pack(chirp)


def row_scale(x):
    peak = jnp.maximum(jnp.max(jnp.abs(x), axis=1, keepdims=True), 1e-30)
    return jnp.floor(jnp.log(peak) * (STEPS / LN2)) + 2.0


def encode(low, high):
    k_low, k_high = row_scale(low), row_scale(high)
    q_low = jnp.round(low * (jnp.exp(k_low * (-LN2 / STEPS)) * LEVELS)).astype(i32)
    q_high = jnp.round(high * (jnp.exp(k_high * (-LN2 / STEPS)) * LEVELS)).astype(i32)
    return (q_high << 16) | (q_low & 0xFFFF), k_low, k_high


def unscale(k):
    return jnp.exp(k.astype(f32) * (LN2 / STEPS)) * (1.0 / LEVELS)


def decode(words, k_low, k_high):
    low = ((words << 16) >> 16).astype(f32) * k_low
    high = (words >> 16).astype(f32) * k_high
    return low, high


def put_scales(scales, rows):
    lane = lax.broadcasted_iota(i32, (rows, LANES), 1)
    out = jnp.zeros((rows, LANES), f32)
    for i, k in enumerate(scales):
        out = jnp.where(lane == i, k, out)
    return out.astype(i32)


def make_plan(geo, counts_ref, positions_ref, map_ref, plan_ref, mine_ref):
    n = geo.owners
    me = lax.axis_index("scan").astype(i32)
    mine_ref[0] = me

    def spare(g):
        return jnp.maximum(counts_ref[g] - MEAN, 0)

    def body(o, carry):
        own = counts_ref[o] >= MEAN

        def behind(state):
            g, used = state
            return jnp.logical_and(
                jnp.logical_not(own),
                jnp.logical_and(used >= spare(g), g < n - 1),
            )

        g, used = lax.while_loop(behind, lambda state: (state[0] + 1, jnp.int32(0)), carry)
        dev = jnp.where(own, o, g)
        slot = jnp.where(own, 1, jnp.minimum(MEAN + used, CAP - 1))
        plan_ref[o] = positions_ref[0, 0, o]
        plan_ref[n + o] = positions_ref[0, 1, o]
        plan_ref[2 * n + o] = positions_ref[slot, 0, dev]
        plan_ref[3 * n + o] = positions_ref[slot, 1, dev]
        plan_ref[4 * n + o] = dev
        plan_ref[5 * n + o] = slot

        @pl.when(map_ref[o] == me)
        def _():
            mine_ref[1] = o

        return g, jnp.where(own, used, used + 1)

    lax.fori_loop(0, n, body, (jnp.int32(0), jnp.int32(0)))


def first_row(geo, slot, o, plan_ref, mine_ref):
    n, columns = geo.owners, geo.columns
    row, col = plan_ref[2 * slot * n + o], plan_ref[(2 * slot + 1) * n + o]
    own_class = mine_ref[1]
    row = row + ((own_class // columns - row) & 7)
    col = col + ((own_class % columns - col) & (columns - 1))
    return (row // 8) * geo.grid_cols + col // columns


def gather_kernel(
    geo, counts_ref, positions_ref, map_ref, tiles_hbm, plan_ref, mine_ref, out_ref, tiles_ref, sems
):
    n, b = geo.owners, geo.cols_b
    at = geo.block_sent - SCALE_ROWS
    copies = [
        pltpu.make_async_copy(tiles_hbm.at[:, pl.ds(j * LANES, LANES)], tiles_ref.at[j], sems.at[j])
        for j in range(2 * BLOCKS)
    ]
    for copy in copies:
        copy.start()
    make_plan(geo, counts_ref, positions_ref, map_ref, plan_ref, mine_ref)
    for copy in copies:
        copy.wait()

    def body(o, _):
        scales = []
        for slot in range(MEAN):
            start = first_row(geo, slot, o, plan_ref, mine_ref)
            for a in range(geo.rows_a):
                x = [tiles_ref[j, pl.ds(start + a * geo.grid_cols, b), :] for j in range(2 * BLOCKS)]
                words, k_low, k_high = encode(
                    jnp.concatenate(x[:BLOCKS], axis=1), jnp.concatenate(x[BLOCKS:], axis=1)
                )
                scales += [k_low, k_high]
                for j in range(BLOCKS):
                    rows = pl.ds(slot * geo.data + j * geo.tiles + a * b, b)
                    out_ref[o, rows, :] = words[:, j * LANES : (j + 1) * LANES]
        out_ref[o, pl.ds(at, b), :] = put_scales(scales, b)
        return 0

    lax.fori_loop(0, n, body, 0, unroll=4)


def gather_tiles(geo, counts, positions, owner_map, tiles):
    return pl.pallas_call(
        functools.partial(gather_kernel, geo),
        out_shape=(
            jax.ShapeDtypeStruct((6 * geo.owners,), i32),
            jax.ShapeDtypeStruct((2,), i32),
            jax.ShapeDtypeStruct((geo.owners, geo.block_sent, LANES), i32),
        ),
        in_specs=[SMEM, SMEM, SMEM, ANY],
        out_specs=(SMEM, SMEM, VMEM),
        scratch_shapes=[
            pltpu.VMEM((2 * BLOCKS, geo.grid_rows * geo.grid_cols, LANES), f32),
            pltpu.SemaphoreType.DMA((2 * BLOCKS,)),
        ],
        compiler_params=params(),
        cost_estimate=pl.CostEstimate(flops=1 << 23, bytes_accessed=4 << 20, transcendentals=0),
        name="gather",
    )(counts, positions, owner_map, tiles)


def moved_kernel(geo, plan_ref, mine_ref, own_ref, near1, near2, near3, out_ref, held_ref, sems):
    n, me = geo.owners, mine_ref[0]
    at = geo.block_moved - SCALE_ROWS
    fetch = [
        pltpu.make_async_copy(near, held_ref.at[k], sems.at[k])
        for k, near in enumerate((own_ref, near1, near2, near3))
    ]
    for copy in fetch:
        copy.start()
    for copy in fetch:
        copy.wait()

    def quarter(o, _):
        dev, spare = plan_ref[4 * n + o], plan_ref[5 * n + o] - MEAN
        near = dev ^ me

        @pl.when(near < SPREAD)
        def _():
            x = held_ref[near & (SPREAD - 1), jnp.maximum(spare, 0)].astype(f32)
            scales = []
            for i in range(QUARTER // 8):
                part = x[8 * i : 8 * (i + 1)]
                k = row_scale(part)
                scaled = jnp.round(part * (jnp.exp(k * (-LN2 / STEPS)) * LEVELS)).astype(i32)
                scales.append(k)
                out_ref[o, pl.ds(8 * i, 8), :] = (scaled[:, LANES:] << 16) | (scaled[:, :LANES] & 0xFFFF)
            out_ref[o, pl.ds(at, SCALE_ROWS), :] = put_scales(scales, SCALE_ROWS)

        return 0

    lax.fori_loop(0, n, quarter, 0)


def moved_quarters(geo, plan, mine, held):
    return pl.pallas_call(
        functools.partial(moved_kernel, geo),
        out_shape=jax.ShapeDtypeStruct((geo.owners, geo.block_moved, LANES), i32),
        in_specs=[SMEM, SMEM] + [ANY] * SPREAD,
        out_specs=VMEM,
        scratch_shapes=[
            pltpu.VMEM((SPREAD, CAP - MEAN, QUARTER, WIN), bf16),
            pltpu.SemaphoreType.DMA((SPREAD,)),
        ],
        compiler_params=params(),
        name="moved",
    )(plan, mine, *held)


def spare_kernel(measured_hbm, *rest):
    outs, measured_ref, sem = rest[:SPREAD], rest[SPREAD], rest[SPREAD + 1]
    copy = pltpu.make_async_copy(measured_hbm.at[pl.ds(MEAN, CAP - MEAN)], measured_ref, sem)
    copy.start()
    copy.wait()
    me = lax.axis_index("scan").astype(i32)
    for k, out_ref in enumerate(outs):
        rows = pl.ds(pl.multiple_of(((me ^ k) & (SPREAD - 1)) * QUARTER, QUARTER), QUARTER)
        for slot in range(CAP - MEAN):
            out_ref[slot] = measured_ref[slot, rows, :]


def near_quarters(geo, measured):
    shape = jax.ShapeDtypeStruct((CAP - MEAN, QUARTER, WIN), bf16)
    quarters = pl.pallas_call(
        spare_kernel,
        out_shape=[shape] * SPREAD,
        in_specs=[ANY],
        out_specs=[VMEM] * SPREAD,
        scratch_shapes=[pltpu.VMEM((CAP - MEAN, WIN, WIN), bf16), pltpu.SemaphoreType.DMA],
        compiler_params=params(),
        name="spare",
    )(measured)
    n = geo.owners
    return [quarters[0]] + [
        lax.ppermute(quarters[k], "scan", [(i, i ^ k) for i in range(n)]) for k in range(1, SPREAD)
    ]


def swap_tile_digits(x):
    blocks = x.shape[0] // 16
    rows = 8 * blocks
    parts = x.reshape(blocks, 2, 8, WIN)
    grid = [[parts[:, r, :, c * LANES : (c + 1) * LANES].reshape(rows, LANES) for c in range(2)] for r in range(2)]
    row = lax.broadcasted_iota(i32, (rows, LANES), 0)
    lane = lax.broadcasted_iota(i32, (rows, LANES), 1)

    def inner(q):
        for s in (4, 2, 1):
            shift = s * 16
            row_bit = (row & s) != 0
            lane_bit = (lane & shift) != 0
            moved = jnp.where(row_bit, pltpu.roll(q, s, 0), pltpu.roll(q, rows - s, 0))
            both = jnp.where(lane_bit, pltpu.roll(moved, shift, 1), pltpu.roll(moved, LANES - shift, 1))
            q = jnp.where(row_bit == lane_bit, q, both)
        return q.reshape(blocks, 1, 8, LANES)

    upper = jnp.concatenate([inner(grid[0][0]), inner(grid[1][0])], axis=3)
    lower = jnp.concatenate([inner(grid[0][1]), inner(grid[1][1])], axis=3)
    return jnp.concatenate([upper, lower], axis=1).reshape(16 * blocks, WIN)


def frequency_digits(x):
    turned = x.T
    lane = lax.broadcasted_iota(i32, (16, LANES), 1)
    halves = []
    for c in range(2):
        rows = [turned[16 * i : 16 * (i + 1), c * LANES : (c + 1) * LANES] for i in range(16)]
        for s in (1, 2, 4, 8):
            lane_bit = (lane & s) != 0
            new = list(rows)
            for i in range(16):
                if i & s == 0:
                    low, high = rows[i], rows[i | s]
                    new[i] = jnp.where(lane_bit, pltpu.roll(high, s, 1), low)
                    new[i | s] = jnp.where(lane_bit, high, pltpu.roll(low, LANES - s, 1))
            rows = new
        halves.append(jnp.concatenate(rows, axis=0))
    return jnp.concatenate(halves, axis=1)


def prepare_kernel(probe_ref, measured_ref, probe_out, measured_out):
    for c in range(2):
        probe_out[c] = swap_tile_digits(probe_ref[c])
    for k in range(MEAN):
        measured_out[k] = frequency_digits(measured_ref[k].astype(f32))


def prepare(probe, measured):
    return pl.pallas_call(
        prepare_kernel,
        out_shape=(
            jax.ShapeDtypeStruct((2, WIN, WIN), f32),
            jax.ShapeDtypeStruct((MEAN, WIN, WIN), f32),
        ),
        grid=(1,),
        in_specs=[
            pl.BlockSpec((2, WIN, WIN), lambda i: (0, 0, 0)),
            pl.BlockSpec((MEAN, WIN, WIN), lambda i: (0, 0, 0)),
        ],
        out_specs=(
            pl.BlockSpec((2, WIN, WIN), lambda i: (0, 0, 0)),
            pl.BlockSpec((MEAN, WIN, WIN), lambda i: (0, 0, 0)),
        ),
        compiler_params=params(),
        cost_estimate=pl.CostEstimate(flops=1 << 22, bytes_accessed=2 << 20, transcendentals=0),
        name="prepare",
    )(probe, measured)


def split(x):
    hi = x.astype(bf16)
    return hi, (x - hi.astype(f32)).astype(bf16)


def times_right(zs, right_ref):
    rows = []
    for z in zs:
        re_hi, re_lo = split(z[0])
        im_hi, im_lo = split(z[1])
        rows.append(jnp.concatenate([re_hi, im_hi, re_lo, im_lo, re_hi, im_hi], axis=1))
    out = jnp.dot(jnp.concatenate(rows, axis=0), right_ref[...], preferred_element_type=f32)
    return [(out[i * WIN : (i + 1) * WIN, :WIN], out[i * WIN : (i + 1) * WIN, WIN:]) for i in range(len(zs))]


def times_left(zs, left_ref):
    columns = []
    for z in zs:
        re_hi, re_lo = split(z[0])
        im_hi, im_lo = split(z[1])
        columns.append(jnp.concatenate([re_hi, im_hi, re_lo, im_lo, re_hi, im_hi], axis=0))
    out = jnp.dot(left_ref[...], jnp.concatenate(columns, axis=1), preferred_element_type=f32)
    return [(out[:WIN, i * WIN : (i + 1) * WIN], out[WIN:, i * WIN : (i + 1) * WIN]) for i in range(len(zs))]


def product(x, y):
    return x[0] * y[0] - x[1] * y[1], x[0] * y[1] + x[1] * y[0]


def product_conj(x, y):
    return x[0] * y[0] + x[1] * y[1], x[0] * y[1] - x[1] * y[0]


def conj(x):
    return x[0], -x[1]


class Fetched:
    def __init__(self, copies):
        self.copies = {}
        for name, (src, dst, sem) in copies.items():
            self.copies[name] = pltpu.make_async_copy(src, dst, sem)
            self.copies[name].start()
        self.refs = {name: dst for name, (_, dst, _) in copies.items()}

    def __getitem__(self, name):
        if name in self.copies:
            self.copies.pop(name).wait()
        return self.refs[name]

    def pair(self, name):
        ref = self[name]
        return ref[0], ref[1]

    def spectrum(self, zs):
        zs = times_left(zs, self["left"])
        return times_right([product(self.pair("twiddle"), z) for z in zs], self["right"])

    def conj_inverse(self, zs):
        zs = times_right(zs, self["right"])
        return times_left([product(self.pair("twiddle"), z) for z in zs], self["left"])


def source(geo, slot, k, plan_ref, mine_ref, map_ref):
    n, columns, me = geo.owners, geo.columns, mine_ref[0]
    row, col = plan_ref[2 * slot * n + me], plan_ref[(2 * slot + 1) * n + me]
    return map_ref[((row + k // columns) & 7) * columns + ((col + k % columns) & (columns - 1))]


def tile_rows(geo, k, a):
    return pl.ds((8 * a + k // geo.columns) * ACROSS + k % geo.columns, geo.cols_b, geo.columns)


def plane(ref, i):
    return jnp.concatenate([ref[2 * i], ref[2 * i + 1]], axis=1)


def put_plane(ref, i, x):
    ref[2 * i] = x[:, :LANES]
    ref[2 * i + 1] = x[:, LANES:]


def put_marks(out_ref, o, at, first, scales):
    rows = scales[0].shape[0]
    lane = lax.broadcasted_iota(i32, (rows, LANES), 1)
    marks = out_ref[o, pl.ds(at, rows), :]
    for i, k in enumerate(scales):
        marks = jnp.where(lane == first + i, k.astype(i32), marks)
    out_ref[o, pl.ds(at, rows), :] = marks


def pack_tiles(geo, slot, refs, tile_ref, out_ref, at, marks_at):
    b = geo.cols_b

    def pack(k, _):
        dst = source(geo, slot, k, *refs)
        scales = []
        for a in range(geo.rows_a):
            x = [tile_ref[j, tile_rows(geo, k, a), :] for j in range(2 * BLOCKS)]
            words, k_low, k_high = encode(
                jnp.concatenate(x[:BLOCKS], axis=1), jnp.concatenate(x[BLOCKS:], axis=1)
            )
            scales += [k_low, k_high]
            for j in range(BLOCKS):
                rows = pl.ds(at + j * geo.tiles + a * b, b)
                out_ref[dst, rows, :] = words[:, j * LANES : (j + 1) * LANES]
        put_marks(out_ref, dst, marks_at, 2 * geo.rows_a * slot, scales)
        return 0

    lax.fori_loop(0, geo.owners, pack, 0, unroll=4)


def backward(fetched, tiles, middle, far, intensity):
    slots = range(MEAN)
    scaled = []
    for s in slots:
        misfit = far[s][0] * far[s][0] + far[s][1] * far[s][1] - intensity[s]
        scaled.append((misfit * far[s][0], -(misfit * far[s][1])))
    near = fetched.conj_inverse(scaled)
    grad_middle = [conj(product((plane(tiles[s], 2), plane(tiles[s], 3)), near[s])) for s in slots]
    for s in slots:
        grad_back = product(middle(s), conj(near[s]))
        put_plane(tiles[s], 2, grad_back[0])
        put_plane(tiles[s], 3, grad_back[1])
    waves = fetched.spectrum(grad_middle)
    enter = [conj(e) for e in fetched.conj_inverse([product_conj(f, fetched.pair("chirp")) for f in waves])]
    parts = [product_conj((plane(tiles[s], 0), plane(tiles[s], 1)), enter[s]) for s in slots]
    for s in slots:
        grad_front = product_conj(fetched.pair("probe"), enter[s])
        put_plane(tiles[s], 0, grad_front[0])
        put_plane(tiles[s], 1, grad_front[1])
    return [parts[0][c] + parts[1][c] for c in range(2)]


def forward_kernel(
    geo, plan_ref, mine_ref, map_ref, in_ref, probe_in, left_in, right_in, twiddle_in, chirp_in,
    tile_hbm, waves_hbm,
    tile_ref, waves_ref, probe_ref, left_ref, right_ref, twiddle_ref, chirp_ref, sems,
):
    fetched = Fetched(
        {
            "probe": (probe_in, probe_ref, sems.at[0]),
            "left": (left_in, left_ref, sems.at[1]),
            "twiddle": (twiddle_in, twiddle_ref, sems.at[2]),
            "right": (right_in, right_ref, sems.at[3]),
            "chirp": (chirp_in, chirp_ref, sems.at[4]),
        }
    )
    n, b = geo.owners, geo.cols_b
    refs = plan_ref, mine_ref, map_ref
    at = geo.block_sent - SCALE_ROWS
    tiles = [tile_ref.at[s] for s in range(MEAN)]

    def unpack(k, _):
        for slot in range(MEAN):
            src = source(geo, slot, k, *refs)
            scales = unscale(in_ref[src, pl.ds(at, b), :])
            for a in range(geo.rows_a):
                c = 2 * (geo.rows_a * slot + a)
                for j in range(BLOCKS):
                    words = in_ref[src, pl.ds(slot * geo.data + j * geo.tiles + a * b, b), :]
                    low, high = decode(words, scales[:, c : c + 1], scales[:, c + 1 : c + 2])
                    tile_ref[slot, j, tile_rows(geo, k, a), :] = low
                    tile_ref[slot, BLOCKS + j, tile_rows(geo, k, a), :] = high
        return 0

    lax.fori_loop(0, n, unpack, 0, unroll=4)
    going = [pltpu.make_async_copy(tile_ref, tile_hbm, sems.at[5])]
    going[0].start()
    entrance = [product(fetched.pair("probe"), (plane(t, 0), plane(t, 1))) for t in tiles]
    waves = fetched.spectrum(entrance)
    middle = fetched.conj_inverse([conj(product(fetched.pair("chirp"), f)) for f in waves])
    for s in range(MEAN):
        for c in range(2):
            waves_ref[2 * (MEAN + s) + c] = middle[s][c]
    far = fetched.spectrum([product_conj(middle[s], (plane(t, 2), plane(t, 3))) for s, t in enumerate(tiles)])
    for s in range(MEAN):
        for c in range(2):
            waves_ref[2 * s + c] = far[s][c]
    going.append(pltpu.make_async_copy(waves_ref, waves_hbm, sems.at[6]))
    going[1].start()
    for copy in going:
        copy.wait()


def backward_kernel(
    geo, plan_ref, mine_ref, map_ref, moved_in, probe_in, intensity_in, tile_in, waves_in,
    left_in, right_in, twiddle_in, chirp_in,
    out_ref, moved_ref, intensity_ref,
    tile_ref, waves_ref, probe_ref, left_ref, right_ref, twiddle_ref, chirp_ref, sems,
):
    n, g, me = geo.owners, geo.group, mine_ref[0]
    marks_at = geo.block_back - SCALE_ROWS
    part = lambda ref, i: ref.at[pl.ds(2 * MEAN * i, 2 * MEAN)]
    fetched = Fetched(
        {
            "intensity": (intensity_in, intensity_ref, sems.at[0]),
            "far": (part(waves_in, 0), part(waves_ref, 0), sems.at[1]),
            "right": (right_in, right_ref, sems.at[2]),
            "twiddle": (twiddle_in, twiddle_ref, sems.at[3]),
            "left": (left_in, left_ref, sems.at[4]),
            "tile": (tile_in, tile_ref, sems.at[5]),
            "middle": (part(waves_in, 1), part(waves_ref, 1), sems.at[6]),
            "chirp": (chirp_in, chirp_ref, sems.at[7]),
            "probe": (probe_in, probe_ref, sems.at[8]),
        }
    )
    refs = plan_ref, mine_ref, map_ref
    dev = plan_ref[4 * n + me]
    for q in range(SPREAD):
        holder = (dev & -SPREAD) + q
        scales = unscale(moved_in[holder, pl.ds(geo.block_moved - SCALE_ROWS, SCALE_ROWS), :])
        for i in range(QUARTER // 8):
            words = moved_in[holder, pl.ds(8 * i, 8), :]
            low, high = decode(words, scales[:, i : i + 1], scales[:, i : i + 1])
            moved_ref[0, pl.ds(q * QUARTER + 8 * i, 8), :] = low
            moved_ref[1, pl.ds(q * QUARTER + 8 * i, 8), :] = high
    arrived = frequency_digits(jnp.concatenate([moved_ref[0], moved_ref[1]], axis=1))
    held = fetched["intensity"]
    intensity = [held[0], jnp.where(dev == me, held[1], arrived)]
    waves = fetched["far"]
    far = [(waves[2 * s], waves[2 * s + 1]) for s in range(MEAN)]

    def middle(s):
        waves = fetched["middle"]
        return waves[2 * s], waves[2 * s + 1]

    fetched["tile"]
    tiles = [tile_ref.at[s] for s in range(MEAN)]
    grad_probe = backward(fetched, tiles, middle, far, intensity)
    for slot in range(MEAN):
        pack_tiles(geo, slot, refs, tiles[slot], out_ref, slot * geo.data, marks_at)
    for c in range(2):
        put_plane(tiles[0], c, grad_probe[c])

    def pieces(o, _):
        scales = []
        for i in range(geo.piece // g):
            x = [tile_ref[0, j, pl.ds(o * geo.piece + i * g, g), :] for j in range(4)]
            words, k_low, k_high = encode(
                jnp.concatenate(x[:2], axis=1), jnp.concatenate(x[2:], axis=1)
            )
            scales += [k_low, k_high]
            for j in range(2):
                at = pl.ds(MEAN * geo.data + j * geo.piece + i * g, g)
                out_ref[o, at, :] = words[:, j * LANES : (j + 1) * LANES]
        put_marks(out_ref, o, marks_at, 2 * geo.rows_a * MEAN, scales)
        return 0

    lax.fori_loop(0, n, pieces, 0, unroll=4)


def wave_scratch(consts, copies):
    return (
        [
            pltpu.VMEM((MEAN, 2 * BLOCKS, WIN, LANES), f32),
            pltpu.VMEM((4 * MEAN, WIN, WIN), f32),
            pltpu.VMEM((2, WIN, WIN), f32),
        ]
        + [pltpu.VMEM(c.shape, c.dtype) for c in consts]
        + [pltpu.SemaphoreType.DMA((copies,))]
    )


def forward(geo, plan, mine, owner_map, come, probe, consts):
    return pl.pallas_call(
        functools.partial(forward_kernel, geo),
        out_shape=(
            jax.ShapeDtypeStruct((MEAN, 2 * BLOCKS, WIN, LANES), f32),
            jax.ShapeDtypeStruct((4 * MEAN, WIN, WIN), f32),
        ),
        in_specs=[SMEM] * 3 + [VMEM] + [ANY] * 5,
        out_specs=(ANY, ANY),
        scratch_shapes=wave_scratch(consts, 7),
        compiler_params=params(),
        cost_estimate=pl.CostEstimate(flops=13 << 30, bytes_accessed=8 << 20, transcendentals=0),
        name="forward",
    )(plan, mine, owner_map, come, probe, *consts)


def both_back(geo, plan, mine, owner_map, moved, probe, intensity, tile, waves, consts):
    return pl.pallas_call(
        functools.partial(backward_kernel, geo),
        out_shape=jax.ShapeDtypeStruct((geo.owners, geo.block_back, LANES), i32),
        in_specs=[SMEM] * 3 + [VMEM] + [ANY] * 8,
        out_specs=VMEM,
        scratch_shapes=[
            pltpu.VMEM((2, WIN, LANES), f32),
            pltpu.VMEM((MEAN, WIN, WIN), f32),
        ]
        + wave_scratch(consts, 9),
        compiler_params=params(),
        cost_estimate=pl.CostEstimate(flops=13 << 30, bytes_accessed=8 << 20, transcendentals=0),
        name="backward",
    )(plan, mine, owner_map, moved, probe, intensity, tile, waves, *consts)


def add_kernel(geo, plan_ref, mine_ref, in_ref, grad_hbm, grad_ref, sems):
    b = geo.cols_b
    grad_ref[...] = jnp.zeros_like(grad_ref)

    def body(o, _):
        scales = unscale(in_ref[o, pl.ds(geo.block_back - SCALE_ROWS, b), :])
        for slot in range(MEAN):
            start = first_row(geo, slot, o, plan_ref, mine_ref)
            for a in range(geo.rows_a):
                at = 2 * (geo.rows_a * slot + a)
                k_low, k_high = scales[:, at : at + 1], scales[:, at + 1 : at + 2]
                rows = pl.ds(start + a * geo.grid_cols, b)
                for j in range(BLOCKS):
                    words = in_ref[o, pl.ds(slot * geo.data + j * geo.tiles + a * b, b), :]
                    low, high = decode(words, k_low, k_high)
                    grad_ref[j, rows, :] += low
                    grad_ref[BLOCKS + j, rows, :] += high
        return 0

    lax.fori_loop(0, geo.owners, body, 0, unroll=2)
    copies = [
        pltpu.make_async_copy(grad_ref.at[j], grad_hbm.at[:, pl.ds(j * LANES, LANES)], sems.at[j])
        for j in range(2 * BLOCKS)
    ]
    for copy in copies:
        copy.start()
    for copy in copies:
        copy.wait()


def add_up(geo, plan, mine, returned):
    return pl.pallas_call(
        functools.partial(add_kernel, geo),
        out_shape=jax.ShapeDtypeStruct((geo.grid_rows * geo.grid_cols, 2 * HALF), f32),
        in_specs=[SMEM, SMEM, VMEM],
        out_specs=ANY,
        scratch_shapes=[
            pltpu.VMEM((2 * BLOCKS, geo.grid_rows * geo.grid_cols, LANES), f32),
            pltpu.SemaphoreType.DMA((2 * BLOCKS,)),
        ],
        compiler_params=params(24),
        cost_estimate=pl.CostEstimate(flops=1 << 23, bytes_accessed=4 << 20, transcendentals=0),
        name="add",
    )(plan, mine, returned)


def sum_kernel(geo, in_hbm, out_ref, in_ref, sem):
    g = geo.group
    rows = geo.block_back - MEAN * geo.data
    copy = pltpu.make_async_copy(in_hbm.at[:, pl.ds(MEAN * geo.data, rows)], in_ref, sem)
    copy.start()
    copy.wait()
    count = geo.piece // g

    def add_piece(o, sums):
        scales = unscale(in_ref[o, pl.ds(rows - SCALE_ROWS, g), :])
        new = []
        for i in range(count):
            at = 2 * (geo.rows_a * MEAN + i)
            k_low, k_high = scales[:, at : at + 1], scales[:, at + 1 : at + 2]
            for j in range(2):
                words = in_ref[o, pl.ds(j * geo.piece + i * g, g), :]
                low, high = decode(words, k_low, k_high)
                new += [sums[len(new)] + low, sums[len(new) + 1] + high]
        return tuple(new)

    sums = lax.fori_loop(0, geo.owners, add_piece, (jnp.zeros((g, LANES), f32),) * (4 * count), unroll=4)
    parts, scales = [], []
    low = jnp.concatenate([jnp.concatenate([sums[4 * i], sums[4 * i + 2]], axis=1) for i in range(count)], axis=0)
    high = jnp.concatenate([jnp.concatenate([sums[4 * i + 1], sums[4 * i + 3]], axis=1) for i in range(count)], axis=0)
    if geo.whole_blocks:
        low, high = swap_tile_digits(low), swap_tile_digits(high)
    for i in range(count):
        rows = slice(i * g, (i + 1) * g)
        words, k_low, k_high = encode(low[rows], high[rows])
        parts.append(words)
        scales += [k_low, k_high]
    marks = put_scales(scales, g)

    def spread(o, _):
        for i in range(count):
            for j in range(2):
                out_ref[o, pl.ds(j * geo.piece + i * g, g), :] = parts[i][:, j * LANES : (j + 1) * LANES]
        out_ref[o, pl.ds(geo.block_probe - SCALE_ROWS, g), :] = marks
        return 0

    lax.fori_loop(0, geo.owners, spread, 0, unroll=4)


def sum_pieces(geo, returned):
    return pl.pallas_call(
        functools.partial(sum_kernel, geo),
        out_shape=jax.ShapeDtypeStruct((geo.owners, geo.block_probe, LANES), i32),
        in_specs=[ANY],
        out_specs=VMEM,
        scratch_shapes=[
            pltpu.VMEM((geo.owners, geo.block_back - MEAN * geo.data, LANES), i32),
            pltpu.SemaphoreType.DMA,
        ],
        compiler_params=params(24),
        name="sum",
    )(returned)


def finish_kernel(geo, in_ref, out_ref, whole_ref):
    g = geo.group

    def place(o, _):
        scales = unscale(in_ref[o, pl.ds(geo.block_probe - SCALE_ROWS, g), :])
        for i in range(geo.piece // g):
            k_low, k_high = scales[:, 2 * i : 2 * i + 1], scales[:, 2 * i + 1 : 2 * i + 2]
            for j in range(2):
                words = in_ref[o, pl.ds(j * geo.piece + i * g, g), :]
                for c, x in enumerate(decode(words, k_low, k_high)):
                    if geo.whole_blocks:
                        rows = pl.ds(pl.multiple_of(o * geo.piece + i * g, g), g)
                        out_ref[c, rows, pl.ds(j * LANES, LANES)] = x
                    else:
                        whole_ref[c, j, pl.ds(o * geo.piece + i * g, g), :] = x
        return 0

    lax.fori_loop(0, geo.owners, place, 0, unroll=4)
    if not geo.whole_blocks:
        for c in range(2):
            out_ref[c] = swap_tile_digits(jnp.concatenate([whole_ref[c, 0], whole_ref[c, 1]], axis=1))


def finish_probe(geo, parts):
    return pl.pallas_call(
        functools.partial(finish_kernel, geo),
        out_shape=jax.ShapeDtypeStruct((2, WIN, WIN), f32),
        in_specs=[VMEM],
        out_specs=VMEM,
        scratch_shapes=[pltpu.VMEM((2, 2, WIN, LANES), f32)],
        compiler_params=params(24),
        name="finish",
    )(parts)


def exchange(x):
    return lax.all_to_all(x, "scan", split_axis=0, concat_axis=0, tiled=True)


def local(object_tiles, probe, measured, positions, counts, owner_map):
    n = lax.axis_size("scan")
    geo = Geometry(n, object_tiles.shape[1], object_tiles.shape[2])
    consts = [jnp.asarray(t) for t in tables()]
    tiles = object_tiles.reshape(geo.grid_rows * geo.grid_cols, 2 * HALF)

    plan, mine, sent = gather_tiles(geo, counts, positions.transpose(1, 2, 0), owner_map, tiles)
    sent, measured, probe = lax.optimization_barrier((sent, measured, probe))
    come = exchange(sent)
    held = near_quarters(geo, measured)
    moved = moved_quarters(geo, plan, mine, held)
    moved, come = lax.optimization_barrier((moved, come))
    moved = exchange(moved)
    probe_t, intensity = prepare(probe, measured)
    tile, waves = forward(geo, plan, mine, owner_map, come, probe_t, consts)
    returned = exchange(both_back(geo, plan, mine, owner_map, moved, probe_t, intensity, tile, waves, consts))
    probe_grad = finish_probe(geo, exchange(sum_pieces(geo, returned)))
    grad = add_up(geo, plan, mine, returned)
    return grad.reshape(object_tiles.shape), probe_grad


def solution(mesh):
    return jax.shard_map(
        local,
        mesh=mesh,
        in_specs=(
            P(("groups", "scan"), None, None, None),
            P("groups", None, None),
            P(("groups", "scan"), None, None),
            P("groups", None, None),
            P("groups"),
            P(),
        ),
        out_specs=(P(("groups", "scan"), None, None, None), P("groups", None, None)),
        check_vma=False,
    )
```

```python
import functools
import math

import jax
import jax.numpy as jnp
import numpy as np
from jax import lax
from jax.experimental import pallas as pl
from jax.experimental.pallas import tpu as pltpu
from jax.sharding import PartitionSpec as P

WIN = 256
TILE = 16
ACROSS = WIN // TILE
SLICES = 2
MEAN = 2
CAP = 6
CHIRP = 1.5
HALF = SLICES * TILE * TILE
LANES = 128
BLOCKS = HALF // LANES
SCALE_ROWS = 8
SPREAD = 4
QUARTER = WIN // SPREAD
STEPS = 32.0
LEVELS = 32700.0
LN2 = math.log(2.0)

f32 = jnp.float32
i32 = jnp.int32
bf16 = jnp.bfloat16
SMEM = pl.BlockSpec(memory_space=pltpu.SMEM)
VMEM = pl.BlockSpec(memory_space=pltpu.VMEM)
ANY = pl.BlockSpec(memory_space=pl.ANY)


class Geometry:
    def __init__(self, owners, grid_rows, grid_cols):
        self.owners = owners
        self.columns = owners // 8
        self.rows_a = ACROSS // 8
        self.cols_b = ACROSS // self.columns
        self.tiles = self.rows_a * self.cols_b
        self.grid_rows = grid_rows
        self.grid_cols = grid_cols
        self.piece = WIN // owners
        self.group = min(8, self.piece)
        self.whole_blocks = self.piece % 16 == 0
        up = lambda rows: -(-(rows + SCALE_ROWS) // 8) * 8
        self.data = BLOCKS * self.tiles
        self.block_sent = up(MEAN * self.data)
        self.block_moved = up(QUARTER)
        self.block_first = up(self.data)
        self.block_second = up(self.data + 2 * self.piece)
        self.block_probe = up(2 * self.piece)


def params(megabytes=58):
    return pltpu.CompilerParams(vmem_limit_bytes=megabytes << 20)


def tables():
    k = np.arange(16)
    root = np.exp(-2j * np.pi * np.outer(k, k) / 16) / 4
    kron = np.kron(root, root)

    def halves(x):
        hi = x.astype(np.float32).astype(jnp.bfloat16)
        lo = (x - hi.astype(np.float64)).astype(np.float32).astype(jnp.bfloat16)
        return hi, lo

    re_hi, re_lo = halves(kron.real)
    im_hi, im_lo = halves(kron.imag)
    hi = np.block([[re_hi, -im_hi], [im_hi, re_hi]])
    lo = np.block([[re_lo, -im_lo], [im_lo, re_lo]])
    left = np.concatenate([hi, hi, lo], axis=1)
    right = np.ascontiguousarray(left.T)
    low_u, low_v = np.divmod(np.arange(256), 16)
    twiddle = np.exp(
        -2j * np.pi * (np.outer(low_u, low_u) + np.outer(low_v, low_v)) / WIN
    )
    u = low_u[:, None] + 16 * low_u[None, :]
    v = low_v[:, None] + 16 * low_v[None, :]
    freq = lambda w: ((w + WIN // 2) % WIN - WIN // 2) / (WIN // 2)
    chirp = np.exp(-1j * CHIRP * (freq(u) ** 2 + freq(v) ** 2))
    pack = lambda z: np.stack([z.real, z.imag]).astype(np.float32)
    return left, right, pack(twiddle), pack(chirp)


def row_scale(x):
    peak = jnp.maximum(jnp.max(jnp.abs(x), axis=1, keepdims=True), 1e-30)
    return jnp.floor(jnp.log(peak) * (STEPS / LN2)) + 2.0


def encode(low, high):
    k_low, k_high = row_scale(low), row_scale(high)
    q_low = jnp.round(low * (jnp.exp(k_low * (-LN2 / STEPS)) * LEVELS)).astype(i32)
    q_high = jnp.round(high * (jnp.exp(k_high * (-LN2 / STEPS)) * LEVELS)).astype(i32)
    return (q_high << 16) | (q_low & 0xFFFF), k_low, k_high


def unscale(k):
    return jnp.exp(k.astype(f32) * (LN2 / STEPS)) * (1.0 / LEVELS)


def decode(words, k_low, k_high):
    low = ((words << 16) >> 16).astype(f32) * k_low
    high = (words >> 16).astype(f32) * k_high
    return low, high


def put_scales(scales, rows):
    lane = lax.broadcasted_iota(i32, (rows, LANES), 1)
    out = jnp.zeros((rows, LANES), f32)
    for i, k in enumerate(scales):
        out = jnp.where(lane == i, k, out)
    return out.astype(i32)


def make_plan(geo, counts_ref, positions_ref, map_ref, plan_ref, mine_ref):
    n = geo.owners
    me = lax.axis_index("scan").astype(i32)
    mine_ref[0] = me

    def spare(g):
        return jnp.maximum(counts_ref[g] - MEAN, 0)

    def body(o, carry):
        own = counts_ref[o] >= MEAN

        def behind(state):
            g, used = state
            return jnp.logical_and(
                jnp.logical_not(own),
                jnp.logical_and(used >= spare(g), g < n - 1),
            )

        g, used = lax.while_loop(behind, lambda state: (state[0] + 1, jnp.int32(0)), carry)
        dev = jnp.where(own, o, g)
        slot = jnp.where(own, 1, jnp.minimum(MEAN + used, CAP - 1))
        plan_ref[o] = positions_ref[0, 0, o]
        plan_ref[n + o] = positions_ref[0, 1, o]
        plan_ref[2 * n + o] = positions_ref[slot, 0, dev]
        plan_ref[3 * n + o] = positions_ref[slot, 1, dev]
        plan_ref[4 * n + o] = dev
        plan_ref[5 * n + o] = slot

        @pl.when(map_ref[o] == me)
        def _():
            mine_ref[1] = o

        return g, jnp.where(own, used, used + 1)

    lax.fori_loop(0, n, body, (jnp.int32(0), jnp.int32(0)))


def first_row(geo, slot, o, plan_ref, mine_ref):
    n, columns = geo.owners, geo.columns
    row, col = plan_ref[2 * slot * n + o], plan_ref[(2 * slot + 1) * n + o]
    own_class = mine_ref[1]
    row = row + ((own_class // columns - row) & 7)
    col = col + ((own_class % columns - col) & (columns - 1))
    return (row // 8) * geo.grid_cols + col // columns


def gather_kernel(
    geo, counts_ref, positions_ref, map_ref, tiles_hbm, plan_ref, mine_ref, out_ref, tiles_ref, sems
):
    n, b = geo.owners, geo.cols_b
    at = geo.block_sent - SCALE_ROWS
    copies = [
        pltpu.make_async_copy(tiles_hbm.at[:, pl.ds(j * LANES, LANES)], tiles_ref.at[j], sems.at[j])
        for j in range(2 * BLOCKS)
    ]
    for copy in copies:
        copy.start()
    make_plan(geo, counts_ref, positions_ref, map_ref, plan_ref, mine_ref)
    for copy in copies:
        copy.wait()

    def body(o, _):
        scales = []
        for slot in range(MEAN):
            start = first_row(geo, slot, o, plan_ref, mine_ref)
            for a in range(geo.rows_a):
                x = [tiles_ref[j, pl.ds(start + a * geo.grid_cols, b), :] for j in range(2 * BLOCKS)]
                words, k_low, k_high = encode(
                    jnp.concatenate(x[:BLOCKS], axis=1), jnp.concatenate(x[BLOCKS:], axis=1)
                )
                scales += [k_low, k_high]
                for j in range(BLOCKS):
                    rows = pl.ds(slot * geo.data + j * geo.tiles + a * b, b)
                    out_ref[o, rows, :] = words[:, j * LANES : (j + 1) * LANES]
        out_ref[o, pl.ds(at, b), :] = put_scales(scales, b)
        return 0

    lax.fori_loop(0, n, body, 0, unroll=4)


def gather_tiles(geo, counts, positions, owner_map, tiles):
    return pl.pallas_call(
        functools.partial(gather_kernel, geo),
        out_shape=(
            jax.ShapeDtypeStruct((6 * geo.owners,), i32),
            jax.ShapeDtypeStruct((2,), i32),
            jax.ShapeDtypeStruct((geo.owners, geo.block_sent, LANES), i32),
        ),
        in_specs=[SMEM, SMEM, SMEM, ANY],
        out_specs=(SMEM, SMEM, VMEM),
        scratch_shapes=[
            pltpu.VMEM((2 * BLOCKS, geo.grid_rows * geo.grid_cols, LANES), f32),
            pltpu.SemaphoreType.DMA((2 * BLOCKS,)),
        ],
        compiler_params=params(),
        cost_estimate=pl.CostEstimate(flops=1 << 23, bytes_accessed=4 << 20, transcendentals=0),
        name="gather",
    )(counts, positions, owner_map, tiles)


def moved_kernel(geo, plan_ref, mine_ref, own_ref, near1, near2, near3, out_ref, held_ref, sems):
    n, me = geo.owners, mine_ref[0]
    at = geo.block_moved - SCALE_ROWS
    fetch = [
        pltpu.make_async_copy(near, held_ref.at[k], sems.at[k])
        for k, near in enumerate((own_ref, near1, near2, near3))
    ]
    for copy in fetch:
        copy.start()
    for copy in fetch:
        copy.wait()

    def quarter(o, _):
        dev, spare = plan_ref[4 * n + o], plan_ref[5 * n + o] - MEAN
        near = dev ^ me

        @pl.when(near < SPREAD)
        def _():
            x = held_ref[near & (SPREAD - 1), jnp.maximum(spare, 0)].astype(f32)
            scales = []
            for i in range(QUARTER // 8):
                part = x[8 * i : 8 * (i + 1)]
                k = row_scale(part)
                scaled = jnp.round(part * (jnp.exp(k * (-LN2 / STEPS)) * LEVELS)).astype(i32)
                scales.append(k)
                out_ref[o, pl.ds(8 * i, 8), :] = (scaled[:, LANES:] << 16) | (scaled[:, :LANES] & 0xFFFF)
            out_ref[o, pl.ds(at, SCALE_ROWS), :] = put_scales(scales, SCALE_ROWS)

        return 0

    lax.fori_loop(0, n, quarter, 0)


def moved_quarters(geo, plan, mine, held):
    return pl.pallas_call(
        functools.partial(moved_kernel, geo),
        out_shape=jax.ShapeDtypeStruct((geo.owners, geo.block_moved, LANES), i32),
        in_specs=[SMEM, SMEM] + [ANY] * SPREAD,
        out_specs=VMEM,
        scratch_shapes=[
            pltpu.VMEM((SPREAD, CAP - MEAN, QUARTER, WIN), bf16),
            pltpu.SemaphoreType.DMA((SPREAD,)),
        ],
        compiler_params=params(),
        name="moved",
    )(plan, mine, *held)


def spare_kernel(measured_hbm, *rest):
    outs, measured_ref, sem = rest[:SPREAD], rest[SPREAD], rest[SPREAD + 1]
    copy = pltpu.make_async_copy(measured_hbm.at[pl.ds(MEAN, CAP - MEAN)], measured_ref, sem)
    copy.start()
    copy.wait()
    me = lax.axis_index("scan").astype(i32)
    for k, out_ref in enumerate(outs):
        rows = pl.ds(pl.multiple_of(((me ^ k) & (SPREAD - 1)) * QUARTER, QUARTER), QUARTER)
        for slot in range(CAP - MEAN):
            out_ref[slot] = measured_ref[slot, rows, :]


def near_quarters(geo, measured):
    shape = jax.ShapeDtypeStruct((CAP - MEAN, QUARTER, WIN), bf16)
    quarters = pl.pallas_call(
        spare_kernel,
        out_shape=[shape] * SPREAD,
        in_specs=[ANY],
        out_specs=[VMEM] * SPREAD,
        scratch_shapes=[pltpu.VMEM((CAP - MEAN, WIN, WIN), bf16), pltpu.SemaphoreType.DMA],
        compiler_params=params(),
        name="spare",
    )(measured)
    n = geo.owners
    return [quarters[0]] + [
        lax.ppermute(quarters[k], "scan", [(i, i ^ k) for i in range(n)]) for k in range(1, SPREAD)
    ]


def swap_tile_digits(x):
    blocks = x.shape[0] // 16
    rows = 8 * blocks
    parts = x.reshape(blocks, 2, 8, WIN)
    grid = [[parts[:, r, :, c * LANES : (c + 1) * LANES].reshape(rows, LANES) for c in range(2)] for r in range(2)]
    row = lax.broadcasted_iota(i32, (rows, LANES), 0)
    lane = lax.broadcasted_iota(i32, (rows, LANES), 1)

    def inner(q):
        for s in (4, 2, 1):
            shift = s * 16
            row_bit = (row & s) != 0
            lane_bit = (lane & shift) != 0
            moved = jnp.where(row_bit, pltpu.roll(q, s, 0), pltpu.roll(q, rows - s, 0))
            both = jnp.where(lane_bit, pltpu.roll(moved, shift, 1), pltpu.roll(moved, LANES - shift, 1))
            q = jnp.where(row_bit == lane_bit, q, both)
        return q.reshape(blocks, 1, 8, LANES)

    upper = jnp.concatenate([inner(grid[0][0]), inner(grid[1][0])], axis=3)
    lower = jnp.concatenate([inner(grid[0][1]), inner(grid[1][1])], axis=3)
    return jnp.concatenate([upper, lower], axis=1).reshape(16 * blocks, WIN)


def frequency_digits(x):
    turned = x.T
    lane = lax.broadcasted_iota(i32, (16, LANES), 1)
    halves = []
    for c in range(2):
        rows = [turned[16 * i : 16 * (i + 1), c * LANES : (c + 1) * LANES] for i in range(16)]
        for s in (1, 2, 4, 8):
            lane_bit = (lane & s) != 0
            new = list(rows)
            for i in range(16):
                if i & s == 0:
                    low, high = rows[i], rows[i | s]
                    new[i] = jnp.where(lane_bit, pltpu.roll(high, s, 1), low)
                    new[i | s] = jnp.where(lane_bit, high, pltpu.roll(low, LANES - s, 1))
            rows = new
        halves.append(jnp.concatenate(rows, axis=0))
    return jnp.concatenate(halves, axis=1)


def prepare_kernel(probe_ref, measured_ref, probe_out, measured_out):
    for c in range(2):
        probe_out[c] = swap_tile_digits(probe_ref[c])
    for k in range(MEAN):
        measured_out[k] = frequency_digits(measured_ref[k].astype(f32))


def prepare(probe, measured):
    return pl.pallas_call(
        prepare_kernel,
        out_shape=(
            jax.ShapeDtypeStruct((2, WIN, WIN), f32),
            jax.ShapeDtypeStruct((MEAN, WIN, WIN), f32),
        ),
        grid=(1,),
        in_specs=[
            pl.BlockSpec((2, WIN, WIN), lambda i: (0, 0, 0)),
            pl.BlockSpec((MEAN, WIN, WIN), lambda i: (0, 0, 0)),
        ],
        out_specs=(
            pl.BlockSpec((2, WIN, WIN), lambda i: (0, 0, 0)),
            pl.BlockSpec((MEAN, WIN, WIN), lambda i: (0, 0, 0)),
        ),
        compiler_params=params(),
        cost_estimate=pl.CostEstimate(flops=1 << 22, bytes_accessed=2 << 20, transcendentals=0),
        name="prepare",
    )(probe, measured)


def split(x):
    hi = x.astype(bf16)
    return hi, (x - hi.astype(f32)).astype(bf16)


def times_right(zs, right_ref):
    rows = []
    for z in zs:
        re_hi, re_lo = split(z[0])
        im_hi, im_lo = split(z[1])
        rows.append(jnp.concatenate([re_hi, im_hi, re_lo, im_lo, re_hi, im_hi], axis=1))
    out = jnp.dot(jnp.concatenate(rows, axis=0), right_ref[...], preferred_element_type=f32)
    return [(out[i * WIN : (i + 1) * WIN, :WIN], out[i * WIN : (i + 1) * WIN, WIN:]) for i in range(len(zs))]


def times_left(zs, left_ref):
    columns = []
    for z in zs:
        re_hi, re_lo = split(z[0])
        im_hi, im_lo = split(z[1])
        columns.append(jnp.concatenate([re_hi, im_hi, re_lo, im_lo, re_hi, im_hi], axis=0))
    out = jnp.dot(left_ref[...], jnp.concatenate(columns, axis=1), preferred_element_type=f32)
    return [(out[:WIN, i * WIN : (i + 1) * WIN], out[WIN:, i * WIN : (i + 1) * WIN]) for i in range(len(zs))]


def product(x, y):
    return x[0] * y[0] - x[1] * y[1], x[0] * y[1] + x[1] * y[0]


def product_conj(x, y):
    return x[0] * y[0] + x[1] * y[1], x[0] * y[1] - x[1] * y[0]


def conj(x):
    return x[0], -x[1]


class Fetched:
    def __init__(self, copies):
        self.copies = {}
        for name, (src, dst, sem) in copies.items():
            self.copies[name] = pltpu.make_async_copy(src, dst, sem)
            self.copies[name].start()
        self.refs = {name: dst for name, (_, dst, _) in copies.items()}

    def __getitem__(self, name):
        if name in self.copies:
            self.copies.pop(name).wait()
        return self.refs[name]

    def pair(self, name):
        ref = self[name]
        return ref[0], ref[1]

    def spectrum(self, zs):
        zs = times_left(zs, self["left"])
        return times_right([product(self.pair("twiddle"), z) for z in zs], self["right"])

    def conj_inverse(self, zs):
        zs = times_right(zs, self["right"])
        return times_left([product(self.pair("twiddle"), z) for z in zs], self["left"])


def source(geo, slot, k, plan_ref, mine_ref, map_ref):
    n, columns, me = geo.owners, geo.columns, mine_ref[0]
    row, col = plan_ref[2 * slot * n + me], plan_ref[(2 * slot + 1) * n + me]
    return map_ref[((row + k // columns) & 7) * columns + ((col + k % columns) & (columns - 1))]


def tile_rows(geo, k, a):
    return pl.ds((8 * a + k // geo.columns) * ACROSS + k % geo.columns, geo.cols_b, geo.columns)


def plane(ref, i):
    return jnp.concatenate([ref[2 * i], ref[2 * i + 1]], axis=1)


def put_plane(ref, i, x):
    ref[2 * i] = x[:, :LANES]
    ref[2 * i + 1] = x[:, LANES:]


def put_marks(out_ref, o, at, first, scales):
    rows = scales[0].shape[0]
    lane = lax.broadcasted_iota(i32, (rows, LANES), 1)
    marks = out_ref[o, pl.ds(at, rows), :]
    for i, k in enumerate(scales):
        marks = jnp.where(lane == first + i, k.astype(i32), marks)
    out_ref[o, pl.ds(at, rows), :] = marks


def pack_tiles(geo, slot, refs, tile_ref, out_ref, at, marks_at):
    b = geo.cols_b

    def pack(k, _):
        dst = source(geo, slot, k, *refs)
        scales = []
        for a in range(geo.rows_a):
            x = [tile_ref[j, tile_rows(geo, k, a), :] for j in range(2 * BLOCKS)]
            words, k_low, k_high = encode(
                jnp.concatenate(x[:BLOCKS], axis=1), jnp.concatenate(x[BLOCKS:], axis=1)
            )
            scales += [k_low, k_high]
            for j in range(BLOCKS):
                rows = pl.ds(at + j * geo.tiles + a * b, b)
                out_ref[dst, rows, :] = words[:, j * LANES : (j + 1) * LANES]
        put_marks(out_ref, dst, marks_at, 2 * geo.rows_a * slot, scales)
        return 0

    lax.fori_loop(0, geo.owners, pack, 0, unroll=4)


def backward(fetched, tile_ref, middle, far, intensity):
    misfit = far[0] * far[0] + far[1] * far[1] - intensity
    (near,) = fetched.conj_inverse([(misfit * far[0], -(misfit * far[1]))])
    grad_middle = conj(product((plane(tile_ref, 2), plane(tile_ref, 3)), near))
    grad_back = product(middle(), conj(near))
    put_plane(tile_ref, 2, grad_back[0])
    put_plane(tile_ref, 3, grad_back[1])
    (f,) = fetched.spectrum([grad_middle])
    (e,) = fetched.conj_inverse([product_conj(f, fetched.pair("chirp"))])
    enter = conj(e)
    grad_probe = product_conj((plane(tile_ref, 0), plane(tile_ref, 1)), enter)
    grad_front = product_conj(fetched.pair("probe"), enter)
    put_plane(tile_ref, 0, grad_front[0])
    put_plane(tile_ref, 1, grad_front[1])
    return grad_probe


def forward_kernel(
    geo, plan_ref, mine_ref, map_ref, in_ref, probe_in, intensity_in, left_in, right_in, twiddle_in, chirp_in,
    out_ref, tile1_hbm, waves_hbm, tile0_ref, tile1_ref, waves_ref, probe_ref, intensity_ref, left_ref, right_ref, twiddle_ref, chirp_ref,
    sems,
):
    fetched = Fetched(
        {
            "probe": (probe_in, probe_ref, sems.at[0]),
            "left": (left_in, left_ref, sems.at[1]),
            "twiddle": (twiddle_in, twiddle_ref, sems.at[2]),
            "right": (right_in, right_ref, sems.at[3]),
            "chirp": (chirp_in, chirp_ref, sems.at[4]),
            "intensity": (intensity_in.at[0], intensity_ref, sems.at[5]),
        }
    )
    n, b = geo.owners, geo.cols_b
    refs = plan_ref, mine_ref, map_ref
    at = geo.block_sent - SCALE_ROWS
    tiles = tile0_ref, tile1_ref

    def unpack(k, _):
        for slot in range(MEAN):
            src = source(geo, slot, k, *refs)
            scales = unscale(in_ref[src, pl.ds(at, b), :])
            for a in range(geo.rows_a):
                c = 2 * (geo.rows_a * slot + a)
                for j in range(BLOCKS):
                    words = in_ref[src, pl.ds(slot * geo.data + j * geo.tiles + a * b, b), :]
                    low, high = decode(words, scales[:, c : c + 1], scales[:, c + 1 : c + 2])
                    tiles[slot][j, tile_rows(geo, k, a), :] = low
                    tiles[slot][BLOCKS + j, tile_rows(geo, k, a), :] = high
        return 0

    lax.fori_loop(0, n, unpack, 0, unroll=4)
    going = [pltpu.make_async_copy(tile1_ref, tile1_hbm, sems.at[6])]
    going[0].start()
    entrance = [product(fetched.pair("probe"), (plane(t, 0), plane(t, 1))) for t in tiles]
    waves = fetched.spectrum(entrance)
    middle = fetched.conj_inverse([conj(product(fetched.pair("chirp"), f)) for f in waves])
    far = fetched.spectrum([product_conj(middle[s], (plane(t, 2), plane(t, 3))) for s, t in enumerate(tiles)])
    for c in range(2):
        waves_ref[c] = far[1][c]
        waves_ref[2 + c] = middle[1][c]
    going.append(pltpu.make_async_copy(waves_ref.at[pl.ds(0, 4)], waves_hbm.at[pl.ds(0, 4)], sems.at[7]))
    going[1].start()
    intensity = fetched["intensity"]
    grad_probe = backward(fetched, tile0_ref, lambda: middle[0], far[0], intensity[...])
    for c in range(2):
        waves_ref[4 + c] = grad_probe[c]
    going.append(pltpu.make_async_copy(waves_ref.at[pl.ds(4, 2)], waves_hbm.at[pl.ds(4, 2)], sems.at[8]))
    going[2].start()
    pack_tiles(geo, 0, refs, tile0_ref, out_ref, 0, geo.block_first - SCALE_ROWS)
    for copy in going:
        copy.wait()


def backward_kernel(
    geo, plan_ref, mine_ref, map_ref, moved_in, probe_in, intensity_in, tile_in, waves_in,
    left_in, right_in, twiddle_in, chirp_in,
    out_ref, tile_ref, moved_ref, waves_ref, probe_ref, intensity_ref, left_ref, right_ref, twiddle_ref, chirp_ref,
    sems,
):
    n, g, me = geo.owners, geo.group, mine_ref[0]
    marks_at = geo.block_second - SCALE_ROWS
    pair = lambda ref, i: ref.at[pl.ds(2 * i, 2)]
    fetched = Fetched(
        {
            "far": (pair(waves_in, 0), pair(waves_ref, 0), sems.at[0]),
            "intensity": (intensity_in.at[1], intensity_ref, sems.at[1]),
            "right": (right_in, right_ref, sems.at[2]),
            "twiddle": (twiddle_in, twiddle_ref, sems.at[3]),
            "left": (left_in, left_ref, sems.at[4]),
            "tile": (tile_in, tile_ref, sems.at[5]),
            "middle": (pair(waves_in, 1), pair(waves_ref, 1), sems.at[6]),
            "chirp": (chirp_in, chirp_ref, sems.at[7]),
            "probe": (probe_in, probe_ref, sems.at[8]),
            "before": (pair(waves_in, 2), pair(waves_ref, 2), sems.at[9]),
        }
    )
    refs = plan_ref, mine_ref, map_ref
    dev = plan_ref[4 * n + me]
    for q in range(SPREAD):
        holder = (dev & -SPREAD) + q
        scales = unscale(moved_in[holder, pl.ds(geo.block_moved - SCALE_ROWS, SCALE_ROWS), :])
        for i in range(QUARTER // 8):
            words = moved_in[holder, pl.ds(8 * i, 8), :]
            low, high = decode(words, scales[:, i : i + 1], scales[:, i : i + 1])
            moved_ref[0, pl.ds(q * QUARTER + 8 * i, 8), :] = low
            moved_ref[1, pl.ds(q * QUARTER + 8 * i, 8), :] = high
    arrived = frequency_digits(jnp.concatenate([moved_ref[0], moved_ref[1]], axis=1))
    intensity = jnp.where(dev == me, fetched["intensity"][...], arrived)
    far = fetched.pair("far")
    fetched["tile"]
    grad_probe = backward(fetched, tile_ref, lambda: fetched.pair("middle"), far, intensity)
    pack_tiles(geo, 1, refs, tile_ref, out_ref, 0, marks_at)
    before = fetched.pair("before")
    for c in range(2):
        put_plane(tile_ref, c, before[c] + grad_probe[c])

    def pieces(o, _):
        scales = []
        for i in range(geo.piece // g):
            x = [tile_ref[j, pl.ds(o * geo.piece + i * g, g), :] for j in range(4)]
            words, k_low, k_high = encode(
                jnp.concatenate(x[:2], axis=1), jnp.concatenate(x[2:], axis=1)
            )
            scales += [k_low, k_high]
            for j in range(2):
                at = pl.ds(geo.data + j * geo.piece + i * g, g)
                out_ref[o, at, :] = words[:, j * LANES : (j + 1) * LANES]
        put_marks(out_ref, o, marks_at, 2 * geo.rows_a * MEAN, scales)
        return 0

    lax.fori_loop(0, n, pieces, 0, unroll=4)


def wave_scratch(consts, copies):
    return (
        [pltpu.VMEM((6, WIN, WIN), f32), pltpu.VMEM((2, WIN, WIN), f32), pltpu.VMEM((WIN, WIN), f32)]
        + [pltpu.VMEM(c.shape, c.dtype) for c in consts]
        + [pltpu.SemaphoreType.DMA((copies,))]
    )


def forward(geo, plan, mine, owner_map, come, probe, intensity, consts):
    tile = (2 * BLOCKS, WIN, LANES)
    return pl.pallas_call(
        functools.partial(forward_kernel, geo),
        out_shape=(
            jax.ShapeDtypeStruct((geo.owners, geo.block_first, LANES), i32),
            jax.ShapeDtypeStruct(tile, f32),
            jax.ShapeDtypeStruct((6, WIN, WIN), f32),
        ),
        in_specs=[SMEM] * 3 + [VMEM] + [ANY] * 6,
        out_specs=(VMEM, ANY, ANY),
        scratch_shapes=[pltpu.VMEM(tile, f32), pltpu.VMEM(tile, f32)] + wave_scratch(consts, 9),
        compiler_params=params(),
        cost_estimate=pl.CostEstimate(flops=20 << 30, bytes_accessed=8 << 20, transcendentals=0),
        name="forward",
    )(plan, mine, owner_map, come, probe, intensity, *consts)


def second_back(geo, plan, mine, owner_map, moved, probe, intensity, tile, waves, consts):
    return pl.pallas_call(
        functools.partial(backward_kernel, geo),
        out_shape=jax.ShapeDtypeStruct((geo.owners, geo.block_second, LANES), i32),
        in_specs=[SMEM] * 3 + [VMEM] + [ANY] * 8,
        out_specs=VMEM,
        scratch_shapes=[pltpu.VMEM(tile.shape, f32), pltpu.VMEM((2, WIN, LANES), f32)] + wave_scratch(consts, 10),
        compiler_params=params(),
        cost_estimate=pl.CostEstimate(flops=6 << 30, bytes_accessed=8 << 20, transcendentals=0),
        name="backward",
    )(plan, mine, owner_map, moved, probe, intensity, tile, waves, *consts)


def add_kernel(geo, plan_ref, mine_ref, first_ref, second_ref, grad_hbm, grad_ref, sems):
    b = geo.cols_b
    grad_ref[...] = jnp.zeros_like(grad_ref)

    def body(o, _):
        for slot, in_ref in enumerate((first_ref, second_ref)):
            scales = unscale(in_ref[o, pl.ds(in_ref.shape[1] - SCALE_ROWS, b), :])
            start = first_row(geo, slot, o, plan_ref, mine_ref)
            for a in range(geo.rows_a):
                at = 2 * (geo.rows_a * slot + a)
                k_low, k_high = scales[:, at : at + 1], scales[:, at + 1 : at + 2]
                rows = pl.ds(start + a * geo.grid_cols, b)
                for j in range(BLOCKS):
                    words = in_ref[o, pl.ds(j * geo.tiles + a * b, b), :]
                    low, high = decode(words, k_low, k_high)
                    grad_ref[j, rows, :] += low
                    grad_ref[BLOCKS + j, rows, :] += high
        return 0

    lax.fori_loop(0, geo.owners, body, 0, unroll=2)
    copies = [
        pltpu.make_async_copy(grad_ref.at[j], grad_hbm.at[:, pl.ds(j * LANES, LANES)], sems.at[j])
        for j in range(2 * BLOCKS)
    ]
    for copy in copies:
        copy.start()
    for copy in copies:
        copy.wait()


def add_up(geo, plan, mine, first, second):
    return pl.pallas_call(
        functools.partial(add_kernel, geo),
        out_shape=jax.ShapeDtypeStruct((geo.grid_rows * geo.grid_cols, 2 * HALF), f32),
        in_specs=[SMEM, SMEM, VMEM, VMEM],
        out_specs=ANY,
        scratch_shapes=[
            pltpu.VMEM((2 * BLOCKS, geo.grid_rows * geo.grid_cols, LANES), f32),
            pltpu.SemaphoreType.DMA((2 * BLOCKS,)),
        ],
        compiler_params=params(24),
        cost_estimate=pl.CostEstimate(flops=1 << 23, bytes_accessed=4 << 20, transcendentals=0),
        name="add",
    )(plan, mine, first, second)


def sum_kernel(geo, in_hbm, out_ref, in_ref, sem):
    g = geo.group
    rows = geo.block_second - geo.data
    copy = pltpu.make_async_copy(in_hbm.at[:, pl.ds(geo.data, rows)], in_ref, sem)
    copy.start()
    copy.wait()
    count = geo.piece // g

    def add_piece(o, sums):
        scales = unscale(in_ref[o, pl.ds(rows - SCALE_ROWS, g), :])
        new = []
        for i in range(count):
            at = 2 * (geo.rows_a * MEAN + i)
            k_low, k_high = scales[:, at : at + 1], scales[:, at + 1 : at + 2]
            for j in range(2):
                words = in_ref[o, pl.ds(j * geo.piece + i * g, g), :]
                low, high = decode(words, k_low, k_high)
                new += [sums[len(new)] + low, sums[len(new) + 1] + high]
        return tuple(new)

    sums = lax.fori_loop(0, geo.owners, add_piece, (jnp.zeros((g, LANES), f32),) * (4 * count), unroll=4)
    parts, scales = [], []
    low = jnp.concatenate([jnp.concatenate([sums[4 * i], sums[4 * i + 2]], axis=1) for i in range(count)], axis=0)
    high = jnp.concatenate([jnp.concatenate([sums[4 * i + 1], sums[4 * i + 3]], axis=1) for i in range(count)], axis=0)
    if geo.whole_blocks:
        low, high = swap_tile_digits(low), swap_tile_digits(high)
    for i in range(count):
        rows = slice(i * g, (i + 1) * g)
        words, k_low, k_high = encode(low[rows], high[rows])
        parts.append(words)
        scales += [k_low, k_high]
    marks = put_scales(scales, g)

    def spread(o, _):
        for i in range(count):
            for j in range(2):
                out_ref[o, pl.ds(j * geo.piece + i * g, g), :] = parts[i][:, j * LANES : (j + 1) * LANES]
        out_ref[o, pl.ds(geo.block_probe - SCALE_ROWS, g), :] = marks
        return 0

    lax.fori_loop(0, geo.owners, spread, 0, unroll=4)


def sum_pieces(geo, returned):
    return pl.pallas_call(
        functools.partial(sum_kernel, geo),
        out_shape=jax.ShapeDtypeStruct((geo.owners, geo.block_probe, LANES), i32),
        in_specs=[ANY],
        out_specs=VMEM,
        scratch_shapes=[
            pltpu.VMEM((geo.owners, geo.block_second - geo.data, LANES), i32),
            pltpu.SemaphoreType.DMA,
        ],
        compiler_params=params(24),
        name="sum",
    )(returned)


def finish_kernel(geo, in_ref, out_ref, whole_ref):
    g = geo.group

    def place(o, _):
        scales = unscale(in_ref[o, pl.ds(geo.block_probe - SCALE_ROWS, g), :])
        for i in range(geo.piece // g):
            k_low, k_high = scales[:, 2 * i : 2 * i + 1], scales[:, 2 * i + 1 : 2 * i + 2]
            for j in range(2):
                words = in_ref[o, pl.ds(j * geo.piece + i * g, g), :]
                for c, x in enumerate(decode(words, k_low, k_high)):
                    if geo.whole_blocks:
                        rows = pl.ds(pl.multiple_of(o * geo.piece + i * g, g), g)
                        out_ref[c, rows, pl.ds(j * LANES, LANES)] = x
                    else:
                        whole_ref[c, j, pl.ds(o * geo.piece + i * g, g), :] = x
        return 0

    lax.fori_loop(0, geo.owners, place, 0, unroll=4)
    if not geo.whole_blocks:
        for c in range(2):
            out_ref[c] = swap_tile_digits(jnp.concatenate([whole_ref[c, 0], whole_ref[c, 1]], axis=1))


def finish_probe(geo, parts):
    return pl.pallas_call(
        functools.partial(finish_kernel, geo),
        out_shape=jax.ShapeDtypeStruct((2, WIN, WIN), f32),
        in_specs=[VMEM],
        out_specs=VMEM,
        scratch_shapes=[pltpu.VMEM((2, 2, WIN, LANES), f32)],
        compiler_params=params(24),
        name="finish",
    )(parts)


def exchange(x):
    return lax.all_to_all(x, "scan", split_axis=0, concat_axis=0, tiled=True)


def local(object_tiles, probe, measured, positions, counts, owner_map):
    n = lax.axis_size("scan")
    geo = Geometry(n, object_tiles.shape[1], object_tiles.shape[2])
    consts = [jnp.asarray(t) for t in tables()]
    tiles = object_tiles.reshape(geo.grid_rows * geo.grid_cols, 2 * HALF)

    plan, mine, sent = gather_tiles(geo, counts, positions.transpose(1, 2, 0), owner_map, tiles)
    sent, measured, probe = lax.optimization_barrier((sent, measured, probe))
    come = exchange(sent)
    held = near_quarters(geo, measured)
    moved = moved_quarters(geo, plan, mine, held)
    moved, come = lax.optimization_barrier((moved, come))
    moved = exchange(moved)
    probe_t, intensity = prepare(probe, measured)
    back, tile, waves = forward(geo, plan, mine, owner_map, come, probe_t, intensity, consts)
    back, tile, moved = lax.optimization_barrier((back, tile, moved))
    first = exchange(back)
    second = second_back(geo, plan, mine, owner_map, moved, probe_t, intensity, tile, waves, consts)
    second, first = lax.optimization_barrier((second, first))
    second = exchange(second)
    probe_grad = finish_probe(geo, exchange(sum_pieces(geo, second)))
    grad = add_up(geo, plan, mine, first, second)
    return grad.reshape(object_tiles.shape), probe_grad


def solution(mesh):
    return jax.shard_map(
        local,
        mesh=mesh,
        in_specs=(
            P(("groups", "scan"), None, None, None),
            P("groups", None, None),
            P(("groups", "scan"), None, None),
            P("groups", None, None),
            P("groups"),
            P(),
        ),
        out_specs=(P(("groups", "scan"), None, None, None), P("groups", None, None)),
        check_vma=False,
    )
```

```python
import functools
import math

import jax
import jax.numpy as jnp
import numpy as np
from jax import lax
from jax.experimental import pallas as pl
from jax.experimental.pallas import tpu as pltpu
from jax.sharding import PartitionSpec as P

WIN = 256
TILE = 16
ACROSS = WIN // TILE
SLICES = 2
MEAN = 2
CAP = 6
CHIRP = 1.5
HALF = SLICES * TILE * TILE
LANES = 128
BLOCKS = HALF // LANES
SCALE_ROWS = 8
SPREAD = 8
QUARTER = WIN // SPREAD
STEPS = 32.0
LEVELS = 32700.0
LN2 = math.log(2.0)

f32 = jnp.float32
i32 = jnp.int32
bf16 = jnp.bfloat16
SMEM = pl.BlockSpec(memory_space=pltpu.SMEM)
VMEM = pl.BlockSpec(memory_space=pltpu.VMEM)
ANY = pl.BlockSpec(memory_space=pl.ANY)


class Geometry:
    def __init__(self, owners, grid_rows, grid_cols):
        self.owners = owners
        self.columns = owners // 8
        self.rows_a = ACROSS // 8
        self.cols_b = ACROSS // self.columns
        self.tiles = self.rows_a * self.cols_b
        self.grid_rows = grid_rows
        self.grid_cols = grid_cols
        self.piece = WIN // owners
        self.group = min(8, self.piece)
        self.whole_blocks = self.piece % 16 == 0
        up = lambda rows: -(-(rows + SCALE_ROWS) // 8) * 8
        self.data = BLOCKS * self.tiles
        self.block_sent = up(MEAN * self.data)
        self.block_moved = up(QUARTER)
        self.block_first = up(self.data)
        self.block_second = up(self.data + 2 * self.piece)
        self.block_probe = up(2 * self.piece)


def params(megabytes=58):
    return pltpu.CompilerParams(vmem_limit_bytes=megabytes << 20)


def tables():
    k = np.arange(16)
    root = np.exp(-2j * np.pi * np.outer(k, k) / 16) / 4
    kron = np.kron(root, root)

    def halves(x):
        hi = x.astype(np.float32).astype(jnp.bfloat16)
        lo = (x - hi.astype(np.float64)).astype(np.float32).astype(jnp.bfloat16)
        return hi, lo

    re_hi, re_lo = halves(kron.real)
    im_hi, im_lo = halves(kron.imag)
    hi = np.block([[re_hi, -im_hi], [im_hi, re_hi]])
    lo = np.block([[re_lo, -im_lo], [im_lo, re_lo]])
    left = np.concatenate([hi, hi, lo], axis=1)
    right = np.ascontiguousarray(left.T)
    low_u, low_v = np.divmod(np.arange(256), 16)
    twiddle = np.exp(
        -2j * np.pi * (np.outer(low_u, low_u) + np.outer(low_v, low_v)) / WIN
    )
    u = low_u[:, None] + 16 * low_u[None, :]
    v = low_v[:, None] + 16 * low_v[None, :]
    freq = lambda w: ((w + WIN // 2) % WIN - WIN // 2) / (WIN // 2)
    chirp = np.exp(-1j * CHIRP * (freq(u) ** 2 + freq(v) ** 2))
    pack = lambda z: np.stack([z.real, z.imag]).astype(np.float32)
    return left, right, pack(twiddle), pack(chirp)


def row_scale(x):
    peak = jnp.maximum(jnp.max(jnp.abs(x), axis=1, keepdims=True), 1e-30)
    return jnp.floor(jnp.log(peak) * (STEPS / LN2)) + 2.0


def encode(low, high):
    k_low, k_high = row_scale(low), row_scale(high)
    q_low = jnp.round(low * (jnp.exp(k_low * (-LN2 / STEPS)) * LEVELS)).astype(i32)
    q_high = jnp.round(high * (jnp.exp(k_high * (-LN2 / STEPS)) * LEVELS)).astype(i32)
    return (q_high << 16) | (q_low & 0xFFFF), k_low, k_high


def unscale(k):
    return jnp.exp(k.astype(f32) * (LN2 / STEPS)) * (1.0 / LEVELS)


def decode(words, k_low, k_high):
    low = ((words << 16) >> 16).astype(f32) * k_low
    high = (words >> 16).astype(f32) * k_high
    return low, high


def put_scales(scales, rows):
    lane = lax.broadcasted_iota(i32, (rows, LANES), 1)
    out = jnp.zeros((rows, LANES), f32)
    for i, k in enumerate(scales):
        out = jnp.where(lane == i, k, out)
    return out.astype(i32)


def make_plan(geo, counts_ref, positions_ref, map_ref, plan_ref, mine_ref):
    n = geo.owners
    me = lax.axis_index("scan").astype(i32)
    mine_ref[0] = me

    def spare(g):
        return jnp.maximum(counts_ref[g] - MEAN, 0)

    def body(o, carry):
        own = counts_ref[o] >= MEAN

        def behind(state):
            g, used = state
            return jnp.logical_and(
                jnp.logical_not(own),
                jnp.logical_and(used >= spare(g), g < n - 1),
            )

        g, used = lax.while_loop(behind, lambda state: (state[0] + 1, jnp.int32(0)), carry)
        dev = jnp.where(own, o, g)
        slot = jnp.where(own, 1, jnp.minimum(MEAN + used, CAP - 1))
        plan_ref[o] = positions_ref[0, 0, o]
        plan_ref[n + o] = positions_ref[0, 1, o]
        plan_ref[2 * n + o] = positions_ref[slot, 0, dev]
        plan_ref[3 * n + o] = positions_ref[slot, 1, dev]
        plan_ref[4 * n + o] = dev
        plan_ref[5 * n + o] = slot

        @pl.when(map_ref[o] == me)
        def _():
            mine_ref[1] = o

        return g, jnp.where(own, used, used + 1)

    lax.fori_loop(0, n, body, (jnp.int32(0), jnp.int32(0)))


def first_row(geo, slot, o, plan_ref, mine_ref):
    n, columns = geo.owners, geo.columns
    row, col = plan_ref[2 * slot * n + o], plan_ref[(2 * slot + 1) * n + o]
    own_class = mine_ref[1]
    row = row + ((own_class // columns - row) & 7)
    col = col + ((own_class % columns - col) & (columns - 1))
    return (row // 8) * geo.grid_cols + col // columns


def gather_kernel(
    geo, counts_ref, positions_ref, map_ref, tiles_hbm, plan_ref, mine_ref, out_ref, tiles_ref, sems
):
    n, b = geo.owners, geo.cols_b
    at = geo.block_sent - SCALE_ROWS
    copies = [
        pltpu.make_async_copy(tiles_hbm.at[:, pl.ds(j * LANES, LANES)], tiles_ref.at[j], sems.at[j])
        for j in range(2 * BLOCKS)
    ]
    for copy in copies:
        copy.start()
    make_plan(geo, counts_ref, positions_ref, map_ref, plan_ref, mine_ref)
    for copy in copies:
        copy.wait()

    def body(o, _):
        scales = []
        for slot in range(MEAN):
            start = first_row(geo, slot, o, plan_ref, mine_ref)
            for a in range(geo.rows_a):
                x = [tiles_ref[j, pl.ds(start + a * geo.grid_cols, b), :] for j in range(2 * BLOCKS)]
                words, k_low, k_high = encode(
                    jnp.concatenate(x[:BLOCKS], axis=1), jnp.concatenate(x[BLOCKS:], axis=1)
                )
                scales += [k_low, k_high]
                for j in range(BLOCKS):
                    rows = pl.ds(slot * geo.data + j * geo.tiles + a * b, b)
                    out_ref[o, rows, :] = words[:, j * LANES : (j + 1) * LANES]
        out_ref[o, pl.ds(at, b), :] = put_scales(scales, b)
        return 0

    lax.fori_loop(0, n, body, 0, unroll=4)


def gather_tiles(geo, counts, positions, owner_map, tiles):
    return pl.pallas_call(
        functools.partial(gather_kernel, geo),
        out_shape=(
            jax.ShapeDtypeStruct((6 * geo.owners,), i32),
            jax.ShapeDtypeStruct((2,), i32),
            jax.ShapeDtypeStruct((geo.owners, geo.block_sent, LANES), i32),
        ),
        in_specs=[SMEM, SMEM, SMEM, ANY],
        out_specs=(SMEM, SMEM, VMEM),
        scratch_shapes=[
            pltpu.VMEM((2 * BLOCKS, geo.grid_rows * geo.grid_cols, LANES), f32),
            pltpu.SemaphoreType.DMA((2 * BLOCKS,)),
        ],
        compiler_params=params(),
        cost_estimate=pl.CostEstimate(flops=1 << 23, bytes_accessed=4 << 20, transcendentals=0),
        name="gather",
    )(counts, positions, owner_map, tiles)


def moved_kernel(geo, plan_ref, mine_ref, *rest):
    held_in, (out_ref, held_ref, sems) = rest[:SPREAD], rest[SPREAD:]
    n, me = geo.owners, mine_ref[0]
    at = geo.block_moved - SCALE_ROWS
    fetch = [
        pltpu.make_async_copy(near, held_ref.at[k], sems.at[k])
        for k, near in enumerate(held_in)
    ]
    for copy in fetch:
        copy.start()
    for copy in fetch:
        copy.wait()

    def quarter(o, _):
        dev, spare = plan_ref[4 * n + o], plan_ref[5 * n + o] - MEAN
        near = dev ^ me

        @pl.when(near < SPREAD)
        def _():
            x = held_ref[near & (SPREAD - 1), jnp.maximum(spare, 0)].astype(f32)
            scales = []
            for i in range(QUARTER // 8):
                part = x[8 * i : 8 * (i + 1)]
                k = row_scale(part)
                scaled = jnp.round(part * (jnp.exp(k * (-LN2 / STEPS)) * LEVELS)).astype(i32)
                scales.append(k)
                out_ref[o, pl.ds(8 * i, 8), :] = (scaled[:, LANES:] << 16) | (scaled[:, :LANES] & 0xFFFF)
            out_ref[o, pl.ds(at, SCALE_ROWS), :] = put_scales(scales, SCALE_ROWS)

        return 0

    lax.fori_loop(0, n, quarter, 0)


def moved_quarters(geo, plan, mine, held):
    return pl.pallas_call(
        functools.partial(moved_kernel, geo),
        out_shape=jax.ShapeDtypeStruct((geo.owners, geo.block_moved, LANES), i32),
        in_specs=[SMEM, SMEM] + [ANY] * SPREAD,
        out_specs=VMEM,
        scratch_shapes=[
            pltpu.VMEM((SPREAD, CAP - MEAN, QUARTER, WIN), bf16),
            pltpu.SemaphoreType.DMA((SPREAD,)),
        ],
        compiler_params=params(),
        name="moved",
    )(plan, mine, *held)


def spare_kernel(measured_hbm, *rest):
    outs, measured_ref, sem = rest[:SPREAD], rest[SPREAD], rest[SPREAD + 1]
    copy = pltpu.make_async_copy(measured_hbm.at[pl.ds(MEAN, CAP - MEAN)], measured_ref, sem)
    copy.start()
    copy.wait()
    me = lax.axis_index("scan").astype(i32)
    for k, out_ref in enumerate(outs):
        rows = pl.ds(pl.multiple_of(((me ^ k) & (SPREAD - 1)) * QUARTER, QUARTER), QUARTER)
        for slot in range(CAP - MEAN):
            out_ref[slot] = measured_ref[slot, rows, :]


def near_quarters(geo, measured):
    shape = jax.ShapeDtypeStruct((CAP - MEAN, QUARTER, WIN), bf16)
    quarters = pl.pallas_call(
        spare_kernel,
        out_shape=[shape] * SPREAD,
        in_specs=[ANY],
        out_specs=[VMEM] * SPREAD,
        scratch_shapes=[pltpu.VMEM((CAP - MEAN, WIN, WIN), bf16), pltpu.SemaphoreType.DMA],
        compiler_params=params(),
        name="spare",
    )(measured)
    n = geo.owners
    return [quarters[0]] + [
        lax.ppermute(quarters[k], "scan", [(i, i ^ k) for i in range(n)]) for k in range(1, SPREAD)
    ]


def swap_tile_digits(x):
    blocks = x.shape[0] // 16
    rows = 8 * blocks
    parts = x.reshape(blocks, 2, 8, WIN)
    grid = [[parts[:, r, :, c * LANES : (c + 1) * LANES].reshape(rows, LANES) for c in range(2)] for r in range(2)]
    row = lax.broadcasted_iota(i32, (rows, LANES), 0)
    lane = lax.broadcasted_iota(i32, (rows, LANES), 1)

    def inner(q):
        for s in (4, 2, 1):
            shift = s * 16
            row_bit = (row & s) != 0
            lane_bit = (lane & shift) != 0
            moved = jnp.where(row_bit, pltpu.roll(q, s, 0), pltpu.roll(q, rows - s, 0))
            both = jnp.where(lane_bit, pltpu.roll(moved, shift, 1), pltpu.roll(moved, LANES - shift, 1))
            q = jnp.where(row_bit == lane_bit, q, both)
        return q.reshape(blocks, 1, 8, LANES)

    upper = jnp.concatenate([inner(grid[0][0]), inner(grid[1][0])], axis=3)
    lower = jnp.concatenate([inner(grid[0][1]), inner(grid[1][1])], axis=3)
    return jnp.concatenate([upper, lower], axis=1).reshape(16 * blocks, WIN)


def frequency_digits(x):
    turned = x.T
    lane = lax.broadcasted_iota(i32, (16, LANES), 1)
    halves = []
    for c in range(2):
        rows = [turned[16 * i : 16 * (i + 1), c * LANES : (c + 1) * LANES] for i in range(16)]
        for s in (1, 2, 4, 8):
            lane_bit = (lane & s) != 0
            new = list(rows)
            for i in range(16):
                if i & s == 0:
                    low, high = rows[i], rows[i | s]
                    new[i] = jnp.where(lane_bit, pltpu.roll(high, s, 1), low)
                    new[i | s] = jnp.where(lane_bit, high, pltpu.roll(low, LANES - s, 1))
            rows = new
        halves.append(jnp.concatenate(rows, axis=0))
    return jnp.concatenate(halves, axis=1)


def prepare_kernel(probe_ref, measured_ref, probe_out, measured_out):
    for c in range(2):
        probe_out[c] = swap_tile_digits(probe_ref[c])
    for k in range(MEAN):
        measured_out[k] = frequency_digits(measured_ref[k].astype(f32))


def prepare(probe, measured):
    return pl.pallas_call(
        prepare_kernel,
        out_shape=(
            jax.ShapeDtypeStruct((2, WIN, WIN), f32),
            jax.ShapeDtypeStruct((MEAN, WIN, WIN), f32),
        ),
        grid=(1,),
        in_specs=[
            pl.BlockSpec((2, WIN, WIN), lambda i: (0, 0, 0)),
            pl.BlockSpec((MEAN, WIN, WIN), lambda i: (0, 0, 0)),
        ],
        out_specs=(
            pl.BlockSpec((2, WIN, WIN), lambda i: (0, 0, 0)),
            pl.BlockSpec((MEAN, WIN, WIN), lambda i: (0, 0, 0)),
        ),
        compiler_params=params(),
        cost_estimate=pl.CostEstimate(flops=1 << 22, bytes_accessed=2 << 20, transcendentals=0),
        name="prepare",
    )(probe, measured)


def split(x):
    hi = x.astype(bf16)
    return hi, (x - hi.astype(f32)).astype(bf16)


def times_right(zs, right_ref):
    rows = []
    for z in zs:
        re_hi, re_lo = split(z[0])
        im_hi, im_lo = split(z[1])
        rows.append(jnp.concatenate([re_hi, im_hi, re_lo, im_lo, re_hi, im_hi], axis=1))
    out = jnp.dot(jnp.concatenate(rows, axis=0), right_ref[...], preferred_element_type=f32)
    return [(out[i * WIN : (i + 1) * WIN, :WIN], out[i * WIN : (i + 1) * WIN, WIN:]) for i in range(len(zs))]


def times_left(zs, left_ref):
    columns = []
    for z in zs:
        re_hi, re_lo = split(z[0])
        im_hi, im_lo = split(z[1])
        columns.append(jnp.concatenate([re_hi, im_hi, re_lo, im_lo, re_hi, im_hi], axis=0))
    out = jnp.dot(left_ref[...], jnp.concatenate(columns, axis=1), preferred_element_type=f32)
    return [(out[:WIN, i * WIN : (i + 1) * WIN], out[WIN:, i * WIN : (i + 1) * WIN]) for i in range(len(zs))]


def product(x, y):
    return x[0] * y[0] - x[1] * y[1], x[0] * y[1] + x[1] * y[0]


def product_conj(x, y):
    return x[0] * y[0] + x[1] * y[1], x[0] * y[1] - x[1] * y[0]


def conj(x):
    return x[0], -x[1]


class Fetched:
    def __init__(self, copies):
        self.copies = {}
        for name, (src, dst, sem) in copies.items():
            self.copies[name] = pltpu.make_async_copy(src, dst, sem)
            self.copies[name].start()
        self.refs = {name: dst for name, (_, dst, _) in copies.items()}

    def __getitem__(self, name):
        if name in self.copies:
            self.copies.pop(name).wait()
        return self.refs[name]

    def pair(self, name):
        ref = self[name]
        return ref[0], ref[1]

    def spectrum(self, zs):
        zs = times_left(zs, self["left"])
        return times_right([product(self.pair("twiddle"), z) for z in zs], self["right"])

    def conj_inverse(self, zs):
        zs = times_right(zs, self["right"])
        return times_left([product(self.pair("twiddle"), z) for z in zs], self["left"])


def source(geo, slot, k, plan_ref, mine_ref, map_ref):
    n, columns, me = geo.owners, geo.columns, mine_ref[0]
    row, col = plan_ref[2 * slot * n + me], plan_ref[(2 * slot + 1) * n + me]
    return map_ref[((row + k // columns) & 7) * columns + ((col + k % columns) & (columns - 1))]


def tile_rows(geo, k, a):
    return pl.ds((8 * a + k // geo.columns) * ACROSS + k % geo.columns, geo.cols_b, geo.columns)


def plane(ref, i):
    return jnp.concatenate([ref[2 * i], ref[2 * i + 1]], axis=1)


def put_plane(ref, i, x):
    ref[2 * i] = x[:, :LANES]
    ref[2 * i + 1] = x[:, LANES:]


def put_marks(out_ref, o, at, first, scales):
    rows = scales[0].shape[0]
    lane = lax.broadcasted_iota(i32, (rows, LANES), 1)
    marks = out_ref[o, pl.ds(at, rows), :]
    for i, k in enumerate(scales):
        marks = jnp.where(lane == first + i, k.astype(i32), marks)
    out_ref[o, pl.ds(at, rows), :] = marks


def pack_tiles(geo, slot, refs, tile_ref, out_ref, at, marks_at):
    b = geo.cols_b

    def pack(k, _):
        dst = source(geo, slot, k, *refs)
        scales = []
        for a in range(geo.rows_a):
            x = [tile_ref[j, tile_rows(geo, k, a), :] for j in range(2 * BLOCKS)]
            words, k_low, k_high = encode(
                jnp.concatenate(x[:BLOCKS], axis=1), jnp.concatenate(x[BLOCKS:], axis=1)
            )
            scales += [k_low, k_high]
            for j in range(BLOCKS):
                rows = pl.ds(at + j * geo.tiles + a * b, b)
                out_ref[dst, rows, :] = words[:, j * LANES : (j + 1) * LANES]
        put_marks(out_ref, dst, marks_at, 2 * geo.rows_a * slot, scales)
        return 0

    lax.fori_loop(0, geo.owners, pack, 0, unroll=4)


def backward(fetched, tile_ref, middle, far, intensity):
    misfit = far[0] * far[0] + far[1] * far[1] - intensity
    (near,) = fetched.conj_inverse([(misfit * far[0], -(misfit * far[1]))])
    grad_middle = conj(product((plane(tile_ref, 2), plane(tile_ref, 3)), near))
    grad_back = product(middle(), conj(near))
    put_plane(tile_ref, 2, grad_back[0])
    put_plane(tile_ref, 3, grad_back[1])
    (f,) = fetched.spectrum([grad_middle])
    (e,) = fetched.conj_inverse([product_conj(f, fetched.pair("chirp"))])
    enter = conj(e)
    grad_probe = product_conj((plane(tile_ref, 0), plane(tile_ref, 1)), enter)
    grad_front = product_conj(fetched.pair("probe"), enter)
    put_plane(tile_ref, 0, grad_front[0])
    put_plane(tile_ref, 1, grad_front[1])
    return grad_probe


def pattern_kernel(geo, slot, plan_ref, mine_ref, map_ref, in_ref, *rest):
    if slot:
        moved_in, before_in, *rest = rest
    probe_in, intensity_in, left_in, right_in, twiddle_in, chirp_in, out_ref, *rest = rest
    if slot:
        moved_ref, before_ref, *rest = rest
    else:
        total_ref, *rest = rest
    tile_ref, probe_ref, intensity_ref, left_ref, right_ref, twiddle_ref, chirp_ref, sems = rest
    copies = {
        "probe": (probe_in, probe_ref, sems.at[0]),
        "left": (left_in, left_ref, sems.at[1]),
        "twiddle": (twiddle_in, twiddle_ref, sems.at[2]),
        "right": (right_in, right_ref, sems.at[3]),
        "chirp": (chirp_in, chirp_ref, sems.at[4]),
        "intensity": (intensity_in.at[slot], intensity_ref, sems.at[5]),
    }
    if slot:
        copies["before"] = (before_in, before_ref, sems.at[6])
    fetched = Fetched(copies)
    n, b, g, me = geo.owners, geo.cols_b, geo.group, mine_ref[0]
    refs = plan_ref, mine_ref, map_ref
    in_at = geo.block_sent - SCALE_ROWS
    marks_at = out_ref.shape[1] - SCALE_ROWS

    def unpack(k, _):
        src = source(geo, slot, k, *refs)
        scales = unscale(in_ref[src, pl.ds(in_at, b), :])
        for a in range(geo.rows_a):
            c = 2 * (geo.rows_a * slot + a)
            for j in range(BLOCKS):
                words = in_ref[src, pl.ds(slot * geo.data + j * geo.tiles + a * b, b), :]
                low, high = decode(words, scales[:, c : c + 1], scales[:, c + 1 : c + 2])
                tile_ref[j, tile_rows(geo, k, a), :] = low
                tile_ref[BLOCKS + j, tile_rows(geo, k, a), :] = high
        return 0

    lax.fori_loop(0, n, unpack, 0, unroll=4)
    entrance = product(fetched.pair("probe"), (plane(tile_ref, 0), plane(tile_ref, 1)))
    (f,) = fetched.spectrum([entrance])
    (middle,) = fetched.conj_inverse([conj(product(fetched.pair("chirp"), f))])
    (far,) = fetched.spectrum([product_conj(middle, (plane(tile_ref, 2), plane(tile_ref, 3)))])
    intensity = fetched["intensity"][...]
    if slot:
        dev = plan_ref[4 * n + me]
        for q in range(SPREAD):
            holder = (dev & -SPREAD) + q
            scales = unscale(moved_in[holder, pl.ds(geo.block_moved - SCALE_ROWS, SCALE_ROWS), :])
            for i in range(QUARTER // 8):
                words = moved_in[holder, pl.ds(8 * i, 8), :]
                low, high = decode(words, scales[:, i : i + 1], scales[:, i : i + 1])
                moved_ref[0, pl.ds(q * QUARTER + 8 * i, 8), :] = low
                moved_ref[1, pl.ds(q * QUARTER + 8 * i, 8), :] = high
        arrived = frequency_digits(jnp.concatenate([moved_ref[0], moved_ref[1]], axis=1))
        intensity = jnp.where(dev == me, intensity, arrived)
    grad_probe = backward(fetched, tile_ref, lambda: middle, far, intensity)
    pack_tiles(geo, slot, refs, tile_ref, out_ref, 0, marks_at)
    if slot == 0:
        total_ref[0], total_ref[1] = grad_probe
        return
    before = fetched.pair("before")
    for c in range(2):
        put_plane(tile_ref, c, before[c] + grad_probe[c])

    def pieces(o, _):
        scales = []
        for i in range(geo.piece // g):
            x = [tile_ref[j, pl.ds(o * geo.piece + i * g, g), :] for j in range(4)]
            words, k_low, k_high = encode(
                jnp.concatenate(x[:2], axis=1), jnp.concatenate(x[2:], axis=1)
            )
            scales += [k_low, k_high]
            for j in range(2):
                at = pl.ds(geo.data + j * geo.piece + i * g, g)
                out_ref[o, at, :] = words[:, j * LANES : (j + 1) * LANES]
        put_marks(out_ref, o, marks_at, 2 * geo.rows_a * MEAN, scales)
        return 0

    lax.fori_loop(0, n, pieces, 0, unroll=4)


def pattern(geo, slot, plan, mine, owner_map, come, probe, intensity, consts, moved=None, before=None):
    whole = jax.ShapeDtypeStruct((2, WIN, WIN), f32)
    rows = geo.block_second if slot else geo.block_first
    out = jax.ShapeDtypeStruct((geo.owners, rows, LANES), i32)
    extra = (moved, before) if slot else ()
    return pl.pallas_call(
        functools.partial(pattern_kernel, geo, slot),
        out_shape=out if slot else (out, whole),
        in_specs=[SMEM] * 3 + [VMEM] + [VMEM, ANY][: len(extra)] + [ANY] * 6,
        out_specs=VMEM if slot else (VMEM, VMEM),
        scratch_shapes=([pltpu.VMEM((2, WIN, LANES), f32), pltpu.VMEM((2, WIN, WIN), f32)] if slot else [])
        + [
            pltpu.VMEM((2 * BLOCKS, WIN, LANES), f32),
            pltpu.VMEM((2, WIN, WIN), f32),
            pltpu.VMEM((WIN, WIN), f32),
        ]
        + [pltpu.VMEM(c.shape, c.dtype) for c in consts]
        + [pltpu.SemaphoreType.DMA((7,))],
        compiler_params=params(),
        cost_estimate=pl.CostEstimate(flops=13 << 30, bytes_accessed=8 << 20, transcendentals=0),
        name=f"pattern{slot}",
    )(plan, mine, owner_map, come, *extra, probe, intensity, *consts)


def add_kernel(geo, plan_ref, mine_ref, first_ref, second_ref, grad_hbm, grad_ref, sems):
    b = geo.cols_b
    grad_ref[...] = jnp.zeros_like(grad_ref)

    def body(o, _):
        for slot, in_ref in enumerate((first_ref, second_ref)):
            scales = unscale(in_ref[o, pl.ds(in_ref.shape[1] - SCALE_ROWS, b), :])
            start = first_row(geo, slot, o, plan_ref, mine_ref)
            for a in range(geo.rows_a):
                at = 2 * (geo.rows_a * slot + a)
                k_low, k_high = scales[:, at : at + 1], scales[:, at + 1 : at + 2]
                rows = pl.ds(start + a * geo.grid_cols, b)
                for j in range(BLOCKS):
                    words = in_ref[o, pl.ds(j * geo.tiles + a * b, b), :]
                    low, high = decode(words, k_low, k_high)
                    grad_ref[j, rows, :] += low
                    grad_ref[BLOCKS + j, rows, :] += high
        return 0

    lax.fori_loop(0, geo.owners, body, 0, unroll=2)
    copies = [
        pltpu.make_async_copy(grad_ref.at[j], grad_hbm.at[:, pl.ds(j * LANES, LANES)], sems.at[j])
        for j in range(2 * BLOCKS)
    ]
    for copy in copies:
        copy.start()
    for copy in copies:
        copy.wait()


def add_up(geo, plan, mine, first, second):
    return pl.pallas_call(
        functools.partial(add_kernel, geo),
        out_shape=jax.ShapeDtypeStruct((geo.grid_rows * geo.grid_cols, 2 * HALF), f32),
        in_specs=[SMEM, SMEM, VMEM, VMEM],
        out_specs=ANY,
        scratch_shapes=[
            pltpu.VMEM((2 * BLOCKS, geo.grid_rows * geo.grid_cols, LANES), f32),
            pltpu.SemaphoreType.DMA((2 * BLOCKS,)),
        ],
        compiler_params=params(24),
        cost_estimate=pl.CostEstimate(flops=1 << 23, bytes_accessed=4 << 20, transcendentals=0),
        name="add",
    )(plan, mine, first, second)


def sum_kernel(geo, in_hbm, out_ref, in_ref, sem):
    g = geo.group
    rows = geo.block_second - geo.data
    copy = pltpu.make_async_copy(in_hbm.at[:, pl.ds(geo.data, rows)], in_ref, sem)
    copy.start()
    copy.wait()
    count = geo.piece // g

    def add_piece(o, sums):
        scales = unscale(in_ref[o, pl.ds(rows - SCALE_ROWS, g), :])
        new = []
        for i in range(count):
            at = 2 * (geo.rows_a * MEAN + i)
            k_low, k_high = scales[:, at : at + 1], scales[:, at + 1 : at + 2]
            for j in range(2):
                words = in_ref[o, pl.ds(j * geo.piece + i * g, g), :]
                low, high = decode(words, k_low, k_high)
                new += [sums[len(new)] + low, sums[len(new) + 1] + high]
        return tuple(new)

    sums = lax.fori_loop(0, geo.owners, add_piece, (jnp.zeros((g, LANES), f32),) * (4 * count), unroll=4)
    parts, scales = [], []
    low = jnp.concatenate([jnp.concatenate([sums[4 * i], sums[4 * i + 2]], axis=1) for i in range(count)], axis=0)
    high = jnp.concatenate([jnp.concatenate([sums[4 * i + 1], sums[4 * i + 3]], axis=1) for i in range(count)], axis=0)
    if geo.whole_blocks:
        low, high = swap_tile_digits(low), swap_tile_digits(high)
    for i in range(count):
        rows = slice(i * g, (i + 1) * g)
        words, k_low, k_high = encode(low[rows], high[rows])
        parts.append(words)
        scales += [k_low, k_high]
    marks = put_scales(scales, g)

    def spread(o, _):
        for i in range(count):
            for j in range(2):
                out_ref[o, pl.ds(j * geo.piece + i * g, g), :] = parts[i][:, j * LANES : (j + 1) * LANES]
        out_ref[o, pl.ds(geo.block_probe - SCALE_ROWS, g), :] = marks
        return 0

    lax.fori_loop(0, geo.owners, spread, 0, unroll=4)


def sum_pieces(geo, returned):
    return pl.pallas_call(
        functools.partial(sum_kernel, geo),
        out_shape=jax.ShapeDtypeStruct((geo.owners, geo.block_probe, LANES), i32),
        in_specs=[ANY],
        out_specs=VMEM,
        scratch_shapes=[
            pltpu.VMEM((geo.owners, geo.block_second - geo.data, LANES), i32),
            pltpu.SemaphoreType.DMA,
        ],
        compiler_params=params(24),
        name="sum",
    )(returned)


def finish_kernel(geo, in_ref, out_ref, whole_ref):
    g = geo.group

    def place(o, _):
        scales = unscale(in_ref[o, pl.ds(geo.block_probe - SCALE_ROWS, g), :])
        for i in range(geo.piece // g):
            k_low, k_high = scales[:, 2 * i : 2 * i + 1], scales[:, 2 * i + 1 : 2 * i + 2]
            for j in range(2):
                words = in_ref[o, pl.ds(j * geo.piece + i * g, g), :]
                for c, x in enumerate(decode(words, k_low, k_high)):
                    if geo.whole_blocks:
                        rows = pl.ds(pl.multiple_of(o * geo.piece + i * g, g), g)
                        out_ref[c, rows, pl.ds(j * LANES, LANES)] = x
                    else:
                        whole_ref[c, j, pl.ds(o * geo.piece + i * g, g), :] = x
        return 0

    lax.fori_loop(0, geo.owners, place, 0, unroll=4)
    if not geo.whole_blocks:
        for c in range(2):
            out_ref[c] = swap_tile_digits(jnp.concatenate([whole_ref[c, 0], whole_ref[c, 1]], axis=1))


def finish_probe(geo, parts):
    return pl.pallas_call(
        functools.partial(finish_kernel, geo),
        out_shape=jax.ShapeDtypeStruct((2, WIN, WIN), f32),
        in_specs=[VMEM],
        out_specs=VMEM,
        scratch_shapes=[pltpu.VMEM((2, 2, WIN, LANES), f32)],
        compiler_params=params(24),
        name="finish",
    )(parts)


def exchange(x):
    return lax.all_to_all(x, "scan", split_axis=0, concat_axis=0, tiled=True)


def local(object_tiles, probe, measured, positions, counts, owner_map):
    n = lax.axis_size("scan")
    geo = Geometry(n, object_tiles.shape[1], object_tiles.shape[2])
    consts = [jnp.asarray(t) for t in tables()]
    tiles = object_tiles.reshape(geo.grid_rows * geo.grid_cols, 2 * HALF)

    plan, mine, sent = gather_tiles(geo, counts, positions.transpose(1, 2, 0), owner_map, tiles)
    sent, measured, probe = lax.optimization_barrier((sent, measured, probe))
    come = exchange(sent)
    held = near_quarters(geo, measured)
    moved = moved_quarters(geo, plan, mine, held)
    moved, come = lax.optimization_barrier((moved, come))
    moved = exchange(moved)
    probe_t, intensity = prepare(probe, measured)
    back, total = pattern(geo, 0, plan, mine, owner_map, come, probe_t, intensity, consts)
    back, total, moved = lax.optimization_barrier((back, total, moved))
    first = exchange(back)
    second = pattern(geo, 1, plan, mine, owner_map, come, probe_t, intensity, consts, moved, total)
    second, first = lax.optimization_barrier((second, first))
    second = exchange(second)
    probe_grad = finish_probe(geo, exchange(sum_pieces(geo, second)))
    grad = add_up(geo, plan, mine, first, second)
    return grad.reshape(object_tiles.shape), probe_grad


def solution(mesh):
    return jax.shard_map(
        local,
        mesh=mesh,
        in_specs=(
            P(("groups", "scan"), None, None, None),
            P("groups", None, None),
            P(("groups", "scan"), None, None),
            P("groups", None, None),
            P("groups"),
            P(),
        ),
        out_specs=(P(("groups", "scan"), None, None, None), P("groups", None, None)),
        check_vma=False,
    )
```

```python
import functools
import math

import jax
import jax.numpy as jnp
import numpy as np
from jax import lax
from jax.experimental import pallas as pl
from jax.experimental.pallas import tpu as pltpu
from jax.sharding import PartitionSpec as P

WIN = 256
TILE = 16
ACROSS = WIN // TILE
SLICES = 2
MEAN = 2
CAP = 6
CHIRP = 1.5
HALF = SLICES * TILE * TILE
LANES = 128
BLOCKS = HALF // LANES
SCALE_ROWS = 8
SPREAD = 4
QUARTER = WIN // SPREAD
STEPS = 32.0
LEVELS = 32700.0
LN2 = math.log(2.0)

f32 = jnp.float32
i32 = jnp.int32
bf16 = jnp.bfloat16
SMEM = pl.BlockSpec(memory_space=pltpu.SMEM)
VMEM = pl.BlockSpec(memory_space=pltpu.VMEM)
ANY = pl.BlockSpec(memory_space=pl.ANY)


class Geometry:
    def __init__(self, owners, grid_rows, grid_cols):
        self.owners = owners
        self.columns = owners // 8
        self.rows_a = ACROSS // 8
        self.cols_b = ACROSS // self.columns
        self.tiles = self.rows_a * self.cols_b
        self.grid_rows = grid_rows
        self.grid_cols = grid_cols
        self.piece = WIN // owners
        self.group = min(8, self.piece)
        self.whole_blocks = self.piece % 16 == 0
        up = lambda rows: -(-(rows + SCALE_ROWS) // 8) * 8
        self.data = BLOCKS * self.tiles
        self.block_sent = up(MEAN * self.data)
        self.block_moved = up(QUARTER)
        self.block_first = -(-self.data // 8) * 8
        self.block_second = up(self.data + 2 * self.piece)
        self.block_probe = up(2 * self.piece)


def params(megabytes=58):
    return pltpu.CompilerParams(vmem_limit_bytes=megabytes << 20)


def tables():
    k = np.arange(16)
    root = np.exp(-2j * np.pi * np.outer(k, k) / 16) / 4
    kron = np.kron(root, root)

    def halves(x):
        hi = x.astype(np.float32).astype(jnp.bfloat16)
        lo = (x - hi.astype(np.float64)).astype(np.float32).astype(jnp.bfloat16)
        return hi, lo

    re_hi, re_lo = halves(kron.real)
    im_hi, im_lo = halves(kron.imag)
    hi = np.block([[re_hi, -im_hi], [im_hi, re_hi]])
    lo = np.block([[re_lo, -im_lo], [im_lo, re_lo]])
    left = np.concatenate([hi, hi, lo], axis=1)
    right = np.ascontiguousarray(left.T)
    low_u, low_v = np.divmod(np.arange(256), 16)
    twiddle = np.exp(
        -2j * np.pi * (np.outer(low_u, low_u) + np.outer(low_v, low_v)) / WIN
    )
    u = low_u[:, None] + 16 * low_u[None, :]
    v = low_v[:, None] + 16 * low_v[None, :]
    freq = lambda w: ((w + WIN // 2) % WIN - WIN // 2) / (WIN // 2)
    chirp = np.exp(-1j * CHIRP * (freq(u) ** 2 + freq(v) ** 2))
    pack = lambda z: np.stack([z.real, z.imag]).astype(np.float32)
    return left, right, pack(twiddle), pack(chirp)


def row_scale(x):
    peak = jnp.maximum(jnp.max(jnp.abs(x), axis=1, keepdims=True), 1e-30)
    return jnp.floor(jnp.log(peak) * (STEPS / LN2)) + 2.0


def encode(low, high):
    k_low, k_high = row_scale(low), row_scale(high)
    q_low = jnp.round(low * (jnp.exp(k_low * (-LN2 / STEPS)) * LEVELS)).astype(i32)
    q_high = jnp.round(high * (jnp.exp(k_high * (-LN2 / STEPS)) * LEVELS)).astype(i32)
    return (q_high << 16) | (q_low & 0xFFFF), k_low, k_high


def unscale(k):
    return jnp.exp(k.astype(f32) * (LN2 / STEPS)) * (1.0 / LEVELS)


def decode(words, k_low, k_high):
    low = ((words << 16) >> 16).astype(f32) * k_low
    high = (words >> 16).astype(f32) * k_high
    return low, high


def put_scales(scales, rows):
    lane = lax.broadcasted_iota(i32, (rows, LANES), 1)
    out = jnp.zeros((rows, LANES), f32)
    for i, k in enumerate(scales):
        out = jnp.where(lane == i, k, out)
    return out.astype(i32)


def make_plan(geo, counts_ref, positions_ref, map_ref, plan_ref, mine_ref):
    n = geo.owners
    me = lax.axis_index("scan").astype(i32)
    mine_ref[0] = me

    def spare(g):
        return jnp.maximum(counts_ref[g] - MEAN, 0)

    def body(o, carry):
        own = counts_ref[o] >= MEAN

        def behind(state):
            g, used = state
            return jnp.logical_and(
                jnp.logical_not(own),
                jnp.logical_and(used >= spare(g), g < n - 1),
            )

        g, used = lax.while_loop(behind, lambda state: (state[0] + 1, jnp.int32(0)), carry)
        dev = jnp.where(own, o, g)
        slot = jnp.where(own, 1, jnp.minimum(MEAN + used, CAP - 1))
        plan_ref[o] = positions_ref[0, 0, o]
        plan_ref[n + o] = positions_ref[0, 1, o]
        plan_ref[2 * n + o] = positions_ref[slot, 0, dev]
        plan_ref[3 * n + o] = positions_ref[slot, 1, dev]
        plan_ref[4 * n + o] = dev
        plan_ref[5 * n + o] = slot

        @pl.when(map_ref[o] == me)
        def _():
            mine_ref[1] = o

        return g, jnp.where(own, used, used + 1)

    lax.fori_loop(0, n, body, (jnp.int32(0), jnp.int32(0)))


def first_row(geo, slot, o, plan_ref, mine_ref):
    n, columns = geo.owners, geo.columns
    row, col = plan_ref[2 * slot * n + o], plan_ref[(2 * slot + 1) * n + o]
    own_class = mine_ref[1]
    row = row + ((own_class // columns - row) & 7)
    col = col + ((own_class % columns - col) & (columns - 1))
    return (row // 8) * geo.grid_cols + col // columns


def gather_kernel(
    geo, counts_ref, positions_ref, map_ref, tiles_hbm, plan_ref, mine_ref, out_ref, tiles_ref, sems
):
    n, b = geo.owners, geo.cols_b
    at = geo.block_sent - SCALE_ROWS
    copies = [
        pltpu.make_async_copy(tiles_hbm.at[:, pl.ds(j * LANES, LANES)], tiles_ref.at[j], sems.at[j])
        for j in range(2 * BLOCKS)
    ]
    for copy in copies:
        copy.start()
    make_plan(geo, counts_ref, positions_ref, map_ref, plan_ref, mine_ref)
    for copy in copies:
        copy.wait()

    def body(o, _):
        scales = []
        for slot in range(MEAN):
            start = first_row(geo, slot, o, plan_ref, mine_ref)
            for a in range(geo.rows_a):
                x = [tiles_ref[j, pl.ds(start + a * geo.grid_cols, b), :] for j in range(2 * BLOCKS)]
                words, k_low, k_high = encode(
                    jnp.concatenate(x[:BLOCKS], axis=1), jnp.concatenate(x[BLOCKS:], axis=1)
                )
                scales += [k_low, k_high]
                for j in range(BLOCKS):
                    rows = pl.ds(slot * geo.data + j * geo.tiles + a * b, b)
                    out_ref[o, rows, :] = words[:, j * LANES : (j + 1) * LANES]
        out_ref[o, pl.ds(at, b), :] = put_scales(scales, b)
        return 0

    lax.fori_loop(0, n, body, 0, unroll=4)


def gather_tiles(geo, counts, positions, owner_map, tiles):
    return pl.pallas_call(
        functools.partial(gather_kernel, geo),
        out_shape=(
            jax.ShapeDtypeStruct((6 * geo.owners,), i32),
            jax.ShapeDtypeStruct((2,), i32),
            jax.ShapeDtypeStruct((geo.owners, geo.block_sent, LANES), i32),
        ),
        in_specs=[SMEM, SMEM, SMEM, ANY],
        out_specs=(SMEM, SMEM, VMEM),
        scratch_shapes=[
            pltpu.VMEM((2 * BLOCKS, geo.grid_rows * geo.grid_cols, LANES), f32),
            pltpu.SemaphoreType.DMA((2 * BLOCKS,)),
        ],
        compiler_params=params(),
        cost_estimate=pl.CostEstimate(flops=1 << 23, bytes_accessed=4 << 20, transcendentals=0),
        name="gather",
    )(counts, positions, owner_map, tiles)


def moved_kernel(geo, plan_ref, mine_ref, own_ref, near1, near2, near3, out_ref, held_ref, sems):
    n, me = geo.owners, mine_ref[0]
    at = geo.block_moved - SCALE_ROWS
    fetch = [
        pltpu.make_async_copy(near, held_ref.at[k], sems.at[k])
        for k, near in enumerate((own_ref, near1, near2, near3))
    ]
    for copy in fetch:
        copy.start()
    for copy in fetch:
        copy.wait()

    def quarter(o, _):
        dev, spare = plan_ref[4 * n + o], plan_ref[5 * n + o] - MEAN
        near = dev ^ me

        @pl.when(near < SPREAD)
        def _():
            x = held_ref[near & (SPREAD - 1), jnp.maximum(spare, 0)].astype(f32)
            scales = []
            for i in range(QUARTER // 8):
                part = x[8 * i : 8 * (i + 1)]
                k = row_scale(part)
                scaled = jnp.round(part * (jnp.exp(k * (-LN2 / STEPS)) * LEVELS)).astype(i32)
                scales.append(k)
                out_ref[o, pl.ds(8 * i, 8), :] = (scaled[:, LANES:] << 16) | (scaled[:, :LANES] & 0xFFFF)
            out_ref[o, pl.ds(at, SCALE_ROWS), :] = put_scales(scales, SCALE_ROWS)

        return 0

    lax.fori_loop(0, n, quarter, 0)


def moved_quarters(geo, plan, mine, held):
    return pl.pallas_call(
        functools.partial(moved_kernel, geo),
        out_shape=jax.ShapeDtypeStruct((geo.owners, geo.block_moved, LANES), i32),
        in_specs=[SMEM, SMEM] + [ANY] * SPREAD,
        out_specs=VMEM,
        scratch_shapes=[
            pltpu.VMEM((SPREAD, CAP - MEAN, QUARTER, WIN), bf16),
            pltpu.SemaphoreType.DMA((SPREAD,)),
        ],
        compiler_params=params(),
        name="moved",
    )(plan, mine, *held)


def spare_kernel(measured_hbm, *rest):
    outs, measured_ref, sem = rest[:SPREAD], rest[SPREAD], rest[SPREAD + 1]
    copy = pltpu.make_async_copy(measured_hbm.at[pl.ds(MEAN, CAP - MEAN)], measured_ref, sem)
    copy.start()
    copy.wait()
    me = lax.axis_index("scan").astype(i32)
    for k, out_ref in enumerate(outs):
        rows = pl.ds(pl.multiple_of(((me ^ k) & (SPREAD - 1)) * QUARTER, QUARTER), QUARTER)
        for slot in range(CAP - MEAN):
            out_ref[slot] = measured_ref[slot, rows, :]


def near_quarters(geo, measured):
    shape = jax.ShapeDtypeStruct((CAP - MEAN, QUARTER, WIN), bf16)
    quarters = pl.pallas_call(
        spare_kernel,
        out_shape=[shape] * SPREAD,
        in_specs=[ANY],
        out_specs=[VMEM] * SPREAD,
        scratch_shapes=[pltpu.VMEM((CAP - MEAN, WIN, WIN), bf16), pltpu.SemaphoreType.DMA],
        compiler_params=params(),
        name="spare",
    )(measured)
    n = geo.owners
    return [quarters[0]] + [
        lax.ppermute(quarters[k], "scan", [(i, i ^ k) for i in range(n)]) for k in range(1, SPREAD)
    ]


def swap_tile_digits(x):
    blocks = x.shape[0] // 16
    rows = 8 * blocks
    parts = x.reshape(blocks, 2, 8, WIN)
    grid = [[parts[:, r, :, c * LANES : (c + 1) * LANES].reshape(rows, LANES) for c in range(2)] for r in range(2)]
    row = lax.broadcasted_iota(i32, (rows, LANES), 0)
    lane = lax.broadcasted_iota(i32, (rows, LANES), 1)

    def inner(q):
        for s in (4, 2, 1):
            shift = s * 16
            row_bit = (row & s) != 0
            lane_bit = (lane & shift) != 0
            moved = jnp.where(row_bit, pltpu.roll(q, s, 0), pltpu.roll(q, rows - s, 0))
            both = jnp.where(lane_bit, pltpu.roll(moved, shift, 1), pltpu.roll(moved, LANES - shift, 1))
            q = jnp.where(row_bit == lane_bit, q, both)
        return q.reshape(blocks, 1, 8, LANES)

    upper = jnp.concatenate([inner(grid[0][0]), inner(grid[1][0])], axis=3)
    lower = jnp.concatenate([inner(grid[0][1]), inner(grid[1][1])], axis=3)
    return jnp.concatenate([upper, lower], axis=1).reshape(16 * blocks, WIN)


def frequency_digits(x):
    turned = x.T
    lane = lax.broadcasted_iota(i32, (16, LANES), 1)
    halves = []
    for c in range(2):
        rows = [turned[16 * i : 16 * (i + 1), c * LANES : (c + 1) * LANES] for i in range(16)]
        for s in (1, 2, 4, 8):
            lane_bit = (lane & s) != 0
            new = list(rows)
            for i in range(16):
                if i & s == 0:
                    low, high = rows[i], rows[i | s]
                    new[i] = jnp.where(lane_bit, pltpu.roll(high, s, 1), low)
                    new[i | s] = jnp.where(lane_bit, high, pltpu.roll(low, LANES - s, 1))
            rows = new
        halves.append(jnp.concatenate(rows, axis=0))
    return jnp.concatenate(halves, axis=1)


def prepare_kernel(probe_ref, measured_ref, probe_out, measured_out):
    for c in range(2):
        probe_out[c] = swap_tile_digits(probe_ref[c])
    for k in range(MEAN):
        measured_out[k] = frequency_digits(measured_ref[k].astype(f32))


def prepare(probe, measured):
    return pl.pallas_call(
        prepare_kernel,
        out_shape=(
            jax.ShapeDtypeStruct((2, WIN, WIN), f32),
            jax.ShapeDtypeStruct((MEAN, WIN, WIN), f32),
        ),
        grid=(1,),
        in_specs=[
            pl.BlockSpec((2, WIN, WIN), lambda i: (0, 0, 0)),
            pl.BlockSpec((MEAN, WIN, WIN), lambda i: (0, 0, 0)),
        ],
        out_specs=(
            pl.BlockSpec((2, WIN, WIN), lambda i: (0, 0, 0)),
            pl.BlockSpec((MEAN, WIN, WIN), lambda i: (0, 0, 0)),
        ),
        compiler_params=params(),
        cost_estimate=pl.CostEstimate(flops=1 << 22, bytes_accessed=2 << 20, transcendentals=0),
        name="prepare",
    )(probe, measured)


def split(x):
    hi = x.astype(bf16)
    return hi, (x - hi.astype(f32)).astype(bf16)


def times_right(zs, right_ref):
    rows = []
    for z in zs:
        re_hi, re_lo = split(z[0])
        im_hi, im_lo = split(z[1])
        rows.append(jnp.concatenate([re_hi, im_hi, re_lo, im_lo, re_hi, im_hi], axis=1))
    out = jnp.dot(jnp.concatenate(rows, axis=0), right_ref[...], preferred_element_type=f32)
    return [(out[i * WIN : (i + 1) * WIN, :WIN], out[i * WIN : (i + 1) * WIN, WIN:]) for i in range(len(zs))]


def times_left(zs, left_ref):
    columns = []
    for z in zs:
        re_hi, re_lo = split(z[0])
        im_hi, im_lo = split(z[1])
        columns.append(jnp.concatenate([re_hi, im_hi, re_lo, im_lo, re_hi, im_hi], axis=0))
    out = jnp.dot(left_ref[...], jnp.concatenate(columns, axis=1), preferred_element_type=f32)
    return [(out[:WIN, i * WIN : (i + 1) * WIN], out[WIN:, i * WIN : (i + 1) * WIN]) for i in range(len(zs))]


def product(x, y):
    return x[0] * y[0] - x[1] * y[1], x[0] * y[1] + x[1] * y[0]


def product_conj(x, y):
    return x[0] * y[0] + x[1] * y[1], x[0] * y[1] - x[1] * y[0]


def conj(x):
    return x[0], -x[1]


class Fetched:
    def __init__(self, copies):
        self.copies = {}
        for name, (src, dst, sem) in copies.items():
            self.copies[name] = pltpu.make_async_copy(src, dst, sem)
            self.copies[name].start()
        self.refs = {name: dst for name, (_, dst, _) in copies.items()}

    def __getitem__(self, name):
        if name in self.copies:
            self.copies.pop(name).wait()
        return self.refs[name]

    def pair(self, name):
        ref = self[name]
        return ref[0], ref[1]

    def spectrum(self, zs):
        zs = times_left(zs, self["left"])
        return times_right([product(self.pair("twiddle"), z) for z in zs], self["right"])

    def conj_inverse(self, zs):
        zs = times_right(zs, self["right"])
        return times_left([product(self.pair("twiddle"), z) for z in zs], self["left"])


def source(geo, slot, k, plan_ref, mine_ref, map_ref):
    n, columns, me = geo.owners, geo.columns, mine_ref[0]
    row, col = plan_ref[2 * slot * n + me], plan_ref[(2 * slot + 1) * n + me]
    return map_ref[((row + k // columns) & 7) * columns + ((col + k % columns) & (columns - 1))]


def tile_rows(geo, k, a):
    return pl.ds((8 * a + k // geo.columns) * ACROSS + k % geo.columns, geo.cols_b, geo.columns)


def plane(ref, i):
    return jnp.concatenate([ref[2 * i], ref[2 * i + 1]], axis=1)


def put_plane(ref, i, x):
    ref[2 * i] = x[:, :LANES]
    ref[2 * i + 1] = x[:, LANES:]


def put_marks(out_ref, o, at, first, scales):
    rows = scales[0].shape[0]
    lane = lax.broadcasted_iota(i32, (rows, LANES), 1)
    marks = out_ref[o, pl.ds(at, rows), :]
    for i, k in enumerate(scales):
        marks = jnp.where(lane == first + i, k.astype(i32), marks)
    out_ref[o, pl.ds(at, rows), :] = marks


def pack_tiles(geo, slot, refs, tile_ref, out_ref, at, marks_ref, marks_at):
    b = geo.cols_b

    def pack(k, _):
        dst = source(geo, slot, k, *refs)
        scales = []
        for a in range(geo.rows_a):
            x = [tile_ref[j, tile_rows(geo, k, a), :] for j in range(2 * BLOCKS)]
            words, k_low, k_high = encode(
                jnp.concatenate(x[:BLOCKS], axis=1), jnp.concatenate(x[BLOCKS:], axis=1)
            )
            scales += [k_low, k_high]
            for j in range(BLOCKS):
                rows = pl.ds(at + j * geo.tiles + a * b, b)
                out_ref[dst, rows, :] = words[:, j * LANES : (j + 1) * LANES]
        put_marks(marks_ref, dst, marks_at, 2 * geo.rows_a * slot, scales)
        return 0

    lax.fori_loop(0, geo.owners, pack, 0, unroll=4)


def backward(fetched, tile_ref, middle, far, intensity):
    misfit = far[0] * far[0] + far[1] * far[1] - intensity
    (near,) = fetched.conj_inverse([(misfit * far[0], -(misfit * far[1]))])
    grad_middle = conj(product((plane(tile_ref, 2), plane(tile_ref, 3)), near))
    grad_back = product(middle(), conj(near))
    put_plane(tile_ref, 2, grad_back[0])
    put_plane(tile_ref, 3, grad_back[1])
    (f,) = fetched.spectrum([grad_middle])
    (e,) = fetched.conj_inverse([product_conj(f, fetched.pair("chirp"))])
    enter = conj(e)
    grad_probe = product_conj((plane(tile_ref, 0), plane(tile_ref, 1)), enter)
    grad_front = product_conj(fetched.pair("probe"), enter)
    put_plane(tile_ref, 0, grad_front[0])
    put_plane(tile_ref, 1, grad_front[1])
    return grad_probe


def forward_kernel(
    geo, plan_ref, mine_ref, map_ref, in_ref, probe_in, intensity_in, left_in, right_in, twiddle_in, chirp_in,
    out_ref, marks_ref, tile1_hbm, waves_hbm, tile0_ref, tile1_ref, waves_ref, probe_ref, intensity_ref, left_ref, right_ref, twiddle_ref, chirp_ref,
    sems,
):
    fetched = Fetched(
        {
            "probe": (probe_in, probe_ref, sems.at[0]),
            "left": (left_in, left_ref, sems.at[1]),
            "twiddle": (twiddle_in, twiddle_ref, sems.at[2]),
            "right": (right_in, right_ref, sems.at[3]),
            "chirp": (chirp_in, chirp_ref, sems.at[4]),
            "intensity": (intensity_in.at[0], intensity_ref, sems.at[5]),
        }
    )
    n, b = geo.owners, geo.cols_b
    refs = plan_ref, mine_ref, map_ref
    at = geo.block_sent - SCALE_ROWS
    tiles = tile0_ref, tile1_ref

    def unpack(k, _):
        for slot in range(MEAN):
            src = source(geo, slot, k, *refs)
            scales = unscale(in_ref[src, pl.ds(at, b), :])
            for a in range(geo.rows_a):
                c = 2 * (geo.rows_a * slot + a)
                for j in range(BLOCKS):
                    words = in_ref[src, pl.ds(slot * geo.data + j * geo.tiles + a * b, b), :]
                    low, high = decode(words, scales[:, c : c + 1], scales[:, c + 1 : c + 2])
                    tiles[slot][j, tile_rows(geo, k, a), :] = low
                    tiles[slot][BLOCKS + j, tile_rows(geo, k, a), :] = high
        return 0

    lax.fori_loop(0, n, unpack, 0, unroll=4)
    going = [pltpu.make_async_copy(tile1_ref, tile1_hbm, sems.at[6])]
    going[0].start()
    entrance = [product(fetched.pair("probe"), (plane(t, 0), plane(t, 1))) for t in tiles]
    waves = fetched.spectrum(entrance)
    middle = fetched.conj_inverse([conj(product(fetched.pair("chirp"), f)) for f in waves])
    far = fetched.spectrum([product_conj(middle[s], (plane(t, 2), plane(t, 3))) for s, t in enumerate(tiles)])
    for c in range(2):
        waves_ref[c] = far[1][c]
        waves_ref[2 + c] = middle[1][c]
    going.append(pltpu.make_async_copy(waves_ref.at[pl.ds(0, 4)], waves_hbm.at[pl.ds(0, 4)], sems.at[7]))
    going[1].start()
    intensity = fetched["intensity"]
    grad_probe = backward(fetched, tile0_ref, lambda: middle[0], far[0], intensity[...])
    for c in range(2):
        waves_ref[4 + c] = grad_probe[c]
    going.append(pltpu.make_async_copy(waves_ref.at[pl.ds(4, 2)], waves_hbm.at[pl.ds(4, 2)], sems.at[8]))
    going[2].start()
    pack_tiles(geo, 0, refs, tile0_ref, out_ref, 0, marks_ref, 0)
    for copy in going:
        copy.wait()


def backward_kernel(
    geo, plan_ref, mine_ref, map_ref, moved_in, marks_in, probe_in, intensity_in, tile_in, waves_in,
    left_in, right_in, twiddle_in, chirp_in,
    out_ref, tile_ref, moved_ref, waves_ref, probe_ref, intensity_ref, left_ref, right_ref, twiddle_ref, chirp_ref,
    sems,
):
    n, g, me = geo.owners, geo.group, mine_ref[0]
    marks_at = geo.block_second - SCALE_ROWS
    pair = lambda ref, i: ref.at[pl.ds(2 * i, 2)]
    fetched = Fetched(
        {
            "far": (pair(waves_in, 0), pair(waves_ref, 0), sems.at[0]),
            "intensity": (intensity_in.at[1], intensity_ref, sems.at[1]),
            "right": (right_in, right_ref, sems.at[2]),
            "twiddle": (twiddle_in, twiddle_ref, sems.at[3]),
            "left": (left_in, left_ref, sems.at[4]),
            "tile": (tile_in, tile_ref, sems.at[5]),
            "middle": (pair(waves_in, 1), pair(waves_ref, 1), sems.at[6]),
            "chirp": (chirp_in, chirp_ref, sems.at[7]),
            "probe": (probe_in, probe_ref, sems.at[8]),
            "before": (pair(waves_in, 2), pair(waves_ref, 2), sems.at[9]),
            "marks": (marks_in, out_ref.at[:, pl.ds(marks_at, SCALE_ROWS)], sems.at[10]),
        }
    )
    refs = plan_ref, mine_ref, map_ref
    dev = plan_ref[4 * n + me]
    for q in range(SPREAD):
        holder = (dev & -SPREAD) + q
        scales = unscale(moved_in[holder, pl.ds(geo.block_moved - SCALE_ROWS, SCALE_ROWS), :])
        for i in range(QUARTER // 8):
            words = moved_in[holder, pl.ds(8 * i, 8), :]
            low, high = decode(words, scales[:, i : i + 1], scales[:, i : i + 1])
            moved_ref[0, pl.ds(q * QUARTER + 8 * i, 8), :] = low
            moved_ref[1, pl.ds(q * QUARTER + 8 * i, 8), :] = high
    arrived = frequency_digits(jnp.concatenate([moved_ref[0], moved_ref[1]], axis=1))
    intensity = jnp.where(dev == me, fetched["intensity"][...], arrived)
    far = fetched.pair("far")
    fetched["tile"]
    grad_probe = backward(fetched, tile_ref, lambda: fetched.pair("middle"), far, intensity)
    fetched["marks"]
    pack_tiles(geo, 1, refs, tile_ref, out_ref, 0, out_ref, marks_at)
    before = fetched.pair("before")
    for c in range(2):
        put_plane(tile_ref, c, before[c] + grad_probe[c])

    def pieces(o, _):
        scales = []
        for i in range(geo.piece // g):
            x = [tile_ref[j, pl.ds(o * geo.piece + i * g, g), :] for j in range(4)]
            words, k_low, k_high = encode(
                jnp.concatenate(x[:2], axis=1), jnp.concatenate(x[2:], axis=1)
            )
            scales += [k_low, k_high]
            for j in range(2):
                at = pl.ds(geo.data + j * geo.piece + i * g, g)
                out_ref[o, at, :] = words[:, j * LANES : (j + 1) * LANES]
        put_marks(out_ref, o, marks_at, 2 * geo.rows_a * MEAN, scales)
        return 0

    lax.fori_loop(0, n, pieces, 0, unroll=4)


def wave_scratch(consts, copies):
    return (
        [pltpu.VMEM((6, WIN, WIN), f32), pltpu.VMEM((2, WIN, WIN), f32), pltpu.VMEM((WIN, WIN), f32)]
        + [pltpu.VMEM(c.shape, c.dtype) for c in consts]
        + [pltpu.SemaphoreType.DMA((copies,))]
    )


def forward(geo, plan, mine, owner_map, come, probe, intensity, consts):
    tile = (2 * BLOCKS, WIN, LANES)
    return pl.pallas_call(
        functools.partial(forward_kernel, geo),
        out_shape=(
            jax.ShapeDtypeStruct((geo.owners, geo.block_first, LANES), i32),
            jax.ShapeDtypeStruct((geo.owners, SCALE_ROWS, LANES), i32),
            jax.ShapeDtypeStruct(tile, f32),
            jax.ShapeDtypeStruct((6, WIN, WIN), f32),
        ),
        in_specs=[SMEM] * 3 + [VMEM] + [ANY] * 6,
        out_specs=(VMEM, VMEM, ANY, ANY),
        scratch_shapes=[pltpu.VMEM(tile, f32), pltpu.VMEM(tile, f32)] + wave_scratch(consts, 9),
        compiler_params=params(),
        cost_estimate=pl.CostEstimate(flops=20 << 30, bytes_accessed=8 << 20, transcendentals=0),
        name="forward",
    )(plan, mine, owner_map, come, probe, intensity, *consts)


def second_back(geo, plan, mine, owner_map, moved, marks, probe, intensity, tile, waves, consts):
    return pl.pallas_call(
        functools.partial(backward_kernel, geo),
        out_shape=jax.ShapeDtypeStruct((geo.owners, geo.block_second, LANES), i32),
        in_specs=[SMEM] * 3 + [VMEM] + [ANY] * 9,
        out_specs=VMEM,
        scratch_shapes=[pltpu.VMEM(tile.shape, f32), pltpu.VMEM((2, WIN, LANES), f32)] + wave_scratch(consts, 11),
        compiler_params=params(),
        cost_estimate=pl.CostEstimate(flops=6 << 30, bytes_accessed=8 << 20, transcendentals=0),
        name="backward",
    )(plan, mine, owner_map, moved, marks, probe, intensity, tile, waves, *consts)


def add_kernel(geo, plan_ref, mine_ref, first_ref, second_ref, grad_hbm, grad_ref, sems):
    b = geo.cols_b
    grad_ref[...] = jnp.zeros_like(grad_ref)

    def body(o, _):
        scales = unscale(second_ref[o, pl.ds(geo.block_second - SCALE_ROWS, b), :])
        for slot, in_ref in enumerate((first_ref, second_ref)):
            start = first_row(geo, slot, o, plan_ref, mine_ref)
            for a in range(geo.rows_a):
                at = 2 * (geo.rows_a * slot + a)
                k_low, k_high = scales[:, at : at + 1], scales[:, at + 1 : at + 2]
                rows = pl.ds(start + a * geo.grid_cols, b)
                for j in range(BLOCKS):
                    words = in_ref[o, pl.ds(j * geo.tiles + a * b, b), :]
                    low, high = decode(words, k_low, k_high)
                    grad_ref[j, rows, :] += low
                    grad_ref[BLOCKS + j, rows, :] += high
        return 0

    lax.fori_loop(0, geo.owners, body, 0, unroll=2)
    copies = [
        pltpu.make_async_copy(grad_ref.at[j], grad_hbm.at[:, pl.ds(j * LANES, LANES)], sems.at[j])
        for j in range(2 * BLOCKS)
    ]
    for copy in copies:
        copy.start()
    for copy in copies:
        copy.wait()


def add_up(geo, plan, mine, first, second):
    return pl.pallas_call(
        functools.partial(add_kernel, geo),
        out_shape=jax.ShapeDtypeStruct((geo.grid_rows * geo.grid_cols, 2 * HALF), f32),
        in_specs=[SMEM, SMEM, VMEM, VMEM],
        out_specs=ANY,
        scratch_shapes=[
            pltpu.VMEM((2 * BLOCKS, geo.grid_rows * geo.grid_cols, LANES), f32),
            pltpu.SemaphoreType.DMA((2 * BLOCKS,)),
        ],
        compiler_params=params(24),
        cost_estimate=pl.CostEstimate(flops=1 << 23, bytes_accessed=4 << 20, transcendentals=0),
        name="add",
    )(plan, mine, first, second)


def sum_kernel(geo, in_hbm, out_ref, in_ref, sem):
    g = geo.group
    rows = geo.block_second - geo.data
    copy = pltpu.make_async_copy(in_hbm.at[:, pl.ds(geo.data, rows)], in_ref, sem)
    copy.start()
    copy.wait()
    count = geo.piece // g

    def add_piece(o, sums):
        scales = unscale(in_ref[o, pl.ds(rows - SCALE_ROWS, g), :])
        new = []
        for i in range(count):
            at = 2 * (geo.rows_a * MEAN + i)
            k_low, k_high = scales[:, at : at + 1], scales[:, at + 1 : at + 2]
            for j in range(2):
                words = in_ref[o, pl.ds(j * geo.piece + i * g, g), :]
                low, high = decode(words, k_low, k_high)
                new += [sums[len(new)] + low, sums[len(new) + 1] + high]
        return tuple(new)

    sums = lax.fori_loop(0, geo.owners, add_piece, (jnp.zeros((g, LANES), f32),) * (4 * count), unroll=4)
    parts, scales = [], []
    low = jnp.concatenate([jnp.concatenate([sums[4 * i], sums[4 * i + 2]], axis=1) for i in range(count)], axis=0)
    high = jnp.concatenate([jnp.concatenate([sums[4 * i + 1], sums[4 * i + 3]], axis=1) for i in range(count)], axis=0)
    if geo.whole_blocks:
        low, high = swap_tile_digits(low), swap_tile_digits(high)
    for i in range(count):
        rows = slice(i * g, (i + 1) * g)
        words, k_low, k_high = encode(low[rows], high[rows])
        parts.append(words)
        scales += [k_low, k_high]
    marks = put_scales(scales, g)

    def spread(o, _):
        for i in range(count):
            for j in range(2):
                out_ref[o, pl.ds(j * geo.piece + i * g, g), :] = parts[i][:, j * LANES : (j + 1) * LANES]
        out_ref[o, pl.ds(geo.block_probe - SCALE_ROWS, g), :] = marks
        return 0

    lax.fori_loop(0, geo.owners, spread, 0, unroll=4)


def sum_pieces(geo, returned):
    return pl.pallas_call(
        functools.partial(sum_kernel, geo),
        out_shape=jax.ShapeDtypeStruct((geo.owners, geo.block_probe, LANES), i32),
        in_specs=[ANY],
        out_specs=VMEM,
        scratch_shapes=[
            pltpu.VMEM((geo.owners, geo.block_second - geo.data, LANES), i32),
            pltpu.SemaphoreType.DMA,
        ],
        compiler_params=params(24),
        name="sum",
    )(returned)


def finish_kernel(geo, in_ref, out_ref, whole_ref):
    g = geo.group

    def place(o, _):
        scales = unscale(in_ref[o, pl.ds(geo.block_probe - SCALE_ROWS, g), :])
        for i in range(geo.piece // g):
            k_low, k_high = scales[:, 2 * i : 2 * i + 1], scales[:, 2 * i + 1 : 2 * i + 2]
            for j in range(2):
                words = in_ref[o, pl.ds(j * geo.piece + i * g, g), :]
                for c, x in enumerate(decode(words, k_low, k_high)):
                    if geo.whole_blocks:
                        rows = pl.ds(pl.multiple_of(o * geo.piece + i * g, g), g)
                        out_ref[c, rows, pl.ds(j * LANES, LANES)] = x
                    else:
                        whole_ref[c, j, pl.ds(o * geo.piece + i * g, g), :] = x
        return 0

    lax.fori_loop(0, geo.owners, place, 0, unroll=4)
    if not geo.whole_blocks:
        for c in range(2):
            out_ref[c] = swap_tile_digits(jnp.concatenate([whole_ref[c, 0], whole_ref[c, 1]], axis=1))


def finish_probe(geo, parts):
    return pl.pallas_call(
        functools.partial(finish_kernel, geo),
        out_shape=jax.ShapeDtypeStruct((2, WIN, WIN), f32),
        in_specs=[VMEM],
        out_specs=VMEM,
        scratch_shapes=[pltpu.VMEM((2, 2, WIN, LANES), f32)],
        compiler_params=params(24),
        name="finish",
    )(parts)


def exchange(x):
    return lax.all_to_all(x, "scan", split_axis=0, concat_axis=0, tiled=True)


def local(object_tiles, probe, measured, positions, counts, owner_map):
    n = lax.axis_size("scan")
    geo = Geometry(n, object_tiles.shape[1], object_tiles.shape[2])
    consts = [jnp.asarray(t) for t in tables()]
    tiles = object_tiles.reshape(geo.grid_rows * geo.grid_cols, 2 * HALF)

    plan, mine, sent = gather_tiles(geo, counts, positions.transpose(1, 2, 0), owner_map, tiles)
    sent, measured, probe = lax.optimization_barrier((sent, measured, probe))
    come = exchange(sent)
    held = near_quarters(geo, measured)
    moved = moved_quarters(geo, plan, mine, held)
    moved, come = lax.optimization_barrier((moved, come))
    moved = exchange(moved)
    probe_t, intensity = prepare(probe, measured)
    back, marks, tile, waves = forward(geo, plan, mine, owner_map, come, probe_t, intensity, consts)
    back, tile, moved = lax.optimization_barrier((back, tile, moved))
    first = exchange(back)
    second = second_back(geo, plan, mine, owner_map, moved, marks, probe_t, intensity, tile, waves, consts)
    second, first = lax.optimization_barrier((second, first))
    second = exchange(second)
    probe_grad = finish_probe(geo, exchange(sum_pieces(geo, second)))
    grad = add_up(geo, plan, mine, first, second)
    return grad.reshape(object_tiles.shape), probe_grad


def solution(mesh):
    return jax.shard_map(
        local,
        mesh=mesh,
        in_specs=(
            P(("groups", "scan"), None, None, None),
            P("groups", None, None),
            P(("groups", "scan"), None, None),
            P("groups", None, None),
            P("groups"),
            P(),
        ),
        out_specs=(P(("groups", "scan"), None, None, None), P("groups", None, None)),
        check_vma=False,
    )
```

```python
import functools
import math

import jax
import jax.numpy as jnp
import numpy as np
from jax import lax
from jax.experimental import pallas as pl
from jax.experimental.pallas import tpu as pltpu
from jax.sharding import PartitionSpec as P

WIN = 256
TILE = 16
ACROSS = WIN // TILE
SLICES = 2
MEAN = 2
CAP = 6
CHIRP = 1.5
HALF = SLICES * TILE * TILE
LANES = 128
BLOCKS = HALF // LANES
SCALE_ROWS = 8
SPREAD = 4
QUARTER = WIN // SPREAD
STEPS = 32.0
LEVELS = 32700.0
LN2 = math.log(2.0)

f32 = jnp.float32
i32 = jnp.int32
bf16 = jnp.bfloat16
SMEM = pl.BlockSpec(memory_space=pltpu.SMEM)
VMEM = pl.BlockSpec(memory_space=pltpu.VMEM)
ANY = pl.BlockSpec(memory_space=pl.ANY)


class Geometry:
    def __init__(self, owners, grid_rows, grid_cols):
        self.owners = owners
        self.columns = owners // 8
        self.rows_a = ACROSS // 8
        self.cols_b = ACROSS // self.columns
        self.tiles = self.rows_a * self.cols_b
        self.grid_rows = grid_rows
        self.grid_cols = grid_cols
        self.piece = WIN // owners
        self.group = min(8, self.piece)
        self.whole_blocks = self.piece % 16 == 0
        up = lambda rows: -(-(rows + SCALE_ROWS) // 8) * 8
        self.data = BLOCKS * self.tiles
        self.block_sent = up(MEAN * self.data)
        self.block_moved = up(QUARTER)
        self.block_first = -(-self.data // 8) * 8
        self.block_second = up(self.data + 2 * self.piece)
        self.block_probe = up(2 * self.piece)


def params(megabytes=58):
    return pltpu.CompilerParams(vmem_limit_bytes=megabytes << 20)


def tables():
    k = np.arange(16)
    root = np.exp(-2j * np.pi * np.outer(k, k) / 16) / 4
    kron = np.kron(root, root)

    def halves(x):
        hi = x.astype(np.float32).astype(jnp.bfloat16)
        lo = (x - hi.astype(np.float64)).astype(np.float32).astype(jnp.bfloat16)
        return hi, lo

    re_hi, re_lo = halves(kron.real)
    im_hi, im_lo = halves(kron.imag)
    hi = np.block([[re_hi, -im_hi], [im_hi, re_hi]])
    lo = np.block([[re_lo, -im_lo], [im_lo, re_lo]])
    left = np.concatenate([hi, hi, lo], axis=1)
    right = np.ascontiguousarray(left.T)
    low_u, low_v = np.divmod(np.arange(256), 16)
    twiddle = np.exp(
        -2j * np.pi * (np.outer(low_u, low_u) + np.outer(low_v, low_v)) / WIN
    )
    u = low_u[:, None] + 16 * low_u[None, :]
    v = low_v[:, None] + 16 * low_v[None, :]
    freq = lambda w: ((w + WIN // 2) % WIN - WIN // 2) / (WIN // 2)
    chirp = np.exp(-1j * CHIRP * (freq(u) ** 2 + freq(v) ** 2))
    pack = lambda z: np.stack([z.real, z.imag]).astype(np.float32)
    return left, right, pack(twiddle), pack(chirp)


def row_scale(x):
    peak = jnp.maximum(jnp.max(jnp.abs(x), axis=1, keepdims=True), 1e-30)
    return jnp.floor(jnp.log(peak) * (STEPS / LN2)) + 2.0


def encode(low, high):
    k_low, k_high = row_scale(low), row_scale(high)
    q_low = jnp.round(low * (jnp.exp(k_low * (-LN2 / STEPS)) * LEVELS)).astype(i32)
    q_high = jnp.round(high * (jnp.exp(k_high * (-LN2 / STEPS)) * LEVELS)).astype(i32)
    return (q_high << 16) | (q_low & 0xFFFF), k_low, k_high


def unscale(k):
    return jnp.exp(k.astype(f32) * (LN2 / STEPS)) * (1.0 / LEVELS)


def decode(words, k_low, k_high):
    low = ((words << 16) >> 16).astype(f32) * k_low
    high = (words >> 16).astype(f32) * k_high
    return low, high


def put_scales(scales, rows):
    lane = lax.broadcasted_iota(i32, (rows, LANES), 1)
    out = jnp.zeros((rows, LANES), f32)
    for i, k in enumerate(scales):
        out = jnp.where(lane == i, k, out)
    return out.astype(i32)


def make_plan(geo, counts_ref, positions_ref, map_ref, plan_ref, mine_ref):
    n = geo.owners
    me = lax.axis_index("scan").astype(i32)
    mine_ref[0] = me

    def spare(g):
        return jnp.maximum(counts_ref[g] - MEAN, 0)

    def body(o, carry):
        own = counts_ref[o] >= MEAN

        def behind(state):
            g, used = state
            return jnp.logical_and(
                jnp.logical_not(own),
                jnp.logical_and(used >= spare(g), g < n - 1),
            )

        g, used = lax.while_loop(behind, lambda state: (state[0] + 1, jnp.int32(0)), carry)
        dev = jnp.where(own, o, g)
        slot = jnp.where(own, 1, jnp.minimum(MEAN + used, CAP - 1))
        plan_ref[o] = positions_ref[0, 0, o]
        plan_ref[n + o] = positions_ref[0, 1, o]
        plan_ref[2 * n + o] = positions_ref[slot, 0, dev]
        plan_ref[3 * n + o] = positions_ref[slot, 1, dev]
        plan_ref[4 * n + o] = dev
        plan_ref[5 * n + o] = slot

        @pl.when(map_ref[o] == me)
        def _():
            mine_ref[1] = o

        return g, jnp.where(own, used, used + 1)

    lax.fori_loop(0, n, body, (jnp.int32(0), jnp.int32(0)))


def first_row(geo, slot, o, plan_ref, mine_ref):
    n, columns = geo.owners, geo.columns
    row, col = plan_ref[2 * slot * n + o], plan_ref[(2 * slot + 1) * n + o]
    own_class = mine_ref[1]
    row = row + ((own_class // columns - row) & 7)
    col = col + ((own_class % columns - col) & (columns - 1))
    return (row // 8) * geo.grid_cols + col // columns


def gather_kernel(
    geo, counts_ref, positions_ref, map_ref, tiles_hbm, plan_ref, mine_ref, out_ref, tiles_ref, sems
):
    n, b = geo.owners, geo.cols_b
    at = geo.block_sent - SCALE_ROWS
    copies = [
        pltpu.make_async_copy(tiles_hbm.at[:, pl.ds(j * LANES, LANES)], tiles_ref.at[j], sems.at[j])
        for j in range(2 * BLOCKS)
    ]
    for copy in copies:
        copy.start()
    make_plan(geo, counts_ref, positions_ref, map_ref, plan_ref, mine_ref)
    for copy in copies:
        copy.wait()

    def body(o, _):
        scales = []
        for slot in range(MEAN):
            start = first_row(geo, slot, o, plan_ref, mine_ref)
            for a in range(geo.rows_a):
                x = [tiles_ref[j, pl.ds(start + a * geo.grid_cols, b), :] for j in range(2 * BLOCKS)]
                words, k_low, k_high = encode(
                    jnp.concatenate(x[:BLOCKS], axis=1), jnp.concatenate(x[BLOCKS:], axis=1)
                )
                scales += [k_low, k_high]
                for j in range(BLOCKS):
                    rows = pl.ds(slot * geo.data + j * geo.tiles + a * b, b)
                    out_ref[o, rows, :] = words[:, j * LANES : (j + 1) * LANES]
        out_ref[o, pl.ds(at, b), :] = put_scales(scales, b)
        return 0

    lax.fori_loop(0, n, body, 0, unroll=8)


def gather_tiles(geo, counts, positions, owner_map, tiles):
    return pl.pallas_call(
        functools.partial(gather_kernel, geo),
        out_shape=(
            jax.ShapeDtypeStruct((6 * geo.owners,), i32),
            jax.ShapeDtypeStruct((2,), i32),
            jax.ShapeDtypeStruct((geo.owners, geo.block_sent, LANES), i32),
        ),
        in_specs=[SMEM, SMEM, SMEM, ANY],
        out_specs=(SMEM, SMEM, VMEM),
        scratch_shapes=[
            pltpu.VMEM((2 * BLOCKS, geo.grid_rows * geo.grid_cols, LANES), f32),
            pltpu.SemaphoreType.DMA((2 * BLOCKS,)),
        ],
        compiler_params=params(),
        cost_estimate=pl.CostEstimate(flops=1 << 23, bytes_accessed=4 << 20, transcendentals=0),
        name="gather",
    )(counts, positions, owner_map, tiles)


def moved_kernel(geo, plan_ref, mine_ref, own_ref, near1, near2, near3, out_ref, held_ref, sems):
    n, me = geo.owners, mine_ref[0]
    at = geo.block_moved - SCALE_ROWS
    fetch = [
        pltpu.make_async_copy(near, held_ref.at[k], sems.at[k])
        for k, near in enumerate((own_ref, near1, near2, near3))
    ]
    for copy in fetch:
        copy.start()
    for copy in fetch:
        copy.wait()

    def quarter(o, _):
        dev, spare = plan_ref[4 * n + o], plan_ref[5 * n + o] - MEAN
        near = dev ^ me

        @pl.when(near < SPREAD)
        def _():
            x = held_ref[near & (SPREAD - 1), jnp.maximum(spare, 0)].astype(f32)
            scales = []
            for i in range(QUARTER // 8):
                part = x[8 * i : 8 * (i + 1)]
                k = row_scale(part)
                scaled = jnp.round(part * (jnp.exp(k * (-LN2 / STEPS)) * LEVELS)).astype(i32)
                scales.append(k)
                out_ref[o, pl.ds(8 * i, 8), :] = (scaled[:, LANES:] << 16) | (scaled[:, :LANES] & 0xFFFF)
            out_ref[o, pl.ds(at, SCALE_ROWS), :] = put_scales(scales, SCALE_ROWS)

        return 0

    lax.fori_loop(0, n, quarter, 0)


def moved_quarters(geo, plan, mine, held):
    return pl.pallas_call(
        functools.partial(moved_kernel, geo),
        out_shape=jax.ShapeDtypeStruct((geo.owners, geo.block_moved, LANES), i32),
        in_specs=[SMEM, SMEM] + [ANY] * SPREAD,
        out_specs=VMEM,
        scratch_shapes=[
            pltpu.VMEM((SPREAD, CAP - MEAN, QUARTER, WIN), bf16),
            pltpu.SemaphoreType.DMA((SPREAD,)),
        ],
        compiler_params=params(),
        name="moved",
    )(plan, mine, *held)


def spare_kernel(measured_hbm, *rest):
    outs, measured_ref, sem = rest[:SPREAD], rest[SPREAD], rest[SPREAD + 1]
    copy = pltpu.make_async_copy(measured_hbm.at[pl.ds(MEAN, CAP - MEAN)], measured_ref, sem)
    copy.start()
    copy.wait()
    me = lax.axis_index("scan").astype(i32)
    for k, out_ref in enumerate(outs):
        rows = pl.ds(pl.multiple_of(((me ^ k) & (SPREAD - 1)) * QUARTER, QUARTER), QUARTER)
        for slot in range(CAP - MEAN):
            out_ref[slot] = measured_ref[slot, rows, :]


def near_quarters(geo, measured):
    shape = jax.ShapeDtypeStruct((CAP - MEAN, QUARTER, WIN), bf16)
    quarters = pl.pallas_call(
        spare_kernel,
        out_shape=[shape] * SPREAD,
        in_specs=[ANY],
        out_specs=[VMEM] * SPREAD,
        scratch_shapes=[pltpu.VMEM((CAP - MEAN, WIN, WIN), bf16), pltpu.SemaphoreType.DMA],
        compiler_params=params(),
        name="spare",
    )(measured)
    n = geo.owners
    return [quarters[0]] + [
        lax.ppermute(quarters[k], "scan", [(i, i ^ k) for i in range(n)]) for k in range(1, SPREAD)
    ]


def swap_tile_digits(x):
    blocks = x.shape[0] // 16
    rows = 8 * blocks
    parts = x.reshape(blocks, 2, 8, WIN)
    grid = [[parts[:, r, :, c * LANES : (c + 1) * LANES].reshape(rows, LANES) for c in range(2)] for r in range(2)]
    row = lax.broadcasted_iota(i32, (rows, LANES), 0)
    lane = lax.broadcasted_iota(i32, (rows, LANES), 1)

    def inner(q):
        for s in (4, 2, 1):
            shift = s * 16
            row_bit = (row & s) != 0
            lane_bit = (lane & shift) != 0
            moved = jnp.where(row_bit, pltpu.roll(q, s, 0), pltpu.roll(q, rows - s, 0))
            both = jnp.where(lane_bit, pltpu.roll(moved, shift, 1), pltpu.roll(moved, LANES - shift, 1))
            q = jnp.where(row_bit == lane_bit, q, both)
        return q.reshape(blocks, 1, 8, LANES)

    upper = jnp.concatenate([inner(grid[0][0]), inner(grid[1][0])], axis=3)
    lower = jnp.concatenate([inner(grid[0][1]), inner(grid[1][1])], axis=3)
    return jnp.concatenate([upper, lower], axis=1).reshape(16 * blocks, WIN)


def frequency_digits(x):
    turned = x.T
    lane = lax.broadcasted_iota(i32, (16, LANES), 1)
    halves = []
    for c in range(2):
        rows = [turned[16 * i : 16 * (i + 1), c * LANES : (c + 1) * LANES] for i in range(16)]
        for s in (1, 2, 4, 8):
            lane_bit = (lane & s) != 0
            new = list(rows)
            for i in range(16):
                if i & s == 0:
                    low, high = rows[i], rows[i | s]
                    new[i] = jnp.where(lane_bit, pltpu.roll(high, s, 1), low)
                    new[i | s] = jnp.where(lane_bit, high, pltpu.roll(low, LANES - s, 1))
            rows = new
        halves.append(jnp.concatenate(rows, axis=0))
    return jnp.concatenate(halves, axis=1)


def prepare_kernel(probe_ref, measured_ref, probe_out, measured_out):
    for c in range(2):
        probe_out[c] = swap_tile_digits(probe_ref[c])
    for k in range(MEAN):
        measured_out[k] = frequency_digits(measured_ref[k].astype(f32))


def prepare(probe, measured):
    return pl.pallas_call(
        prepare_kernel,
        out_shape=(
            jax.ShapeDtypeStruct((2, WIN, WIN), f32),
            jax.ShapeDtypeStruct((MEAN, WIN, WIN), f32),
        ),
        grid=(1,),
        in_specs=[
            pl.BlockSpec((2, WIN, WIN), lambda i: (0, 0, 0)),
            pl.BlockSpec((MEAN, WIN, WIN), lambda i: (0, 0, 0)),
        ],
        out_specs=(
            pl.BlockSpec((2, WIN, WIN), lambda i: (0, 0, 0)),
            pl.BlockSpec((MEAN, WIN, WIN), lambda i: (0, 0, 0)),
        ),
        compiler_params=params(),
        cost_estimate=pl.CostEstimate(flops=1 << 22, bytes_accessed=2 << 20, transcendentals=0),
        name="prepare",
    )(probe, measured)


def split(x):
    hi = x.astype(bf16)
    return hi, (x - hi.astype(f32)).astype(bf16)


def times_right(zs, right_ref):
    rows = []
    for z in zs:
        re_hi, re_lo = split(z[0])
        im_hi, im_lo = split(z[1])
        rows.append(jnp.concatenate([re_hi, im_hi, re_lo, im_lo, re_hi, im_hi], axis=1))
    out = jnp.dot(jnp.concatenate(rows, axis=0), right_ref[...], preferred_element_type=f32)
    return [(out[i * WIN : (i + 1) * WIN, :WIN], out[i * WIN : (i + 1) * WIN, WIN:]) for i in range(len(zs))]


def times_left(zs, left_ref):
    columns = []
    for z in zs:
        re_hi, re_lo = split(z[0])
        im_hi, im_lo = split(z[1])
        columns.append(jnp.concatenate([re_hi, im_hi, re_lo, im_lo, re_hi, im_hi], axis=0))
    out = jnp.dot(left_ref[...], jnp.concatenate(columns, axis=1), preferred_element_type=f32)
    return [(out[:WIN, i * WIN : (i + 1) * WIN], out[WIN:, i * WIN : (i + 1) * WIN]) for i in range(len(zs))]


def product(x, y):
    return x[0] * y[0] - x[1] * y[1], x[0] * y[1] + x[1] * y[0]


def product_conj(x, y):
    return x[0] * y[0] + x[1] * y[1], x[0] * y[1] - x[1] * y[0]


def conj(x):
    return x[0], -x[1]


class Fetched:
    def __init__(self, copies):
        self.copies = {}
        for name, (src, dst, sem) in copies.items():
            self.copies[name] = pltpu.make_async_copy(src, dst, sem)
            self.copies[name].start()
        self.refs = {name: dst for name, (_, dst, _) in copies.items()}

    def __getitem__(self, name):
        if name in self.copies:
            self.copies.pop(name).wait()
        return self.refs[name]

    def pair(self, name):
        ref = self[name]
        return ref[0], ref[1]

    def spectrum(self, zs):
        zs = times_left(zs, self["left"])
        return times_right([product(self.pair("twiddle"), z) for z in zs], self["right"])

    def conj_inverse(self, zs):
        zs = times_right(zs, self["right"])
        return times_left([product(self.pair("twiddle"), z) for z in zs], self["left"])


def source(geo, slot, k, plan_ref, mine_ref, map_ref):
    n, columns, me = geo.owners, geo.columns, mine_ref[0]
    row, col = plan_ref[2 * slot * n + me], plan_ref[(2 * slot + 1) * n + me]
    return map_ref[((row + k // columns) & 7) * columns + ((col + k % columns) & (columns - 1))]


def tile_rows(geo, k, a):
    return pl.ds((8 * a + k // geo.columns) * ACROSS + k % geo.columns, geo.cols_b, geo.columns)


def plane(ref, i):
    return jnp.concatenate([ref[2 * i], ref[2 * i + 1]], axis=1)


def put_plane(ref, i, x):
    ref[2 * i] = x[:, :LANES]
    ref[2 * i + 1] = x[:, LANES:]


def put_marks(out_ref, o, at, first, scales):
    rows = scales[0].shape[0]
    lane = lax.broadcasted_iota(i32, (rows, LANES), 1)
    marks = out_ref[o, pl.ds(at, rows), :]
    for i, k in enumerate(scales):
        marks = jnp.where(lane == first + i, k.astype(i32), marks)
    out_ref[o, pl.ds(at, rows), :] = marks


def pack_tiles(geo, slot, refs, tile_ref, out_ref, at, marks_ref, marks_at):
    b = geo.cols_b

    def pack(k, _):
        dst = source(geo, slot, k, *refs)
        scales = []
        for a in range(geo.rows_a):
            x = [tile_ref[j, tile_rows(geo, k, a), :] for j in range(2 * BLOCKS)]
            words, k_low, k_high = encode(
                jnp.concatenate(x[:BLOCKS], axis=1), jnp.concatenate(x[BLOCKS:], axis=1)
            )
            scales += [k_low, k_high]
            for j in range(BLOCKS):
                rows = pl.ds(at + j * geo.tiles + a * b, b)
                out_ref[dst, rows, :] = words[:, j * LANES : (j + 1) * LANES]
        put_marks(marks_ref, dst, marks_at, 2 * geo.rows_a * slot, scales)
        return 0

    lax.fori_loop(0, geo.owners, pack, 0, unroll=4)


def backward(fetched, tile_ref, middle, far, intensity):
    misfit = far[0] * far[0] + far[1] * far[1] - intensity
    (near,) = fetched.conj_inverse([(misfit * far[0], -(misfit * far[1]))])
    grad_middle = conj(product((plane(tile_ref, 2), plane(tile_ref, 3)), near))
    grad_back = product(middle(), conj(near))
    put_plane(tile_ref, 2, grad_back[0])
    put_plane(tile_ref, 3, grad_back[1])
    (f,) = fetched.spectrum([grad_middle])
    (e,) = fetched.conj_inverse([product_conj(f, fetched.pair("chirp"))])
    enter = conj(e)
    grad_probe = product_conj((plane(tile_ref, 0), plane(tile_ref, 1)), enter)
    grad_front = product_conj(fetched.pair("probe"), enter)
    put_plane(tile_ref, 0, grad_front[0])
    put_plane(tile_ref, 1, grad_front[1])
    return grad_probe


def forward_kernel(
    geo, plan_ref, mine_ref, map_ref, in_ref, probe_in, intensity_in, left_in, right_in, twiddle_in, chirp_in,
    out_ref, marks_ref, tile1_hbm, waves_hbm, tile0_ref, tile1_ref, waves_ref, probe_ref, intensity_ref, left_ref, right_ref, twiddle_ref, chirp_ref,
    sems,
):
    fetched = Fetched(
        {
            "probe": (probe_in, probe_ref, sems.at[0]),
            "left": (left_in, left_ref, sems.at[1]),
            "twiddle": (twiddle_in, twiddle_ref, sems.at[2]),
            "right": (right_in, right_ref, sems.at[3]),
            "chirp": (chirp_in, chirp_ref, sems.at[4]),
            "intensity": (intensity_in.at[0], intensity_ref, sems.at[5]),
        }
    )
    n, b = geo.owners, geo.cols_b
    refs = plan_ref, mine_ref, map_ref
    at = geo.block_sent - SCALE_ROWS
    tiles = tile0_ref, tile1_ref

    def unpack(k, _):
        for slot in range(MEAN):
            src = source(geo, slot, k, *refs)
            scales = unscale(in_ref[src, pl.ds(at, b), :])
            for a in range(geo.rows_a):
                c = 2 * (geo.rows_a * slot + a)
                for j in range(BLOCKS):
                    words = in_ref[src, pl.ds(slot * geo.data + j * geo.tiles + a * b, b), :]
                    low, high = decode(words, scales[:, c : c + 1], scales[:, c + 1 : c + 2])
                    tiles[slot][j, tile_rows(geo, k, a), :] = low
                    tiles[slot][BLOCKS + j, tile_rows(geo, k, a), :] = high
        return 0

    lax.fori_loop(0, n, unpack, 0, unroll=4)
    going = [pltpu.make_async_copy(tile1_ref, tile1_hbm, sems.at[6])]
    going[0].start()
    entrance = [product(fetched.pair("probe"), (plane(t, 0), plane(t, 1))) for t in tiles]
    waves = fetched.spectrum(entrance)
    middle = fetched.conj_inverse([conj(product(fetched.pair("chirp"), f)) for f in waves])
    far = fetched.spectrum([product_conj(middle[s], (plane(t, 2), plane(t, 3))) for s, t in enumerate(tiles)])
    for c in range(2):
        waves_ref[c] = far[1][c]
        waves_ref[2 + c] = middle[1][c]
    going.append(pltpu.make_async_copy(waves_ref.at[pl.ds(0, 4)], waves_hbm.at[pl.ds(0, 4)], sems.at[7]))
    going[1].start()
    intensity = fetched["intensity"]
    grad_probe = backward(fetched, tile0_ref, lambda: middle[0], far[0], intensity[...])
    for c in range(2):
        waves_ref[4 + c] = grad_probe[c]
    going.append(pltpu.make_async_copy(waves_ref.at[pl.ds(4, 2)], waves_hbm.at[pl.ds(4, 2)], sems.at[8]))
    going[2].start()
    pack_tiles(geo, 0, refs, tile0_ref, out_ref, 0, marks_ref, 0)
    for copy in going:
        copy.wait()


def backward_kernel(
    geo, plan_ref, mine_ref, map_ref, moved_in, marks_in, probe_in, intensity_in, tile_in, waves_in,
    left_in, right_in, twiddle_in, chirp_in,
    out_ref, tile_ref, moved_ref, waves_ref, probe_ref, intensity_ref, left_ref, right_ref, twiddle_ref, chirp_ref,
    sems,
):
    n, g, me = geo.owners, geo.group, mine_ref[0]
    marks_at = geo.block_second - SCALE_ROWS
    pair = lambda ref, i: ref.at[pl.ds(2 * i, 2)]
    fetched = Fetched(
        {
            "far": (pair(waves_in, 0), pair(waves_ref, 0), sems.at[0]),
            "intensity": (intensity_in.at[1], intensity_ref, sems.at[1]),
            "right": (right_in, right_ref, sems.at[2]),
            "twiddle": (twiddle_in, twiddle_ref, sems.at[3]),
            "left": (left_in, left_ref, sems.at[4]),
            "tile": (tile_in, tile_ref, sems.at[5]),
            "middle": (pair(waves_in, 1), pair(waves_ref, 1), sems.at[6]),
            "chirp": (chirp_in, chirp_ref, sems.at[7]),
            "probe": (probe_in, probe_ref, sems.at[8]),
            "before": (pair(waves_in, 2), pair(waves_ref, 2), sems.at[9]),
            "marks": (marks_in, out_ref.at[:, pl.ds(marks_at, SCALE_ROWS)], sems.at[10]),
        }
    )
    refs = plan_ref, mine_ref, map_ref
    dev = plan_ref[4 * n + me]
    for q in range(SPREAD):
        holder = (dev & -SPREAD) + q
        scales = unscale(moved_in[holder, pl.ds(geo.block_moved - SCALE_ROWS, SCALE_ROWS), :])
        for i in range(QUARTER // 8):
            words = moved_in[holder, pl.ds(8 * i, 8), :]
            low, high = decode(words, scales[:, i : i + 1], scales[:, i : i + 1])
            moved_ref[0, pl.ds(q * QUARTER + 8 * i, 8), :] = low
            moved_ref[1, pl.ds(q * QUARTER + 8 * i, 8), :] = high
    arrived = frequency_digits(jnp.concatenate([moved_ref[0], moved_ref[1]], axis=1))
    intensity = jnp.where(dev == me, fetched["intensity"][...], arrived)
    far = fetched.pair("far")
    fetched["tile"]
    grad_probe = backward(fetched, tile_ref, lambda: fetched.pair("middle"), far, intensity)
    fetched["marks"]
    pack_tiles(geo, 1, refs, tile_ref, out_ref, 0, out_ref, marks_at)
    before = fetched.pair("before")
    for c in range(2):
        put_plane(tile_ref, c, before[c] + grad_probe[c])

    def pieces(o, _):
        scales = []
        for i in range(geo.piece // g):
            x = [tile_ref[j, pl.ds(o * geo.piece + i * g, g), :] for j in range(4)]
            words, k_low, k_high = encode(
                jnp.concatenate(x[:2], axis=1), jnp.concatenate(x[2:], axis=1)
            )
            scales += [k_low, k_high]
            for j in range(2):
                at = pl.ds(geo.data + j * geo.piece + i * g, g)
                out_ref[o, at, :] = words[:, j * LANES : (j + 1) * LANES]
        put_marks(out_ref, o, marks_at, 2 * geo.rows_a * MEAN, scales)
        return 0

    lax.fori_loop(0, n, pieces, 0, unroll=4)


def wave_scratch(consts, copies):
    return (
        [pltpu.VMEM((6, WIN, WIN), f32), pltpu.VMEM((2, WIN, WIN), f32), pltpu.VMEM((WIN, WIN), f32)]
        + [pltpu.VMEM(c.shape, c.dtype) for c in consts]
        + [pltpu.SemaphoreType.DMA((copies,))]
    )


def forward(geo, plan, mine, owner_map, come, probe, intensity, consts):
    tile = (2 * BLOCKS, WIN, LANES)
    return pl.pallas_call(
        functools.partial(forward_kernel, geo),
        out_shape=(
            jax.ShapeDtypeStruct((geo.owners, geo.block_first, LANES), i32),
            jax.ShapeDtypeStruct((geo.owners, SCALE_ROWS, LANES), i32),
            jax.ShapeDtypeStruct(tile, f32),
            jax.ShapeDtypeStruct((6, WIN, WIN), f32),
        ),
        in_specs=[SMEM] * 3 + [VMEM] + [ANY] * 6,
        out_specs=(VMEM, VMEM, ANY, ANY),
        scratch_shapes=[pltpu.VMEM(tile, f32), pltpu.VMEM(tile, f32)] + wave_scratch(consts, 9),
        compiler_params=params(),
        cost_estimate=pl.CostEstimate(flops=20 << 30, bytes_accessed=8 << 20, transcendentals=0),
        name="forward",
    )(plan, mine, owner_map, come, probe, intensity, *consts)


def second_back(geo, plan, mine, owner_map, moved, marks, probe, intensity, tile, waves, consts):
    return pl.pallas_call(
        functools.partial(backward_kernel, geo),
        out_shape=jax.ShapeDtypeStruct((geo.owners, geo.block_second, LANES), i32),
        in_specs=[SMEM] * 3 + [VMEM] + [ANY] * 9,
        out_specs=VMEM,
        scratch_shapes=[pltpu.VMEM(tile.shape, f32), pltpu.VMEM((2, WIN, LANES), f32)] + wave_scratch(consts, 11),
        compiler_params=params(),
        cost_estimate=pl.CostEstimate(flops=6 << 30, bytes_accessed=8 << 20, transcendentals=0),
        name="backward",
    )(plan, mine, owner_map, moved, marks, probe, intensity, tile, waves, *consts)


def add_kernel(geo, plan_ref, mine_ref, first_ref, second_ref, grad_hbm, grad_ref, sems):
    b = geo.cols_b
    grad_ref[...] = jnp.zeros_like(grad_ref)

    def body(o, _):
        scales = unscale(second_ref[o, pl.ds(geo.block_second - SCALE_ROWS, b), :])
        for slot, in_ref in enumerate((first_ref, second_ref)):
            start = first_row(geo, slot, o, plan_ref, mine_ref)
            for a in range(geo.rows_a):
                at = 2 * (geo.rows_a * slot + a)
                k_low, k_high = scales[:, at : at + 1], scales[:, at + 1 : at + 2]
                rows = pl.ds(start + a * geo.grid_cols, b)
                for j in range(BLOCKS):
                    words = in_ref[o, pl.ds(j * geo.tiles + a * b, b), :]
                    low, high = decode(words, k_low, k_high)
                    grad_ref[j, rows, :] += low
                    grad_ref[BLOCKS + j, rows, :] += high
        return 0

    lax.fori_loop(0, geo.owners, body, 0, unroll=2)
    copies = [
        pltpu.make_async_copy(grad_ref.at[j], grad_hbm.at[:, pl.ds(j * LANES, LANES)], sems.at[j])
        for j in range(2 * BLOCKS)
    ]
    for copy in copies:
        copy.start()
    for copy in copies:
        copy.wait()


def add_up(geo, plan, mine, first, second):
    return pl.pallas_call(
        functools.partial(add_kernel, geo),
        out_shape=jax.ShapeDtypeStruct((geo.grid_rows * geo.grid_cols, 2 * HALF), f32),
        in_specs=[SMEM, SMEM, VMEM, VMEM],
        out_specs=ANY,
        scratch_shapes=[
            pltpu.VMEM((2 * BLOCKS, geo.grid_rows * geo.grid_cols, LANES), f32),
            pltpu.SemaphoreType.DMA((2 * BLOCKS,)),
        ],
        compiler_params=params(24),
        cost_estimate=pl.CostEstimate(flops=1 << 23, bytes_accessed=4 << 20, transcendentals=0),
        name="add",
    )(plan, mine, first, second)


def sum_kernel(geo, in_hbm, out_ref, in_ref, sem):
    g = geo.group
    rows = geo.block_second - geo.data
    copy = pltpu.make_async_copy(in_hbm.at[:, pl.ds(geo.data, rows)], in_ref, sem)
    copy.start()
    copy.wait()
    count = geo.piece // g

    def add_piece(o, sums):
        scales = unscale(in_ref[o, pl.ds(rows - SCALE_ROWS, g), :])
        new = []
        for i in range(count):
            at = 2 * (geo.rows_a * MEAN + i)
            k_low, k_high = scales[:, at : at + 1], scales[:, at + 1 : at + 2]
            for j in range(2):
                words = in_ref[o, pl.ds(j * geo.piece + i * g, g), :]
                low, high = decode(words, k_low, k_high)
                new += [sums[len(new)] + low, sums[len(new) + 1] + high]
        return tuple(new)

    sums = lax.fori_loop(0, geo.owners, add_piece, (jnp.zeros((g, LANES), f32),) * (4 * count), unroll=4)
    parts, scales = [], []
    low = jnp.concatenate([jnp.concatenate([sums[4 * i], sums[4 * i + 2]], axis=1) for i in range(count)], axis=0)
    high = jnp.concatenate([jnp.concatenate([sums[4 * i + 1], sums[4 * i + 3]], axis=1) for i in range(count)], axis=0)
    if geo.whole_blocks:
        low, high = swap_tile_digits(low), swap_tile_digits(high)
    for i in range(count):
        rows = slice(i * g, (i + 1) * g)
        words, k_low, k_high = encode(low[rows], high[rows])
        parts.append(words)
        scales += [k_low, k_high]
    marks = put_scales(scales, g)

    def spread(o, _):
        for i in range(count):
            for j in range(2):
                out_ref[o, pl.ds(j * geo.piece + i * g, g), :] = parts[i][:, j * LANES : (j + 1) * LANES]
        out_ref[o, pl.ds(geo.block_probe - SCALE_ROWS, g), :] = marks
        return 0

    lax.fori_loop(0, geo.owners, spread, 0, unroll=4)


def sum_pieces(geo, returned):
    return pl.pallas_call(
        functools.partial(sum_kernel, geo),
        out_shape=jax.ShapeDtypeStruct((geo.owners, geo.block_probe, LANES), i32),
        in_specs=[ANY],
        out_specs=VMEM,
        scratch_shapes=[
            pltpu.VMEM((geo.owners, geo.block_second - geo.data, LANES), i32),
            pltpu.SemaphoreType.DMA,
        ],
        compiler_params=params(24),
        name="sum",
    )(returned)


def finish_kernel(geo, in_ref, out_ref, whole_ref):
    g = geo.group

    def place(o, _):
        scales = unscale(in_ref[o, pl.ds(geo.block_probe - SCALE_ROWS, g), :])
        for i in range(geo.piece // g):
            k_low, k_high = scales[:, 2 * i : 2 * i + 1], scales[:, 2 * i + 1 : 2 * i + 2]
            for j in range(2):
                words = in_ref[o, pl.ds(j * geo.piece + i * g, g), :]
                for c, x in enumerate(decode(words, k_low, k_high)):
                    if geo.whole_blocks:
                        rows = pl.ds(pl.multiple_of(o * geo.piece + i * g, g), g)
                        out_ref[c, rows, pl.ds(j * LANES, LANES)] = x
                    else:
                        whole_ref[c, j, pl.ds(o * geo.piece + i * g, g), :] = x
        return 0

    lax.fori_loop(0, geo.owners, place, 0, unroll=4)
    if not geo.whole_blocks:
        for c in range(2):
            out_ref[c] = swap_tile_digits(jnp.concatenate([whole_ref[c, 0], whole_ref[c, 1]], axis=1))


def finish_probe(geo, parts):
    return pl.pallas_call(
        functools.partial(finish_kernel, geo),
        out_shape=jax.ShapeDtypeStruct((2, WIN, WIN), f32),
        in_specs=[VMEM],
        out_specs=VMEM,
        scratch_shapes=[pltpu.VMEM((2, 2, WIN, LANES), f32)],
        compiler_params=params(24),
        name="finish",
    )(parts)


def exchange(x):
    return lax.all_to_all(x, "scan", split_axis=0, concat_axis=0, tiled=True)


def local(object_tiles, probe, measured, positions, counts, owner_map):
    n = lax.axis_size("scan")
    geo = Geometry(n, object_tiles.shape[1], object_tiles.shape[2])
    consts = [jnp.asarray(t) for t in tables()]
    tiles = object_tiles.reshape(geo.grid_rows * geo.grid_cols, 2 * HALF)

    plan, mine, sent = gather_tiles(geo, counts, positions.transpose(1, 2, 0), owner_map, tiles)
    sent, measured, probe = lax.optimization_barrier((sent, measured, probe))
    come = exchange(sent)
    held = near_quarters(geo, measured)
    moved = moved_quarters(geo, plan, mine, held)
    moved, come = lax.optimization_barrier((moved, come))
    moved = exchange(moved)
    probe_t, intensity = prepare(probe, measured)
    back, marks, tile, waves = forward(geo, plan, mine, owner_map, come, probe_t, intensity, consts)
    back, tile, moved = lax.optimization_barrier((back, tile, moved))
    first = exchange(back)
    second = second_back(geo, plan, mine, owner_map, moved, marks, probe_t, intensity, tile, waves, consts)
    second, first = lax.optimization_barrier((second, first))
    second = exchange(second)
    probe_grad = finish_probe(geo, exchange(sum_pieces(geo, second)))
    grad = add_up(geo, plan, mine, first, second)
    return grad.reshape(object_tiles.shape), probe_grad


def solution(mesh):
    return jax.shard_map(
        local,
        mesh=mesh,
        in_specs=(
            P(("groups", "scan"), None, None, None),
            P("groups", None, None),
            P(("groups", "scan"), None, None),
            P("groups", None, None),
            P("groups"),
            P(),
        ),
        out_specs=(P(("groups", "scan"), None, None, None), P("groups", None, None)),
        check_vma=False,
    )
```

```python
import functools
import math

import jax
import jax.numpy as jnp
import numpy as np
from jax import lax
from jax.experimental import pallas as pl
from jax.experimental.pallas import tpu as pltpu
from jax.sharding import PartitionSpec as P

WIN = 256
TILE = 16
ACROSS = WIN // TILE
SLICES = 2
MEAN = 2
CAP = 6
CHIRP = 1.5
HALF = SLICES * TILE * TILE
LANES = 128
BLOCKS = HALF // LANES
SCALE_ROWS = 8
SPREAD = 4
QUARTER = WIN // SPREAD
STEPS = 32.0
LEVELS = 32700.0
LN2 = math.log(2.0)

f32 = jnp.float32
i32 = jnp.int32
bf16 = jnp.bfloat16
SMEM = pl.BlockSpec(memory_space=pltpu.SMEM)
VMEM = pl.BlockSpec(memory_space=pltpu.VMEM)
ANY = pl.BlockSpec(memory_space=pl.ANY)


class Geometry:
    def __init__(self, owners, grid_rows, grid_cols):
        self.owners = owners
        self.columns = owners // 8
        self.rows_a = ACROSS // 8
        self.cols_b = ACROSS // self.columns
        self.tiles = self.rows_a * self.cols_b
        self.grid_rows = grid_rows
        self.grid_cols = grid_cols
        self.piece = WIN // owners
        self.group = min(8, self.piece)
        self.whole_blocks = self.piece % 16 == 0
        up = lambda rows: -(-(rows + SCALE_ROWS) // 8) * 8
        self.data = BLOCKS * self.tiles
        self.block_sent = up(MEAN * self.data)
        self.block_moved = up(QUARTER)
        self.block_first = -(-self.data // 8) * 8
        self.block_second = up(self.data + 2 * self.piece)
        self.block_probe = up(2 * self.piece)


def params(megabytes=58):
    return pltpu.CompilerParams(vmem_limit_bytes=megabytes << 20)


def tables():
    k = np.arange(16)
    root = np.exp(-2j * np.pi * np.outer(k, k) / 16) / 4
    kron = np.kron(root, root)

    def halves(x):
        hi = x.astype(np.float32).astype(jnp.bfloat16)
        lo = (x - hi.astype(np.float64)).astype(np.float32).astype(jnp.bfloat16)
        return hi, lo

    re_hi, re_lo = halves(kron.real)
    im_hi, im_lo = halves(kron.imag)
    hi = np.block([[re_hi, -im_hi], [im_hi, re_hi]])
    lo = np.block([[re_lo, -im_lo], [im_lo, re_lo]])
    left = np.concatenate([hi, hi, lo], axis=1)
    right = np.ascontiguousarray(left.T)
    low_u, low_v = np.divmod(np.arange(256), 16)
    twiddle = np.exp(
        -2j * np.pi * (np.outer(low_u, low_u) + np.outer(low_v, low_v)) / WIN
    )
    u = low_u[:, None] + 16 * low_u[None, :]
    v = low_v[:, None] + 16 * low_v[None, :]
    freq = lambda w: ((w + WIN // 2) % WIN - WIN // 2) / (WIN // 2)
    chirp = np.exp(-1j * CHIRP * (freq(u) ** 2 + freq(v) ** 2))
    pack = lambda z: np.stack([z.real, z.imag]).astype(np.float32)
    return left, right, pack(twiddle), pack(chirp)


def row_scale(x):
    peak = jnp.maximum(jnp.max(jnp.abs(x), axis=1, keepdims=True), 1e-30)
    return jnp.floor(jnp.log(peak) * (STEPS / LN2)) + 2.0


def encode(low, high):
    k_low, k_high = row_scale(low), row_scale(high)
    q_low = jnp.round(low * (jnp.exp(k_low * (-LN2 / STEPS)) * LEVELS)).astype(i32)
    q_high = jnp.round(high * (jnp.exp(k_high * (-LN2 / STEPS)) * LEVELS)).astype(i32)
    return (q_high << 16) | (q_low & 0xFFFF), k_low, k_high


def unscale(k):
    return jnp.exp(k.astype(f32) * (LN2 / STEPS)) * (1.0 / LEVELS)


def decode(words, k_low, k_high):
    low = ((words << 16) >> 16).astype(f32) * k_low
    high = (words >> 16).astype(f32) * k_high
    return low, high


def put_scales(scales, rows):
    lane = lax.broadcasted_iota(i32, (rows, LANES), 1)
    out = jnp.zeros((rows, LANES), f32)
    for i, k in enumerate(scales):
        out = jnp.where(lane == i, k, out)
    return out.astype(i32)


def make_plan(geo, counts_ref, positions_ref, map_ref, plan_ref, mine_ref):
    n = geo.owners
    me = lax.axis_index("scan").astype(i32)
    mine_ref[0] = me

    def spare(g):
        return jnp.maximum(counts_ref[g] - MEAN, 0)

    def body(o, carry):
        own = counts_ref[o] >= MEAN

        def behind(state):
            g, used = state
            return jnp.logical_and(
                jnp.logical_not(own),
                jnp.logical_and(used >= spare(g), g < n - 1),
            )

        g, used = lax.while_loop(behind, lambda state: (state[0] + 1, jnp.int32(0)), carry)
        dev = jnp.where(own, o, g)
        slot = jnp.where(own, 1, jnp.minimum(MEAN + used, CAP - 1))
        plan_ref[o] = positions_ref[0, 0, o]
        plan_ref[n + o] = positions_ref[0, 1, o]
        plan_ref[2 * n + o] = positions_ref[slot, 0, dev]
        plan_ref[3 * n + o] = positions_ref[slot, 1, dev]
        plan_ref[4 * n + o] = dev
        plan_ref[5 * n + o] = slot

        @pl.when(map_ref[o] == me)
        def _():
            mine_ref[1] = o

        return g, jnp.where(own, used, used + 1)

    lax.fori_loop(0, n, body, (jnp.int32(0), jnp.int32(0)))


def first_row(geo, slot, o, plan_ref, mine_ref):
    n, columns = geo.owners, geo.columns
    row, col = plan_ref[2 * slot * n + o], plan_ref[(2 * slot + 1) * n + o]
    own_class = mine_ref[1]
    row = row + ((own_class // columns - row) & 7)
    col = col + ((own_class % columns - col) & (columns - 1))
    return (row // 8) * geo.grid_cols + col // columns


def gather_kernel(
    geo, counts_ref, positions_ref, map_ref, tiles_hbm, plan_ref, mine_ref, out_ref, tiles_ref, sems
):
    n, b = geo.owners, geo.cols_b
    at = geo.block_sent - SCALE_ROWS
    copies = [
        pltpu.make_async_copy(tiles_hbm.at[:, pl.ds(j * LANES, LANES)], tiles_ref.at[j], sems.at[j])
        for j in range(2 * BLOCKS)
    ]
    for copy in copies:
        copy.start()
    make_plan(geo, counts_ref, positions_ref, map_ref, plan_ref, mine_ref)
    for copy in copies:
        copy.wait()

    def body(o, _):
        scales = []
        for slot in range(MEAN):
            start = first_row(geo, slot, o, plan_ref, mine_ref)
            for a in range(geo.rows_a):
                x = [tiles_ref[j, pl.ds(start + a * geo.grid_cols, b), :] for j in range(2 * BLOCKS)]
                words, k_low, k_high = encode(
                    jnp.concatenate(x[:BLOCKS], axis=1), jnp.concatenate(x[BLOCKS:], axis=1)
                )
                scales += [k_low, k_high]
                for j in range(BLOCKS):
                    rows = pl.ds(slot * geo.data + j * geo.tiles + a * b, b)
                    out_ref[o, rows, :] = words[:, j * LANES : (j + 1) * LANES]
        out_ref[o, pl.ds(at, b), :] = put_scales(scales, b)
        return 0

    lax.fori_loop(0, n, body, 0, unroll=8)


def gather_tiles(geo, counts, positions, owner_map, tiles):
    return pl.pallas_call(
        functools.partial(gather_kernel, geo),
        out_shape=(
            jax.ShapeDtypeStruct((6 * geo.owners,), i32),
            jax.ShapeDtypeStruct((2,), i32),
            jax.ShapeDtypeStruct((geo.owners, geo.block_sent, LANES), i32),
        ),
        in_specs=[SMEM, SMEM, SMEM, ANY],
        out_specs=(SMEM, SMEM, VMEM),
        scratch_shapes=[
            pltpu.VMEM((2 * BLOCKS, geo.grid_rows * geo.grid_cols, LANES), f32),
            pltpu.SemaphoreType.DMA((2 * BLOCKS,)),
        ],
        compiler_params=params(),
        cost_estimate=pl.CostEstimate(flops=1 << 23, bytes_accessed=4 << 20, transcendentals=0),
        name="gather",
    )(counts, positions, owner_map, tiles)


def moved_kernel(geo, plan_ref, mine_ref, own_ref, near1, near2, near3, out_ref, held_ref, sems):
    n, me = geo.owners, mine_ref[0]
    at = geo.block_moved - SCALE_ROWS
    fetch = [
        pltpu.make_async_copy(near, held_ref.at[k], sems.at[k])
        for k, near in enumerate((own_ref, near1, near2, near3))
    ]
    for copy in fetch:
        copy.start()
    for copy in fetch:
        copy.wait()

    def quarter(o, _):
        dev, spare = plan_ref[4 * n + o], plan_ref[5 * n + o] - MEAN
        near = dev ^ me

        @pl.when(near < SPREAD)
        def _():
            x = held_ref[near & (SPREAD - 1), jnp.maximum(spare, 0)].astype(f32)
            scales = []
            for i in range(QUARTER // 8):
                part = x[8 * i : 8 * (i + 1)]
                k = row_scale(part)
                scaled = jnp.round(part * (jnp.exp(k * (-LN2 / STEPS)) * LEVELS)).astype(i32)
                scales.append(k)
                out_ref[o, pl.ds(8 * i, 8), :] = (scaled[:, LANES:] << 16) | (scaled[:, :LANES] & 0xFFFF)
            out_ref[o, pl.ds(at, SCALE_ROWS), :] = put_scales(scales, SCALE_ROWS)

        return 0

    lax.fori_loop(0, n, quarter, 0)


def moved_quarters(geo, plan, mine, held):
    return pl.pallas_call(
        functools.partial(moved_kernel, geo),
        out_shape=jax.ShapeDtypeStruct((geo.owners, geo.block_moved, LANES), i32),
        in_specs=[SMEM, SMEM] + [ANY] * SPREAD,
        out_specs=VMEM,
        scratch_shapes=[
            pltpu.VMEM((SPREAD, CAP - MEAN, QUARTER, WIN), bf16),
            pltpu.SemaphoreType.DMA((SPREAD,)),
        ],
        compiler_params=params(),
        name="moved",
    )(plan, mine, *held)


def spare_kernel(measured_hbm, *rest):
    outs, measured_ref, sem = rest[:SPREAD], rest[SPREAD], rest[SPREAD + 1]
    copy = pltpu.make_async_copy(measured_hbm.at[pl.ds(MEAN, CAP - MEAN)], measured_ref, sem)
    copy.start()
    copy.wait()
    me = lax.axis_index("scan").astype(i32)
    for k, out_ref in enumerate(outs):
        rows = pl.ds(pl.multiple_of(((me ^ k) & (SPREAD - 1)) * QUARTER, QUARTER), QUARTER)
        for slot in range(CAP - MEAN):
            out_ref[slot] = measured_ref[slot, rows, :]


def near_quarters(geo, measured):
    shape = jax.ShapeDtypeStruct((CAP - MEAN, QUARTER, WIN), bf16)
    quarters = pl.pallas_call(
        spare_kernel,
        out_shape=[shape] * SPREAD,
        in_specs=[ANY],
        out_specs=[VMEM] * SPREAD,
        scratch_shapes=[pltpu.VMEM((CAP - MEAN, WIN, WIN), bf16), pltpu.SemaphoreType.DMA],
        compiler_params=params(),
        name="spare",
    )(measured)
    n = geo.owners
    return [quarters[0]] + [
        lax.ppermute(quarters[k], "scan", [(i, i ^ k) for i in range(n)]) for k in range(1, SPREAD)
    ]


def swap_tile_digits(x):
    blocks = x.shape[0] // 16
    rows = 8 * blocks
    parts = x.reshape(blocks, 2, 8, WIN)
    grid = [[parts[:, r, :, c * LANES : (c + 1) * LANES].reshape(rows, LANES) for c in range(2)] for r in range(2)]
    row = lax.broadcasted_iota(i32, (rows, LANES), 0)
    lane = lax.broadcasted_iota(i32, (rows, LANES), 1)

    def inner(q):
        for s in (4, 2, 1):
            shift = s * 16
            row_bit = (row & s) != 0
            lane_bit = (lane & shift) != 0
            moved = jnp.where(row_bit, pltpu.roll(q, s, 0), pltpu.roll(q, rows - s, 0))
            both = jnp.where(lane_bit, pltpu.roll(moved, shift, 1), pltpu.roll(moved, LANES - shift, 1))
            q = jnp.where(row_bit == lane_bit, q, both)
        return q.reshape(blocks, 1, 8, LANES)

    upper = jnp.concatenate([inner(grid[0][0]), inner(grid[1][0])], axis=3)
    lower = jnp.concatenate([inner(grid[0][1]), inner(grid[1][1])], axis=3)
    return jnp.concatenate([upper, lower], axis=1).reshape(16 * blocks, WIN)


def frequency_digits(x):
    turned = x.T
    lane = lax.broadcasted_iota(i32, (16, LANES), 1)
    halves = []
    for c in range(2):
        rows = [turned[16 * i : 16 * (i + 1), c * LANES : (c + 1) * LANES] for i in range(16)]
        for s in (1, 2, 4, 8):
            lane_bit = (lane & s) != 0
            new = list(rows)
            for i in range(16):
                if i & s == 0:
                    low, high = rows[i], rows[i | s]
                    new[i] = jnp.where(lane_bit, pltpu.roll(high, s, 1), low)
                    new[i | s] = jnp.where(lane_bit, high, pltpu.roll(low, LANES - s, 1))
            rows = new
        halves.append(jnp.concatenate(rows, axis=0))
    return jnp.concatenate(halves, axis=1)


def prepare_kernel(probe_ref, measured_ref, probe_out, measured_out):
    for c in range(2):
        probe_out[c] = swap_tile_digits(probe_ref[c])
    for k in range(MEAN):
        measured_out[k] = frequency_digits(measured_ref[k].astype(f32))


def prepare(probe, measured):
    return pl.pallas_call(
        prepare_kernel,
        out_shape=(
            jax.ShapeDtypeStruct((2, WIN, WIN), f32),
            jax.ShapeDtypeStruct((MEAN, WIN, WIN), f32),
        ),
        grid=(1,),
        in_specs=[
            pl.BlockSpec((2, WIN, WIN), lambda i: (0, 0, 0)),
            pl.BlockSpec((MEAN, WIN, WIN), lambda i: (0, 0, 0)),
        ],
        out_specs=(
            pl.BlockSpec((2, WIN, WIN), lambda i: (0, 0, 0)),
            pl.BlockSpec((MEAN, WIN, WIN), lambda i: (0, 0, 0)),
        ),
        compiler_params=params(),
        cost_estimate=pl.CostEstimate(flops=1 << 22, bytes_accessed=2 << 20, transcendentals=0),
        name="prepare",
    )(probe, measured)


def split(x):
    hi = x.astype(bf16)
    return hi, (x - hi.astype(f32)).astype(bf16)


def times_right(zs, right_ref):
    rows = []
    for z in zs:
        re_hi, re_lo = split(z[0])
        im_hi, im_lo = split(z[1])
        rows.append(jnp.concatenate([re_hi, im_hi, re_lo, im_lo, re_hi, im_hi], axis=1))
    out = jnp.dot(jnp.concatenate(rows, axis=0), right_ref[...], preferred_element_type=f32)
    return [(out[i * WIN : (i + 1) * WIN, :WIN], out[i * WIN : (i + 1) * WIN, WIN:]) for i in range(len(zs))]


def times_left(zs, left_ref):
    columns = []
    for z in zs:
        re_hi, re_lo = split(z[0])
        im_hi, im_lo = split(z[1])
        columns.append(jnp.concatenate([re_hi, im_hi, re_lo, im_lo, re_hi, im_hi], axis=0))
    out = jnp.dot(left_ref[...], jnp.concatenate(columns, axis=1), preferred_element_type=f32)
    return [(out[:WIN, i * WIN : (i + 1) * WIN], out[WIN:, i * WIN : (i + 1) * WIN]) for i in range(len(zs))]


def product(x, y):
    return x[0] * y[0] - x[1] * y[1], x[0] * y[1] + x[1] * y[0]


def product_conj(x, y):
    return x[0] * y[0] + x[1] * y[1], x[0] * y[1] - x[1] * y[0]


def conj(x):
    return x[0], -x[1]


class Fetched:
    def __init__(self, copies):
        self.copies = {}
        for name, (src, dst, sem) in copies.items():
            self.copies[name] = pltpu.make_async_copy(src, dst, sem)
            self.copies[name].start()
        self.refs = {name: dst for name, (_, dst, _) in copies.items()}

    def __getitem__(self, name):
        if name in self.copies:
            self.copies.pop(name).wait()
        return self.refs[name]

    def pair(self, name):
        ref = self[name]
        return ref[0], ref[1]

    def spectrum(self, zs):
        zs = times_left(zs, self["left"])
        return times_right([product(self.pair("twiddle"), z) for z in zs], self["right"])

    def conj_inverse(self, zs):
        zs = times_right(zs, self["right"])
        return times_left([product(self.pair("twiddle"), z) for z in zs], self["left"])


def source(geo, slot, k, plan_ref, mine_ref, map_ref):
    n, columns, me = geo.owners, geo.columns, mine_ref[0]
    row, col = plan_ref[2 * slot * n + me], plan_ref[(2 * slot + 1) * n + me]
    return map_ref[((row + k // columns) & 7) * columns + ((col + k % columns) & (columns - 1))]


def tile_rows(geo, k, a):
    return pl.ds((8 * a + k // geo.columns) * ACROSS + k % geo.columns, geo.cols_b, geo.columns)


def plane(ref, i):
    return jnp.concatenate([ref[2 * i], ref[2 * i + 1]], axis=1)


def put_plane(ref, i, x):
    ref[2 * i] = x[:, :LANES]
    ref[2 * i + 1] = x[:, LANES:]


def put_marks(out_ref, o, at, first, scales):
    rows = scales[0].shape[0]
    lane = lax.broadcasted_iota(i32, (rows, LANES), 1)
    marks = out_ref[o, pl.ds(at, rows), :]
    for i, k in enumerate(scales):
        marks = jnp.where(lane == first + i, k.astype(i32), marks)
    out_ref[o, pl.ds(at, rows), :] = marks


def pack_tiles(geo, slot, refs, tile_ref, out_ref, at, marks_ref, marks_at):
    b = geo.cols_b

    def pack(k, _):
        dst = source(geo, slot, k, *refs)
        scales = []
        for a in range(geo.rows_a):
            x = [tile_ref[j, tile_rows(geo, k, a), :] for j in range(2 * BLOCKS)]
            words, k_low, k_high = encode(
                jnp.concatenate(x[:BLOCKS], axis=1), jnp.concatenate(x[BLOCKS:], axis=1)
            )
            scales += [k_low, k_high]
            for j in range(BLOCKS):
                rows = pl.ds(at + j * geo.tiles + a * b, b)
                out_ref[dst, rows, :] = words[:, j * LANES : (j + 1) * LANES]
        put_marks(marks_ref, dst, marks_at, 2 * geo.rows_a * slot, scales)
        return 0

    lax.fori_loop(0, geo.owners, pack, 0, unroll=4)


def backward(fetched, tile_ref, middle, far, intensity):
    misfit = far[0] * far[0] + far[1] * far[1] - intensity
    (near,) = fetched.conj_inverse([(misfit * far[0], -(misfit * far[1]))])
    grad_middle = conj(product((plane(tile_ref, 2), plane(tile_ref, 3)), near))
    grad_back = product(middle(), conj(near))
    put_plane(tile_ref, 2, grad_back[0])
    put_plane(tile_ref, 3, grad_back[1])
    (f,) = fetched.spectrum([grad_middle])
    (e,) = fetched.conj_inverse([product_conj(f, fetched.pair("chirp"))])
    enter = conj(e)
    grad_probe = product_conj((plane(tile_ref, 0), plane(tile_ref, 1)), enter)
    grad_front = product_conj(fetched.pair("probe"), enter)
    put_plane(tile_ref, 0, grad_front[0])
    put_plane(tile_ref, 1, grad_front[1])
    return grad_probe


def forward_kernel(
    geo, plan_ref, mine_ref, map_ref, in_ref, probe_in, intensity_in, left_in, right_in, twiddle_in, chirp_in,
    out_ref, marks_ref, tile1_hbm, waves_hbm, tile0_ref, tile1_ref, waves_ref, probe_ref, intensity_ref, left_ref, right_ref, twiddle_ref, chirp_ref,
    sems,
):
    fetched = Fetched(
        {
            "probe": (probe_in, probe_ref, sems.at[0]),
            "left": (left_in, left_ref, sems.at[1]),
            "twiddle": (twiddle_in, twiddle_ref, sems.at[2]),
            "right": (right_in, right_ref, sems.at[3]),
            "chirp": (chirp_in, chirp_ref, sems.at[4]),
            "intensity": (intensity_in.at[0], intensity_ref, sems.at[5]),
        }
    )
    n, b = geo.owners, geo.cols_b
    refs = plan_ref, mine_ref, map_ref
    at = geo.block_sent - SCALE_ROWS
    tiles = tile0_ref, tile1_ref

    def unpack(k, _):
        for slot in range(MEAN):
            src = source(geo, slot, k, *refs)
            scales = unscale(in_ref[src, pl.ds(at, b), :])
            for a in range(geo.rows_a):
                c = 2 * (geo.rows_a * slot + a)
                for j in range(BLOCKS):
                    words = in_ref[src, pl.ds(slot * geo.data + j * geo.tiles + a * b, b), :]
                    low, high = decode(words, scales[:, c : c + 1], scales[:, c + 1 : c + 2])
                    tiles[slot][j, tile_rows(geo, k, a), :] = low
                    tiles[slot][BLOCKS + j, tile_rows(geo, k, a), :] = high
        return 0

    lax.fori_loop(0, n, unpack, 0, unroll=4)
    going = [pltpu.make_async_copy(tile1_ref, tile1_hbm, sems.at[6])]
    going[0].start()
    entrance = [product(fetched.pair("probe"), (plane(t, 0), plane(t, 1))) for t in tiles]
    waves = fetched.spectrum(entrance)
    middle = fetched.conj_inverse([conj(product(fetched.pair("chirp"), f)) for f in waves])
    far = fetched.spectrum([product_conj(middle[s], (plane(t, 2), plane(t, 3))) for s, t in enumerate(tiles)])
    for c in range(2):
        waves_ref[c] = far[1][c]
        waves_ref[2 + c] = middle[1][c]
    going.append(pltpu.make_async_copy(waves_ref.at[pl.ds(0, 4)], waves_hbm.at[pl.ds(0, 4)], sems.at[7]))
    going[1].start()
    intensity = fetched["intensity"]
    grad_probe = backward(fetched, tile0_ref, lambda: middle[0], far[0], intensity[...])
    for c in range(2):
        waves_ref[4 + c] = grad_probe[c]
    going.append(pltpu.make_async_copy(waves_ref.at[pl.ds(4, 2)], waves_hbm.at[pl.ds(4, 2)], sems.at[8]))
    going[2].start()
    pack_tiles(geo, 0, refs, tile0_ref, out_ref, 0, marks_ref, 0)
    for copy in going:
        copy.wait()


def backward_kernel(
    geo, plan_ref, mine_ref, map_ref, moved_in, marks_in, probe_in, intensity_in, tile_in, waves_in,
    left_in, right_in, twiddle_in, chirp_in,
    out_ref, tile_ref, moved_ref, waves_ref, probe_ref, intensity_ref, left_ref, right_ref, twiddle_ref, chirp_ref,
    sems,
):
    n, g, me = geo.owners, geo.group, mine_ref[0]
    marks_at = geo.block_second - SCALE_ROWS
    pair = lambda ref, i: ref.at[pl.ds(2 * i, 2)]
    fetched = Fetched(
        {
            "far": (pair(waves_in, 0), pair(waves_ref, 0), sems.at[0]),
            "intensity": (intensity_in.at[1], intensity_ref, sems.at[1]),
            "right": (right_in, right_ref, sems.at[2]),
            "twiddle": (twiddle_in, twiddle_ref, sems.at[3]),
            "left": (left_in, left_ref, sems.at[4]),
            "tile": (tile_in, tile_ref, sems.at[5]),
            "middle": (pair(waves_in, 1), pair(waves_ref, 1), sems.at[6]),
            "chirp": (chirp_in, chirp_ref, sems.at[7]),
            "probe": (probe_in, probe_ref, sems.at[8]),
            "before": (pair(waves_in, 2), pair(waves_ref, 2), sems.at[9]),
            "marks": (marks_in, out_ref.at[:, pl.ds(marks_at, SCALE_ROWS)], sems.at[10]),
        }
    )
    refs = plan_ref, mine_ref, map_ref
    dev = plan_ref[4 * n + me]
    for q in range(SPREAD):
        holder = (dev & -SPREAD) + q
        scales = unscale(moved_in[holder, pl.ds(geo.block_moved - SCALE_ROWS, SCALE_ROWS), :])
        for i in range(QUARTER // 8):
            words = moved_in[holder, pl.ds(8 * i, 8), :]
            low, high = decode(words, scales[:, i : i + 1], scales[:, i : i + 1])
            moved_ref[0, pl.ds(q * QUARTER + 8 * i, 8), :] = low
            moved_ref[1, pl.ds(q * QUARTER + 8 * i, 8), :] = high
    arrived = frequency_digits(jnp.concatenate([moved_ref[0], moved_ref[1]], axis=1))
    intensity = jnp.where(dev == me, fetched["intensity"][...], arrived)
    far = fetched.pair("far")
    fetched["tile"]
    grad_probe = backward(fetched, tile_ref, lambda: fetched.pair("middle"), far, intensity)
    fetched["marks"]
    pack_tiles(geo, 1, refs, tile_ref, out_ref, 0, out_ref, marks_at)
    before = fetched.pair("before")
    for c in range(2):
        put_plane(tile_ref, c, before[c] + grad_probe[c])

    def pieces(o, _):
        scales = []
        for i in range(geo.piece // g):
            x = [tile_ref[j, pl.ds(o * geo.piece + i * g, g), :] for j in range(4)]
            words, k_low, k_high = encode(
                jnp.concatenate(x[:2], axis=1), jnp.concatenate(x[2:], axis=1)
            )
            scales += [k_low, k_high]
            for j in range(2):
                at = pl.ds(geo.data + j * geo.piece + i * g, g)
                out_ref[o, at, :] = words[:, j * LANES : (j + 1) * LANES]
        put_marks(out_ref, o, marks_at, 2 * geo.rows_a * MEAN, scales)
        return 0

    lax.fori_loop(0, n, pieces, 0, unroll=4)


def wave_scratch(consts, copies):
    return (
        [pltpu.VMEM((6, WIN, WIN), f32), pltpu.VMEM((2, WIN, WIN), f32), pltpu.VMEM((WIN, WIN), f32)]
        + [pltpu.VMEM(c.shape, c.dtype) for c in consts]
        + [pltpu.SemaphoreType.DMA((copies,))]
    )


def forward(geo, plan, mine, owner_map, come, probe, intensity, consts):
    tile = (2 * BLOCKS, WIN, LANES)
    return pl.pallas_call(
        functools.partial(forward_kernel, geo),
        out_shape=(
            jax.ShapeDtypeStruct((geo.owners, geo.block_first, LANES), i32),
            jax.ShapeDtypeStruct((geo.owners, SCALE_ROWS, LANES), i32),
            jax.ShapeDtypeStruct(tile, f32),
            jax.ShapeDtypeStruct((6, WIN, WIN), f32),
        ),
        in_specs=[SMEM] * 3 + [VMEM] + [ANY] * 6,
        out_specs=(VMEM, VMEM, ANY, ANY),
        scratch_shapes=[pltpu.VMEM(tile, f32), pltpu.VMEM(tile, f32)] + wave_scratch(consts, 9),
        compiler_params=params(),
        cost_estimate=pl.CostEstimate(flops=20 << 30, bytes_accessed=8 << 20, transcendentals=0),
        name="forward",
    )(plan, mine, owner_map, come, probe, intensity, *consts)


def second_back(geo, plan, mine, owner_map, moved, marks, probe, intensity, tile, waves, consts):
    return pl.pallas_call(
        functools.partial(backward_kernel, geo),
        out_shape=jax.ShapeDtypeStruct((geo.owners, geo.block_second, LANES), i32),
        in_specs=[SMEM] * 3 + [VMEM] + [ANY] * 9,
        out_specs=VMEM,
        scratch_shapes=[pltpu.VMEM(tile.shape, f32), pltpu.VMEM((2, WIN, LANES), f32)] + wave_scratch(consts, 11),
        compiler_params=params(),
        cost_estimate=pl.CostEstimate(flops=6 << 30, bytes_accessed=8 << 20, transcendentals=0),
        name="backward",
    )(plan, mine, owner_map, moved, marks, probe, intensity, tile, waves, *consts)


def add_kernel(geo, plan_ref, mine_ref, first_ref, second_ref, grad_hbm, grad_ref, sems):
    b = geo.cols_b
    grad_ref[...] = jnp.zeros_like(grad_ref)

    def body(o, _):
        scales = unscale(second_ref[o, pl.ds(geo.block_second - SCALE_ROWS, b), :])
        for slot, in_ref in enumerate((first_ref, second_ref)):
            start = first_row(geo, slot, o, plan_ref, mine_ref)
            for a in range(geo.rows_a):
                at = 2 * (geo.rows_a * slot + a)
                k_low, k_high = scales[:, at : at + 1], scales[:, at + 1 : at + 2]
                rows = pl.ds(start + a * geo.grid_cols, b)
                for j in range(BLOCKS):
                    words = in_ref[o, pl.ds(j * geo.tiles + a * b, b), :]
                    low, high = decode(words, k_low, k_high)
                    grad_ref[j, rows, :] += low
                    grad_ref[BLOCKS + j, rows, :] += high
        return 0

    lax.fori_loop(0, geo.owners, body, 0, unroll=2)
    copies = [
        pltpu.make_async_copy(grad_ref.at[j], grad_hbm.at[:, pl.ds(j * LANES, LANES)], sems.at[j])
        for j in range(2 * BLOCKS)
    ]
    for copy in copies:
        copy.start()
    for copy in copies:
        copy.wait()


def add_up(geo, plan, mine, first, second):
    return pl.pallas_call(
        functools.partial(add_kernel, geo),
        out_shape=jax.ShapeDtypeStruct((geo.grid_rows * geo.grid_cols, 2 * HALF), f32),
        in_specs=[SMEM, SMEM, VMEM, VMEM],
        out_specs=ANY,
        scratch_shapes=[
            pltpu.VMEM((2 * BLOCKS, geo.grid_rows * geo.grid_cols, LANES), f32),
            pltpu.SemaphoreType.DMA((2 * BLOCKS,)),
        ],
        compiler_params=params(24),
        cost_estimate=pl.CostEstimate(flops=1 << 23, bytes_accessed=4 << 20, transcendentals=0),
        name="add",
    )(plan, mine, first, second)


def sum_kernel(geo, in_hbm, out_ref, in_ref, sem):
    g = geo.group
    rows = geo.block_second - geo.data
    copy = pltpu.make_async_copy(in_hbm.at[:, pl.ds(geo.data, rows)], in_ref, sem)
    copy.start()
    copy.wait()
    count = geo.piece // g

    def add_piece(o, sums):
        scales = unscale(in_ref[o, pl.ds(rows - SCALE_ROWS, g), :])
        new = []
        for i in range(count):
            at = 2 * (geo.rows_a * MEAN + i)
            k_low, k_high = scales[:, at : at + 1], scales[:, at + 1 : at + 2]
            for j in range(2):
                words = in_ref[o, pl.ds(j * geo.piece + i * g, g), :]
                low, high = decode(words, k_low, k_high)
                new += [sums[len(new)] + low, sums[len(new) + 1] + high]
        return tuple(new)

    sums = lax.fori_loop(0, geo.owners, add_piece, (jnp.zeros((g, LANES), f32),) * (4 * count), unroll=8)
    parts, scales = [], []
    low = jnp.concatenate([jnp.concatenate([sums[4 * i], sums[4 * i + 2]], axis=1) for i in range(count)], axis=0)
    high = jnp.concatenate([jnp.concatenate([sums[4 * i + 1], sums[4 * i + 3]], axis=1) for i in range(count)], axis=0)
    if geo.whole_blocks:
        low, high = swap_tile_digits(low), swap_tile_digits(high)
    for i in range(count):
        rows = slice(i * g, (i + 1) * g)
        words, k_low, k_high = encode(low[rows], high[rows])
        parts.append(words)
        scales += [k_low, k_high]
    marks = put_scales(scales, g)

    def spread(o, _):
        for i in range(count):
            for j in range(2):
                out_ref[o, pl.ds(j * geo.piece + i * g, g), :] = parts[i][:, j * LANES : (j + 1) * LANES]
        out_ref[o, pl.ds(geo.block_probe - SCALE_ROWS, g), :] = marks
        return 0

    lax.fori_loop(0, geo.owners, spread, 0, unroll=8)


def sum_pieces(geo, returned):
    return pl.pallas_call(
        functools.partial(sum_kernel, geo),
        out_shape=jax.ShapeDtypeStruct((geo.owners, geo.block_probe, LANES), i32),
        in_specs=[ANY],
        out_specs=VMEM,
        scratch_shapes=[
            pltpu.VMEM((geo.owners, geo.block_second - geo.data, LANES), i32),
            pltpu.SemaphoreType.DMA,
        ],
        compiler_params=params(24),
        name="sum",
    )(returned)


def finish_kernel(geo, in_ref, out_ref, whole_ref):
    g = geo.group

    def place(o, _):
        scales = unscale(in_ref[o, pl.ds(geo.block_probe - SCALE_ROWS, g), :])
        for i in range(geo.piece // g):
            k_low, k_high = scales[:, 2 * i : 2 * i + 1], scales[:, 2 * i + 1 : 2 * i + 2]
            for j in range(2):
                words = in_ref[o, pl.ds(j * geo.piece + i * g, g), :]
                for c, x in enumerate(decode(words, k_low, k_high)):
                    if geo.whole_blocks:
                        rows = pl.ds(pl.multiple_of(o * geo.piece + i * g, g), g)
                        out_ref[c, rows, pl.ds(j * LANES, LANES)] = x
                    else:
                        whole_ref[c, j, pl.ds(o * geo.piece + i * g, g), :] = x
        return 0

    lax.fori_loop(0, geo.owners, place, 0, unroll=8)
    if not geo.whole_blocks:
        for c in range(2):
            out_ref[c] = swap_tile_digits(jnp.concatenate([whole_ref[c, 0], whole_ref[c, 1]], axis=1))


def finish_probe(geo, parts):
    return pl.pallas_call(
        functools.partial(finish_kernel, geo),
        out_shape=jax.ShapeDtypeStruct((2, WIN, WIN), f32),
        in_specs=[VMEM],
        out_specs=VMEM,
        scratch_shapes=[pltpu.VMEM((2, 2, WIN, LANES), f32)],
        compiler_params=params(24),
        name="finish",
    )(parts)


def exchange(x):
    return lax.all_to_all(x, "scan", split_axis=0, concat_axis=0, tiled=True)


def local(object_tiles, probe, measured, positions, counts, owner_map):
    n = lax.axis_size("scan")
    geo = Geometry(n, object_tiles.shape[1], object_tiles.shape[2])
    consts = [jnp.asarray(t) for t in tables()]
    tiles = object_tiles.reshape(geo.grid_rows * geo.grid_cols, 2 * HALF)

    plan, mine, sent = gather_tiles(geo, counts, positions.transpose(1, 2, 0), owner_map, tiles)
    sent, measured, probe = lax.optimization_barrier((sent, measured, probe))
    come = exchange(sent)
    held = near_quarters(geo, measured)
    moved = moved_quarters(geo, plan, mine, held)
    moved, come = lax.optimization_barrier((moved, come))
    moved = exchange(moved)
    probe_t, intensity = prepare(probe, measured)
    back, marks, tile, waves = forward(geo, plan, mine, owner_map, come, probe_t, intensity, consts)
    back, tile, moved = lax.optimization_barrier((back, tile, moved))
    first = exchange(back)
    second = second_back(geo, plan, mine, owner_map, moved, marks, probe_t, intensity, tile, waves, consts)
    second, first = lax.optimization_barrier((second, first))
    second = exchange(second)
    probe_grad = finish_probe(geo, exchange(sum_pieces(geo, second)))
    grad = add_up(geo, plan, mine, first, second)
    return grad.reshape(object_tiles.shape), probe_grad


def solution(mesh):
    return jax.shard_map(
        local,
        mesh=mesh,
        in_specs=(
            P(("groups", "scan"), None, None, None),
            P("groups", None, None),
            P(("groups", "scan"), None, None),
            P("groups", None, None),
            P("groups"),
            P(),
        ),
        out_specs=(P(("groups", "scan"), None, None, None), P("groups", None, None)),
        check_vma=False,
    )
```
